32 devices in a mesh: dp: 16 (over z, x, core), tensor: 2 (over y).
Axes of the slice: x: 2, y: 2, z: 4, core: 2. Of those that a mesh axis runs over, the one named last changes fastest.
Arguments:
- activations: bfloat16 [10240, 1024], P('dp'), may hold values from -6 to 6
- cotangent: bfloat16 [10240, 1024], P('dp'), may hold values from -6 to 6
- parent_slot: int32 [80], replicated, may hold values from -1 to 79, as said below
- attention_gain: bfloat16 [1024], replicated, may hold values from 0.5 to 1.5
- attention_shift: bfloat16 [1024], replicated, may hold values from -1.75 to 1.75
- joined_weight: bfloat16 [1024, 3072], P(None, 'tensor'), may hold values from -0.25 to 0.25
- joined_bias: bfloat16 [2048], P('tensor'), may hold values from -3 to 3
- output_weight: bfloat16 [1024, 1024], P('tensor'), may hold values from -1.5 to 1.5
- output_bias: bfloat16 [1024], replicated, may hold values from -3 to 3
- feed_gain: bfloat16 [1024], replicated, may hold values from 0.5 to 1.5
- feed_shift: bfloat16 [1024], replicated, may hold values from -1.75 to 1.75
- expand_weight: bfloat16 [1024, 4096], P(None, 'tensor'), may hold values from -0.1875 to 0.1875
- expand_bias: bfloat16 [4096], P('tensor'), may hold values from -3 to 3
- contract_weight: bfloat16 [4096, 1024], P('tensor'), may hold values from -0.1875 to 0.1875
- contract_bias: bfloat16 [1024], replicated, may hold values from -3 to 3
Outputs:
- layer_output: bfloat16 [10240, 1024], P('dp')
- input_gradient: bfloat16 [10240, 1024], P('dp')
- attention_gain_gradient: float32 [1024], P('dp')
- attention_shift_gradient: float32 [1024], P('dp')
- joined_weight_gradient: float32 [1024, 3072], P('dp', 'tensor')
- joined_bias_gradient: float32 [1024, 2], P('dp', 'tensor')
- output_weight_gradient: float32 [1024, 1024], P('dp', 'tensor')
- output_bias_gradient: float32 [1024], P('dp')
- feed_gain_gradient: float32 [1024], P('dp')
- feed_shift_gradient: float32 [1024], P('dp')
- expand_weight_gradient: float32 [1024, 4096], P('dp', 'tensor')
- expand_bias_gradient: float32 [2048, 2], P('dp', 'tensor')
- contract_weight_gradient: float32 [1024, 4096], P('dp', 'tensor')
- contract_bias_gradient: float32 [1024], P('dp')
The draws below stay inside these ranges and needn't reach their ends.
Inputs may be any that keep to these rules, and one draw needn't show every extreme that they name: parent_slot[s] is the slot of segment s's parent, -1 for a tree's root. Each tree has 8 trunk segments in a chain from the root, 4 branch segments whose parent is the last trunk segment, and 2 leaf segments under each branch; the 20 segments of a tree occupy 20 cyclically consecutive slots in any order.
All inputs are finite; a program needn't handle non-finite values.
Results may differ from the reference program's by a relative error of at most 0.017.
Values may be sent and summed in bfloat16 or wider, within the bound.
No kernel may reach another device: no remote copies, remote signals or barrier semaphores. Data moves between devices by JAX's collectives and lax.ppermute only.
A program may use at most 256 MiB of HBM per device.

```python
import jax
import jax.numpy as jnp
from jax import lax

D = 1024
H = 16
HD = 64
FF = 4096
SEG = 128
TRUNK_SEGS = 8
BRANCHES = 4
LEAVES = 2
SEG_DEV = 5
TREE_SEGS = 20
ANC = 10
SEGS = 80
TOKENS = 10240
TREES = 4
N_TENSOR = 2


def tree_order(key):
    return jax.random.permutation(key, TREE_SEGS)


def draw_parent_slot(key, part):
    key = jax.random.fold_in(key, 7)
    shift_key, order_key = jax.random.split(key)
    offset = jax.random.randint(shift_key, (), 1, TREE_SEGS - 1)
    offset = jnp.where(offset % SEG_DEV == 0, offset + 1, offset)
    orders = jax.vmap(tree_order)(jax.random.split(order_key, TREES))
    places = jnp.argsort(orders, axis=1, stable=True)
    roles = jnp.arange(TREE_SEGS)
    parent_role = jnp.where(roles < TRUNK_SEGS, roles - 1, jnp.where(roles < TRUNK_SEGS + BRANCHES, TRUNK_SEGS - 1, TRUNK_SEGS + (roles - TRUNK_SEGS - BRANCHES) // LEAVES))
    wanted = parent_role[orders]
    parent_place = jnp.take_along_axis(places, jnp.maximum(wanted, 0), axis=1)
    starts = jnp.arange(TREES)[:, None] * TREE_SEGS
    linked = jnp.where(wanted >= 0, (offset + starts + parent_place) % SEGS, -1).reshape(-1)
    return jnp.roll(linked, offset).astype(jnp.int32)


def raised(values, key, source, target, blocks, factor):
    owner, partner = [(jnp.arange(values.shape[axis_at]) // (values.shape[axis_at] // blocks)).reshape([-1 if axis == axis_at else 1 for axis in range(values.ndim)]) for axis_at in (source, target)]
    chosen = jax.random.permutation(key, blocks)[partner]
    strong = (owner == chosen) | (owner == (partner + blocks // 2) % blocks)
    return jnp.where(strong, factor * values, values)


def block_scale(stream_key, shape, shards, low, high):
    def one(position, parts):
        heights = jax.random.uniform(jax.random.fold_in(jax.random.fold_in(stream_key, 6), position), (parts,), jnp.float32, low / len(shards), high / len(shards))
        return jnp.repeat(jnp.exp(heights), shape[position] // parts).reshape((-1,) + (1,) * (len(shape) - position - 1))

    level = one(*shards[0])
    for cut in shards[1:]:
        level = level * one(*cut)
    return level


def centred(own_key, shape, scale, bound, cuts=(), kind=jnp.bfloat16):
    values = scale * jax.random.normal(own_key, shape, jnp.float32)
    if cuts:
        values = values * block_scale(own_key, shape, cuts, -0.22, 0.18)
    return jnp.clip(values, -bound, bound).astype(kind)


def bell_draw_with(key, shape, scale, bound, shards, heavy, kind=jnp.bfloat16):
    values = scale * jax.random.normal(key, shape, jnp.float32)
    if shards:
        values = values * block_scale(key, shape, shards, -0.22, 0.18)
    return jnp.clip(raised(values, jax.random.fold_in(key, 3), *heavy), -bound, bound).astype(kind)


def setup_inputs(seed: int = 0) -> dict:
    key_list = jax.random.split(jax.random.key(seed), 16)
    return {
        "activations": centred(key_list[0], (TOKENS, D), 1.0, 6.0, ((0, 16),)),
        "cotangent": bell_draw_with(key_list[1], (TOKENS, D), 1.0, 6.0, ((0, 16),), (0, 1, 16, 2.0)),
        "parent_slot": draw_parent_slot(jax.random.fold_in(key_list[15], 71), 0),
        "attention_gain": jnp.clip(1.0 + 0.1 * jax.random.normal(key_list[3], (D,), jnp.float32), 0.5, 1.5).astype(jnp.bfloat16),
        "attention_shift": centred(key_list[4], (D,), 0.3, 1.75),
        "joined_weight": centred(key_list[5], (D, 3 * H * HD), (D // 2) ** -0.5, 0.25, ((1, 2),)),
        "joined_bias": centred(key_list[6], (H * 2 * HD,), 0.5, 3.0, ((0, 2),)),
        "output_weight": centred(key_list[7], (H * HD, D), (H * HD // 64) ** -0.5, 1.5, ((0, 2),)),
        "output_bias": centred(key_list[8], (D,), 0.5, 3.0),
        "feed_gain": jnp.clip(1.0 + 0.1 * jax.random.normal(key_list[9], (D,), jnp.float32), 0.5, 1.5).astype(jnp.bfloat16),
        "feed_shift": centred(key_list[10], (D,), 0.3, 1.75),
        "expand_weight": centred(key_list[11], (D, FF), D ** -0.5, 0.1875, ((1, 2),)),
        "expand_bias": centred(key_list[12], (FF,), 0.5, 3.0, ((0, 2),)),
        "contract_weight": centred(key_list[13], (FF, D), (FF // 4) ** -0.5, 0.1875, ((0, 2),)),
        "contract_bias": centred(key_list[14], (D,), 0.5, 3.0),
    }


EPSILON = 1e-05
NEGATIVE = -1e+30
HIGH = lax.Precision.HIGHEST

@jax.custom_vjp
def low(v):
    return lax.optimization_barrier(v.astype(jnp.bfloat16)).astype(jnp.float32)

@jax.custom_vjp
def low_back(v):
    return v

def low_keep(v):
    return (low(v), None)

def low_pass(kept, grad):
    return (grad,)

def back_keep(v):
    return (v, None)

def back_low(kept, grad):
    return (low(grad),)
low.defvjp(low_keep, low_pass)
low_back.defvjp(back_keep, back_low)

def norm_rows(rows, gain, shift):
    centered = rows - lax.optimization_barrier(jnp.mean(rows, axis=-1, keepdims=True))
    variance = lax.optimization_barrier(jnp.mean(centered * centered, axis=-1, keepdims=True))
    return centered * lax.rsqrt(variance + EPSILON) * gain + shift

def ancestors_of(parent_slot):
    current = jnp.arange(parent_slot.shape[0], dtype=jnp.int32)
    chain = []
    for level in range(ANC):
        chain.append(current)
        upward = jnp.take(parent_slot, jnp.maximum(current, 0).astype(jnp.int32))
        current = jnp.where(current >= 0, upward, -1).astype(jnp.int32)
    return jnp.stack(chain, axis=1)

def section_one(block, gain, shift, weight, bias):
    normed = low(norm_rows(block, gain, shift))
    joined = jnp.dot(normed, weight, precision=HIGH).reshape(block.shape[0], H, 3, HD)
    pair = bias.reshape(H, 2, HD)
    scale = HD ** (-0.5)
    queries = low_back(low((joined[:, :, 0] + pair[:, 0]) * scale))
    keys = low_back(low(joined[:, :, 1]))
    values = low_back(low(joined[:, :, 2] + pair[:, 1]))
    return (queries, keys, values)

def section_three(block, mixed, out_weight, out_bias, gain, shift, up_weight, up_bias, down_weight, down_bias):
    mixed_low = low_back(low(mixed))
    middle = block + (low_back(jnp.dot(mixed_low, out_weight, precision=HIGH)) + out_bias)
    normed = low(norm_rows(middle, gain, shift))
    pre = low_back(jnp.dot(normed, up_weight, precision=HIGH) + up_bias)
    act = low(jax.nn.gelu(pre, approximate=True))
    return middle + (low_back(jnp.dot(act, down_weight, precision=HIGH)) + down_bias)

def reference(activations, cotangent, parent_slot, attention_gain, attention_shift, joined_weight, joined_bias, output_weight, output_bias, feed_gain, feed_shift, expand_weight, expand_bias, contract_weight, contract_bias):
    weights = tuple((w.astype(jnp.float32) for w in (attention_gain, attention_shift, joined_weight, joined_bias, output_weight, output_bias, feed_gain, feed_shift, expand_weight, expand_bias, contract_weight, contract_bias)))
    residual = activations.astype(jnp.float32)
    ancestors = ancestors_of(parent_slot)
    valid = ancestors >= 0
    picks = jnp.maximum(ancestors, 0).astype(jnp.int32)
    slopes = jnp.exp2(-8.0 * jnp.arange(1, H + 1, dtype=jnp.float32) / H)
    block_rows = TREE_SEGS * SEG
    group = 4
    span = ANC * SEG
    query_pos = jnp.arange(SEG, dtype=jnp.int32)[:, None]
    key_pos = jnp.arange(span, dtype=jnp.int32)[None, :]
    level = key_pos // SEG
    distance = (level * SEG + query_pos - key_pos % SEG).astype(jnp.float32)
    causal = (level > 0) | (key_pos % SEG <= query_pos)

    def forward(rows, params):
        gain_a, shift_a, weight_f, bias_f, weight_o, bias_o, gain_f, shift_f, weight_e, bias_e, weight_c, bias_c = params
        blocks = rows.reshape(-1, block_rows, D)

        def project(block):
            return section_one(block, gain_a, shift_a, weight_f, bias_f)
        queries, keys, values = lax.map(jax.checkpoint(project), blocks)
        query_segs = queries.reshape(SEGS, SEG, H, HD)
        key_segs = keys.reshape(SEGS, SEG, H, HD)
        value_segs = values.reshape(SEGS, SEG, H, HD)

        def attend(start):
            query_block = lax.dynamic_slice_in_dim(query_segs, start, group, 0)
            pick_block = lax.dynamic_slice_in_dim(picks, start, group, 0)
            valid_block = lax.dynamic_slice_in_dim(valid, start, group, 0)
            key_anc = jnp.take(key_segs, pick_block.reshape(-1), axis=0).reshape(group, span, H, HD)
            value_anc = jnp.take(value_segs, pick_block.reshape(-1), axis=0).reshape(group, span, H, HD)
            raw = low_back(jnp.einsum('jqhd,jkhd->jhqk', query_block, key_anc, precision=HIGH))
            allowed = causal[None, None] & jnp.repeat(valid_block, SEG, axis=1)[:, None, None, :]
            scores = jnp.where(allowed, raw - slopes[None, :, None, None] * distance[None, None], NEGATIVE)
            probs = jax.nn.softmax(scores, axis=-1)
            return jnp.einsum('jhqk,jkhd->jqhd', low(probs), value_anc, precision=HIGH)
        starts = jnp.arange(0, SEGS, group, dtype=jnp.int32)
        mixed = lax.map(jax.checkpoint(attend), starts).reshape(-1, block_rows, H * HD)

        def finish(pair):
            return section_three(pair[0], pair[1], weight_o, bias_o, gain_f, shift_f, weight_e, bias_e, weight_c, bias_c)
        return lax.map(jax.checkpoint(finish), (blocks, mixed)).reshape(TOKENS, D)
    output, pullback = jax.vjp(forward, residual, weights)
    input_grad, grads = pullback(cotangent.astype(jnp.float32))
    gain_a, shift_a, weight_f, bias_f, weight_o, bias_o, gain_f, shift_f, weight_e, bias_e, weight_c, bias_c = grads
    return (output.astype(jnp.bfloat16), input_grad.astype(jnp.bfloat16), gain_a, shift_a, weight_f, bias_f.reshape(N_TENSOR, -1).T, weight_o.T, bias_o, gain_f, shift_f, weight_e, bias_e.reshape(N_TENSOR, -1).T, weight_c.T, bias_c)
```

```python
from functools import partial

import jax
import jax.numpy as jnp
from jax import lax
from jax.experimental import pallas as pl
from jax.experimental.pallas import tpu as pltpu
from jax.sharding import PartitionSpec as P

H = 16
HD = 64
SEG = 128
SEG_DEV = 5
ANC = 10
TREE = 20
INNER = 12
MEMBERS = 4
PAIR = 2 * HD
POOL = TREE + 2 * INNER
EMPTY = POOL

EPSILON = 1e-05
NEGATIVE = -1e30

F32 = jnp.float32
BF16 = jnp.bfloat16

DEPTH_AT = TREE * ANC
UP_AT = DEPTH_AT + TREE
DOWN_AT = UP_AT + INNER
TABLE = 256

VM = pl.BlockSpec(memory_space=pltpu.VMEM)
SM = pl.BlockSpec(memory_space=pltpu.SMEM)
ANY = pl.BlockSpec(memory_space=pl.ANY)


def shaped(shape, kind):
    return jax.ShapeDtypeStruct(shape, kind)


def params(mib=48):
    return pltpu.CompilerParams(vmem_limit_bytes=mib * 2**20)


def dot(a, b, dims=((1,), (0,))):
    return lax.dot_general(a, b, (dims, ((), ())), preferred_element_type=F32)


def lanes(shape):
    return lax.broadcasted_iota(jnp.int32, shape, len(shape) - 1)


def rows_of(shape):
    return lax.broadcasted_iota(jnp.int32, shape, len(shape) - 2)


def table_kernel(count, meta, parent, out, inner, place):
    member, group = meta[0], meta[1]
    groups = count // TREE
    below = lax.rem(group + groups - 1, groups)
    above = lax.rem(group + 1, groups)

    def clear(i, _):
        inner[i] = 0
        place[i] = EMPTY
        return _

    lax.fori_loop(0, count, clear, 0)

    def mark(i, _):
        up = parent[i]

        @pl.when(up >= 0)
        def _mark():
            inner[up] = 1

        return _

    lax.fori_loop(0, count, mark, 0)

    def cover(i, mask):
        up = parent[i]
        ahead = lax.rem(up - i + count, count)
        forward = ahead < TREE
        low = jnp.where(forward, i, up)
        length = jnp.where(forward, ahead, count - ahead)
        length = jnp.where(up >= 0, length, 0)
        start = lax.rem(low + 1 + TREE, TREE)
        bits = lax.shift_left(1, length) - 1
        room = TREE - start
        first = lax.shift_left(bits & (lax.shift_left(1, room) - 1), start)
        second = lax.shift_right_logical(bits, room)
        return mask | first | second

    mask = lax.fori_loop(0, 2 * TREE - 1, cover, 0)

    def find(c, found):
        free = (lax.shift_right_logical(mask, c) & 1) == 0
        return jnp.where(free, c, found)

    offset = lax.fori_loop(0, TREE, find, 0)

    for i in range(2 * INNER):
        out[UP_AT + i] = -1

    def own(p, ranks):
        up_rank, down_rank = ranks
        spot = ((p // SEG_DEV) ^ member) * SEG_DEV + lax.rem(p, SEG_DEV)
        slot = group * TREE + p
        place[slot] = spot
        has = inner[slot] == 1
        goes_up = has & (p >= offset) & (offset > 0) & (up_rank < INNER)
        goes_down = has & (p < offset) & (down_rank < INNER)

        @pl.when(goes_up)
        def _up():
            out[UP_AT + up_rank] = spot

        @pl.when(goes_down)
        def _down():
            out[DOWN_AT + down_rank] = spot

        return up_rank + goes_up.astype(jnp.int32), down_rank + goes_down.astype(jnp.int32)

    lax.fori_loop(0, TREE, own, (0, 0))

    def others(p, ranks):
        low_rank, high_rank = ranks
        low_slot = below * TREE + p
        high_slot = above * TREE + p
        low = (inner[low_slot] == 1) & (p >= offset) & (offset > 0) & (low_rank < INNER)
        high = (inner[high_slot] == 1) & (p < offset) & (high_rank < INNER)

        @pl.when(low)
        def _low():
            place[low_slot] = TREE + low_rank

        @pl.when(high)
        def _high():
            place[high_slot] = TREE + INNER + high_rank

        return low_rank + low.astype(jnp.int32), high_rank + high.astype(jnp.int32)

    lax.fori_loop(0, TREE, others, (0, 0))

    def chain(q, _):
        slot = group * TREE + ((q // SEG_DEV) ^ member) * SEG_DEV + lax.rem(q, SEG_DEV)

        def step(a, state):
            at, depth = state
            good = at >= 0
            safe = jnp.maximum(at, 0)
            out[q * ANC + a] = jnp.where(good, place[safe], EMPTY)
            return jnp.where(good, parent[safe], -1), depth + good.astype(jnp.int32)

        _end, depth = lax.fori_loop(0, ANC, step, (slot, 0))
        out[DEPTH_AT + q] = depth
        return _

    lax.fori_loop(0, TREE, chain, 0)


def make_tables(meta, parent):
    count = parent.shape[0]
    return pl.pallas_call(
        partial(table_kernel, count),
        out_shape=shaped((TABLE,), jnp.int32),
        in_specs=[SM, SM],
        out_specs=SM,
        scratch_shapes=[pltpu.SMEM((count,), jnp.int32), pltpu.SMEM((count,), jnp.int32)],
        name="tables",
    )(meta, parent)


def normal(block):
    centered = block - jnp.mean(block, axis=-1, keepdims=True)
    variance = jnp.mean(centered * centered, axis=-1, keepdims=True)
    scale = lax.rsqrt(variance + EPSILON)
    return centered * scale, scale


def project_kernel(meta, x, gain, shift, weight, bias, normed, *outs):
    member = meta[0]
    rows = x.shape[0]
    step = 64

    def norm_step(i, _):
        at = pl.ds(pl.multiple_of(i * step, step), step)
        hat, _scale = normal(x[at, :].astype(F32))
        normed[at, :] = (hat * gain[...].astype(F32) + shift[...].astype(F32)).astype(BF16)
        return _

    lax.fori_loop(0, rows // step, norm_step, 0)
    low = lanes((1, PAIR)) < HD

    def one(d, _):
        pair = member ^ d
        block = weight[:, pl.ds(pl.multiple_of(pair * 3 * PAIR, PAIR), 3 * PAIR)]
        both = bias[:, pl.ds(pl.multiple_of(pair * 2 * PAIR, PAIR), 2 * PAIR)].astype(F32)
        first, second = both[:, :PAIR], both[:, PAIR:]
        query_bias = jnp.where(low, first, pltpu.roll(second, HD, 1))
        value_bias = jnp.where(low, pltpu.roll(first, HD, 1), second)
        joined = dot(normed[...], block)
        t0, t1, t2 = joined[:, :PAIR], joined[:, PAIR : 2 * PAIR], joined[:, 2 * PAIR :]
        queries = (jnp.where(low, t0, t1) + query_bias) * (HD ** (-0.5))
        keys = pltpu.roll(jnp.where(low, t2, t0), HD, 1)
        values = jnp.where(low, t1, t2) + value_bias
        for j in range(MEMBERS):

            @pl.when(d == j)
            def _store():
                outs[j][...] = queries.astype(BF16)
                outs[MEMBERS + j][:, :PAIR] = keys.astype(BF16)
                outs[MEMBERS + j][:, PAIR:] = values.astype(BF16)

        return _

    lax.fori_loop(0, MEMBERS, one, 0)


def project(meta, x, gain, shift, weight, bias):
    rows, width = x.shape
    outs = pl.pallas_call(
        project_kernel,
        out_shape=[shaped((rows, width), BF16)]
        + [shaped((rows, PAIR), BF16)] * MEMBERS
        + [shaped((rows, 2 * PAIR), BF16)] * MEMBERS,
        in_specs=[SM] + [VM] * 5,
        out_specs=[VM] * (1 + 2 * MEMBERS),
        compiler_params=params(),
        name="project",
    )(meta, x, gain, shift, weight, bias)
    return outs[0], outs[1 : 1 + MEMBERS], outs[1 + MEMBERS :]


def pack_kernel(table, kv0, kv1, kv2, kv3, up, down, sem):
    sources = (kv0, kv1, kv2, kv3)
    for side, at, target in ((0, UP_AT, up), (1, DOWN_AT, down)):
        for i in range(INNER):
            spot = jnp.maximum(table[at + i], 0)
            d, s = spot // SEG_DEV, lax.rem(spot, SEG_DEV)
            for j in range(MEMBERS):

                @pl.when(d == j)
                def _start():
                    pltpu.make_async_copy(
                        sources[j].at[pl.ds(pl.multiple_of(s * SEG, SEG), SEG)],
                        target.at[pl.ds(i * SEG, SEG)],
                        sem.at[side * INNER + i],
                    ).start()

    for side, target in ((0, up), (1, down)):
        for i in range(INNER):
            piece = target.at[pl.ds(i * SEG, SEG)]
            pltpu.make_async_copy(piece, piece, sem.at[side * INNER + i]).wait()


def pack(table, pairs):
    out = shaped((INNER * SEG, 2 * PAIR), BF16)
    return pl.pallas_call(
        pack_kernel,
        out_shape=[out, out],
        in_specs=[SM] + [ANY] * MEMBERS,
        out_specs=[ANY] * 2,
        scratch_shapes=[pltpu.SemaphoreType.DMA((2 * INNER,))],
        compiler_params=params(8),
        name="pack",
    )(table, *pairs)


LEVELS = (2, 4, 6, 8, 10)


def split_heads(tile):
    low = lanes((SEG, PAIR)) < HD
    wide = tile.astype(F32)
    zero = jnp.zeros_like(wide)
    return jnp.concatenate(
        [jnp.where(low, wide, zero), jnp.where(low, zero, wide)], axis=0
    ).astype(BF16)


def join_heads(turned):
    top = rows_of((PAIR, SEG)) < HD
    return jnp.where(top, turned[:, :SEG], turned[:, SEG:]).T


def slope_row(slopes, meta):
    first = meta[2]
    return jnp.where(lanes((1, 2 * SEG)) < SEG, slopes[first], slopes[first + 1])


def fill_bias(bias, slope):
    shape = (SEG, 2 * SEG)
    offset = lax.rem(lanes(shape), SEG)
    key = rows_of(shape)
    gap = slope * (key - offset).astype(F32)
    bias[0] = jnp.where(key <= offset, gap, NEGATIVE)
    bias[1] = gap


def load_pool(sources, table_unused, pool, sem):
    kvs, from_below, from_above = sources
    rows = SEG_DEV * SEG
    copies = []
    for j in range(MEMBERS):
        copies.append(
            pltpu.make_async_copy(kvs[j], pool.at[pl.ds(j * rows, rows)], sem.at[j])
        )
    for k, source in enumerate((from_below, from_above)):
        copies.append(
            pltpu.make_async_copy(
                source,
                pool.at[pl.ds((TREE + k * INNER) * SEG, INNER * SEG)],
                sem.at[MEMBERS + k],
            )
        )
    return copies


def segment(ref, at):
    return ref.at[pl.ds(pl.multiple_of(at * SEG, SEG), SEG)]


def attend_kernel(
    table, meta, slopes, q0, q1, q2, q3, kv0, kv1, kv2, kv3, below, above,
    o0, o1, o2, o3, lse, pool, turned, queries, result, bias, sem,
):
    rows = SEG_DEV * SEG
    copies = load_pool(((kv0, kv1, kv2, kv3), below, above), table, pool, sem)
    for j, source in enumerate((q0, q1, q2, q3)):
        copies.append(
            pltpu.make_async_copy(
                source, queries.at[pl.ds(j * rows, rows)], sem.at[MEMBERS + 2 + j]
            )
        )
    for copy in copies:
        copy.start()
    slope = slope_row(slopes, meta)
    fill_bias(bias, slope)
    pool[POOL * SEG :, :] = jnp.zeros((SEG, 2 * PAIR), BF16)
    for copy in copies:
        copy.wait()

    def turn(i, _):
        turned[i] = segment(pool, i)[:, PAIR:].astype(F32).T.astype(BF16)
        return _

    lax.fori_loop(0, POOL + 1, turn, 0)

    def one(s, _):
        depth = table[DEPTH_AT + s]
        for span in LEVELS:

            @pl.when((depth > span - 2) & (depth <= span))
            def _run():
                stacked = split_heads(segment(queries, s)[...])
                spots = [table[s * ANC + a] for a in range(span)]
                scores = []
                for a in range(span):
                    raw = dot(segment(pool, spots[a])[:, :PAIR], stacked, ((1,), (1,)))
                    level = slope * (-float(a * SEG))
                    if a == span - 1:
                        level = level + jnp.where(depth < span, NEGATIVE, 0.0)
                    scores.append(raw + bias[0 if a == 0 else 1] + level)
                top = scores[0]
                for part in scores[1:]:
                    top = jnp.maximum(top, part)
                top = jnp.max(top, axis=0, keepdims=True)
                total = jnp.zeros((1, 2 * SEG), F32)
                out = jnp.zeros((PAIR, 2 * SEG), F32)
                for a in range(span):
                    weights = jnp.exp(scores[a] - top)
                    total = total + jnp.sum(weights, axis=0, keepdims=True)
                    out = out + dot(turned[spots[a]], weights.astype(BF16))
                out = out * (1.0 / total)
                segment(result, s)[...] = join_heads(out).astype(BF16)
                lse[s] = top + jnp.log(total)

        return _

    lax.fori_loop(0, TREE, one, 0)
    copies = [
        pltpu.make_async_copy(result.at[pl.ds(j * rows, rows)], target, sem.at[j])
        for j, target in enumerate((o0, o1, o2, o3))
    ]
    for copy in copies:
        copy.start()
    for copy in copies:
        copy.wait()


def attend(table, meta, slopes, queries, pairs, below, above):
    rows = queries[0].shape[0]
    outs = pl.pallas_call(
        attend_kernel,
        out_shape=[shaped((rows, PAIR), BF16)] * MEMBERS + [shaped((TREE, 1, 2 * SEG), F32)],
        in_specs=[SM] * 3 + [ANY] * (2 * MEMBERS + 2),
        out_specs=[ANY] * MEMBERS + [VM],
        scratch_shapes=[
            pltpu.VMEM(((POOL + 1) * SEG, 2 * PAIR), BF16),
            pltpu.VMEM((POOL + 1, PAIR, SEG), BF16),
            pltpu.VMEM((TREE * SEG, PAIR), BF16),
            pltpu.VMEM((TREE * SEG, PAIR), BF16),
            pltpu.VMEM((2, SEG, 2 * SEG), F32),
            pltpu.SemaphoreType.DMA((2 * MEMBERS + 2,)),
        ],
        compiler_params=params(),
        name="attend",
    )(table, meta, slopes, *queries, *pairs, below, above)
    return outs[:MEMBERS], outs[MEMBERS]


def attend_back_kernel(
    table, meta, slopes, q0, q1, q2, q3, kv0, kv1, kv2, kv3, below, above,
    o0, o1, o2, o3, g0, g1, g2, g3, lse,
    dq0, dq1, dq2, dq3, own, to_below, to_above,
    pool, turned, queries, outs, grads, result, total, small, bias, sem,
):
    rows = SEG_DEV * SEG
    copies = load_pool(((kv0, kv1, kv2, kv3), below, above), table, pool, sem)
    base = MEMBERS + 2
    for k, (sources, target) in enumerate(
        (((q0, q1, q2, q3), queries), ((o0, o1, o2, o3), outs), ((g0, g1, g2, g3), grads))
    ):
        for j, source in enumerate(sources):
            copies.append(
                pltpu.make_async_copy(
                    source, target.at[pl.ds(j * rows, rows)], sem.at[base + k * MEMBERS + j]
                )
            )
    for copy in copies:
        copy.start()
    slope = slope_row(slopes, meta)
    fill_bias(bias, slope)
    pool[POOL * SEG :, :] = jnp.zeros((SEG, 2 * PAIR), BF16)

    def clear(i, _):
        segment(total, i)[...] = jnp.zeros((SEG, 2 * PAIR), F32)
        return _

    lax.fori_loop(0, POOL + 1, clear, 0)
    for copy in copies:
        copy.wait()

    def turn(i, _):
        turned[i] = segment(pool, i)[:, :PAIR].astype(F32).T.astype(BF16)
        return _

    lax.fori_loop(0, POOL + 1, turn, 0)

    def one(s, _):
        depth = table[DEPTH_AT + s]
        for span in LEVELS:

            @pl.when((depth > span - 2) & (depth <= span))
            def _run():
                stacked = split_heads(segment(queries, s)[...])
                grad = segment(grads, s)[...]
                stacked_grad = split_heads(grad)
                product = (grad.astype(F32) * segment(outs, s)[...].astype(F32)).T
                delta = jnp.concatenate(
                    [
                        jnp.sum(product[:HD], axis=0, keepdims=True),
                        jnp.sum(product[HD:], axis=0, keepdims=True),
                    ],
                    axis=1,
                )
                log_total = lse[s]
                spots = [table[s * ANC + a] for a in range(span)]
                query_grad = jnp.zeros((PAIR, 2 * SEG), F32)
                for a in range(span):
                    block = segment(pool, spots[a])
                    raw = dot(block[:, :PAIR], stacked, ((1,), (1,)))
                    level = slope * (-float(a * SEG)) - log_total
                    if a == span - 1:
                        level = level + jnp.where(depth < span, NEGATIVE, 0.0)
                    probs = jnp.exp(raw + bias[0 if a == 0 else 1] + level)
                    prob_grad = dot(block[:, PAIR:], stacked_grad, ((1,), (1,)))
                    score_grad = (probs * (prob_grad - delta)).astype(BF16)
                    into = segment(total, spots[a])
                    into[:, :PAIR] += dot(score_grad, stacked)
                    into[:, PAIR:] += dot(probs.astype(BF16), stacked_grad)
                    query_grad = query_grad + dot(turned[spots[a]], score_grad)
                segment(result, s)[...] = join_heads(query_grad).astype(BF16)

        return _

    lax.fori_loop(0, TREE, one, 0)
    copies = [
        pltpu.make_async_copy(result.at[pl.ds(j * rows, rows)], target, sem.at[j])
        for j, target in enumerate((dq0, dq1, dq2, dq3))
    ]
    copies.append(
        pltpu.make_async_copy(total.at[pl.ds(0, TREE * SEG)], own, sem.at[MEMBERS])
    )
    for copy in copies:
        copy.start()

    def shorten(i, _):
        segment(small, i)[...] = segment(total, TREE + i)[...].astype(BF16)
        return _

    lax.fori_loop(0, 2 * INNER, shorten, 0)
    for k, target in enumerate((to_below, to_above)):
        copy = pltpu.make_async_copy(
            small.at[pl.ds(k * INNER * SEG, INNER * SEG)], target, sem.at[MEMBERS + 1 + k]
        )
        copy.start()
        copies.append(copy)
    for copy in copies:
        copy.wait()


def attend_back(table, meta, slopes, queries, pairs, below, above, outs, grads, lse):
    rows = queries[0].shape[0]
    side = shaped((INNER * SEG, 2 * PAIR), BF16)
    result = pl.pallas_call(
        attend_back_kernel,
        out_shape=[shaped((rows, PAIR), BF16)] * MEMBERS
        + [shaped((TREE * SEG, 2 * PAIR), F32), side, side],
        in_specs=[SM] * 3 + [ANY] * (4 * MEMBERS + 2) + [VM],
        out_specs=[ANY] * (MEMBERS + 3),
        scratch_shapes=[
            pltpu.VMEM(((POOL + 1) * SEG, 2 * PAIR), BF16),
            pltpu.VMEM((POOL + 1, PAIR, SEG), BF16),
            pltpu.VMEM((TREE * SEG, PAIR), BF16),
            pltpu.VMEM((TREE * SEG, PAIR), BF16),
            pltpu.VMEM((TREE * SEG, PAIR), BF16),
            pltpu.VMEM((TREE * SEG, PAIR), BF16),
            pltpu.VMEM(((POOL + 1) * SEG, 2 * PAIR), F32),
            pltpu.VMEM((2 * INNER * SEG, 2 * PAIR), BF16),
            pltpu.VMEM((2, SEG, 2 * SEG), F32),
            pltpu.SemaphoreType.DMA((4 * MEMBERS + 2,)),
        ],
        compiler_params=params(),
        name="attend_back",
    )(table, meta, slopes, *queries, *pairs, below, above, *outs, *grads, lse)
    return result[:MEMBERS], result[MEMBERS], result[MEMBERS + 1], result[MEMBERS + 2]


def gather_back_kernel(table, own, from_above, from_below, k0, k1, k2, k3, total, sem):
    rows = SEG_DEV * SEG
    copy = pltpu.make_async_copy(own, total, sem)
    copy.start()
    copy.wait()
    for at, source in ((UP_AT, from_above), (DOWN_AT, from_below)):

        def add(i, _):
            spot = table[at + i]

            @pl.when(spot >= 0)
            def _add():
                segment(total, spot)[...] += segment(source, i)[...].astype(F32)

            return _

        lax.fori_loop(0, INNER, add, 0)
    for j, target in enumerate((k0, k1, k2, k3)):

        def short(i, _):
            segment(target, i)[...] = segment(total, j * SEG_DEV + i)[...].astype(BF16)
            return _

        lax.fori_loop(0, SEG_DEV, short, 0)


def gather_back(table, own, from_above, from_below):
    rows = SEG_DEV * SEG
    return pl.pallas_call(
        gather_back_kernel,
        out_shape=[shaped((rows, 2 * PAIR), BF16)] * MEMBERS,
        in_specs=[SM, ANY, VM, VM],
        out_specs=[VM] * MEMBERS,
        scratch_shapes=[
            pltpu.VMEM((TREE * SEG, 2 * PAIR), F32),
            pltpu.SemaphoreType.DMA(()),
        ],
        compiler_params=params(),
        name="gather_back",
    )(table, own, from_above, from_below)


def output_kernel(
    meta, x, bias, gain, shift, w_own, w_other, a0, a1, a2, a3, b0, b1, b2, b3,
    mixed_own, middle, normed, mixed, weight, sem,
):
    member, rank = meta[0], meta[3]
    rows, width = x.shape
    half = width // 2
    copies = []
    for k, source in enumerate((w_own, w_other)):
        at = pl.multiple_of((rank ^ k) * half, half)
        copies.append(pltpu.make_async_copy(source, weight.at[pl.ds(at, half)], sem.at[k]))
    for copy in copies:
        copy.start()
    for k, parts in enumerate(((a0, a1, a2, a3), (b0, b1, b2, b3))):
        for d in range(MEMBERS):
            inside = (member ^ d) * PAIR
            at = pl.multiple_of((rank ^ k) * half + inside, PAIR)
            mixed[:, pl.ds(at, PAIR)] = parts[d][...]
            if k == 0:
                mixed_own[:, pl.ds(pl.multiple_of(inside, PAIR), PAIR)] = parts[d][...]
    for copy in copies:
        copy.wait()
    tile = 256

    def column(t, _):
        at = pl.ds(pl.multiple_of(t * tile, tile), tile)
        middle[:, at] = (
            x[:, at].astype(F32) + (dot(mixed[...], weight[:, at]) + bias[:, at].astype(F32))
        )
        return _

    lax.fori_loop(0, width // tile, column, 0)
    step = 64

    def norm_step(i, _):
        at = pl.ds(pl.multiple_of(i * step, step), step)
        hat, _scale = normal(middle[at, :])
        normed[at, :] = (hat * gain[...].astype(F32) + shift[...].astype(F32)).astype(BF16)
        return _

    lax.fori_loop(0, rows // step, norm_step, 0)


def output_stage(meta, x, bias, gain, shift, w_own, w_other, parts_own, parts_other):
    rows, width = x.shape
    return pl.pallas_call(
        output_kernel,
        out_shape=[
            shaped((rows, width // 2), BF16),
            shaped((rows, width), F32),
            shaped((rows, width), BF16),
        ],
        in_specs=[SM] + [VM] * 4 + [ANY] * 2 + [VM] * (2 * MEMBERS),
        out_specs=[VM] * 3,
        scratch_shapes=[
            pltpu.VMEM((rows, width), BF16),
            pltpu.VMEM((width, width), BF16),
            pltpu.SemaphoreType.DMA((2,)),
        ],
        compiler_params=params(),
        name="output_stage",
    )(meta, x, bias, gain, shift, w_own, w_other, *parts_own, *parts_other)


def norm_back(hat, scale, up):
    mean_up = jnp.mean(up, axis=-1, keepdims=True)
    mean_both = jnp.mean(up * hat, axis=-1, keepdims=True)
    return scale * (up - mean_up - hat * mean_both)


def middle_back_kernel(
    meta, middle, part, other, grad, gain, weight,
    middle_grad, branch, vectors, g0, g1, g2, g3,
):
    member = meta[0]
    rows, width = middle.shape
    step = 64
    vectors[...] = jnp.zeros_like(vectors)

    def norm_step(i, _):
        at = pl.ds(pl.multiple_of(i * step, step), step)
        hat, scale = normal(middle[at, :])
        second = part[at, :].astype(F32) + other[at, :].astype(F32)
        back = grad[at, :].astype(F32) + norm_back(hat, scale, second * gain[...].astype(F32))
        middle_grad[at, :] = back
        branch[at, :] = back.astype(BF16)
        vectors[0:1, :] += jnp.sum(second * hat, axis=0, keepdims=True)
        vectors[1:2, :] += jnp.sum(second, axis=0, keepdims=True)
        vectors[2:3, :] += jnp.sum(back, axis=0, keepdims=True)
        vectors[3:4, :] += jnp.sum(grad[at, :].astype(F32), axis=0, keepdims=True)
        return _

    lax.fori_loop(0, rows // step, norm_step, 0)
    for d, target in enumerate((g0, g1, g2, g3)):
        at = pl.multiple_of((member ^ d) * PAIR, PAIR)
        target[...] = dot(branch[...], weight[pl.ds(at, PAIR), :], ((1,), (1,))).astype(BF16)


def middle_back(meta, middle, part, other, grad, gain, weight):
    rows, width = middle.shape
    outs = pl.pallas_call(
        middle_back_kernel,
        out_shape=[shaped((rows, width), F32), shaped((rows, width), BF16), shaped((8, width), F32)]
        + [shaped((rows, PAIR), BF16)] * MEMBERS,
        in_specs=[SM] + [VM] * 6,
        out_specs=[VM] * (3 + MEMBERS),
        compiler_params=params(),
        name="middle_back",
    )(meta, middle, part, other, grad, gain, weight)
    return outs[0], outs[1], outs[2], outs[3:]


def join_kernel(
    meta, x, gain_unused, weight, q0, q1, q2, q3, k0, k1, k2, k3, joined, part, vectors, sums
):
    member = meta[0]
    low = lanes((1, PAIR)) < HD
    for d, (query, both) in enumerate(((q0, k0), (q1, k1), (q2, k2), (q3, k3))):
        wide_q = query[...].astype(F32) * (HD ** (-0.5))
        wide_k = pltpu.roll(both[:, :PAIR].astype(F32), HD, 1)
        wide_v = both[:, PAIR:].astype(F32)
        at = (member ^ d) * 3 * PAIR
        for k, tile in enumerate(
            (
                jnp.where(low, wide_q, wide_k),
                jnp.where(low, wide_v, wide_q),
                jnp.where(low, wide_k, wide_v),
            )
        ):
            spot = pl.ds(pl.multiple_of(at + k * PAIR, PAIR), PAIR)
            joined[:, spot] = tile.astype(BF16)
            sums[0:1, spot] = jnp.sum(tile, axis=0, keepdims=True)
    rows, width = x.shape
    tile = 256

    def column(t, _):
        at = pl.ds(pl.multiple_of(t * tile, tile), tile)
        part[:, at] = dot(joined[...], weight[at, :], ((1,), (1,))).astype(BF16)
        return _

    lax.fori_loop(0, width // tile, column, 0)
    step = 64
    vectors[...] = jnp.zeros_like(vectors)

    def norm_step(i, _):
        at = pl.ds(pl.multiple_of(i * step, step), step)
        hat, _scale = normal(x[at, :].astype(F32))
        first = part[at, :].astype(F32)
        vectors[0:1, :] += jnp.sum(first * hat, axis=0, keepdims=True)
        vectors[1:2, :] += jnp.sum(first, axis=0, keepdims=True)
        return _

    lax.fori_loop(0, rows // step, norm_step, 0)


def join_stage(meta, x, gain, weight, query_grads, pair_grads):
    rows, width = x.shape
    across = weight.shape[1]
    return pl.pallas_call(
        join_kernel,
        out_shape=[
            shaped((rows, across), BF16),
            shaped((rows, width), BF16),
            shaped((8, width), F32),
            shaped((8, across), F32),
        ],
        in_specs=[SM] + [VM] * (3 + 2 * MEMBERS),
        out_specs=[VM] * 4,
        compiler_params=params(),
        name="join_stage",
    )(meta, x, gain, weight, *query_grads, *pair_grads)


def input_back_kernel(x, part, other, gain, middle_grad, out):
    rows = x.shape[0]
    step = 64

    def norm_step(i, _):
        at = pl.ds(pl.multiple_of(i * step, step), step)
        hat, scale = normal(x[at, :].astype(F32))
        first = part[at, :].astype(F32) + other[at, :].astype(F32)
        back = norm_back(hat, scale, first * gain[...].astype(F32))
        out[at, :] = (back + middle_grad[at, :]).astype(BF16)
        return _

    lax.fori_loop(0, rows // step, norm_step, 0)


def input_back(x, part, other, gain, middle_grad):
    return pl.pallas_call(
        input_back_kernel,
        out_shape=shaped(x.shape, BF16),
        in_specs=[VM] * 5,
        out_specs=VM,
        compiler_params=params(),
        name="input_back",
    )(x, part, other, gain, middle_grad)


def swap(value):
    return lax.ppermute(value, "tensor", [(0, 1), (1, 0)])


def to_member(value, d):
    count = lax.axis_size("dp")
    return lax.ppermute(value, "dp", [(i, i ^ d) for i in range(count)])


def to_member_across(value, d):
    count = lax.axis_size("dp")
    pairs = [(i * 2 + t, (i ^ d) * 2 + (1 - t)) for i in range(count) for t in range(2)]
    return lax.ppermute(value, ("dp", "tensor"), pairs)


def to_group(value, by):
    count = lax.axis_size("dp")
    step = by * MEMBERS
    return lax.ppermute(value, "dp", [(i, (i + step) % count) for i in range(count)])


def within(parts):
    return [parts[0]] + [to_member(parts[d], d) for d in range(1, MEMBERS)]


def reduce_rows(value):
    return lax.psum_scatter(value, "dp", scatter_dimension=0, tiled=True)


def reduce_low(value):
    return reduce_rows(value.astype(BF16)).astype(F32)


def shards(
    activations,
    cotangent,
    parent_slot,
    attention_gain,
    attention_shift,
    joined_weight,
    joined_bias,
    output_weight,
    output_bias,
    feed_gain,
    feed_shift,
    expand_weight,
    expand_bias,
    contract_weight,
    contract_bias,
):
    device = lax.axis_index("dp")
    rank = lax.axis_index("tensor")
    member = lax.rem(device, MEMBERS)
    heads_here = joined_weight.shape[1] // (3 * HD)
    meta = jnp.stack(
        [member, device // MEMBERS, rank * heads_here + 2 * member, rank]
    ).astype(jnp.int32)
    slopes = jnp.exp2(-8.0 * jnp.arange(1, H + 1, dtype=F32) / H)

    def row(v):
        return v.reshape(1, -1)

    gain_a, shift_a = row(attention_gain), row(attention_shift)
    gain_f, shift_f = row(feed_gain), row(feed_shift)

    table = make_tables(meta, parent_slot)
    first_low, queries, pairs = project(
        meta, activations, gain_a, shift_a, joined_weight, row(joined_bias)
    )
    other_output_weight = swap(output_weight)
    pairs = within(pairs)
    up, down = pack(table, pairs)
    below = to_group(up, 1)
    above = to_group(down, -1)
    queries = within(queries)
    outs, lse = attend(table, meta, slopes, queries, pairs, below, above)
    parts_own = within(outs)
    parts_other = [to_member_across(outs[d], d) for d in range(MEMBERS)]
    mixed, middle, second_low = output_stage(
        meta, activations, row(output_bias), gain_f, shift_f,
        output_weight, other_output_weight, parts_own, parts_other,
    )

    hidden_grad = jnp.einsum("td,fd->tf", cotangent, contract_weight, preferred_element_type=F32)
    hidden_pre = jnp.dot(second_low, expand_weight, preferred_element_type=F32) + expand_bias.astype(F32)
    hidden_act, gelu_back = jax.vjp(partial(jax.nn.gelu, approximate=True), hidden_pre)
    hidden_low = hidden_act.astype(BF16)
    pre_grad = gelu_back(hidden_grad)[0].astype(BF16)
    second_part = jnp.einsum("tf,df->td", pre_grad, expand_weight, preferred_element_type=F32).astype(BF16)
    second_other = swap(second_part)
    middle_grad, branch_low, feed_vectors, grad_parts = middle_back(
        meta, middle, second_part, second_other, cotangent, gain_f, output_weight
    )
    grad_parts = within(grad_parts)

    feed_part = jnp.dot(hidden_low, contract_weight, preferred_element_type=F32).astype(BF16)
    feed_other = swap(feed_part)
    layer_output = (
        middle + (feed_part.astype(F32) + feed_other.astype(F32)) + contract_bias.astype(F32)
    ).astype(BF16)
    contract_grad = jnp.einsum("td,tf->df", cotangent, hidden_low, preferred_element_type=F32)
    expand_grad = jnp.einsum("td,tf->df", second_low, pre_grad, preferred_element_type=F32)
    expand_bias_grad = jnp.sum(pre_grad.astype(F32), axis=0)
    output_grad = jnp.einsum("td,tf->df", branch_low, mixed, preferred_element_type=F32)

    query_grads, own, to_below, to_above = attend_back(
        table, meta, slopes, queries, pairs, below, above, outs, grad_parts, lse
    )
    from_above = to_group(to_below, -1)
    from_below = to_group(to_above, 1)
    query_grads = within(query_grads)
    pair_grads = within(gather_back(table, own, from_above, from_below))
    joined_grad, first_part, norm_vectors, joined_sums = join_stage(
        meta, activations, gain_a, joined_weight, query_grads, pair_grads
    )
    first_other = swap(first_part)
    input_gradient = input_back(activations, first_part, first_other, gain_a, middle_grad)
    joined_weight_grad = jnp.einsum("td,tf->df", first_low, joined_grad, preferred_element_type=F32)

    width = activations.shape[1]
    chosen = joined_sums[0].reshape(heads_here, 3, HD)
    joined_bias_grad = jnp.stack([chosen[:, 0], chosen[:, 2]], axis=1).reshape(width)
    small = jnp.concatenate(
        [
            feed_vectors[:4].T,
            norm_vectors[:2].T,
            joined_bias_grad.reshape(width, 1),
            expand_bias_grad.reshape(width, 2),
        ],
        axis=1,
    )
    high = small.astype(BF16)
    rest = (small - high.astype(F32)).astype(BF16)
    room = jnp.zeros((width, PAIR - 18), BF16)
    last = reduce_rows(
        jnp.concatenate([joined_weight_grad.astype(BF16), high, rest, room], axis=1)
    ).astype(F32)
    across = joined_weight.shape[1]
    smalls = last[:, across : across + 9] + last[:, across + 9 : across + 18]
    norms = smalls[:, 4:6].T
    norms = norms + swap(norms)

    return (
        layer_output,
        input_gradient,
        norms[0],
        norms[1],
        last[:, :across],
        smalls[:, 6:7],
        reduce_low(output_grad),
        smalls[:, 2],
        smalls[:, 0],
        smalls[:, 1],
        reduce_low(expand_grad),
        smalls[:, 7:9].reshape(-1, 1),
        reduce_low(contract_grad),
        smalls[:, 3],
    )


def solution(mesh):
    in_specs = (
        P("dp", None),
        P("dp", None),
        P(),
        P(),
        P(),
        P(None, "tensor"),
        P("tensor"),
        P("tensor", None),
        P(),
        P(),
        P(),
        P(None, "tensor"),
        P("tensor"),
        P("tensor", None),
        P(),
    )
    out_specs = (
        P("dp", None),
        P("dp", None),
        P("dp"),
        P("dp"),
        P("dp", "tensor"),
        P("dp", "tensor"),
        P("dp", "tensor"),
        P("dp"),
        P("dp"),
        P("dp"),
        P("dp", "tensor"),
        P("dp", "tensor"),
        P("dp", "tensor"),
        P("dp"),
    )
    return jax.shard_map(shards, mesh=mesh, in_specs=in_specs, out_specs=out_specs, check_vma=False)
```

```python
from functools import partial

import jax
import jax.numpy as jnp
from jax import lax
from jax.experimental import pallas as pl
from jax.experimental.pallas import tpu as pltpu
from jax.sharding import PartitionSpec as P

H = 16
HD = 64
SEG = 128
SEG_DEV = 5
ANC = 10
TREE = 20
INNER = 12
MEMBERS = 4
PAIR = 2 * HD
POOL = TREE + 2 * INNER
EMPTY = POOL

EPSILON = 1e-05
NEGATIVE = -1e30

F32 = jnp.float32
BF16 = jnp.bfloat16

LISTS = TREE * ANC
SLOT_AT = (0, 2 * LISTS)
LEVEL_AT = (LISTS, 3 * LISTS)
COUNT_AT = (4 * LISTS, 4 * LISTS + TREE)
UP_AT = 4 * LISTS + 2 * TREE
DOWN_AT = UP_AT + INNER
TABLE = 896

VM = pl.BlockSpec(memory_space=pltpu.VMEM)
SM = pl.BlockSpec(memory_space=pltpu.SMEM)
ANY = pl.BlockSpec(memory_space=pl.ANY)


def shaped(shape, kind):
    return jax.ShapeDtypeStruct(shape, kind)


def params(mib=60):
    return pltpu.CompilerParams(vmem_limit_bytes=mib * 2**20)


def dot(a, b, dims=((1,), (0,))):
    return lax.dot_general(a, b, (dims, ((), ())), preferred_element_type=F32)


def lanes(shape):
    return lax.broadcasted_iota(jnp.int32, shape, len(shape) - 1)


def rows_of(shape):
    return lax.broadcasted_iota(jnp.int32, shape, len(shape) - 2)


def table_kernel(count, meta, parent, out, inner, place):
    member, group = meta[0], meta[1]
    groups = count // TREE
    below = lax.rem(group + groups - 1, groups)
    above = lax.rem(group + 1, groups)

    def clear(i, _):
        inner[i] = 0
        place[i] = EMPTY
        return _

    lax.fori_loop(0, count, clear, 0)

    def mark(i, _):
        up = parent[i]

        @pl.when(up >= 0)
        def _mark():
            inner[up] = 1

        return _

    lax.fori_loop(0, count, mark, 0)

    def cover(i, mask):
        up = parent[i]
        ahead = lax.rem(up - i + count, count)
        forward = ahead < TREE
        low = jnp.where(forward, i, up)
        length = jnp.where(forward, ahead, count - ahead)
        length = jnp.where(up >= 0, length, 0)
        start = lax.rem(low + 1 + TREE, TREE)
        bits = lax.shift_left(1, length) - 1
        room = TREE - start
        first = lax.shift_left(bits & (lax.shift_left(1, room) - 1), start)
        second = lax.shift_right_logical(bits, room)
        return mask | first | second

    mask = lax.fori_loop(0, 2 * TREE - 1, cover, 0)

    def find(c, found):
        free = (lax.shift_right_logical(mask, c) & 1) == 0
        return jnp.where(free, c, found)

    offset = lax.fori_loop(0, TREE, find, 0)

    for i in range(2 * INNER):
        out[UP_AT + i] = -1

    def own(p, ranks):
        up_rank, down_rank = ranks
        spot = ((p // SEG_DEV) ^ member) * SEG_DEV + lax.rem(p, SEG_DEV)
        slot = group * TREE + p
        place[slot] = spot
        has = inner[slot] == 1
        goes_up = has & (p >= offset) & (offset > 0) & (up_rank < INNER)
        goes_down = has & (p < offset) & (down_rank < INNER)

        @pl.when(goes_up)
        def _up():
            out[UP_AT + up_rank] = spot

        @pl.when(goes_down)
        def _down():
            out[DOWN_AT + down_rank] = spot

        return up_rank + goes_up.astype(jnp.int32), down_rank + goes_down.astype(jnp.int32)

    lax.fori_loop(0, TREE, own, (0, 0))

    def others(p, ranks):
        low_rank, high_rank = ranks
        low_slot = below * TREE + p
        high_slot = above * TREE + p
        low = (inner[low_slot] == 1) & (p >= offset) & (offset > 0) & (low_rank < INNER)
        high = (inner[high_slot] == 1) & (p < offset) & (high_rank < INNER)

        @pl.when(low)
        def _low():
            place[low_slot] = TREE + low_rank

        @pl.when(high)
        def _high():
            place[high_slot] = TREE + INNER + high_rank

        return low_rank + low.astype(jnp.int32), high_rank + high.astype(jnp.int32)

    lax.fori_loop(0, TREE, others, (0, 0))

    def chain(q, _):
        slot = group * TREE + ((q // SEG_DEV) ^ member) * SEG_DEV + lax.rem(q, SEG_DEV)
        for i in range(ANC):
            out[SLOT_AT[0] + q * ANC + i] = TREE
            out[SLOT_AT[1] + q * ANC + i] = 2 * INNER
            out[LEVEL_AT[0] + q * ANC + i] = 0
            out[LEVEL_AT[1] + q * ANC + i] = 0

        def step(a, state):
            at, near, far = state
            good = at >= 0
            safe = jnp.maximum(at, 0)
            spot = place[safe]
            is_near = good & (spot < TREE)
            is_far = good & (spot >= TREE)

            @pl.when(is_near)
            def _near():
                out[SLOT_AT[0] + q * ANC + near] = spot
                out[LEVEL_AT[0] + q * ANC + near] = a

            @pl.when(is_far)
            def _far():
                out[SLOT_AT[1] + q * ANC + far] = spot - TREE
                out[LEVEL_AT[1] + q * ANC + far] = a

            return (
                jnp.where(good, parent[safe], -1),
                near + is_near.astype(jnp.int32),
                far + is_far.astype(jnp.int32),
            )

        _end, near, far = lax.fori_loop(0, ANC, step, (slot, 0, 0))
        out[COUNT_AT[0] + q] = near
        out[COUNT_AT[1] + q] = far
        return _

    lax.fori_loop(0, TREE, chain, 0)


def make_tables(meta, parent):
    count = parent.shape[0]
    return pl.pallas_call(
        partial(table_kernel, count),
        out_shape=shaped((TABLE,), jnp.int32),
        in_specs=[SM, SM],
        out_specs=SM,
        scratch_shapes=[pltpu.SMEM((count,), jnp.int32), pltpu.SMEM((count,), jnp.int32)],
        name="tables",
    )(meta, parent)


def normal(block):
    centered = block - jnp.mean(block, axis=-1, keepdims=True)
    variance = jnp.mean(centered * centered, axis=-1, keepdims=True)
    scale = lax.rsqrt(variance + EPSILON)
    return centered * scale, scale


def project_kernel(meta, x, gain, shift, weight, bias, normed, *outs):
    member = meta[0]
    rows = x.shape[0]
    step = 64

    def norm_step(i, _):
        at = pl.ds(pl.multiple_of(i * step, step), step)
        hat, _scale = normal(x[at, :].astype(F32))
        normed[at, :] = (hat * gain[...].astype(F32) + shift[...].astype(F32)).astype(BF16)
        return _

    lax.fori_loop(0, rows // step, norm_step, 0)
    low = lanes((1, PAIR)) < HD

    def one(d, _):
        pair = member ^ d
        block = weight[:, pl.ds(pl.multiple_of(pair * 3 * PAIR, PAIR), 3 * PAIR)]
        both = bias[:, pl.ds(pl.multiple_of(pair * 2 * PAIR, PAIR), 2 * PAIR)].astype(F32)
        first, second = both[:, :PAIR], both[:, PAIR:]
        query_bias = jnp.where(low, first, pltpu.roll(second, HD, 1))
        value_bias = jnp.where(low, pltpu.roll(first, HD, 1), second)
        joined = dot(normed[...], block)
        t0, t1, t2 = joined[:, :PAIR], joined[:, PAIR : 2 * PAIR], joined[:, 2 * PAIR :]
        queries = (jnp.where(low, t0, t1) + query_bias) * (HD ** (-0.5))
        keys = pltpu.roll(jnp.where(low, t2, t0), HD, 1)
        values = jnp.where(low, t1, t2) + value_bias
        for j in range(MEMBERS):

            @pl.when(d == j)
            def _store():
                outs[j][...] = queries.astype(BF16)
                outs[MEMBERS + j][:, :PAIR] = keys.astype(BF16)
                outs[MEMBERS + j][:, PAIR:] = values.astype(BF16)

        return _

    lax.fori_loop(0, MEMBERS, one, 0)


def project(meta, x, gain, shift, weight, bias):
    rows, width = x.shape
    outs = pl.pallas_call(
        project_kernel,
        out_shape=[shaped((rows, width), BF16)]
        + [shaped((rows, PAIR), BF16)] * MEMBERS
        + [shaped((rows, 2 * PAIR), BF16)] * MEMBERS,
        in_specs=[SM] + [VM] * 5,
        out_specs=[VM] * (1 + 2 * MEMBERS),
        compiler_params=params(),
        name="project",
    )(meta, x, gain, shift, weight, bias)
    return outs[0], outs[1 : 1 + MEMBERS], outs[1 + MEMBERS :]


def pack_kernel(table, kv0, kv1, kv2, kv3, up, down, sem):
    sources = (kv0, kv1, kv2, kv3)
    for side, at, target in ((0, UP_AT, up), (1, DOWN_AT, down)):
        for i in range(INNER):
            spot = jnp.maximum(table[at + i], 0)
            d, s = spot // SEG_DEV, lax.rem(spot, SEG_DEV)
            for j in range(MEMBERS):

                @pl.when(d == j)
                def _start():
                    pltpu.make_async_copy(
                        sources[j].at[pl.ds(pl.multiple_of(s * SEG, SEG), SEG)],
                        target.at[pl.ds(i * SEG, SEG)],
                        sem.at[side * INNER + i],
                    ).start()

    for side, target in ((0, up), (1, down)):
        for i in range(INNER):
            piece = target.at[pl.ds(i * SEG, SEG)]
            pltpu.make_async_copy(piece, piece, sem.at[side * INNER + i]).wait()


def pack(table, pairs):
    out = shaped((INNER * SEG, 2 * PAIR), BF16)
    return pl.pallas_call(
        pack_kernel,
        out_shape=[out, out],
        in_specs=[SM] + [ANY] * MEMBERS,
        out_specs=[ANY] * 2,
        scratch_shapes=[pltpu.SemaphoreType.DMA((2 * INNER,))],
        compiler_params=params(8),
        name="pack",
    )(table, *pairs)


LEVELS = (2, 4, 6, 8, 10)


def split_heads(tile):
    low = lanes((SEG, PAIR)) < HD
    wide = tile.astype(F32)
    zero = jnp.zeros_like(wide)
    return jnp.concatenate(
        [jnp.where(low, wide, zero), jnp.where(low, zero, wide)], axis=0
    ).astype(BF16)


def join_heads(turned):
    top = rows_of((PAIR, SEG)) < HD
    return jnp.where(top, turned[:, :SEG], turned[:, SEG:]).T


def slope_row(slopes, meta):
    first = meta[2]
    return jnp.where(lanes((1, 2 * SEG)) < SEG, slopes[first], slopes[first + 1])


def fill_bias(bias, slope):
    shape = (SEG, 2 * SEG)
    offset = lax.rem(lanes(shape), SEG)
    key = rows_of(shape)
    gap = slope * (key - offset).astype(F32)
    bias[0] = jnp.where(key <= offset, gap, NEGATIVE)
    bias[1] = gap


def start_all(copies):
    for copy in copies:
        copy.start()


def wait_all(copies):
    for copy in copies:
        copy.wait()


def loads(sources, target, sem, first):
    copies, at = [], 0
    for k, source in enumerate(sources):
        rows = source.shape[0]
        copies.append(
            pltpu.make_async_copy(source, target.at[pl.ds(at, rows)], sem.at[first + k])
        )
        at += rows
    return copies


def segment(ref, at):
    return ref.at[pl.ds(pl.multiple_of(at * SEG, SEG), SEG)]


def turn_all(pool, turned, count, first):
    def turn(i, _):
        turned[i] = segment(pool, i)[:, first : first + PAIR].astype(F32).T.astype(BF16)
        return _

    lax.fori_loop(0, count, turn, 0)


def entries(table, side, s, span):
    at = s * ANC
    spots = [table[SLOT_AT[side] + at + i] for i in range(span)]
    levels = [table[LEVEL_AT[side] + at + i] for i in range(span)]
    return spots, levels


def level_row(slope, levels, i, count, span):
    row = slope * (levels[i] * (-SEG)).astype(F32)
    if i == span - 1:
        row = row + jnp.where(count < span, NEGATIVE, 0.0)
    return row


def chosen_heads(wide):
    top = rows_of((PAIR, SEG)) < HD
    return jnp.where(top, wide[:, :SEG], wide[:, SEG:])


def weigh(side, span, table, s, slope, bias, pool, turned, stacked):
    count = table[COUNT_AT[side] + s]
    spots, levels = entries(table, side, s, span)
    scores = []
    for i in range(span):
        raw = dot(segment(pool, spots[i])[:, :PAIR], stacked, ((1,), (1,)))
        own = side == 0 and i == 0
        scores.append(raw + bias[0 if own else 1] + level_row(slope, levels, i, count, span))
    top = scores[0]
    for part in scores[1:]:
        top = jnp.maximum(top, part)
    top = jnp.max(top, axis=0, keepdims=True)
    sums, out = None, None
    for i in range(span):
        weights = jnp.exp(scores[i] - top)
        part = dot(turned[spots[i]], weights.astype(BF16))
        sums = weights if sums is None else sums + weights
        out = part if out is None else out + part
    return top, jnp.sum(sums, axis=0, keepdims=True), chosen_heads(out)


def attend_near_kernel(
    table, meta, slopes, q0, q1, q2, q3, kv0, kv1, kv2, kv3,
    kept, stats, pool, turned, queries, bias, sem,
):
    copies = loads((kv0, kv1, kv2, kv3), pool, sem, 0)
    copies += loads((q0, q1, q2, q3), queries, sem, MEMBERS)
    start_all(copies)
    slope = slope_row(slopes, meta)
    fill_bias(bias, slope)
    pool[TREE * SEG :, :] = jnp.zeros((SEG, 2 * PAIR), BF16)
    wait_all(copies)
    turn_all(pool, turned, TREE + 1, PAIR)

    def one(s, _):
        count = table[COUNT_AT[0] + s]
        stacked = split_heads(segment(queries, s)[...])
        for span in LEVELS:

            @pl.when((count > span - 2) & (count <= span))
            def _run():
                top, total, out = weigh(
                    0, span, table, s, slope, bias, pool, turned, stacked
                )
                stats[s, 0:1, :] = top
                stats[s, 1:2, :] = total
                kept[s] = out

        return _

    lax.fori_loop(0, TREE, one, 0)


def attend_near(table, meta, slopes, queries, pairs):
    return pl.pallas_call(
        attend_near_kernel,
        out_shape=[shaped((TREE, PAIR, SEG), F32), shaped((TREE, 8, 2 * SEG), F32)],
        in_specs=[SM] * 3 + [ANY] * (2 * MEMBERS),
        out_specs=[VM, VM],
        scratch_shapes=[
            pltpu.VMEM(((TREE + 1) * SEG, 2 * PAIR), BF16),
            pltpu.VMEM((TREE + 1, PAIR, SEG), BF16),
            pltpu.VMEM((TREE * SEG, PAIR), BF16),
            pltpu.VMEM((2, SEG, 2 * SEG), F32),
            pltpu.SemaphoreType.DMA((2 * MEMBERS,)),
        ],
        compiler_params=params(),
        name="attend_near",
    )(table, meta, slopes, *queries, *pairs)


def attend_far_kernel(
    table, meta, slopes, q0, q1, q2, q3, below, above, kept, stats,
    o0, o1, o2, o3, lse, pool, turned, queries, result, bias, sem,
):
    rows = SEG_DEV * SEG
    copies = loads((below, above), pool, sem, 0)
    copies += loads((q0, q1, q2, q3), queries, sem, 2)
    start_all(copies)
    slope = slope_row(slopes, meta)
    fill_bias(bias, slope)
    pool[2 * INNER * SEG :, :] = jnp.zeros((SEG, 2 * PAIR), BF16)
    wait_all(copies)
    turn_all(pool, turned, 2 * INNER + 1, PAIR)

    def finish(s, top, total, out):
        wide = 1.0 / total
        segment(result, s)[...] = (out * chosen_heads(jnp.broadcast_to(wide, (PAIR, 2 * SEG)))).T.astype(BF16)
        lse[s] = top + jnp.log(total)

    def one(s, _):
        count = table[COUNT_AT[1] + s]

        @pl.when(count == 0)
        def _none():
            finish(s, stats[s, 0:1, :], stats[s, 1:2, :], kept[s])

        for span in LEVELS:

            @pl.when((count > span - 2) & (count <= span) & (count > 0))
            def _run():
                stacked = split_heads(segment(queries, s)[...])
                top, total, out = weigh(
                    1, span, table, s, slope, bias, pool, turned, stacked
                )
                near = stats[s, 0:1, :]
                both = jnp.maximum(near, top)
                near_scale = jnp.exp(near - both)
                far_scale = jnp.exp(top - both)
                total = stats[s, 1:2, :] * near_scale + total * far_scale
                shape = (PAIR, 2 * SEG)
                out = kept[s] * chosen_heads(jnp.broadcast_to(near_scale, shape)) + out * (
                    chosen_heads(jnp.broadcast_to(far_scale, shape))
                )
                finish(s, both, total, out)

        return _

    lax.fori_loop(0, TREE, one, 0)
    copies = [
        pltpu.make_async_copy(result.at[pl.ds(j * rows, rows)], target, sem.at[j])
        for j, target in enumerate((o0, o1, o2, o3))
    ]
    start_all(copies)
    wait_all(copies)


def attend_far(table, meta, slopes, queries, below, above, kept, stats):
    rows = queries[0].shape[0]
    outs = pl.pallas_call(
        attend_far_kernel,
        out_shape=[shaped((rows, PAIR), BF16)] * MEMBERS + [shaped((TREE, 1, 2 * SEG), F32)],
        in_specs=[SM] * 3 + [ANY] * (MEMBERS + 2) + [VM] * 2,
        out_specs=[ANY] * MEMBERS + [VM],
        scratch_shapes=[
            pltpu.VMEM(((2 * INNER + 1) * SEG, 2 * PAIR), BF16),
            pltpu.VMEM((2 * INNER + 1, PAIR, SEG), BF16),
            pltpu.VMEM((TREE * SEG, PAIR), BF16),
            pltpu.VMEM((TREE * SEG, PAIR), BF16),
            pltpu.VMEM((2, SEG, 2 * SEG), F32),
            pltpu.SemaphoreType.DMA((MEMBERS + 2,)),
        ],
        compiler_params=params(),
        name="attend_far",
    )(table, meta, slopes, *queries, below, above, kept, stats)
    return outs[:MEMBERS], outs[MEMBERS]


def spread(side, span, table, s, slope, bias, pool, turned, total, queries, outs, grads, lse):
    count = table[COUNT_AT[side] + s]
    stacked = split_heads(segment(queries, s)[...])
    grad = segment(grads, s)[...]
    stacked_grad = split_heads(grad)
    product = (grad.astype(F32) * segment(outs, s)[...].astype(F32)).T
    delta = jnp.concatenate(
        [
            jnp.sum(product[:HD], axis=0, keepdims=True),
            jnp.sum(product[HD:], axis=0, keepdims=True),
        ],
        axis=1,
    )
    log_total = lse[s]
    spots, levels = entries(table, side, s, span)
    query_grad = None
    for i in range(span):
        block = segment(pool, spots[i])
        raw = dot(block[:, :PAIR], stacked, ((1,), (1,)))
        row = level_row(slope, levels, i, count, span) - log_total
        own = side == 0 and i == 0
        probs = jnp.exp(raw + bias[0 if own else 1] + row)
        prob_grad = dot(block[:, PAIR:], stacked_grad, ((1,), (1,)))
        score_grad = (probs * (prob_grad - delta)).astype(BF16)
        into = segment(total, spots[i])
        into[:, :PAIR] += dot(score_grad, stacked)
        into[:, PAIR:] += dot(probs.astype(BF16), stacked_grad)
        part = dot(turned[spots[i]], score_grad)
        query_grad = part if query_grad is None else query_grad + part
    return chosen_heads(query_grad)


def clear_all(total, count):
    def clear(i, _):
        segment(total, i)[...] = jnp.zeros((SEG, 2 * PAIR), F32)
        return _

    lax.fori_loop(0, count, clear, 0)


def back_far_kernel(
    table, meta, slopes, q0, q1, q2, q3, below, above, o0, o1, o2, o3, g0, g1, g2, g3, lse,
    to_below, to_above, kept,
    pool, turned, queries, outs, grads, total, small, bias, sem,
):
    copies = loads((below, above), pool, sem, 0)
    copies += loads((q0, q1, q2, q3), queries, sem, 2)
    copies += loads((o0, o1, o2, o3), outs, sem, 2 + MEMBERS)
    copies += loads((g0, g1, g2, g3), grads, sem, 2 + 2 * MEMBERS)
    start_all(copies)
    slope = slope_row(slopes, meta)
    fill_bias(bias, slope)
    pool[2 * INNER * SEG :, :] = jnp.zeros((SEG, 2 * PAIR), BF16)
    clear_all(total, 2 * INNER + 1)
    wait_all(copies)
    turn_all(pool, turned, 2 * INNER + 1, 0)

    def one(s, _):
        count = table[COUNT_AT[1] + s]

        @pl.when(count == 0)
        def _none():
            kept[s] = jnp.zeros((PAIR, SEG), F32)

        for span in LEVELS:

            @pl.when((count > span - 2) & (count <= span) & (count > 0))
            def _run():
                kept[s] = spread(
                    1, span, table, s, slope, bias, pool, turned, total, queries, outs, grads, lse
                )

        return _

    lax.fori_loop(0, TREE, one, 0)

    def shorten(i, _):
        segment(small, i)[...] = segment(total, i)[...].astype(BF16)
        return _

    lax.fori_loop(0, 2 * INNER, shorten, 0)
    copies = [
        pltpu.make_async_copy(
            small.at[pl.ds(k * INNER * SEG, INNER * SEG)], target, sem.at[k]
        )
        for k, target in enumerate((to_below, to_above))
    ]
    start_all(copies)
    wait_all(copies)


def back_far(table, meta, slopes, queries, below, above, outs, grads, lse):
    side = shaped((INNER * SEG, 2 * PAIR), BF16)
    return pl.pallas_call(
        back_far_kernel,
        out_shape=[side, side, shaped((TREE, PAIR, SEG), F32)],
        in_specs=[SM] * 3 + [ANY] * (3 * MEMBERS + 2) + [VM],
        out_specs=[ANY] * 2 + [VM],
        scratch_shapes=[
            pltpu.VMEM(((2 * INNER + 1) * SEG, 2 * PAIR), BF16),
            pltpu.VMEM((2 * INNER + 1, PAIR, SEG), BF16),
            pltpu.VMEM((TREE * SEG, PAIR), BF16),
            pltpu.VMEM((TREE * SEG, PAIR), BF16),
            pltpu.VMEM((TREE * SEG, PAIR), BF16),
            pltpu.VMEM(((2 * INNER + 1) * SEG, 2 * PAIR), F32),
            pltpu.VMEM((2 * INNER * SEG, 2 * PAIR), BF16),
            pltpu.VMEM((2, SEG, 2 * SEG), F32),
            pltpu.SemaphoreType.DMA((3 * MEMBERS + 2,)),
        ],
        compiler_params=params(),
        name="back_far",
    )(table, meta, slopes, *queries, below, above, *outs, *grads, lse)


def back_near_kernel(
    table, meta, slopes, q0, q1, q2, q3, kv0, kv1, kv2, kv3, o0, o1, o2, o3, g0, g1, g2, g3,
    lse, kept, dq0, dq1, dq2, dq3, own,
    pool, turned, queries, outs, grads, result, total, bias, sem,
):
    rows = SEG_DEV * SEG
    copies = loads((kv0, kv1, kv2, kv3), pool, sem, 0)
    copies += loads((q0, q1, q2, q3), queries, sem, MEMBERS)
    copies += loads((o0, o1, o2, o3), outs, sem, 2 * MEMBERS)
    copies += loads((g0, g1, g2, g3), grads, sem, 3 * MEMBERS)
    start_all(copies)
    slope = slope_row(slopes, meta)
    fill_bias(bias, slope)
    pool[TREE * SEG :, :] = jnp.zeros((SEG, 2 * PAIR), BF16)
    clear_all(total, TREE + 1)
    wait_all(copies)
    turn_all(pool, turned, TREE + 1, 0)

    def one(s, _):
        count = table[COUNT_AT[0] + s]
        for span in LEVELS:

            @pl.when((count > span - 2) & (count <= span))
            def _run():
                part = spread(
                    0, span, table, s, slope, bias, pool, turned, total, queries, outs, grads, lse
                )
                segment(result, s)[...] = (kept[s] + part).T.astype(BF16)

        return _

    lax.fori_loop(0, TREE, one, 0)
    copies = [
        pltpu.make_async_copy(result.at[pl.ds(j * rows, rows)], target, sem.at[j])
        for j, target in enumerate((dq0, dq1, dq2, dq3))
    ]
    copies.append(
        pltpu.make_async_copy(total.at[pl.ds(0, TREE * SEG)], own, sem.at[MEMBERS])
    )
    start_all(copies)
    wait_all(copies)


def back_near(table, meta, slopes, queries, pairs, outs, grads, lse, kept):
    rows = queries[0].shape[0]
    result = pl.pallas_call(
        back_near_kernel,
        out_shape=[shaped((rows, PAIR), BF16)] * MEMBERS + [shaped((TREE * SEG, 2 * PAIR), F32)],
        in_specs=[SM] * 3 + [ANY] * (4 * MEMBERS) + [VM] * 2,
        out_specs=[ANY] * (MEMBERS + 1),
        scratch_shapes=[
            pltpu.VMEM(((TREE + 1) * SEG, 2 * PAIR), BF16),
            pltpu.VMEM((TREE + 1, PAIR, SEG), BF16),
            pltpu.VMEM((TREE * SEG, PAIR), BF16),
            pltpu.VMEM((TREE * SEG, PAIR), BF16),
            pltpu.VMEM((TREE * SEG, PAIR), BF16),
            pltpu.VMEM((TREE * SEG, PAIR), BF16),
            pltpu.VMEM(((TREE + 1) * SEG, 2 * PAIR), F32),
            pltpu.VMEM((2, SEG, 2 * SEG), F32),
            pltpu.SemaphoreType.DMA((4 * MEMBERS,)),
        ],
        compiler_params=params(),
        name="back_near",
    )(table, meta, slopes, *queries, *pairs, *outs, *grads, lse, kept)
    return result[:MEMBERS], result[MEMBERS]


def gather_back_kernel(table, own, from_above, from_below, k0, k1, k2, k3, total, sem):
    rows = SEG_DEV * SEG
    copy = pltpu.make_async_copy(own, total, sem)
    copy.start()
    copy.wait()
    for at, source in ((UP_AT, from_above), (DOWN_AT, from_below)):

        def add(i, _):
            spot = table[at + i]

            @pl.when(spot >= 0)
            def _add():
                segment(total, spot)[...] += segment(source, i)[...].astype(F32)

            return _

        lax.fori_loop(0, INNER, add, 0)
    for j, target in enumerate((k0, k1, k2, k3)):

        def short(i, _):
            segment(target, i)[...] = segment(total, j * SEG_DEV + i)[...].astype(BF16)
            return _

        lax.fori_loop(0, SEG_DEV, short, 0)


def gather_back(table, own, from_above, from_below):
    rows = SEG_DEV * SEG
    return pl.pallas_call(
        gather_back_kernel,
        out_shape=[shaped((rows, 2 * PAIR), BF16)] * MEMBERS,
        in_specs=[SM, ANY, VM, VM],
        out_specs=[VM] * MEMBERS,
        scratch_shapes=[
            pltpu.VMEM((TREE * SEG, 2 * PAIR), F32),
            pltpu.SemaphoreType.DMA(()),
        ],
        compiler_params=params(),
        name="gather_back",
    )(table, own, from_above, from_below)


TILE = 256
NORM_ROWS = 32


def norm_loop(rows, body):
    def step(i, _):
        body(pl.ds(pl.multiple_of(i * NORM_ROWS, NORM_ROWS), NORM_ROWS))
        return _

    lax.fori_loop(0, rows // NORM_ROWS, step, 0)


def feed_kernel(
    meta, x, out_bias, gain, shift, up_bias, a0, a1, a2, a3, b0, b1, b2, b3,
    w_own, w_other, w_up, hidden_grad,
    mixed_out, middle_out, normed_out, act_out, pre_out, part, sums,
    mixed_own, middle, normed, act, pre_grad, mixed, weight, up, hidden, sem, out_sem,
):
    member, rank = meta[0], meta[3]
    rows, width = x.shape
    half = width // 2
    inner = w_up.shape[1]
    copies = []
    for k, source in enumerate((w_own, w_other)):
        at = pl.multiple_of((rank ^ k) * half, half)
        copies.append(pltpu.make_async_copy(source, weight.at[pl.ds(at, half)], sem.at[k]))
    late = [
        pltpu.make_async_copy(w_up, up, sem.at[2]),
        pltpu.make_async_copy(hidden_grad, hidden, sem.at[3]),
    ]
    start_all(copies + late)
    for k, parts in enumerate(((a0, a1, a2, a3), (b0, b1, b2, b3))):
        for d in range(MEMBERS):
            inside = (member ^ d) * PAIR
            at = pl.multiple_of((rank ^ k) * half + inside, PAIR)
            mixed[:, pl.ds(at, PAIR)] = parts[d][...]
            if k == 0:
                mixed_own[:, pl.ds(pl.multiple_of(inside, PAIR), PAIR)] = parts[d][...]
    stores = [pltpu.make_async_copy(mixed_own, mixed_out, out_sem.at[0])]
    stores[0].start()
    wait_all(copies)

    def column(t, _):
        at = pl.ds(pl.multiple_of(t * TILE, TILE), TILE)
        middle[:, at] = (
            x[:, at].astype(F32) + (dot(mixed[...], weight[:, at]) + out_bias[:, at].astype(F32))
        )
        return _

    lax.fori_loop(0, width // TILE, column, 0)
    stores.append(pltpu.make_async_copy(middle, middle_out, out_sem.at[1]))
    stores[1].start()

    def norm_step(at):
        hat, _scale = normal(middle[at, :])
        normed[at, :] = (hat * gain[...].astype(F32) + shift[...].astype(F32)).astype(BF16)

    norm_loop(rows, norm_step)
    stores.append(pltpu.make_async_copy(normed, normed_out, out_sem.at[2]))
    stores[2].start()
    wait_all(late)

    def hidden_step(t, _):
        at = pl.ds(pl.multiple_of(t * TILE, TILE), TILE)
        pre = dot(normed[...], up[:, at]) + up_bias[:, at].astype(F32)
        square = pre * pre
        c = 0.7978845608028654
        t_ = jnp.tanh(pre * (c + (c * 0.044715) * square))
        low = 0.5 * (1.0 + t_)
        act[:, at] = (pre * low).astype(BF16)
        slope = low + (0.5 * pre) * (1.0 - t_ * t_) * (c + (3.0 * c * 0.044715) * square)
        grad = (hidden[:, at] * slope).astype(BF16)
        pre_grad[:, at] = grad
        sums[0:1, at] = jnp.sum(grad.astype(F32), axis=0, keepdims=True)
        return _

    lax.fori_loop(0, inner // TILE, hidden_step, 0)
    stores.append(pltpu.make_async_copy(act, act_out, out_sem.at[3]))
    stores.append(pltpu.make_async_copy(pre_grad, pre_out, out_sem.at[4]))
    start_all(stores[3:])

    def back(t, _):
        at = pl.ds(pl.multiple_of(t * TILE, TILE), TILE)
        part[:, at] = dot(pre_grad[...], up[at, :], ((1,), (1,))).astype(BF16)
        return _

    lax.fori_loop(0, width // TILE, back, 0)
    wait_all(stores)


def feed(meta, x, out_bias, gain, shift, up_bias, parts_own, parts_other, w_own, w_other, w_up, hidden_grad):
    rows, width = x.shape
    inner = w_up.shape[1]
    half = width // 2
    return pl.pallas_call(
        feed_kernel,
        out_shape=[
            shaped((rows, half), BF16),
            shaped((rows, width), F32),
            shaped((rows, width), BF16),
            shaped((rows, inner), BF16),
            shaped((rows, inner), BF16),
            shaped((rows, width), BF16),
            shaped((8, inner), F32),
        ],
        in_specs=[SM] + [VM] * (5 + 2 * MEMBERS) + [ANY] * 4,
        out_specs=[ANY] * 5 + [VM] * 2,
        scratch_shapes=[
            pltpu.VMEM((rows, half), BF16),
            pltpu.VMEM((rows, width), F32),
            pltpu.VMEM((rows, width), BF16),
            pltpu.VMEM((rows, inner), BF16),
            pltpu.VMEM((rows, inner), BF16),
            pltpu.VMEM((rows, width), BF16),
            pltpu.VMEM((width, width), BF16),
            pltpu.VMEM((width, inner), BF16),
            pltpu.VMEM((rows, inner), F32),
            pltpu.SemaphoreType.DMA((4,)),
            pltpu.SemaphoreType.DMA((5,)),
        ],
        compiler_params=params(),
        name="feed",
    )(meta, x, out_bias, gain, shift, up_bias, *parts_own, *parts_other, w_own, w_other, w_up, hidden_grad)


def turn_rows(source, target):
    def step(i, _):
        at = pl.ds(pl.multiple_of(i * SEG, SEG), SEG)
        target[at, :] = source[:, at].astype(F32).T.astype(BF16)
        return _

    lax.fori_loop(0, source.shape[1] // SEG, step, 0)


def feed_grads_kernel(grad, act, normed, pre_grad, out, turned):
    t = pl.program_id(0)
    tiles = pl.num_programs(0) // 2

    @pl.when(t == 0)
    def _first():
        turn_rows(grad, turned)

    @pl.when(t == tiles)
    def _second():
        turn_rows(normed, turned)

    @pl.when(t < tiles)
    def _contract():
        out[...] = dot(turned[...], act[...]).astype(BF16)

    @pl.when(t >= tiles)
    def _expand():
        out[...] = dot(turned[...], pre_grad[...]).astype(BF16)


def feed_grads(grad, act, normed, pre_grad, across):
    rows, width = grad.shape
    tiles = act.shape[1] // TILE
    whole = pl.BlockSpec((rows, width), lambda t: (0, 0))
    return pl.pallas_call(
        feed_grads_kernel,
        grid=(2 * tiles,),
        out_shape=shaped((width, across), BF16),
        in_specs=[
            whole,
            pl.BlockSpec((rows, TILE), lambda t: (0, jnp.minimum(t, tiles - 1))),
            whole,
            pl.BlockSpec((rows, TILE), lambda t: (0, jnp.maximum(t - tiles, 0))),
        ],
        out_specs=pl.BlockSpec((width, TILE), lambda t: (0, t)),
        scratch_shapes=[pltpu.VMEM((width, rows), BF16)],
        compiler_params=params(),
        name="feed_grads",
    )(grad, act, normed, pre_grad)


def in_two(rows8):
    high = rows8.astype(BF16).astype(F32)
    low = rows8 - high
    return jnp.concatenate([high, low, jnp.zeros((SEG - 16, rows8.shape[1]), F32)], axis=0)


def output_grads_kernel(branch, mixed, vectors, extra, held, out, turned, result, small, sem):
    width, half = branch.shape[1], mixed.shape[1]
    turn_rows(branch, turned)

    def column(t, _):
        at = pl.ds(pl.multiple_of(t * TILE, TILE), TILE)
        result[:, at] = dot(turned[...], mixed[:, at]).astype(BF16)
        return _

    lax.fori_loop(0, half // TILE, column, 0)
    for i in range(width // SEG):
        at = slice(i * SEG, (i + 1) * SEG)
        rows8 = jnp.concatenate([vectors[0:4, at], extra[0:2, at], jnp.zeros((2, SEG), F32)], axis=0)
        small[at, :] = in_two(rows8).T.astype(BF16)
    first = out.shape[1] - half - SEG
    copies = [
        pltpu.make_async_copy(result, out.at[:, pl.ds(first, half)], sem.at[0]),
        pltpu.make_async_copy(small, out.at[:, pl.ds(first + half, SEG)], sem.at[1]),
    ]
    start_all(copies)
    wait_all(copies)


def output_grads(branch, mixed, vectors, extra, held):
    rows, width = branch.shape
    half = mixed.shape[1]
    return pl.pallas_call(
        output_grads_kernel,
        out_shape=shaped(held.shape, held.dtype),
        in_specs=[VM] * 4 + [ANY],
        out_specs=ANY,
        input_output_aliases={4: 0},
        scratch_shapes=[
            pltpu.VMEM((width, rows), BF16),
            pltpu.VMEM((width, half), BF16),
            pltpu.VMEM((width, SEG), BF16),
            pltpu.SemaphoreType.DMA((2,)),
        ],
        compiler_params=params(),
        name="output_grads",
    )(branch, mixed, vectors, extra, held)


def feed_finish_kernel(inner, got, contract, expand, output, v0, v1, v2, v3, bias):
    rows = got.shape[0]
    half = output.shape[1]
    contract[...] = got[:, :inner].astype(F32)
    expand[...] = got[:, inner : 2 * inner].astype(F32)
    output[...] = got[:, 2 * inner : 2 * inner + half].astype(F32)
    small = got[:, 2 * inner + half :].astype(F32).T
    whole = small[0:8] + small[8:16]
    for k, target in enumerate((v0, v1, v2, v3)):
        target[...] = whole[k : k + 1]
    bias[...] = whole[4:6]


def feed_finish(got, inner, half):
    rows = got.shape[0]
    return pl.pallas_call(
        partial(feed_finish_kernel, inner),
        out_shape=[shaped((rows, inner), F32)] * 2
        + [shaped((rows, half), F32)]
        + [shaped((1, rows), F32)] * 4
        + [shaped((2, rows), F32)],
        in_specs=[VM],
        out_specs=[VM] * 8,
        compiler_params=params(),
        name="feed_finish",
    )(got)


def norm_back(hat, scale, up):
    mean_up = jnp.mean(up, axis=-1, keepdims=True)
    mean_both = jnp.mean(up * hat, axis=-1, keepdims=True)
    return scale * (up - mean_up - hat * mean_both)


def middle_back_kernel(
    meta, middle, part, other, grad, gain, weight,
    middle_grad, branch, vectors, g0, g1, g2, g3,
):
    member = meta[0]
    rows, width = middle.shape
    step = 64
    vectors[...] = jnp.zeros_like(vectors)

    def norm_step(i, _):
        at = pl.ds(pl.multiple_of(i * step, step), step)
        hat, scale = normal(middle[at, :])
        second = part[at, :].astype(F32) + other[at, :].astype(F32)
        back = grad[at, :].astype(F32) + norm_back(hat, scale, second * gain[...].astype(F32))
        middle_grad[at, :] = back
        branch[at, :] = back.astype(BF16)
        vectors[0:1, :] += jnp.sum(second * hat, axis=0, keepdims=True)
        vectors[1:2, :] += jnp.sum(second, axis=0, keepdims=True)
        vectors[2:3, :] += jnp.sum(back, axis=0, keepdims=True)
        vectors[3:4, :] += jnp.sum(grad[at, :].astype(F32), axis=0, keepdims=True)
        return _

    lax.fori_loop(0, rows // step, norm_step, 0)
    for d, target in enumerate((g0, g1, g2, g3)):
        at = pl.multiple_of((member ^ d) * PAIR, PAIR)
        target[...] = dot(branch[...], weight[pl.ds(at, PAIR), :], ((1,), (1,))).astype(BF16)


def middle_back(meta, middle, part, other, grad, gain, weight):
    rows, width = middle.shape
    outs = pl.pallas_call(
        middle_back_kernel,
        out_shape=[shaped((rows, width), F32), shaped((rows, width), BF16), shaped((8, width), F32)]
        + [shaped((rows, PAIR), BF16)] * MEMBERS,
        in_specs=[SM] + [VM] * 6,
        out_specs=[VM] * (3 + MEMBERS),
        compiler_params=params(),
        name="middle_back",
    )(meta, middle, part, other, grad, gain, weight)
    return outs[0], outs[1], outs[2], outs[3:]


def join_kernel(meta, weight, q0, q1, q2, q3, k0, k1, k2, k3, joined, part, sums):
    member = meta[0]
    low = lanes((1, PAIR)) < HD
    for d, (query, both) in enumerate(((q0, k0), (q1, k1), (q2, k2), (q3, k3))):
        wide_q = query[...].astype(F32) * (HD ** (-0.5))
        wide_k = pltpu.roll(both[:, :PAIR].astype(F32), HD, 1)
        wide_v = both[:, PAIR:].astype(F32)
        at = (member ^ d) * 3 * PAIR
        for k, tile in enumerate(
            (
                jnp.where(low, wide_q, wide_k),
                jnp.where(low, wide_v, wide_q),
                jnp.where(low, wide_k, wide_v),
            )
        ):
            joined[:, pl.ds(pl.multiple_of(at + k * PAIR, PAIR), PAIR)] = tile.astype(BF16)
        sum_q = jnp.sum(wide_q, axis=0, keepdims=True)
        sum_v = jnp.sum(wide_v, axis=0, keepdims=True)
        spot = pl.multiple_of((member ^ d) * 2 * PAIR, PAIR)
        sums[0:1, pl.ds(spot, PAIR)] = jnp.where(low, sum_q, pltpu.roll(sum_v, HD, 1))
        sums[0:1, pl.ds(pl.multiple_of(spot + PAIR, PAIR), PAIR)] = jnp.where(
            low, pltpu.roll(sum_q, HD, 1), sum_v
        )
    width = weight.shape[0]

    def column(t, _):
        at = pl.ds(pl.multiple_of(t * TILE, TILE), TILE)
        part[:, at] = dot(joined[...], weight[at, :], ((1,), (1,))).astype(BF16)
        return _

    lax.fori_loop(0, width // TILE, column, 0)


def join_stage(meta, weight, query_grads, pair_grads):
    rows = query_grads[0].shape[0]
    width, across = weight.shape
    return pl.pallas_call(
        join_kernel,
        out_shape=[
            shaped((rows, across), BF16),
            shaped((rows, width), BF16),
            shaped((8, 2 * MEMBERS * PAIR), F32),
        ],
        in_specs=[SM] + [VM] * (1 + 2 * MEMBERS),
        out_specs=[VM] * 3,
        compiler_params=params(),
        name="join_stage",
    )(meta, weight, *query_grads, *pair_grads)


ORDERS = ((0, 1, 2, 3), (0, 2, 3, 1))
FIRST_PART = 1024


def block_place(relative, order):
    place = 0
    for bit in order:
        place = place * 2 + (lax.shift_right_logical(relative, bit) & 1)
    return place


def turn_ordered(tile, target, i, device, order, share):
    for k in range(SEG // share):
        block = i * (SEG // share) + k
        at = block_place(block ^ device, order) * share
        target[pl.ds(pl.multiple_of(at, share), share), :] = tile[k * share : (k + 1) * share]


def turn_source(source, target, device, order, share):
    def step(i, _):
        at = pl.ds(pl.multiple_of(i * SEG, SEG), SEG)
        tile = source[:, at].astype(F32).T.astype(BF16)
        turn_ordered(tile, target, i, device, order, share)
        return _

    lax.fori_loop(0, source.shape[1] // SEG, step, 0)


def joined_first_kernel(meta, x, part, normed, joined, keep, send, vectors, turned):
    rows, width = x.shape
    device = meta[4]
    turn_source(normed, turned, device, ORDERS[0], width // 16)
    half = width // 2
    tile = TILE

    def column(t, _):
        at = pl.ds(pl.multiple_of(t * tile, tile), tile)
        keep[:, at] = dot(turned[:half], joined[:, at])
        send[:, at] = dot(turned[half:], joined[:, at]).astype(BF16)
        return _

    lax.fori_loop(0, keep.shape[1] // tile, column, 0)
    vectors[...] = jnp.zeros_like(vectors)

    def norm_step(at):
        hat, _scale = normal(x[at, :].astype(F32))
        first = part[at, :].astype(F32)
        vectors[0:1, :] += jnp.sum(first * hat, axis=0, keepdims=True)
        vectors[1:2, :] += jnp.sum(first, axis=0, keepdims=True)

    norm_loop(rows, norm_step)


def joined_first(meta, x, part, normed, joined):
    rows, width = x.shape
    half = width // 2
    return pl.pallas_call(
        joined_first_kernel,
        out_shape=[
            shaped((half, FIRST_PART), F32),
            shaped((half, FIRST_PART), BF16),
            shaped((8, width), F32),
        ],
        in_specs=[SM] + [VM] * 4,
        out_specs=[VM] * 3,
        scratch_shapes=[pltpu.VMEM((width, rows), BF16)],
        compiler_params=params(),
        name="joined_first",
    )(meta, x, part, normed, joined)


def joined_second_kernel(meta, normed, joined, vectors, other, sums, keep, send, turned, small):
    width = normed.shape[1]
    device = meta[4]
    share = width // 16
    turn_source(normed, turned, device, ORDERS[1], share)
    half = width // 2
    across = joined.shape[1] - FIRST_PART
    tile = TILE

    def column(t, _):
        at = pl.ds(pl.multiple_of(t * tile, tile), tile)
        source = pl.ds(pl.multiple_of(FIRST_PART + t * tile, tile), tile)
        keep[:, at] = dot(turned[:half], joined[:, source])
        send[:, at] = dot(turned[half:], joined[:, source]).astype(BF16)
        return _

    lax.fori_loop(0, across // tile, column, 0)
    for i in range(width // SEG):
        at = slice(i * SEG, (i + 1) * SEG)
        rows8 = jnp.concatenate(
            [vectors[0:2, at] + other[0:2, at], sums[0:1, at], jnp.zeros((5, SEG), F32)], axis=0
        )
        turn_ordered(in_two(rows8).T, small, i, device, ORDERS[1], share)
    keep[:, across:] = small[:half]
    send[:, across:] = small[half:].astype(BF16)


def joined_second(meta, normed, joined, vectors, other, sums):
    rows, width = normed.shape
    half = width // 2
    across = joined.shape[1] - FIRST_PART + SEG
    return pl.pallas_call(
        joined_second_kernel,
        out_shape=[shaped((half, across), F32), shaped((half, across), BF16)],
        in_specs=[SM] + [VM] * 5,
        out_specs=[VM] * 2,
        scratch_shapes=[pltpu.VMEM((width, rows), BF16), pltpu.VMEM((width, SEG), F32)],
        compiler_params=params(),
        name="joined_second",
    )(meta, normed, joined, vectors, other, sums)


def joined_finish_kernel(a, got_a, b, got_b, weight, v0, v1, v2):
    total = b[...] + got_b[...].astype(F32)
    cut = a.shape[1]
    rest = b.shape[1] - SEG
    weight[:, :cut] = a[...] + got_a[...].astype(F32)
    weight[:, cut:] = total[:, :rest]
    small = total[:, rest:].T
    whole = small[0:8] + small[8:16]
    for k, target in enumerate((v0, v1, v2)):
        target[...] = whole[k : k + 1]


def joined_finish(a, got_a, b, got_b):
    rows = a.shape[0]
    across = a.shape[1] + b.shape[1] - SEG
    return pl.pallas_call(
        joined_finish_kernel,
        out_shape=[shaped((rows, across), F32)] + [shaped((1, rows), F32)] * 3,
        in_specs=[VM] * 4,
        out_specs=[VM] * 4,
        compiler_params=params(),
        name="joined_finish",
    )(a, got_a, b, got_b)


def input_back_kernel(x, part, other, gain, middle_grad, out):
    rows = x.shape[0]
    step = 64

    def norm_step(i, _):
        at = pl.ds(pl.multiple_of(i * step, step), step)
        hat, scale = normal(x[at, :].astype(F32))
        first = part[at, :].astype(F32) + other[at, :].astype(F32)
        back = norm_back(hat, scale, first * gain[...].astype(F32))
        out[at, :] = (back + middle_grad[at, :]).astype(BF16)
        return _

    lax.fori_loop(0, rows // step, norm_step, 0)


def input_back(x, part, other, gain, middle_grad):
    return pl.pallas_call(
        input_back_kernel,
        out_shape=shaped(x.shape, BF16),
        in_specs=[VM] * 5,
        out_specs=VM,
        compiler_params=params(),
        name="input_back",
    )(x, part, other, gain, middle_grad)


def swap(value):
    return lax.ppermute(value, "tensor", [(0, 1), (1, 0)])


def to_member(value, d):
    count = lax.axis_size("dp")
    return lax.ppermute(value, "dp", [(i, i ^ d) for i in range(count)])


def to_member_across(value, d):
    count = lax.axis_size("dp")
    pairs = [(i * 2 + t, (i ^ d) * 2 + (1 - t)) for i in range(count) for t in range(2)]
    return lax.ppermute(value, ("dp", "tensor"), pairs)


def to_group(value, by):
    count = lax.axis_size("dp")
    step = by * MEMBERS
    return lax.ppermute(value, "dp", [(i, (i + step) % count) for i in range(count)])


def within(parts):
    return [parts[0]] + [to_member(parts[d], d) for d in range(1, MEMBERS)]


def reduce_rows(value):
    return lax.psum_scatter(value, "dp", scatter_dimension=0, tiled=True)


def after(value, *others):
    return lax.optimization_barrier((value, *others))[0]


def halve(keep, send, bits):
    for bit in bits[:-1]:
        total = keep + to_member(send, 1 << bit).astype(F32)
        half = total.shape[0] // 2
        keep, send = total[:half], total[half:].astype(BF16)
    return keep, to_member(send, 1 << bits[-1])


def joined_sums(meta, x, part, first_low, joined_grad, sums):
    count = lax.axis_size("dp")
    width, across = x.shape[1], joined_grad.shape[1]
    if count == 16:
        keep_a, send_a, vectors = joined_first(meta, x, part, first_low, joined_grad)
        other = swap(vectors)
        keep_b, send_b = joined_second(meta, first_low, joined_grad, vectors, other, sums)
        last_a = halve(keep_a, send_a, ORDERS[0])
        last_b = halve(keep_b, send_b, ORDERS[1])
        return joined_finish(*last_a, *last_b)
    hat, _scale = normal(x.astype(F32))
    wide = part.astype(F32)
    vectors = jnp.stack([jnp.sum(wide * hat, axis=0), jnp.sum(wide, axis=0)], axis=1)
    vectors = jnp.concatenate([vectors + swap(vectors), sums[:1].T], axis=1)
    grad = jnp.einsum("td,tf->df", first_low, joined_grad, preferred_element_type=F32)
    high = vectors.astype(BF16)
    rest = (vectors - high.astype(F32)).astype(BF16)
    room = jnp.zeros((width, PAIR - 6), BF16)
    got = reduce_rows(jnp.concatenate([grad.astype(BF16), high, rest, room], axis=1)).astype(F32)
    small = got[:, across : across + 3] + got[:, across + 3 : across + 6]
    return got[:, :across], small[:, 0], small[:, 1], small[:, 2]


def shards(
    activations,
    cotangent,
    parent_slot,
    attention_gain,
    attention_shift,
    joined_weight,
    joined_bias,
    output_weight,
    output_bias,
    feed_gain,
    feed_shift,
    expand_weight,
    expand_bias,
    contract_weight,
    contract_bias,
):
    device = lax.axis_index("dp")
    count = lax.axis_size("dp")
    rank = lax.axis_index("tensor")
    member = lax.rem(device, MEMBERS)
    heads_here = joined_weight.shape[1] // (3 * HD)
    width = activations.shape[1]
    inner = expand_weight.shape[1]
    half = output_weight.shape[0]
    meta = jnp.stack(
        [member, device // MEMBERS, rank * heads_here + 2 * member, rank, device]
    ).astype(jnp.int32)
    slopes = jnp.exp2(-8.0 * jnp.arange(1, H + 1, dtype=F32) / H)

    def row(v):
        return v.reshape(1, -1)

    gain_a, shift_a = row(attention_gain), row(attention_shift)
    gain_f, shift_f = row(feed_gain), row(feed_shift)

    first_low, queries, pairs = project(
        meta, activations, gain_a, shift_a, joined_weight, row(joined_bias)
    )
    table = make_tables(meta, parent_slot)
    pairs = within(pairs)
    queries = within(queries)
    hidden_grad = jnp.einsum("td,fd->tf", cotangent, contract_weight, preferred_element_type=F32)
    table = after(table, hidden_grad)
    up, down = pack(table, pairs)
    below = to_group(up, 1)
    above = to_group(down, -1)
    other_output_weight = swap(after(output_weight, up))
    kept, stats = attend_near(table, meta, slopes, queries, pairs)
    outs, lse = attend_far(table, meta, slopes, queries, below, above, kept, stats)
    parts_other = [to_member_across(outs[d], d) for d in range(MEMBERS)]
    parts_own = within(outs)
    mixed, middle, second_low, hidden_low, pre_grad, second_part, bias_sums = feed(
        meta, activations, row(output_bias), gain_f, shift_f, row(expand_bias),
        parts_own, parts_other, output_weight, other_output_weight, expand_weight, hidden_grad,
    )
    second_other = swap(second_part)
    held = feed_grads(cotangent, hidden_low, second_low, pre_grad, 2 * inner + half + SEG)
    feed_part = jnp.dot(hidden_low, contract_weight, preferred_element_type=F32).astype(BF16)
    second_other = after(second_other, held, feed_part)
    middle_grad, branch_low, feed_vectors, grad_parts = middle_back(
        meta, middle, second_part, second_other, cotangent, gain_f, output_weight
    )
    grad_parts = within(grad_parts)
    feed_part = after(feed_part, branch_low)
    feed_other = swap(feed_part)
    extra = bias_sums[0].reshape(count, 2, width // count).transpose(1, 0, 2).reshape(2, width)
    held = output_grads(branch_low, mixed, feed_vectors, extra, held)
    grad_parts[1] = after(grad_parts[1], held)
    feed_sums = reduce_rows(held)

    to_below, to_above, kept_grad = back_far(
        table, meta, slopes, queries, below, above, outs, grad_parts, lse
    )
    from_above = to_group(to_below, -1)
    from_below = to_group(to_above, 1)
    kept_grad = after(kept_grad, feed_other)
    query_grads, own = back_near(
        table, meta, slopes, queries, pairs, outs, grad_parts, lse, kept_grad
    )
    query_grads = within(query_grads)
    layer_output = (
        middle + (feed_part.astype(F32) + feed_other.astype(F32)) + contract_bias.astype(F32)
    ).astype(BF16)
    from_above = after(from_above, layer_output)
    pair_grads = within(gather_back(table, own, from_above, from_below))
    joined_grad, first_part, joined_bias_sums = join_stage(
        meta, joined_weight, query_grads, pair_grads
    )
    first_other = swap(first_part)
    joined_done, gain_grad, shift_grad, joined_bias_grad = joined_sums(
        meta, activations, first_part, first_low, joined_grad, joined_bias_sums
    )
    input_gradient = input_back(activations, first_part, first_other, gain_a, middle_grad)
    (
        contract_done, expand_done, output_done,
        feed_gain_grad, feed_shift_grad, output_bias_grad, contract_bias_grad, expand_bias_grad,
    ) = feed_finish(feed_sums, inner, half)

    return (
        layer_output,
        input_gradient,
        gain_grad.reshape(-1),
        shift_grad.reshape(-1),
        joined_done,
        joined_bias_grad.reshape(-1, 1),
        output_done,
        output_bias_grad.reshape(-1),
        feed_gain_grad.reshape(-1),
        feed_shift_grad.reshape(-1),
        expand_done,
        expand_bias_grad.reshape(-1, 1),
        contract_done,
        contract_bias_grad.reshape(-1),
    )


def solution(mesh):
    in_specs = (
        P("dp", None),
        P("dp", None),
        P(),
        P(),
        P(),
        P(None, "tensor"),
        P("tensor"),
        P("tensor", None),
        P(),
        P(),
        P(),
        P(None, "tensor"),
        P("tensor"),
        P("tensor", None),
        P(),
    )
    out_specs = (
        P("dp", None),
        P("dp", None),
        P("dp"),
        P("dp"),
        P("dp", "tensor"),
        P("dp", "tensor"),
        P("dp", "tensor"),
        P("dp"),
        P("dp"),
        P("dp"),
        P("dp", "tensor"),
        P("dp", "tensor"),
        P("dp", "tensor"),
        P("dp"),
    )
    return jax.shard_map(shards, mesh=mesh, in_specs=in_specs, out_specs=out_specs, check_vma=False)
```

```python
from functools import partial

import jax
import jax.numpy as jnp
from jax import lax
from jax.experimental import pallas as pl
from jax.experimental.pallas import tpu as pltpu
from jax.sharding import PartitionSpec as P

H = 16
HD = 64
SEG = 128
SEG_DEV = 5
ANC = 10
TREE = 20
INNER = 12
MEMBERS = 4
PAIR = 2 * HD
POOL = TREE + 2 * INNER
EMPTY = POOL

EPSILON = 1e-05
NEGATIVE = -1e30

F32 = jnp.float32
BF16 = jnp.bfloat16

LISTS = TREE * ANC
SLOT_AT = (0, 2 * LISTS)
LEVEL_AT = (LISTS, 3 * LISTS)
COUNT_AT = (4 * LISTS, 4 * LISTS + TREE)
UP_AT = 4 * LISTS + 2 * TREE
DOWN_AT = UP_AT + INNER
ORDER_AT = (DOWN_AT + INNER, DOWN_AT + INNER + TREE)
TABLE = 1024
GROUP = 4

GAIN_A, SHIFT_A, GAIN_F, SHIFT_F, OUT_BIAS, CONTRACT_BIAS, JOINED_BIAS, UP_BIAS = range(8)

VM = pl.BlockSpec(memory_space=pltpu.VMEM)
SM = pl.BlockSpec(memory_space=pltpu.SMEM)
ANY = pl.BlockSpec(memory_space=pl.ANY)


def shaped(shape, kind):
    return jax.ShapeDtypeStruct(shape, kind)


def params(mib=60):
    return pltpu.CompilerParams(vmem_limit_bytes=mib * 2**20)


LASTS = {
    "project": 9, "tables": 9, "pack": 4, "attend_near": 14, "hidden_grad": 5, "attend_far": 15,
    "feed": 18, "feed_grads": 20, "middle_back": 8, "output_grads": 9, "back_far": 14,
    "back_near": 15, "second_step": 5, "gather_back": 5, "third_step": 3, "join_stage": 7,
    "joined_first": 9, "joined_second": 6, "fourth_step": 3, "fifth_step": 4,
    "sixth_step": 2, "seventh_step": 2, "add": 1,
    "input_back": 6, "finish": 2, "feed_part": 4, "after_all": 0,
}
FLOPS_PER_US = 500_000_000


def lasting(name):
    return pl.CostEstimate(flops=LASTS[name] * FLOPS_PER_US, bytes_accessed=0, transcendentals=0)


def skipping(kernel, used, skipped):
    def run(*refs):
        kernel(*refs[:used], *refs[used + skipped :])

    return run


def dot(a, b, dims=((1,), (0,))):
    return lax.dot_general(a, b, (dims, ((), ())), preferred_element_type=F32)


def lanes(shape):
    return lax.broadcasted_iota(jnp.int32, shape, len(shape) - 1)


def rows_of(shape):
    return lax.broadcasted_iota(jnp.int32, shape, len(shape) - 2)


def table_kernel(count, meta, parent, out, inner, place, starts):
    member, group = meta[0], meta[1]
    groups = count // TREE
    below = lax.rem(group + groups - 1, groups)
    above = lax.rem(group + 1, groups)

    def clear(i, _):
        inner[i] = 0
        place[i] = EMPTY
        return _

    lax.fori_loop(0, count, clear, 0)

    def mark(i, _):
        up = parent[i]

        @pl.when(up >= 0)
        def _mark():
            inner[up] = 1

        return _

    lax.fori_loop(0, count, mark, 0)

    def cover(i, mask):
        up = parent[i]
        ahead = lax.rem(up - i + count, count)
        forward = ahead < TREE
        low = jnp.where(forward, i, up)
        length = jnp.where(forward, ahead, count - ahead)
        length = jnp.where(up >= 0, length, 0)
        start = lax.rem(low + 1 + TREE, TREE)
        bits = lax.shift_left(1, length) - 1
        room = TREE - start
        first = lax.shift_left(bits & (lax.shift_left(1, room) - 1), start)
        second = lax.shift_right_logical(bits, room)
        return mask | first | second

    mask = lax.fori_loop(0, 2 * TREE - 1, cover, 0)

    def find(c, found):
        free = (lax.shift_right_logical(mask, c) & 1) == 0
        return jnp.where(free, c, found)

    offset = lax.fori_loop(0, TREE, find, 0)

    for i in range(2 * INNER):
        out[UP_AT + i] = -1

    def own(p, ranks):
        up_rank, down_rank = ranks
        spot = ((p // SEG_DEV) ^ member) * SEG_DEV + lax.rem(p, SEG_DEV)
        slot = group * TREE + p
        place[slot] = spot
        has = inner[slot] == 1
        goes_up = has & (p >= offset) & (offset > 0) & (up_rank < INNER)
        goes_down = has & (p < offset) & (down_rank < INNER)

        @pl.when(goes_up)
        def _up():
            out[UP_AT + up_rank] = spot

        @pl.when(goes_down)
        def _down():
            out[DOWN_AT + down_rank] = spot

        return up_rank + goes_up.astype(jnp.int32), down_rank + goes_down.astype(jnp.int32)

    lax.fori_loop(0, TREE, own, (0, 0))

    def others(p, ranks):
        low_rank, high_rank = ranks
        low_slot = below * TREE + p
        high_slot = above * TREE + p
        low = (inner[low_slot] == 1) & (p >= offset) & (offset > 0) & (low_rank < INNER)
        high = (inner[high_slot] == 1) & (p < offset) & (high_rank < INNER)

        @pl.when(low)
        def _low():
            place[low_slot] = TREE + low_rank

        @pl.when(high)
        def _high():
            place[high_slot] = TREE + INNER + high_rank

        return low_rank + low.astype(jnp.int32), high_rank + high.astype(jnp.int32)

    lax.fori_loop(0, TREE, others, (0, 0))

    def chain(q, _):
        slot = group * TREE + ((q // SEG_DEV) ^ member) * SEG_DEV + lax.rem(q, SEG_DEV)
        for i in range(ANC):
            out[SLOT_AT[0] + q * ANC + i] = TREE
            out[SLOT_AT[1] + q * ANC + i] = 2 * INNER
            out[LEVEL_AT[0] + q * ANC + i] = 0
            out[LEVEL_AT[1] + q * ANC + i] = 0

        def step(a, state):
            at, near, far = state
            good = at >= 0
            safe = jnp.maximum(at, 0)
            spot = place[safe]
            is_near = good & (spot < TREE)
            is_far = good & (spot >= TREE)

            @pl.when(is_near)
            def _near():
                out[SLOT_AT[0] + q * ANC + near] = spot
                out[LEVEL_AT[0] + q * ANC + near] = a

            @pl.when(is_far)
            def _far():
                out[SLOT_AT[1] + q * ANC + far] = spot - TREE
                out[LEVEL_AT[1] + q * ANC + far] = a

            return (
                jnp.where(good, parent[safe], -1),
                near + is_near.astype(jnp.int32),
                far + is_far.astype(jnp.int32),
            )

        _end, near, far = lax.fori_loop(0, ANC, step, (slot, 0, 0))
        out[COUNT_AT[0] + q] = near
        out[COUNT_AT[1] + q] = far
        return _

    lax.fori_loop(0, TREE, chain, 0)

    for side in range(2):
        for i in range(ANC + 1):
            starts[i] = 0

        def tally(q, _):
            starts[out[COUNT_AT[side] + q]] += 1
            return _

        lax.fori_loop(0, TREE, tally, 0)

        def running(i, n):
            number = starts[ANC - i]
            starts[ANC - i] = n
            return n + number

        lax.fori_loop(0, ANC + 1, running, 0)

        def put(q, _):
            number = out[COUNT_AT[side] + q]
            at = starts[number]
            out[ORDER_AT[side] + at] = q
            starts[number] = at + 1
            return _

        lax.fori_loop(0, TREE, put, 0)


def make_tables(meta, parent):
    count = parent.shape[0]
    return pl.pallas_call(
        partial(table_kernel, count),
        out_shape=shaped((TABLE,), jnp.int32),
        in_specs=[SM, SM],
        out_specs=SM,
        scratch_shapes=[pltpu.SMEM((size,), jnp.int32) for size in (count, count, 16)],
        name="tables",
    )(meta, parent)


def normal(block):
    centered = block - jnp.mean(block, axis=-1, keepdims=True)
    variance = jnp.mean(centered * centered, axis=-1, keepdims=True)
    scale = lax.rsqrt(variance + EPSILON)
    return centered * scale, scale


NORM_ROWS = 128


def norm_loop(rows, body):
    def step(i, _):
        body(pl.ds(pl.multiple_of(i * NORM_ROWS, NORM_ROWS), NORM_ROWS))
        return _

    lax.fori_loop(0, rows // NORM_ROWS, step, 0)


def project_kernel(meta, x, vectors, weight, normed, *outs):
    member = meta[0]
    rows = x.shape[0]

    def norm_step(at):
        hat, _scale = normal(x[at, :].astype(F32))
        normed[at, :] = (
            hat * vectors[GAIN_A : GAIN_A + 1] + vectors[SHIFT_A : SHIFT_A + 1]
        ).astype(BF16)

    norm_loop(rows, norm_step)
    low = lanes((1, PAIR)) < HD

    def one(d, _):
        pair = member ^ d
        block = weight[:, pl.ds(pl.multiple_of(pair * 3 * PAIR, PAIR), 3 * PAIR)]
        both = vectors[JOINED_BIAS : JOINED_BIAS + 1, pl.ds(pl.multiple_of(pair * 2 * PAIR, PAIR), 2 * PAIR)]
        first, second = both[:, :PAIR], both[:, PAIR:]
        query_bias = jnp.where(low, first, pltpu.roll(second, HD, 1))
        value_bias = jnp.where(low, pltpu.roll(first, HD, 1), second)
        joined = dot(normed[...], block)
        t0, t1, t2 = joined[:, :PAIR], joined[:, PAIR : 2 * PAIR], joined[:, 2 * PAIR :]
        queries = (jnp.where(low, t0, t1) + query_bias) * (HD ** (-0.5))
        keys = pltpu.roll(jnp.where(low, t2, t0), HD, 1)
        values = jnp.where(low, t1, t2) + value_bias
        for j in range(MEMBERS):

            @pl.when(d == j)
            def _store():
                outs[j][...] = queries.astype(BF16)
                outs[MEMBERS + j][:, :PAIR] = keys.astype(BF16)
                outs[MEMBERS + j][:, PAIR:] = values.astype(BF16)

        return _

    lax.fori_loop(0, MEMBERS, one, 0)


def project(meta, x, vectors, weight):
    rows, width = x.shape
    outs = pl.pallas_call(
        project_kernel,
        out_shape=[shaped((rows, width), BF16)]
        + [shaped((rows, PAIR), BF16)] * MEMBERS
        + [shaped((rows, 2 * PAIR), BF16)] * MEMBERS,
        in_specs=[SM] + [VM] * 3,
        out_specs=[VM] * (1 + 2 * MEMBERS),
        compiler_params=params(),
        cost_estimate=lasting("project"),
        name="project",
    )(meta, x, vectors, weight)
    return outs[0], outs[1 : 1 + MEMBERS], outs[1 + MEMBERS :]


def pack_kernel(table, kv0, kv1, kv2, kv3, up, down, sem):
    sources = (kv0, kv1, kv2, kv3)
    for side, at, target in ((0, UP_AT, up), (1, DOWN_AT, down)):
        for i in range(INNER):
            spot = jnp.maximum(table[at + i], 0)
            d, s = spot // SEG_DEV, lax.rem(spot, SEG_DEV)
            for j in range(MEMBERS):

                @pl.when(d == j)
                def _start():
                    pltpu.make_async_copy(
                        sources[j].at[pl.ds(pl.multiple_of(s * SEG, SEG), SEG)],
                        target.at[pl.ds(i * SEG, SEG)],
                        sem.at[side * INNER + i],
                    ).start()

    for side, target in ((0, up), (1, down)):
        for i in range(INNER):
            piece = target.at[pl.ds(i * SEG, SEG)]
            pltpu.make_async_copy(piece, piece, sem.at[side * INNER + i]).wait()


def pack(table, pairs):
    out = shaped((INNER * SEG, 2 * PAIR), BF16)
    return pl.pallas_call(
        pack_kernel,
        out_shape=[out, out],
        in_specs=[SM] + [ANY] * MEMBERS,
        out_specs=[ANY] * 2,
        scratch_shapes=[pltpu.SemaphoreType.DMA((2 * INNER,))],
        compiler_params=params(8),
        cost_estimate=lasting("pack"),
        name="pack",
    )(table, *pairs)


LEVELS = (1, 2, 3, 4, 5, 6, 8, 10)


def split_heads(tile):
    low = lanes((SEG, PAIR)) < HD
    wide = tile.astype(F32)
    zero = jnp.zeros_like(wide)
    return jnp.concatenate(
        [jnp.where(low, wide, zero), jnp.where(low, zero, wide)], axis=0
    ).astype(BF16)


def join_heads(turned):
    top = rows_of((PAIR, SEG)) < HD
    return jnp.where(top, turned[:, :SEG], turned[:, SEG:]).T


def slope_row(slopes, meta):
    first = meta[2]
    return jnp.where(lanes((1, 2 * SEG)) < SEG, slopes[first], slopes[first + 1])


def fill_bias(bias, slope):
    shape = (SEG, 2 * SEG)
    offset = lax.rem(lanes(shape), SEG)
    key = rows_of(shape)
    gap = slope * (key - offset).astype(F32)
    bias[0] = jnp.where(key <= offset, gap, NEGATIVE)
    bias[1] = gap


def split_turned(tile):
    top = rows_of((PAIR, SEG)) < HD
    wide = tile.astype(F32).T
    zero = jnp.zeros_like(wide)
    return jnp.concatenate(
        [jnp.where(top, wide, zero), jnp.where(top, zero, wide)], axis=1
    ).astype(BF16)


def start_all(copies):
    for copy in copies:
        copy.start()


def wait_all(copies):
    for copy in copies:
        copy.wait()


def loads(sources, target, sem, first):
    copies, at = [], 0
    for k, source in enumerate(sources):
        rows = source.shape[0]
        copies.append(
            pltpu.make_async_copy(source, target.at[pl.ds(at, rows)], sem.at[first + k])
        )
        at += rows
    return copies


def segment(ref, at):
    return ref.at[pl.ds(pl.multiple_of(at * SEG, SEG), SEG)]


def turn_all(pool, turned, count, first):
    def turn(i, _):
        turned[i] = segment(pool, i)[:, first : first + PAIR].astype(F32).T.astype(BF16)
        return _

    lax.fori_loop(0, count, turn, 0, unroll=4)
    turned[count] = jnp.zeros((PAIR, SEG), BF16)


def entries(table, side, s, span):
    at = s * ANC
    spots = [table[SLOT_AT[side] + at + i] for i in range(span)]
    levels = [table[LEVEL_AT[side] + at + i] for i in range(span)]
    return spots, levels


def level_row(slope, levels, i, count):
    row = slope * (levels[i] * (-SEG)).astype(F32)
    return row + jnp.where(count <= i, NEGATIVE, 0.0)


def by_groups(table, side, body, empty=None):
    def step(g, _):
        group = [table[ORDER_AT[side] + g * GROUP + k] for k in range(GROUP)]
        most = table[COUNT_AT[side] + group[0]]
        if empty is not None:

            @pl.when(most == 0)
            def _none():
                empty(group)

        for below, span in zip((0,) + LEVELS[:-1], LEVELS):

            @pl.when((most > below) & (most <= span))
            def _run():
                body(group, span)

        return _

    lax.fori_loop(0, TREE // GROUP, step, 0)


def chosen_heads(wide):
    top = rows_of((PAIR, SEG)) < HD
    return jnp.where(top, wide[:, :SEG], wide[:, SEG:])


def weigh(side, span, table, s, slope, bias, pool, turned, stacked):
    count = table[COUNT_AT[side] + s]
    spots, levels = entries(table, side, s, span)
    keys = jnp.concatenate([segment(pool, spot)[:, :PAIR] for spot in spots], axis=0)
    whole = dot(keys, stacked)
    scores = []
    for i in range(span):
        raw = whole[i * SEG : (i + 1) * SEG]
        own = side == 0 and i == 0
        scores.append(raw + bias[0 if own else 1] + level_row(slope, levels, i, count))
    top = scores[0]
    for part in scores[1:]:
        top = jnp.maximum(top, part)
    top = jnp.max(top, axis=0, keepdims=True)
    sums, short = None, []
    for i in range(span):
        weights = jnp.exp(scores[i] - top)
        short.append(weights.astype(BF16))
        sums = weights if sums is None else sums + weights
    values = jnp.concatenate([turned[spot] for spot in spots], axis=1)
    out = dot(values, jnp.concatenate(short, axis=0))
    return top, jnp.sum(sums, axis=0, keepdims=True), chosen_heads(out)


def attend_near_kernel(
    table, meta, slopes, q0, q1, q2, q3, kv0, kv1, kv2, kv3,
    kept, stats, pool, turned, queries, bias, sem,
):
    copies = loads((kv0, kv1, kv2, kv3), pool, sem, 0)
    copies += loads((q0, q1, q2, q3), queries, sem, MEMBERS)
    start_all(copies)
    slope = slope_row(slopes, meta)
    fill_bias(bias, slope)
    pool[TREE * SEG :, :] = jnp.zeros((SEG, 2 * PAIR), BF16)
    wait_all(copies)
    turn_all(pool, turned, TREE, PAIR)

    def body(group, span):
        for s in group:
            stacked = split_turned(segment(queries, s)[...])
            top, total, out = weigh(0, span, table, s, slope, bias, pool, turned, stacked)
            stats[s, 0:1, :] = top
            stats[s, 1:2, :] = total
            kept[s] = out

    by_groups(table, 0, body)


def attend_near(table, meta, slopes, queries, pairs):
    return pl.pallas_call(
        attend_near_kernel,
        out_shape=[shaped((TREE, PAIR, SEG), F32), shaped((TREE, 8, 2 * SEG), F32)],
        in_specs=[SM] * 3 + [ANY] * (2 * MEMBERS),
        out_specs=[VM, VM],
        scratch_shapes=[
            pltpu.VMEM(((TREE + 1) * SEG, 2 * PAIR), BF16),
            pltpu.VMEM((TREE + 1, PAIR, SEG), BF16),
            pltpu.VMEM((TREE * SEG, PAIR), BF16),
            pltpu.VMEM((2, SEG, 2 * SEG), F32),
            pltpu.SemaphoreType.DMA((2 * MEMBERS,)),
        ],
        compiler_params=params(),
        cost_estimate=lasting("attend_near"),
        name="attend_near",
    )(table, meta, slopes, *queries, *pairs)


def attend_far_kernel(
    table, meta, slopes, q0, q1, q2, q3, below, above, kept, stats,
    o0, o1, o2, o3, lse, pool, turned, queries, result, bias, sem,
):
    rows = SEG_DEV * SEG
    copies = loads((below, above), pool, sem, 0)
    copies += loads((q0, q1, q2, q3), queries, sem, 2)
    start_all(copies)
    slope = slope_row(slopes, meta)
    fill_bias(bias, slope)
    pool[2 * INNER * SEG :, :] = jnp.zeros((SEG, 2 * PAIR), BF16)
    wait_all(copies)
    turn_all(pool, turned, 2 * INNER, PAIR)

    def finish(s, top, total, out):
        wide = 1.0 / total
        segment(result, s)[...] = (out * chosen_heads(jnp.broadcast_to(wide, (PAIR, 2 * SEG)))).T.astype(BF16)
        lse[s] = top + jnp.log(total)

    def alone(group):
        for s in group:
            finish(s, stats[s, 0:1, :], stats[s, 1:2, :], kept[s])

    def body(group, span):
        shape = (PAIR, 2 * SEG)
        for s in group:
            stacked = split_turned(segment(queries, s)[...])
            top, total, out = weigh(1, span, table, s, slope, bias, pool, turned, stacked)
            near = stats[s, 0:1, :]
            both = jnp.maximum(near, top)
            near_scale = jnp.exp(near - both)
            far_scale = jnp.exp(top - both)
            total = stats[s, 1:2, :] * near_scale + total * far_scale
            out = kept[s] * chosen_heads(jnp.broadcast_to(near_scale, shape)) + out * (
                chosen_heads(jnp.broadcast_to(far_scale, shape))
            )
            finish(s, both, total, out)

    by_groups(table, 1, body, alone)
    copies = [
        pltpu.make_async_copy(result.at[pl.ds(j * rows, rows)], target, sem.at[j])
        for j, target in enumerate((o0, o1, o2, o3))
    ]
    start_all(copies)
    wait_all(copies)


def attend_far(table, meta, slopes, queries, below, above, kept, stats, deps=()):
    rows = queries[0].shape[0]
    specs = [SM] * 3 + [ANY] * (MEMBERS + 2) + [VM] * 2
    used = len(specs)
    outs = pl.pallas_call(
        skipping(attend_far_kernel, used, len(deps)),
        out_shape=[shaped((rows, PAIR), BF16)] * MEMBERS + [shaped((TREE, 1, 2 * SEG), F32)],
        in_specs=specs + [ANY] * len(deps),
        out_specs=[ANY] * MEMBERS + [VM],
        scratch_shapes=[
            pltpu.VMEM(((2 * INNER + 1) * SEG, 2 * PAIR), BF16),
            pltpu.VMEM((2 * INNER + 1, PAIR, SEG), BF16),
            pltpu.VMEM((TREE * SEG, PAIR), BF16),
            pltpu.VMEM((TREE * SEG, PAIR), BF16),
            pltpu.VMEM((2, SEG, 2 * SEG), F32),
            pltpu.SemaphoreType.DMA((MEMBERS + 2,)),
        ],
        compiler_params=params(),
        cost_estimate=lasting("attend_far"),
        name="attend_far",
    )(table, meta, slopes, *queries, below, above, kept, stats, *deps)
    return outs[:MEMBERS], outs[MEMBERS]


def spread(side, span, table, s, slope, bias, pool, turned, total, queries, outs, grads, lse):
    count = table[COUNT_AT[side] + s]
    query = segment(queries, s)[...]
    stacked = split_heads(query)
    grad = segment(grads, s)[...]
    stacked_grad = split_heads(grad)
    product = (grad.astype(F32) * segment(outs, s)[...].astype(F32)).T
    delta = jnp.concatenate(
        [
            jnp.sum(product[:HD], axis=0, keepdims=True),
            jnp.sum(product[HD:], axis=0, keepdims=True),
        ],
        axis=1,
    )
    log_total = lse[s]
    spots, levels = entries(table, side, s, span)
    keys = jnp.concatenate([segment(pool, spot)[:, :PAIR] for spot in spots], axis=0)
    values = jnp.concatenate([segment(pool, spot)[:, PAIR:] for spot in spots], axis=0)
    raw = dot(keys, split_turned(query))
    prob_grad = dot(values, split_turned(grad))
    probs, score_grads = [], []
    for i in range(span):
        at = slice(i * SEG, (i + 1) * SEG)
        row = level_row(slope, levels, i, count) - log_total
        own = side == 0 and i == 0
        prob = jnp.exp(raw[at] + bias[0 if own else 1] + row)
        score_grads.append((prob * (prob_grad[at] - delta)).astype(BF16))
        probs.append(prob.astype(BF16))
    score_grad = jnp.concatenate(score_grads, axis=0)
    key_grad = dot(score_grad, stacked)
    value_grad = dot(jnp.concatenate(probs, axis=0), stacked_grad)
    for i in range(span):
        at = slice(i * SEG, (i + 1) * SEG)
        into = segment(total, spots[i])
        into[:, :PAIR] += key_grad[at]
        into[:, PAIR:] += value_grad[at]
    across = jnp.concatenate([turned[spot] for spot in spots], axis=1)
    return chosen_heads(dot(across, score_grad))


def clear_all(total, count):
    def clear(i, _):
        segment(total, i)[...] = jnp.zeros((SEG, 2 * PAIR), F32)
        return _

    lax.fori_loop(0, count, clear, 0, unroll=True)


def back_far_kernel(
    table, meta, slopes, q0, q1, q2, q3, below, above, o0, o1, o2, o3, g0, g1, g2, g3, lse,
    to_below, to_above, kept,
    pool, turned, queries, outs, grads, total, small, bias, sem,
):
    copies = loads((below, above), pool, sem, 0)
    copies += loads((q0, q1, q2, q3), queries, sem, 2)
    copies += loads((o0, o1, o2, o3), outs, sem, 2 + MEMBERS)
    copies += loads((g0, g1, g2, g3), grads, sem, 2 + 2 * MEMBERS)
    start_all(copies)
    slope = slope_row(slopes, meta)
    fill_bias(bias, slope)
    pool[2 * INNER * SEG :, :] = jnp.zeros((SEG, 2 * PAIR), BF16)
    clear_all(total, 2 * INNER + 1)
    wait_all(copies)
    turn_all(pool, turned, 2 * INNER, 0)

    def alone(group):
        for s in group:
            kept[s] = jnp.zeros((PAIR, SEG), F32)

    def body(group, span):
        for s in group:
            kept[s] = spread(
                1, span, table, s, slope, bias, pool, turned, total, queries, outs, grads, lse
            )

    by_groups(table, 1, body, alone)

    def shorten(i, _):
        segment(small, i)[...] = segment(total, i)[...].astype(BF16)
        return _

    lax.fori_loop(0, 2 * INNER, shorten, 0)
    copies = [
        pltpu.make_async_copy(
            small.at[pl.ds(k * INNER * SEG, INNER * SEG)], target, sem.at[k]
        )
        for k, target in enumerate((to_below, to_above))
    ]
    start_all(copies)
    wait_all(copies)


def back_far(table, meta, slopes, queries, below, above, outs, grads, lse, deps=()):
    side = shaped((INNER * SEG, 2 * PAIR), BF16)
    specs = [SM] * 3 + [ANY] * (3 * MEMBERS + 2) + [VM]
    used = len(specs)
    return pl.pallas_call(
        skipping(back_far_kernel, used, len(deps)),
        out_shape=[side, side, shaped((TREE, PAIR, SEG), F32)],
        in_specs=specs + [ANY] * len(deps),
        out_specs=[ANY] * 2 + [VM],
        scratch_shapes=[
            pltpu.VMEM(((2 * INNER + 1) * SEG, 2 * PAIR), BF16),
            pltpu.VMEM((2 * INNER + 1, PAIR, SEG), BF16),
            pltpu.VMEM((TREE * SEG, PAIR), BF16),
            pltpu.VMEM((TREE * SEG, PAIR), BF16),
            pltpu.VMEM((TREE * SEG, PAIR), BF16),
            pltpu.VMEM(((2 * INNER + 1) * SEG, 2 * PAIR), F32),
            pltpu.VMEM((2 * INNER * SEG, 2 * PAIR), BF16),
            pltpu.VMEM((2, SEG, 2 * SEG), F32),
            pltpu.SemaphoreType.DMA((3 * MEMBERS + 2,)),
        ],
        compiler_params=params(),
        cost_estimate=lasting("back_far"),
        name="back_far",
    )(table, meta, slopes, *queries, below, above, *outs, *grads, lse, *deps)


def back_near_kernel(
    table, meta, slopes, q0, q1, q2, q3, kv0, kv1, kv2, kv3, o0, o1, o2, o3, g0, g1, g2, g3,
    lse, kept, dq0, dq1, dq2, dq3, own,
    pool, turned, queries, outs, grads, result, total, bias, sem,
):
    rows = SEG_DEV * SEG
    copies = loads((kv0, kv1, kv2, kv3), pool, sem, 0)
    copies += loads((q0, q1, q2, q3), queries, sem, MEMBERS)
    copies += loads((o0, o1, o2, o3), outs, sem, 2 * MEMBERS)
    copies += loads((g0, g1, g2, g3), grads, sem, 3 * MEMBERS)
    start_all(copies)
    slope = slope_row(slopes, meta)
    fill_bias(bias, slope)
    pool[TREE * SEG :, :] = jnp.zeros((SEG, 2 * PAIR), BF16)
    clear_all(total, TREE + 1)
    wait_all(copies)
    turn_all(pool, turned, TREE, 0)

    def body(group, span):
        for s in group:
            part = spread(
                0, span, table, s, slope, bias, pool, turned, total, queries, outs, grads, lse
            )
            segment(result, s)[...] = (kept[s] + part).T.astype(BF16)

    by_groups(table, 0, body)
    copies = [
        pltpu.make_async_copy(result.at[pl.ds(j * rows, rows)], target, sem.at[j])
        for j, target in enumerate((dq0, dq1, dq2, dq3))
    ]
    copies.append(
        pltpu.make_async_copy(total.at[pl.ds(0, TREE * SEG)], own, sem.at[MEMBERS])
    )
    start_all(copies)
    wait_all(copies)


def back_near(table, meta, slopes, queries, pairs, outs, grads, lse, kept, deps=()):
    rows = queries[0].shape[0]
    specs = [SM] * 3 + [ANY] * (4 * MEMBERS) + [VM] * 2
    used = len(specs)
    result = pl.pallas_call(
        skipping(back_near_kernel, used, len(deps)),
        out_shape=[shaped((rows, PAIR), BF16)] * MEMBERS + [shaped((TREE * SEG, 2 * PAIR), F32)],
        in_specs=specs + [ANY] * len(deps),
        out_specs=[ANY] * (MEMBERS + 1),
        scratch_shapes=[
            pltpu.VMEM(((TREE + 1) * SEG, 2 * PAIR), BF16),
            pltpu.VMEM((TREE + 1, PAIR, SEG), BF16),
            pltpu.VMEM((TREE * SEG, PAIR), BF16),
            pltpu.VMEM((TREE * SEG, PAIR), BF16),
            pltpu.VMEM((TREE * SEG, PAIR), BF16),
            pltpu.VMEM((TREE * SEG, PAIR), BF16),
            pltpu.VMEM(((TREE + 1) * SEG, 2 * PAIR), F32),
            pltpu.VMEM((2, SEG, 2 * SEG), F32),
            pltpu.SemaphoreType.DMA((4 * MEMBERS,)),
        ],
        compiler_params=params(),
        cost_estimate=lasting("back_near"),
        name="back_near",
    )(table, meta, slopes, *queries, *pairs, *outs, *grads, lse, kept, *deps)
    return result[:MEMBERS], result[MEMBERS]


def gather_back_kernel(table, own, from_above, from_below, k0, k1, k2, k3, total, sem):
    rows = SEG_DEV * SEG
    copy = pltpu.make_async_copy(own, total, sem)
    copy.start()
    copy.wait()
    for at, source in ((UP_AT, from_above), (DOWN_AT, from_below)):

        def add(i, _):
            spot = table[at + i]

            @pl.when(spot >= 0)
            def _add():
                segment(total, spot)[...] += segment(source, i)[...].astype(F32)

            return _

        lax.fori_loop(0, INNER, add, 0)
    for j, target in enumerate((k0, k1, k2, k3)):

        def short(i, _):
            segment(target, i)[...] = segment(total, j * SEG_DEV + i)[...].astype(BF16)
            return _

        lax.fori_loop(0, SEG_DEV, short, 0)


def gather_back(table, own, from_above, from_below, deps=()):
    rows = SEG_DEV * SEG
    specs = [SM, ANY, VM, VM]
    used = len(specs)
    return pl.pallas_call(
        skipping(gather_back_kernel, used, len(deps)),
        out_shape=[shaped((rows, 2 * PAIR), BF16)] * MEMBERS,
        in_specs=specs + [ANY] * len(deps),
        out_specs=[VM] * MEMBERS,
        scratch_shapes=[
            pltpu.VMEM((TREE * SEG, 2 * PAIR), F32),
            pltpu.SemaphoreType.DMA(()),
        ],
        compiler_params=params(),
        cost_estimate=lasting("gather_back"),
        name="gather_back",
    )(table, own, from_above, from_below, *deps)


TILE = 256
def feed_kernel(
    meta, x, vectors, a0, a1, a2, a3, b0, b1, b2, b3,
    w_own, w_other, w_up, hidden_grad,
    mixed_out, middle_out, normed_out, act_out, pre_out, part, sums,
    mixed_own, middle, normed, act, pre_grad, mixed, weight, up, hidden, sem, out_sem,
):
    member, rank = meta[0], meta[3]
    rows, width = x.shape
    half = width // 2
    inner = w_up.shape[1]
    copies = []
    for k, source in enumerate((w_own, w_other)):
        at = pl.multiple_of((rank ^ k) * half, half)
        copies.append(pltpu.make_async_copy(source, weight.at[pl.ds(at, half)], sem.at[k]))
    late = [
        pltpu.make_async_copy(w_up, up, sem.at[2]),
        pltpu.make_async_copy(hidden_grad, hidden, sem.at[3]),
    ]
    start_all(copies + late)
    for k, parts in enumerate(((a0, a1, a2, a3), (b0, b1, b2, b3))):
        for d in range(MEMBERS):
            inside = (member ^ d) * PAIR
            at = pl.multiple_of((rank ^ k) * half + inside, PAIR)
            mixed[:, pl.ds(at, PAIR)] = parts[d][...]
            if k == 0:
                mixed_own[:, pl.ds(pl.multiple_of(inside, PAIR), PAIR)] = parts[d][...]
    stores = [pltpu.make_async_copy(mixed_own, mixed_out, out_sem.at[0])]
    stores[0].start()
    wait_all(copies)

    def column(t, _):
        at = pl.ds(pl.multiple_of(t * TILE, TILE), TILE)
        middle[:, at] = (
            x[:, at].astype(F32) + (dot(mixed[...], weight[:, at]) + vectors[OUT_BIAS : OUT_BIAS + 1, at])
        )
        return _

    lax.fori_loop(0, width // TILE, column, 0)
    stores.append(pltpu.make_async_copy(middle, middle_out, out_sem.at[1]))
    stores[1].start()

    def norm_step(at):
        hat, _scale = normal(middle[at, :])
        normed[at, :] = (hat * vectors[GAIN_F : GAIN_F + 1] + vectors[SHIFT_F : SHIFT_F + 1]).astype(BF16)

    norm_loop(rows, norm_step)
    stores.append(pltpu.make_async_copy(normed, normed_out, out_sem.at[2]))
    stores[2].start()
    wait_all(late)

    def hidden_step(t, _):
        at = pl.ds(pl.multiple_of(t * TILE, TILE), TILE)
        per = width // TILE
        bias = vectors[pl.ds(UP_BIAS + t // per, 1), pl.ds(pl.multiple_of(lax.rem(t, per) * TILE, TILE), TILE)]
        pre = dot(normed[...], up[:, at]) + bias
        square = pre * pre
        c = 0.7978845608028654
        t_ = jnp.tanh(pre * (c + (c * 0.044715) * square))
        low = 0.5 * (1.0 + t_)
        act[:, at] = (pre * low).astype(BF16)
        slope = low + (0.5 * pre) * (1.0 - t_ * t_) * (c + (3.0 * c * 0.044715) * square)
        grad = (hidden[:, at] * slope).astype(BF16)
        pre_grad[:, at] = grad
        sums[0:1, at] = jnp.sum(grad.astype(F32), axis=0, keepdims=True)
        return _

    lax.fori_loop(0, inner // TILE, hidden_step, 0)
    stores.append(pltpu.make_async_copy(act, act_out, out_sem.at[3]))
    stores.append(pltpu.make_async_copy(pre_grad, pre_out, out_sem.at[4]))
    start_all(stores[3:])

    def back(t, _):
        at = pl.ds(pl.multiple_of(t * TILE, TILE), TILE)
        part[:, at] = dot(pre_grad[...], up[at, :], ((1,), (1,))).astype(BF16)
        return _

    lax.fori_loop(0, width // TILE, back, 0)
    wait_all(stores)


def feed(meta, x, vectors, parts_own, parts_other, w_own, w_other, w_up, hidden_grad):
    rows, width = x.shape
    inner = w_up.shape[1]
    half = width // 2
    return pl.pallas_call(
        feed_kernel,
        out_shape=[
            shaped((rows, half), BF16),
            shaped((rows, width), F32),
            shaped((rows, width), BF16),
            shaped((rows, inner), BF16),
            shaped((rows, inner), BF16),
            shaped((rows, width), BF16),
            shaped((8, inner), F32),
        ],
        in_specs=[SM] + [VM] * (2 + 2 * MEMBERS) + [ANY] * 4,
        out_specs=[ANY] * 5 + [VM] * 2,
        scratch_shapes=[
            pltpu.VMEM((rows, half), BF16),
            pltpu.VMEM((rows, width), F32),
            pltpu.VMEM((rows, width), BF16),
            pltpu.VMEM((rows, inner), BF16),
            pltpu.VMEM((rows, inner), BF16),
            pltpu.VMEM((rows, width), BF16),
            pltpu.VMEM((width, width), BF16),
            pltpu.VMEM((width, inner), BF16),
            pltpu.VMEM((rows, inner), F32),
            pltpu.SemaphoreType.DMA((4,)),
            pltpu.SemaphoreType.DMA((5,)),
        ],
        compiler_params=params(),
        cost_estimate=lasting("feed"),
        name="feed",
    )(meta, x, vectors, *parts_own, *parts_other, w_own, w_other, w_up, hidden_grad)


def product_kernel(dims, left, right, out):
    out[...] = dot(left[...], right[...], dims).astype(out.dtype)


def product(name, left, right, turned, kind, deps=()):
    rows, depth = left.shape
    across = right.shape[0] if turned else right.shape[1]
    block = (TILE, depth) if turned else (depth, TILE)
    return pl.pallas_call(
        skipping(partial(product_kernel, ((1,), (1,) if turned else (0,))), 2, len(deps)),
        grid=(across // TILE,),
        out_shape=shaped((rows, across), kind),
        in_specs=[
            pl.BlockSpec((rows, depth), lambda t: (0, 0)),
            pl.BlockSpec(block, (lambda t: (t, 0)) if turned else (lambda t: (0, t))),
        ]
        + [ANY] * len(deps),
        out_specs=pl.BlockSpec((rows, TILE), lambda t: (0, t)),
        compiler_params=params(),
        cost_estimate=lasting(name),
        name=name,
    )(left, right, *deps)


def turn_rows(source, target):
    def step(i, _):
        at = pl.ds(pl.multiple_of(i * SEG, SEG), SEG)
        target[at, :] = source[:, at].astype(F32).T.astype(BF16)
        return _

    lax.fori_loop(0, source.shape[1] // SEG, step, 0)


X_FIRST = (0, 1, 2, 3)
Z_FIRST = (0, 2, 3, 1)
MIXED = (0, 2, 1, 3)
DEVICES = 16


def block_place(relative, order):
    place = 0
    for bit in order:
        place = place * 2 + (lax.shift_right_logical(relative, bit) & 1)
    return place


def turn_ordered(tile, target, i, device, order, share):
    for k in range(SEG // share):
        block = i * (SEG // share) + k
        at = block_place(block ^ device, order) * share
        target[pl.ds(pl.multiple_of(at, share), share), :] = tile[k * share : (k + 1) * share]


def turn_source(source, target, device, order, share):
    def step(i, _):
        at = pl.ds(pl.multiple_of(i * SEG, SEG), SEG)
        tile = source[:, at].astype(F32).T.astype(BF16)
        turn_ordered(tile, target, i, device, order, share)
        return _

    lax.fori_loop(0, source.shape[1] // SEG, step, 0)


def feed_grads_kernel(
    meta, grad, act, normed, pre_grad, weight,
    keep_c, send_c0, send_c1, keep_e, send_e0, send_e1, part, turned,
):
    t = pl.program_id(0)
    tiles = pl.num_programs(0) // 2
    width = grad.shape[1]
    half = width // 2
    tile = pre_grad.shape[1]

    @pl.when(t == 0)
    def _first():
        turn_source(grad, turned, meta[4], MIXED, width // DEVICES)

    @pl.when(t == tiles)
    def _second():
        turn_source(normed, turned, meta[4], X_FIRST, width // DEVICES)

    @pl.when(t < tiles)
    def _contract():
        right = act[:, pl.ds(pl.multiple_of(t * tile, tile), tile)]
        keep_c[...] = dot(turned[:half], right).astype(BF16)
        leave = dot(turned[half:], right).astype(BF16)

        @pl.when(t < tiles // 2)
        def _low():
            send_c0[...] = leave

        @pl.when(t >= tiles // 2)
        def _high():
            send_c1[...] = leave

    @pl.when(t >= tiles)
    def _expand():
        keep_e[...] = dot(turned[:half], pre_grad[...]).astype(BF16)
        leave = dot(turned[half:], pre_grad[...]).astype(BF16)

        @pl.when(t < tiles + tiles // 2)
        def _low():
            send_e0[...] = leave

        @pl.when(t >= tiles + tiles // 2)
        def _high():
            send_e1[...] = leave

    part[...] = dot(act[...], weight[...]).astype(BF16)


def feed_grads(meta, grad, act, normed, pre_grad, weight):
    rows, width = grad.shape
    inner = act.shape[1]
    tile = 2 * TILE
    tiles = inner // tile
    piece = width // (2 * tiles)

    def steps(start, number):
        return pl.BlockSpec((width // 2, tile), lambda t: (0, jnp.clip(t - start, 0, number - 1)))

    both = [steps(0, tiles), steps(0, tiles // 2), steps(tiles // 2, tiles // 2)]
    both += [steps(tiles, tiles), steps(tiles, tiles // 2), steps(tiles + tiles // 2, tiles // 2)]
    kept, sent = shaped((width // 2, inner), BF16), shaped((width // 2, inner // 2), BF16)
    whole = pl.BlockSpec((rows, width), lambda t: (0, 0))
    return pl.pallas_call(
        feed_grads_kernel,
        grid=(2 * tiles,),
        out_shape=[kept, sent, sent, kept, sent, sent, shaped((rows, width), BF16)],
        in_specs=[
            SM,
            whole,
            pl.BlockSpec((rows, inner), lambda t: (0, 0)),
            whole,
            pl.BlockSpec((rows, tile), lambda t: (0, jnp.maximum(t - tiles, 0))),
            pl.BlockSpec((inner, piece), lambda t: (0, t)),
        ],
        out_specs=both + [pl.BlockSpec((rows, piece), lambda t: (0, t))],
        scratch_shapes=[pltpu.VMEM((width, rows), BF16)],
        compiler_params=params(),
        cost_estimate=lasting("feed_grads"),
        name="feed_grads",
    )(meta, grad, act, normed, pre_grad, weight)


def in_two(rows8):
    high = rows8.astype(BF16).astype(F32)
    low = rows8 - high
    return jnp.concatenate([high, low, jnp.zeros((SEG - 16, rows8.shape[1]), F32)], axis=0)


def add_half(keep, got, stay, leave):
    half = stay.shape[0]
    stay[...] = keep[:half].astype(F32) + got[:half].astype(F32)
    leave[...] = (keep[half:].astype(F32) + got[half:].astype(F32)).astype(BF16)


TAKE_STEPS = 4


def take_specs(shape):
    rows, across = shape
    if across % (TAKE_STEPS * PAIR) == 0:
        tile, at = across // TAKE_STEPS, lambda t: (0, t)
    else:
        tile, at = across, lambda t: (0, 0)
    return pl.BlockSpec((rows, tile), at), pl.BlockSpec((rows // 2, tile), at)


def add_halves(flags, ins, outs):
    for k, split in enumerate(flags):
        step = partial(add_half, ins[2 * k], ins[2 * k + 1], outs[2 * k], outs[2 * k + 1])
        if split:
            step()
        else:
            pl.when(pl.program_id(0) == 0)(step)


def halves_of(pairs):
    specs, outs, shapes, flags, args = [], [], [], [], []
    for keep, got in pairs:
        whole, part = take_specs(keep.shape)
        half = (keep.shape[0] // 2, keep.shape[1])
        specs += [whole, whole]
        outs += [part, part]
        shapes += [shaped(half, F32), shaped(half, BF16)]
        flags.append(whole.block_shape[1] != keep.shape[1])
        args += [keep, got]
    return specs, outs, shapes, flags, args


def takes_kernel(flags, count, *refs):
    ins, outs = refs[: 2 * len(flags)], refs[2 * len(flags) + count :]
    add_halves(flags, ins, outs)


def takes(name, pairs, deps=()):
    specs, outs, shapes, flags, args = halves_of(pairs)
    got = pl.pallas_call(
        partial(takes_kernel, flags, len(deps)),
        grid=(TAKE_STEPS,),
        out_shape=shapes,
        in_specs=specs + [ANY] * len(deps),
        out_specs=outs,
        compiler_params=params(),
        cost_estimate=lasting(name),
        name=name,
    )(*args, *deps)
    return [tuple(got[2 * k : 2 * k + 2]) for k in range(len(pairs))]


def output_grads_kernel(count, meta, branch, mixed, vectors, extra, *refs):
    ins = refs[: 3 * count]
    keep, send = refs[3 * count : 3 * count + 2]
    outs = refs[3 * count + 2 : -2]
    turned, small = refs[-2:]
    t = pl.program_id(0)
    width, across = branch.shape[1], mixed.shape[1]
    share = width // DEVICES
    half = width // 2

    @pl.when(t == 0)
    def _first():
        turn_source(branch, turned, meta[4], X_FIRST, share)
        for i in range(width // SEG):
            at = slice(i * SEG, (i + 1) * SEG)
            rows8 = jnp.concatenate(
                [vectors[0:4, at], extra[0:2, at], jnp.zeros((2, SEG), F32)], axis=0
            )
            turn_ordered(in_two(rows8).T, small, i, meta[4], X_FIRST, share)
        keep[:, across:] = small[:half].astype(BF16)
        send[:, across:] = small[half:].astype(BF16)

    tile = across // TAKE_STEPS
    at = pl.ds(pl.multiple_of(t * tile, tile), tile)
    keep[:, at] = dot(turned[:half], mixed[:, at]).astype(BF16)
    send[:, at] = dot(turned[half:], mixed[:, at]).astype(BF16)
    for k in range(count):
        kept, low, high = ins[3 * k : 3 * k + 3]

        @pl.when(t < TAKE_STEPS // 2)
        def _low():
            add_half(kept, low, outs[2 * k], outs[2 * k + 1])

        @pl.when(t >= TAKE_STEPS // 2)
        def _high():
            add_half(kept, high, outs[2 * k], outs[2 * k + 1])


def output_grads(meta, branch, mixed, vectors, extra, pairs):
    rows, width = branch.shape
    across = mixed.shape[1]
    half_steps = TAKE_STEPS // 2
    specs, outs, shapes, args = [], [], [], []
    for kept, low, high in pairs:
        high_rows, cols = kept.shape
        tile = cols // TAKE_STEPS
        specs += [
            pl.BlockSpec((high_rows, tile), lambda t: (0, t)),
            pl.BlockSpec((high_rows, tile), lambda t: (0, jnp.minimum(t, half_steps - 1))),
            pl.BlockSpec((high_rows, tile), lambda t: (0, jnp.maximum(t - half_steps, 0))),
        ]
        outs += [pl.BlockSpec((high_rows // 2, tile), lambda t: (0, t))] * 2
        shapes += [shaped((high_rows // 2, cols), F32), shaped((high_rows // 2, cols), BF16)]
        args += [kept, low, high]

    def whole(shape):
        return pl.BlockSpec(shape, lambda t: (0, 0))

    own = whole((width // 2, across + SEG))
    got = pl.pallas_call(
        partial(output_grads_kernel, len(pairs)),
        grid=(TAKE_STEPS,),
        out_shape=[shaped((width // 2, across + SEG), BF16)] * 2 + shapes,
        in_specs=[SM, whole(branch.shape), whole(mixed.shape), whole(vectors.shape), whole(extra.shape)]
        + specs,
        out_specs=[own, own] + outs,
        scratch_shapes=[pltpu.VMEM((width, rows), BF16), pltpu.VMEM((width, SEG), F32)],
        compiler_params=params(),
        cost_estimate=lasting("output_grads"),
        name="output_grads",
    )(meta, branch, mixed, vectors, extra, *args)
    return (got[0], got[1]), [tuple(got[2 + 2 * k : 4 + 2 * k]) for k in range(len(pairs))]


def add_kernel(keep, got, out):
    out[...] = keep[...] + got[...].astype(F32)


def add(keep, got):
    return pl.pallas_call(
        add_kernel,
        out_shape=shaped(keep.shape, F32),
        in_specs=[VM] * 2,
        out_specs=VM,
        compiler_params=params(),
        cost_estimate=lasting("add"),
        name="add",
    )(keep, got)


def finish_kernel(
    o, got_o, a, got_a, b, got_b,
    output, weight, v0, v1, v2, v3, bias, w0, w1, w2,
):
    total = o[...] + got_o[...].astype(F32)
    across = output.shape[1]
    output[...] = total[:, :across]
    small = total[:, across:].T
    whole = small[0:8] + small[8:16]
    for k, target in enumerate((v0, v1, v2, v3)):
        target[...] = whole[k : k + 1]
    bias[...] = jnp.concatenate([whole[4:5], whole[5:6]], axis=1)
    total = b[...] + got_b[...].astype(F32)
    cut = a.shape[1]
    rest = b.shape[1] - SEG
    weight[:, :cut] = a[...] + got_a[...].astype(F32)
    weight[:, cut:] = total[:, :rest]
    small = total[:, rest:].T
    whole = small[0:8] + small[8:16]
    for k, target in enumerate((w0, w1, w2)):
        target[...] = whole[k : k + 1]


def finish(o, a, b):
    rows = o[0].shape[0]
    vector = shaped((1, rows), F32)
    return pl.pallas_call(
        finish_kernel,
        out_shape=[
            shaped((rows, o[0].shape[1] - SEG), F32),
            shaped((rows, a[0].shape[1] + b[0].shape[1] - SEG), F32),
        ]
        + [vector] * 4
        + [shaped((1, 2 * rows), F32)]
        + [vector] * 3,
        in_specs=[VM] * 6,
        out_specs=[VM] * 10,
        compiler_params=params(),
        cost_estimate=lasting("finish"),
        name="finish",
    )(*o, *a, *b)


def norm_back(hat, scale, up):
    mean_up = jnp.mean(up, axis=-1, keepdims=True)
    mean_both = jnp.mean(up * hat, axis=-1, keepdims=True)
    return scale * (up - mean_up - hat * mean_both)


def middle_back_kernel(
    meta, middle, part, other, grad, gains, weight,
    branch, vectors, g0, g1, g2, g3,
):
    member = meta[0]
    rows, width = middle.shape
    vectors[...] = jnp.zeros_like(vectors)

    def norm_step(at):
        hat, scale = normal(middle[at, :])
        second = part[at, :].astype(F32) + other[at, :].astype(F32)
        given = grad[at, :].astype(F32)
        back = given + norm_back(hat, scale, second * gains[GAIN_F : GAIN_F + 1])
        branch[at, :] = back.astype(BF16)
        vectors[0:1, :] += jnp.sum(second * hat, axis=0, keepdims=True)
        vectors[1:2, :] += jnp.sum(second, axis=0, keepdims=True)
        vectors[2:3, :] += jnp.sum(back, axis=0, keepdims=True)
        vectors[3:4, :] += jnp.sum(given, axis=0, keepdims=True)

    norm_loop(rows, norm_step)
    for d, target in enumerate((g0, g1, g2, g3)):
        at = pl.multiple_of((member ^ d) * PAIR, PAIR)
        target[...] = dot(branch[...], weight[pl.ds(at, PAIR), :], ((1,), (1,))).astype(BF16)


def middle_back(meta, middle, part, other, grad, gains, weight, deps=()):
    rows, width = middle.shape
    specs = [SM] + [VM] * 6
    used = len(specs)
    outs = pl.pallas_call(
        skipping(middle_back_kernel, used, len(deps)),
        out_shape=[shaped((rows, width), BF16), shaped((8, width), F32)]
        + [shaped((rows, PAIR), BF16)] * MEMBERS,
        in_specs=specs + [ANY] * len(deps),
        out_specs=[VM] * (2 + MEMBERS),
        compiler_params=params(),
        cost_estimate=lasting("middle_back"),
        name="middle_back",
    )(meta, middle, part, other, grad, gains, weight, *deps)
    return outs[0], outs[1], outs[2:]


def join_kernel(meta, weight, q0, q1, q2, q3, k0, k1, k2, k3, joined, part, sums):
    member = meta[0]
    low = lanes((1, PAIR)) < HD
    for d, (query, both) in enumerate(((q0, k0), (q1, k1), (q2, k2), (q3, k3))):
        wide_q = query[...].astype(F32) * (HD ** (-0.5))
        wide_k = pltpu.roll(both[:, :PAIR].astype(F32), HD, 1)
        wide_v = both[:, PAIR:].astype(F32)
        at = (member ^ d) * 3 * PAIR
        for k, tile in enumerate(
            (
                jnp.where(low, wide_q, wide_k),
                jnp.where(low, wide_v, wide_q),
                jnp.where(low, wide_k, wide_v),
            )
        ):
            joined[:, pl.ds(pl.multiple_of(at + k * PAIR, PAIR), PAIR)] = tile.astype(BF16)
        sum_q = jnp.sum(wide_q, axis=0, keepdims=True)
        sum_v = jnp.sum(wide_v, axis=0, keepdims=True)
        spot = pl.multiple_of((member ^ d) * 2 * PAIR, PAIR)
        sums[0:1, pl.ds(spot, PAIR)] = jnp.where(low, sum_q, pltpu.roll(sum_v, HD, 1))
        sums[0:1, pl.ds(pl.multiple_of(spot + PAIR, PAIR), PAIR)] = jnp.where(
            low, pltpu.roll(sum_q, HD, 1), sum_v
        )
    width = weight.shape[0]

    def column(t, _):
        at = pl.ds(pl.multiple_of(t * TILE, TILE), TILE)
        part[:, at] = dot(joined[...], weight[at, :], ((1,), (1,))).astype(BF16)
        return _

    lax.fori_loop(0, width // TILE, column, 0)


def join_stage(meta, weight, query_grads, pair_grads, deps=()):
    rows = query_grads[0].shape[0]
    width, across = weight.shape
    specs = [SM] + [VM] * (1 + 2 * MEMBERS)
    used = len(specs)
    return pl.pallas_call(
        skipping(join_kernel, used, len(deps)),
        out_shape=[
            shaped((rows, across), BF16),
            shaped((rows, width), BF16),
            shaped((8, 2 * MEMBERS * PAIR), F32),
        ],
        in_specs=specs + [ANY] * len(deps),
        out_specs=[VM] * 3,
        compiler_params=params(),
        cost_estimate=lasting("join_stage"),
        name="join_stage",
    )(meta, weight, *query_grads, *pair_grads, *deps)


FIRST_PART = 1024


def joined_first_kernel(meta, x, part, normed, joined, keep, send, vectors, turned):
    rows, width = x.shape
    device = meta[4]
    turn_source(normed, turned, device, X_FIRST, width // DEVICES)
    half = width // 2
    tile = TILE

    def column(t, _):
        at = pl.ds(pl.multiple_of(t * tile, tile), tile)
        keep[:, at] = dot(turned[:half], joined[:, at])
        send[:, at] = dot(turned[half:], joined[:, at]).astype(BF16)
        return _

    lax.fori_loop(0, keep.shape[1] // tile, column, 0)
    vectors[...] = jnp.zeros_like(vectors)

    def norm_step(at):
        hat, _scale = normal(x[at, :].astype(F32))
        first = part[at, :].astype(F32)
        vectors[0:1, :] += jnp.sum(first * hat, axis=0, keepdims=True)
        vectors[1:2, :] += jnp.sum(first, axis=0, keepdims=True)

    norm_loop(rows, norm_step)


def joined_first(meta, x, part, normed, joined, deps=()):
    rows, width = x.shape
    half = width // 2
    return pl.pallas_call(
        skipping(joined_first_kernel, 5, len(deps)),
        out_shape=[
            shaped((half, FIRST_PART), F32),
            shaped((half, FIRST_PART), BF16),
            shaped((8, width), F32),
        ],
        in_specs=[SM] + [VM] * 4 + [ANY] * len(deps),
        out_specs=[VM] * 3,
        scratch_shapes=[pltpu.VMEM((width, rows), BF16)],
        compiler_params=params(),
        cost_estimate=lasting("joined_first"),
        name="joined_first",
    )(meta, x, part, normed, joined, *deps)


def joined_second_kernel(meta, normed, joined, vectors, other, sums, keep, send, turned, small):
    width = normed.shape[1]
    device = meta[4]
    share = width // DEVICES
    turn_source(normed, turned, device, Z_FIRST, share)
    half = width // 2
    across = joined.shape[1] - FIRST_PART
    tile = TILE

    def column(t, _):
        at = pl.ds(pl.multiple_of(t * tile, tile), tile)
        source = pl.ds(pl.multiple_of(FIRST_PART + t * tile, tile), tile)
        keep[:, at] = dot(turned[:half], joined[:, source])
        send[:, at] = dot(turned[half:], joined[:, source]).astype(BF16)
        return _

    lax.fori_loop(0, across // tile, column, 0)
    for i in range(width // SEG):
        at = slice(i * SEG, (i + 1) * SEG)
        rows8 = jnp.concatenate(
            [vectors[0:2, at] + other[0:2, at], sums[0:1, at], jnp.zeros((5, SEG), F32)], axis=0
        )
        turn_ordered(in_two(rows8).T, small, i, device, Z_FIRST, share)
    keep[:, across:] = small[:half]
    send[:, across:] = small[half:].astype(BF16)


def joined_second(meta, normed, joined, vectors, other, sums, deps=()):
    rows, width = normed.shape
    half = width // 2
    across = joined.shape[1] - FIRST_PART + SEG
    return pl.pallas_call(
        skipping(joined_second_kernel, 6, len(deps)),
        out_shape=[shaped((half, across), F32), shaped((half, across), BF16)],
        in_specs=[SM] + [VM] * 5 + [ANY] * len(deps),
        out_specs=[VM] * 2,
        scratch_shapes=[pltpu.VMEM((width, rows), BF16), pltpu.VMEM((width, SEG), F32)],
        compiler_params=params(),
        cost_estimate=lasting("joined_second"),
        name="joined_second",
    )(meta, normed, joined, vectors, other, sums, *deps)


def input_back_kernel(x, part, other, gains, middle_grad, out):
    def norm_step(at):
        hat, scale = normal(x[at, :].astype(F32))
        first = part[at, :].astype(F32) + other[at, :].astype(F32)
        back = norm_back(hat, scale, first * gains[GAIN_A : GAIN_A + 1])
        out[at, :] = (back + middle_grad[at, :].astype(F32)).astype(BF16)

    norm_loop(x.shape[0], norm_step)


def input_back(x, part, other, gains, middle_grad):
    return pl.pallas_call(
        input_back_kernel,
        out_shape=shaped(x.shape, BF16),
        in_specs=[VM] * 5,
        out_specs=VM,
        compiler_params=params(),
        cost_estimate=lasting("input_back"),
        name="input_back",
    )(x, part, other, gains, middle_grad)


def stack_kernel(*refs):
    out, at = refs[-1], 0
    for ref in refs[:-1]:
        rows = ref.shape[0] // out.shape[1]
        out[at : at + rows, :] = ref[...].astype(F32).reshape(rows, out.shape[1])
        at += rows


def stack_vectors(*vectors):
    width = vectors[0].shape[0]
    rows = sum(vector.shape[0] for vector in vectors) // width
    return pl.pallas_call(
        stack_kernel,
        out_shape=shaped((rows, width), F32),
        in_specs=[VM] * len(vectors),
        out_specs=VM,
        name="stack_vectors",
    )(*vectors)


def swap(value):
    return lax.ppermute(value, "tensor", [(0, 1), (1, 0)])


def to_member(value, d):
    count = lax.axis_size("dp")
    return lax.ppermute(value, "dp", [(i, i ^ d) for i in range(count)])


def to_member_across(value, d):
    count = lax.axis_size("dp")
    pairs = [(i * 2 + t, (i ^ d) * 2 + (1 - t)) for i in range(count) for t in range(2)]
    return lax.ppermute(value, ("dp", "tensor"), pairs)


def to_group(value, by):
    count = lax.axis_size("dp")
    step = by * MEMBERS
    return lax.ppermute(value, "dp", [(i, (i + step) % count) for i in range(count)])


def within(parts):
    return [parts[0]] + [to_member(parts[d], d) for d in range(1, MEMBERS)]


def same_kernel(*refs):
    pass


def after_all(value, *others):
    return pl.pallas_call(
        same_kernel,
        out_shape=shaped(value.shape, value.dtype),
        in_specs=[ANY] * (1 + len(others)),
        out_specs=ANY,
        input_output_aliases={0: 0},
        cost_estimate=lasting("after_all"),
        name="after_all",
    )(value, *others)


def reduce_rows(value):
    return lax.psum_scatter(value, "dp", scatter_dimension=0, tiled=True)


def plain_sum(left, right):
    grad = jnp.einsum("td,tf->df", left, right, preferred_element_type=F32)
    return reduce_rows(grad.astype(BF16)).astype(F32)


def plain_sums(x, part, first_low, joined_grad, sums, cotangent, hidden_low, second_low, pre_grad, branch_low, mixed, feed_vectors, extra):
    hat, _scale = normal(x.astype(F32))
    wide = part.astype(F32)
    vectors = jnp.stack([jnp.sum(wide * hat, axis=0), jnp.sum(wide, axis=0)], axis=0)
    vectors = vectors + swap(vectors)
    small = reduce_rows(jnp.concatenate([feed_vectors[:4], extra, vectors, sums[:1]], axis=0).T)
    return (
        plain_sum(cotangent, hidden_low), plain_sum(second_low, pre_grad),
        plain_sum(branch_low, mixed), plain_sum(first_low, joined_grad),
        small[:, 0], small[:, 1], small[:, 2], small[:, 3], small[:, 4:6].T,
        small[:, 6], small[:, 7], small[:, 8],
    )


def shards(
    activations,
    cotangent,
    parent_slot,
    attention_gain,
    attention_shift,
    joined_weight,
    joined_bias,
    output_weight,
    output_bias,
    feed_gain,
    feed_shift,
    expand_weight,
    expand_bias,
    contract_weight,
    contract_bias,
):
    device = lax.axis_index("dp")
    count = lax.axis_size("dp")
    rank = lax.axis_index("tensor")
    member = lax.rem(device, MEMBERS)
    heads_here = joined_weight.shape[1] // (3 * HD)
    width = activations.shape[1]
    inner = expand_weight.shape[1]
    half = output_weight.shape[0]
    meta = jnp.stack(
        [member, device // MEMBERS, rank * heads_here + 2 * member, rank, device]
    ).astype(jnp.int32)
    slopes = jnp.exp2(-8.0 * jnp.arange(1, H + 1, dtype=F32) / H)

    vectors = stack_vectors(
        attention_gain, attention_shift, feed_gain, feed_shift, output_bias, contract_bias,
        joined_bias, expand_bias,
    )
    first_low, queries, pairs = project(meta, activations, vectors, joined_weight)
    table = make_tables(meta, parent_slot)
    pairs = within(pairs)
    queries = within(queries)
    up, down = pack(table, pairs)
    below = to_group(up, 1)
    above = to_group(down, -1)
    hidden_grad = product("hidden_grad", cotangent, contract_weight, True, F32, deps=(up,))
    other_output_weight = swap(output_weight)
    kept, stats = attend_near(table, meta, slopes, queries, pairs)
    outs, lse = attend_far(
        table, meta, slopes, queries, below, above, kept, stats,
        deps=(hidden_grad, other_output_weight),
    )
    parts_other = [to_member_across(outs[d], d) for d in range(MEMBERS)]
    parts_own = within(outs)
    mixed, middle, second_low, hidden_low, pre_grad, second_part, bias_sums = feed(
        meta, activations, vectors,
        parts_own, parts_other, output_weight, other_output_weight, expand_weight, hidden_grad,
    )
    second_other = swap(second_part)
    extra = bias_sums[0].reshape(count, 2, width // count).transpose(1, 0, 2).reshape(2, width)
    by_halves = count == DEVICES
    if by_halves:
        keep_c, c0, c1, keep_e, e0, e1, feed_part = feed_grads(
            meta, cotangent, hidden_low, second_low, pre_grad, contract_weight
        )
        c0, c1, e0, e1 = (to_member(part, 1) for part in (c0, c1, e0, e1))
    else:
        feed_part = product("feed_part", hidden_low, contract_weight, False, BF16)
    branch_low, feed_vectors, grad_parts = middle_back(
        meta, middle, second_part, second_other, cotangent, vectors, output_weight,
        deps=(feed_part,),
    )
    grad_parts = within(grad_parts)
    feed_other = swap(after_all(feed_part, branch_low))
    fill = ()
    if by_halves:
        (keep_o, send_o), ((keep_c, send_c), (keep_e, send_e)) = output_grads(
            meta, branch_low, mixed, feed_vectors, extra, [(keep_c, c0, c1), (keep_e, e0, e1)]
        )
        got_o, got_c, got_e = to_member(send_o, 1), to_member(send_c, 4), to_member(send_e, 2)
        fill = (keep_o,)
    to_below, to_above, kept_grad = back_far(
        table, meta, slopes, queries, below, above, outs, grad_parts, lse, deps=fill
    )
    from_above = to_group(to_below, -1)
    from_below = to_group(to_above, 1)
    query_grads, own = back_near(
        table, meta, slopes, queries, pairs, outs, grad_parts, lse, kept_grad, deps=(feed_other,)
    )
    query_grads = within(query_grads)
    layer_output = (
        middle + (feed_part.astype(F32) + feed_other.astype(F32)) + vectors[CONTRACT_BIAS]
    ).astype(BF16)
    fill = ()
    if by_halves:
        (keep_c, send_c), (keep_e, send_e), (keep_o, send_o) = takes(
            "second_step", [(keep_c, got_c), (keep_e, got_e), (keep_o, got_o)], deps=(own,)
        )
        got_c, got_o = to_member(send_c, 2), to_member(send_o, 2)
        fill = (keep_o,)
    own_pairs = gather_back(
        table, own, from_above, from_below, deps=tuple(query_grads) + (layer_output,) + fill
    )
    pair_grads = within(own_pairs)
    fill = ()
    if by_halves:
        got_e = to_member(after_all(send_e, own_pairs[0]), 4)
        (keep_c, send_c), (keep_o, send_o) = takes(
            "third_step", [(keep_c, got_c), (keep_o, got_o)], deps=(own_pairs[0],)
        )
        got_c, got_o = to_member(send_c, 8), to_member(send_o, 4)
        fill = (keep_o,)
    joined_grad, first_part, joined_bias_sums = join_stage(
        meta, joined_weight, query_grads, pair_grads, deps=fill
    )
    first_other = swap(first_part)
    input_gradient = input_back(activations, first_part, first_other, vectors, branch_low)
    if by_halves:
        (keep_e, send_e), (keep_o, send_o) = takes(
            "fourth_step", [(keep_e, got_e), (keep_o, got_o)], deps=(first_part,)
        )
        got_e, got_o = to_member(send_e, 8), to_member(send_o, 8)
        keep_a, send_a, norm_vectors = joined_first(
            meta, activations, first_part, first_low, joined_grad, deps=(keep_o,)
        )
        got_a = to_member(send_a, 1)
        contract_done = add(keep_c, got_c)
        norm_other = swap(norm_vectors)
        keep_b, send_b = joined_second(
            meta, first_low, joined_grad, norm_vectors, norm_other, joined_bias_sums,
            deps=(contract_done,),
        )
        got_b = to_member(send_b, 1)
        (keep_a, send_a), (keep_b, send_b) = takes(
            "fifth_step", [(keep_a, got_a), (keep_b, got_b)]
        )
        got_a, got_b = to_member(send_a, 2), to_member(send_b, 4)
        (keep_a, send_a), (keep_b, send_b) = takes(
            "sixth_step", [(keep_a, got_a), (keep_b, got_b)]
        )
        got_a, got_b = to_member(send_a, 4), to_member(send_b, 8)
        expand_done = add(keep_e, got_e)
        (keep_a, send_a), (keep_b, send_b) = takes(
            "seventh_step", [(keep_a, got_a), (keep_b, got_b)], deps=(input_gradient, expand_done)
        )
        got_a, got_b = to_member(send_a, 8), to_member(send_b, 2)
        done = (contract_done, expand_done) + tuple(
            finish((keep_o, got_o), (keep_a, got_a), (keep_b, got_b))
        )
    else:
        done = plain_sums(
            activations, first_part, first_low, joined_grad, joined_bias_sums, cotangent,
            hidden_low, second_low, pre_grad, branch_low, mixed, feed_vectors, extra,
        )
    (
        contract_done, expand_done, output_done, joined_done,
        feed_gain_grad, feed_shift_grad, output_bias_grad, contract_bias_grad, expand_bias_grad,
        gain_grad, shift_grad, joined_bias_grad,
    ) = done

    return (
        layer_output,
        input_gradient,
        gain_grad.reshape(-1),
        shift_grad.reshape(-1),
        joined_done,
        joined_bias_grad.reshape(-1, 1),
        output_done,
        output_bias_grad.reshape(-1),
        feed_gain_grad.reshape(-1),
        feed_shift_grad.reshape(-1),
        expand_done,
        expand_bias_grad.reshape(-1, 1),
        contract_done,
        contract_bias_grad.reshape(-1),
    )


def solution(mesh):
    in_specs = (
        P("dp", None),
        P("dp", None),
        P(),
        P(),
        P(),
        P(None, "tensor"),
        P("tensor"),
        P("tensor", None),
        P(),
        P(),
        P(),
        P(None, "tensor"),
        P("tensor"),
        P("tensor", None),
        P(),
    )
    out_specs = (
        P("dp", None),
        P("dp", None),
        P("dp"),
        P("dp"),
        P("dp", "tensor"),
        P("dp", "tensor"),
        P("dp", "tensor"),
        P("dp"),
        P("dp"),
        P("dp"),
        P("dp", "tensor"),
        P("dp", "tensor"),
        P("dp", "tensor"),
        P("dp"),
    )
    return jax.shard_map(shards, mesh=mesh, in_specs=in_specs, out_specs=out_specs, check_vma=False)
```

```python
from functools import partial

import jax
import jax.numpy as jnp
from jax import lax
from jax.experimental import pallas as pl
from jax.experimental.pallas import tpu as pltpu
from jax.sharding import PartitionSpec as P

H = 16
HD = 64
SEG = 128
SEG_DEV = 5
ANC = 10
TREE = 20
INNER = 12
MEMBERS = 4
PAIR = 2 * HD
POOL = TREE + 2 * INNER
EMPTY = POOL

EPSILON = 1e-05
NEGATIVE = -1e30

F32 = jnp.float32
BF16 = jnp.bfloat16

LISTS = TREE * ANC
SLOT_AT = (0, 2 * LISTS)
LEVEL_AT = (LISTS, 3 * LISTS)
COUNT_AT = (4 * LISTS, 4 * LISTS + TREE)
UP_AT = 4 * LISTS + 2 * TREE
DOWN_AT = UP_AT + INNER
ORDER_AT = (DOWN_AT + INNER, DOWN_AT + INNER + TREE)
TABLE = 1024
GROUP = 4

GAIN_A, SHIFT_A, GAIN_F, SHIFT_F, OUT_BIAS, CONTRACT_BIAS, JOINED_BIAS, UP_BIAS = range(8)

VM = pl.BlockSpec(memory_space=pltpu.VMEM)
SM = pl.BlockSpec(memory_space=pltpu.SMEM)
ANY = pl.BlockSpec(memory_space=pl.ANY)


def shaped(shape, kind):
    return jax.ShapeDtypeStruct(shape, kind)


def params(mib=60):
    return pltpu.CompilerParams(vmem_limit_bytes=mib * 2**20)


LASTS = {
    "project": 9, "tables": 9, "pack": 4, "attend_near": 14, "hidden_grad": 5, "attend_far": 15,
    "feed": 18, "feed_grads": 20, "middle_back": 8, "output_grads": 9, "back_far": 14,
    "back_near": 15, "second_step": 5, "gather_back": 5, "third_step": 3, "join_stage": 7,
    "joined_first": 9, "joined_second": 60, "first_sums": 1, "second_sums": 1,
    "input_back": 6, "finish": 2, "feed_part": 4, "after_all": 0,
}
FLOPS_PER_US = 500_000_000


def lasting(name):
    return pl.CostEstimate(flops=LASTS[name] * FLOPS_PER_US, bytes_accessed=0, transcendentals=0)


def skipping(kernel, used, skipped):
    def run(*refs):
        kernel(*refs[:used], *refs[used + skipped :])

    return run


def dot(a, b, dims=((1,), (0,))):
    return lax.dot_general(a, b, (dims, ((), ())), preferred_element_type=F32)


def lanes(shape):
    return lax.broadcasted_iota(jnp.int32, shape, len(shape) - 1)


def rows_of(shape):
    return lax.broadcasted_iota(jnp.int32, shape, len(shape) - 2)


def table_kernel(count, meta, parent, out, inner, place, starts):
    member, group = meta[0], meta[1]
    groups = count // TREE
    below = lax.rem(group + groups - 1, groups)
    above = lax.rem(group + 1, groups)

    def clear(i, _):
        inner[i] = 0
        place[i] = EMPTY
        return _

    lax.fori_loop(0, count, clear, 0)

    def mark(i, _):
        up = parent[i]

        @pl.when(up >= 0)
        def _mark():
            inner[up] = 1

        return _

    lax.fori_loop(0, count, mark, 0)

    def cover(i, mask):
        up = parent[i]
        ahead = lax.rem(up - i + count, count)
        forward = ahead < TREE
        low = jnp.where(forward, i, up)
        length = jnp.where(forward, ahead, count - ahead)
        length = jnp.where(up >= 0, length, 0)
        start = lax.rem(low + 1 + TREE, TREE)
        bits = lax.shift_left(1, length) - 1
        room = TREE - start
        first = lax.shift_left(bits & (lax.shift_left(1, room) - 1), start)
        second = lax.shift_right_logical(bits, room)
        return mask | first | second

    mask = lax.fori_loop(0, 2 * TREE - 1, cover, 0)

    def find(c, found):
        free = (lax.shift_right_logical(mask, c) & 1) == 0
        return jnp.where(free, c, found)

    offset = lax.fori_loop(0, TREE, find, 0)

    for i in range(2 * INNER):
        out[UP_AT + i] = -1

    def own(p, ranks):
        up_rank, down_rank = ranks
        spot = ((p // SEG_DEV) ^ member) * SEG_DEV + lax.rem(p, SEG_DEV)
        slot = group * TREE + p
        place[slot] = spot
        has = inner[slot] == 1
        goes_up = has & (p >= offset) & (offset > 0) & (up_rank < INNER)
        goes_down = has & (p < offset) & (down_rank < INNER)

        @pl.when(goes_up)
        def _up():
            out[UP_AT + up_rank] = spot

        @pl.when(goes_down)
        def _down():
            out[DOWN_AT + down_rank] = spot

        return up_rank + goes_up.astype(jnp.int32), down_rank + goes_down.astype(jnp.int32)

    lax.fori_loop(0, TREE, own, (0, 0))

    def others(p, ranks):
        low_rank, high_rank = ranks
        low_slot = below * TREE + p
        high_slot = above * TREE + p
        low = (inner[low_slot] == 1) & (p >= offset) & (offset > 0) & (low_rank < INNER)
        high = (inner[high_slot] == 1) & (p < offset) & (high_rank < INNER)

        @pl.when(low)
        def _low():
            place[low_slot] = TREE + low_rank

        @pl.when(high)
        def _high():
            place[high_slot] = TREE + INNER + high_rank

        return low_rank + low.astype(jnp.int32), high_rank + high.astype(jnp.int32)

    lax.fori_loop(0, TREE, others, (0, 0))

    def chain(q, _):
        slot = group * TREE + ((q // SEG_DEV) ^ member) * SEG_DEV + lax.rem(q, SEG_DEV)
        for i in range(ANC):
            out[SLOT_AT[0] + q * ANC + i] = TREE
            out[SLOT_AT[1] + q * ANC + i] = 2 * INNER
            out[LEVEL_AT[0] + q * ANC + i] = 0
            out[LEVEL_AT[1] + q * ANC + i] = 0

        def step(a, state):
            at, near, far = state
            good = at >= 0
            safe = jnp.maximum(at, 0)
            spot = place[safe]
            is_near = good & (spot < TREE)
            is_far = good & (spot >= TREE)

            @pl.when(is_near)
            def _near():
                out[SLOT_AT[0] + q * ANC + near] = spot
                out[LEVEL_AT[0] + q * ANC + near] = a

            @pl.when(is_far)
            def _far():
                out[SLOT_AT[1] + q * ANC + far] = spot - TREE
                out[LEVEL_AT[1] + q * ANC + far] = a

            return (
                jnp.where(good, parent[safe], -1),
                near + is_near.astype(jnp.int32),
                far + is_far.astype(jnp.int32),
            )

        _end, near, far = lax.fori_loop(0, ANC, step, (slot, 0, 0))
        out[COUNT_AT[0] + q] = near
        out[COUNT_AT[1] + q] = far
        return _

    lax.fori_loop(0, TREE, chain, 0)

    for side in range(2):
        for i in range(ANC + 1):
            starts[i] = 0

        def tally(q, _):
            starts[out[COUNT_AT[side] + q]] += 1
            return _

        lax.fori_loop(0, TREE, tally, 0)

        def running(i, n):
            number = starts[ANC - i]
            starts[ANC - i] = n
            return n + number

        lax.fori_loop(0, ANC + 1, running, 0)

        def put(q, _):
            number = out[COUNT_AT[side] + q]
            at = starts[number]
            out[ORDER_AT[side] + at] = q
            starts[number] = at + 1
            return _

        lax.fori_loop(0, TREE, put, 0)


def make_tables(meta, parent):
    count = parent.shape[0]
    return pl.pallas_call(
        partial(table_kernel, count),
        out_shape=shaped((TABLE,), jnp.int32),
        in_specs=[SM, SM],
        out_specs=SM,
        scratch_shapes=[pltpu.SMEM((size,), jnp.int32) for size in (count, count, 16)],
        name="tables",
    )(meta, parent)


def normal(block):
    centered = block - jnp.mean(block, axis=-1, keepdims=True)
    variance = jnp.mean(centered * centered, axis=-1, keepdims=True)
    scale = lax.rsqrt(variance + EPSILON)
    return centered * scale, scale


NORM_ROWS = 128


def norm_loop(rows, body):
    def step(i, _):
        body(pl.ds(pl.multiple_of(i * NORM_ROWS, NORM_ROWS), NORM_ROWS))
        return _

    lax.fori_loop(0, rows // NORM_ROWS, step, 0)


def project_kernel(meta, x, vectors, weight, normed, *outs):
    member = meta[0]
    rows = x.shape[0]

    def norm_step(at):
        hat, _scale = normal(x[at, :].astype(F32))
        normed[at, :] = (
            hat * vectors[GAIN_A : GAIN_A + 1] + vectors[SHIFT_A : SHIFT_A + 1]
        ).astype(BF16)

    norm_loop(rows, norm_step)
    low = lanes((1, PAIR)) < HD

    def one(d, _):
        pair = member ^ d
        block = weight[:, pl.ds(pl.multiple_of(pair * 3 * PAIR, PAIR), 3 * PAIR)]
        both = vectors[JOINED_BIAS : JOINED_BIAS + 1, pl.ds(pl.multiple_of(pair * 2 * PAIR, PAIR), 2 * PAIR)]
        first, second = both[:, :PAIR], both[:, PAIR:]
        query_bias = jnp.where(low, first, pltpu.roll(second, HD, 1))
        value_bias = jnp.where(low, pltpu.roll(first, HD, 1), second)
        joined = dot(normed[...], block)
        t0, t1, t2 = joined[:, :PAIR], joined[:, PAIR : 2 * PAIR], joined[:, 2 * PAIR :]
        queries = (jnp.where(low, t0, t1) + query_bias) * (HD ** (-0.5))
        keys = pltpu.roll(jnp.where(low, t2, t0), HD, 1)
        values = jnp.where(low, t1, t2) + value_bias
        for j in range(MEMBERS):

            @pl.when(d == j)
            def _store():
                outs[j][...] = queries.astype(BF16)
                outs[MEMBERS + j][:, :PAIR] = keys.astype(BF16)
                outs[MEMBERS + j][:, PAIR:] = values.astype(BF16)

        return _

    lax.fori_loop(0, MEMBERS, one, 0)


def project(meta, x, vectors, weight):
    rows, width = x.shape
    outs = pl.pallas_call(
        project_kernel,
        out_shape=[shaped((rows, width), BF16)]
        + [shaped((rows, PAIR), BF16)] * MEMBERS
        + [shaped((rows, 2 * PAIR), BF16)] * MEMBERS,
        in_specs=[SM] + [VM] * 3,
        out_specs=[VM] * (1 + 2 * MEMBERS),
        compiler_params=params(),
        cost_estimate=lasting("project"),
        name="project",
    )(meta, x, vectors, weight)
    return outs[0], outs[1 : 1 + MEMBERS], outs[1 + MEMBERS :]


def pack_kernel(table, kv0, kv1, kv2, kv3, up, down, sem):
    sources = (kv0, kv1, kv2, kv3)
    for side, at, target in ((0, UP_AT, up), (1, DOWN_AT, down)):
        for i in range(INNER):
            spot = jnp.maximum(table[at + i], 0)
            d, s = spot // SEG_DEV, lax.rem(spot, SEG_DEV)
            for j in range(MEMBERS):

                @pl.when(d == j)
                def _start():
                    pltpu.make_async_copy(
                        sources[j].at[pl.ds(pl.multiple_of(s * SEG, SEG), SEG)],
                        target.at[pl.ds(i * SEG, SEG)],
                        sem.at[side * INNER + i],
                    ).start()

    for side, target in ((0, up), (1, down)):
        for i in range(INNER):
            piece = target.at[pl.ds(i * SEG, SEG)]
            pltpu.make_async_copy(piece, piece, sem.at[side * INNER + i]).wait()


def pack(table, pairs):
    out = shaped((INNER * SEG, 2 * PAIR), BF16)
    return pl.pallas_call(
        pack_kernel,
        out_shape=[out, out],
        in_specs=[SM] + [ANY] * MEMBERS,
        out_specs=[ANY] * 2,
        scratch_shapes=[pltpu.SemaphoreType.DMA((2 * INNER,))],
        compiler_params=params(8),
        cost_estimate=lasting("pack"),
        name="pack",
    )(table, *pairs)


LEVELS = (1, 2, 3, 4, 5, 6, 8, 10)


def split_heads(tile):
    low = lanes((SEG, PAIR)) < HD
    wide = tile.astype(F32)
    zero = jnp.zeros_like(wide)
    return jnp.concatenate(
        [jnp.where(low, wide, zero), jnp.where(low, zero, wide)], axis=0
    ).astype(BF16)


def join_heads(turned):
    top = rows_of((PAIR, SEG)) < HD
    return jnp.where(top, turned[:, :SEG], turned[:, SEG:]).T


def slope_row(slopes, meta):
    first = meta[2]
    return jnp.where(lanes((1, 2 * SEG)) < SEG, slopes[first], slopes[first + 1])


def fill_bias(bias, slope):
    shape = (SEG, 2 * SEG)
    offset = lax.rem(lanes(shape), SEG)
    key = rows_of(shape)
    gap = slope * (key - offset).astype(F32)
    bias[0] = jnp.where(key <= offset, gap, NEGATIVE)
    bias[1] = gap


def split_turned(tile):
    top = rows_of((PAIR, SEG)) < HD
    wide = tile.astype(F32).T
    zero = jnp.zeros_like(wide)
    return jnp.concatenate(
        [jnp.where(top, wide, zero), jnp.where(top, zero, wide)], axis=1
    ).astype(BF16)


def start_all(copies):
    for copy in copies:
        copy.start()


def wait_all(copies):
    for copy in copies:
        copy.wait()


def loads(sources, target, sem, first):
    copies, at = [], 0
    for k, source in enumerate(sources):
        rows = source.shape[0]
        copies.append(
            pltpu.make_async_copy(source, target.at[pl.ds(at, rows)], sem.at[first + k])
        )
        at += rows
    return copies


def segment(ref, at):
    return ref.at[pl.ds(pl.multiple_of(at * SEG, SEG), SEG)]


def turn_all(pool, turned, count, first):
    def turn(i, _):
        turned[i] = segment(pool, i)[:, first : first + PAIR].astype(F32).T.astype(BF16)
        return _

    lax.fori_loop(0, count, turn, 0, unroll=4)
    turned[count] = jnp.zeros((PAIR, SEG), BF16)


def entries(table, side, s, span):
    at = s * ANC
    spots = [table[SLOT_AT[side] + at + i] for i in range(span)]
    levels = [table[LEVEL_AT[side] + at + i] for i in range(span)]
    return spots, levels


def level_row(slope, levels, i, count):
    row = slope * (levels[i] * (-SEG)).astype(F32)
    return row + jnp.where(count <= i, NEGATIVE, 0.0)


def by_groups(table, side, body, empty=None):
    def step(g, _):
        group = [table[ORDER_AT[side] + g * GROUP + k] for k in range(GROUP)]
        most = table[COUNT_AT[side] + group[0]]
        if empty is not None:

            @pl.when(most == 0)
            def _none():
                empty(group)

        for below, span in zip((0,) + LEVELS[:-1], LEVELS):

            @pl.when((most > below) & (most <= span))
            def _run():
                body(group, span)

        return _

    lax.fori_loop(0, TREE // GROUP, step, 0)


def chosen_heads(wide):
    top = rows_of((PAIR, SEG)) < HD
    return jnp.where(top, wide[:, :SEG], wide[:, SEG:])


def weigh(side, span, table, s, slope, bias, pool, turned, stacked):
    count = table[COUNT_AT[side] + s]
    spots, levels = entries(table, side, s, span)
    keys = jnp.concatenate([segment(pool, spot)[:, :PAIR] for spot in spots], axis=0)
    whole = dot(keys, stacked)
    scores = []
    for i in range(span):
        raw = whole[i * SEG : (i + 1) * SEG]
        own = side == 0 and i == 0
        scores.append(raw + bias[0 if own else 1] + level_row(slope, levels, i, count))
    top = scores[0]
    for part in scores[1:]:
        top = jnp.maximum(top, part)
    top = jnp.max(top, axis=0, keepdims=True)
    sums, short = None, []
    for i in range(span):
        weights = jnp.exp(scores[i] - top)
        short.append(weights.astype(BF16))
        sums = weights if sums is None else sums + weights
    values = jnp.concatenate([turned[spot] for spot in spots], axis=1)
    out = dot(values, jnp.concatenate(short, axis=0))
    return top, jnp.sum(sums, axis=0, keepdims=True), chosen_heads(out)


def attend_near_kernel(
    table, meta, slopes, q0, q1, q2, q3, kv0, kv1, kv2, kv3,
    kept, stats, pool, turned, queries, bias, sem,
):
    copies = loads((kv0, kv1, kv2, kv3), pool, sem, 0)
    copies += loads((q0, q1, q2, q3), queries, sem, MEMBERS)
    start_all(copies)
    slope = slope_row(slopes, meta)
    fill_bias(bias, slope)
    pool[TREE * SEG :, :] = jnp.zeros((SEG, 2 * PAIR), BF16)
    wait_all(copies)
    turn_all(pool, turned, TREE, PAIR)

    def body(group, span):
        for s in group:
            stacked = split_turned(segment(queries, s)[...])
            top, total, out = weigh(0, span, table, s, slope, bias, pool, turned, stacked)
            stats[s, 0:1, :] = top
            stats[s, 1:2, :] = total
            kept[s] = out

    by_groups(table, 0, body)


def attend_near(table, meta, slopes, queries, pairs):
    return pl.pallas_call(
        attend_near_kernel,
        out_shape=[shaped((TREE, PAIR, SEG), F32), shaped((TREE, 8, 2 * SEG), F32)],
        in_specs=[SM] * 3 + [ANY] * (2 * MEMBERS),
        out_specs=[VM, VM],
        scratch_shapes=[
            pltpu.VMEM(((TREE + 1) * SEG, 2 * PAIR), BF16),
            pltpu.VMEM((TREE + 1, PAIR, SEG), BF16),
            pltpu.VMEM((TREE * SEG, PAIR), BF16),
            pltpu.VMEM((2, SEG, 2 * SEG), F32),
            pltpu.SemaphoreType.DMA((2 * MEMBERS,)),
        ],
        compiler_params=params(),
        cost_estimate=lasting("attend_near"),
        name="attend_near",
    )(table, meta, slopes, *queries, *pairs)


def attend_far_kernel(
    table, meta, slopes, q0, q1, q2, q3, below, above, kept, stats,
    o0, o1, o2, o3, lse, pool, turned, queries, result, bias, sem,
):
    rows = SEG_DEV * SEG
    copies = loads((below, above), pool, sem, 0)
    copies += loads((q0, q1, q2, q3), queries, sem, 2)
    start_all(copies)
    slope = slope_row(slopes, meta)
    fill_bias(bias, slope)
    pool[2 * INNER * SEG :, :] = jnp.zeros((SEG, 2 * PAIR), BF16)
    wait_all(copies)
    turn_all(pool, turned, 2 * INNER, PAIR)

    def finish(s, top, total, out):
        wide = 1.0 / total
        segment(result, s)[...] = (out * chosen_heads(jnp.broadcast_to(wide, (PAIR, 2 * SEG)))).T.astype(BF16)
        lse[s] = top + jnp.log(total)

    def alone(group):
        for s in group:
            finish(s, stats[s, 0:1, :], stats[s, 1:2, :], kept[s])

    def body(group, span):
        shape = (PAIR, 2 * SEG)
        for s in group:
            stacked = split_turned(segment(queries, s)[...])
            top, total, out = weigh(1, span, table, s, slope, bias, pool, turned, stacked)
            near = stats[s, 0:1, :]
            both = jnp.maximum(near, top)
            near_scale = jnp.exp(near - both)
            far_scale = jnp.exp(top - both)
            total = stats[s, 1:2, :] * near_scale + total * far_scale
            out = kept[s] * chosen_heads(jnp.broadcast_to(near_scale, shape)) + out * (
                chosen_heads(jnp.broadcast_to(far_scale, shape))
            )
            finish(s, both, total, out)

    by_groups(table, 1, body, alone)
    copies = [
        pltpu.make_async_copy(result.at[pl.ds(j * rows, rows)], target, sem.at[j])
        for j, target in enumerate((o0, o1, o2, o3))
    ]
    start_all(copies)
    wait_all(copies)


def attend_far(table, meta, slopes, queries, below, above, kept, stats, deps=()):
    rows = queries[0].shape[0]
    specs = [SM] * 3 + [ANY] * (MEMBERS + 2) + [VM] * 2
    used = len(specs)
    outs = pl.pallas_call(
        skipping(attend_far_kernel, used, len(deps)),
        out_shape=[shaped((rows, PAIR), BF16)] * MEMBERS + [shaped((TREE, 1, 2 * SEG), F32)],
        in_specs=specs + [ANY] * len(deps),
        out_specs=[ANY] * MEMBERS + [VM],
        scratch_shapes=[
            pltpu.VMEM(((2 * INNER + 1) * SEG, 2 * PAIR), BF16),
            pltpu.VMEM((2 * INNER + 1, PAIR, SEG), BF16),
            pltpu.VMEM((TREE * SEG, PAIR), BF16),
            pltpu.VMEM((TREE * SEG, PAIR), BF16),
            pltpu.VMEM((2, SEG, 2 * SEG), F32),
            pltpu.SemaphoreType.DMA((MEMBERS + 2,)),
        ],
        compiler_params=params(),
        cost_estimate=lasting("attend_far"),
        name="attend_far",
    )(table, meta, slopes, *queries, below, above, kept, stats, *deps)
    return outs[:MEMBERS], outs[MEMBERS]


def spread(side, span, table, s, slope, bias, pool, turned, total, queries, outs, grads, lse):
    count = table[COUNT_AT[side] + s]
    query = segment(queries, s)[...]
    stacked = split_heads(query)
    grad = segment(grads, s)[...]
    stacked_grad = split_heads(grad)
    product = (grad.astype(F32) * segment(outs, s)[...].astype(F32)).T
    delta = jnp.concatenate(
        [
            jnp.sum(product[:HD], axis=0, keepdims=True),
            jnp.sum(product[HD:], axis=0, keepdims=True),
        ],
        axis=1,
    )
    log_total = lse[s]
    spots, levels = entries(table, side, s, span)
    keys = jnp.concatenate([segment(pool, spot)[:, :PAIR] for spot in spots], axis=0)
    values = jnp.concatenate([segment(pool, spot)[:, PAIR:] for spot in spots], axis=0)
    raw = dot(keys, split_turned(query))
    prob_grad = dot(values, split_turned(grad))
    probs, score_grads = [], []
    for i in range(span):
        at = slice(i * SEG, (i + 1) * SEG)
        row = level_row(slope, levels, i, count) - log_total
        own = side == 0 and i == 0
        prob = jnp.exp(raw[at] + bias[0 if own else 1] + row)
        score_grads.append((prob * (prob_grad[at] - delta)).astype(BF16))
        probs.append(prob.astype(BF16))
    score_grad = jnp.concatenate(score_grads, axis=0)
    key_grad = dot(score_grad, stacked)
    value_grad = dot(jnp.concatenate(probs, axis=0), stacked_grad)
    for i in range(span):
        at = slice(i * SEG, (i + 1) * SEG)
        into = segment(total, spots[i])
        into[:, :PAIR] += key_grad[at]
        into[:, PAIR:] += value_grad[at]
    across = jnp.concatenate([turned[spot] for spot in spots], axis=1)
    return chosen_heads(dot(across, score_grad))


def clear_all(total, count):
    def clear(i, _):
        segment(total, i)[...] = jnp.zeros((SEG, 2 * PAIR), F32)
        return _

    lax.fori_loop(0, count, clear, 0, unroll=True)


def back_far_kernel(
    table, meta, slopes, q0, q1, q2, q3, below, above, o0, o1, o2, o3, g0, g1, g2, g3, lse,
    to_below, to_above, kept,
    pool, turned, queries, outs, grads, total, small, bias, sem,
):
    copies = loads((below, above), pool, sem, 0)
    copies += loads((q0, q1, q2, q3), queries, sem, 2)
    copies += loads((o0, o1, o2, o3), outs, sem, 2 + MEMBERS)
    copies += loads((g0, g1, g2, g3), grads, sem, 2 + 2 * MEMBERS)
    start_all(copies)
    slope = slope_row(slopes, meta)
    fill_bias(bias, slope)
    pool[2 * INNER * SEG :, :] = jnp.zeros((SEG, 2 * PAIR), BF16)
    clear_all(total, 2 * INNER + 1)
    wait_all(copies)
    turn_all(pool, turned, 2 * INNER, 0)

    def alone(group):
        for s in group:
            kept[s] = jnp.zeros((PAIR, SEG), F32)

    def body(group, span):
        for s in group:
            kept[s] = spread(
                1, span, table, s, slope, bias, pool, turned, total, queries, outs, grads, lse
            )

    by_groups(table, 1, body, alone)

    def shorten(i, _):
        segment(small, i)[...] = segment(total, i)[...].astype(BF16)
        return _

    lax.fori_loop(0, 2 * INNER, shorten, 0)
    copies = [
        pltpu.make_async_copy(
            small.at[pl.ds(k * INNER * SEG, INNER * SEG)], target, sem.at[k]
        )
        for k, target in enumerate((to_below, to_above))
    ]
    start_all(copies)
    wait_all(copies)


def back_far(table, meta, slopes, queries, below, above, outs, grads, lse, deps=()):
    side = shaped((INNER * SEG, 2 * PAIR), BF16)
    specs = [SM] * 3 + [ANY] * (3 * MEMBERS + 2) + [VM]
    used = len(specs)
    return pl.pallas_call(
        skipping(back_far_kernel, used, len(deps)),
        out_shape=[side, side, shaped((TREE, PAIR, SEG), F32)],
        in_specs=specs + [ANY] * len(deps),
        out_specs=[ANY] * 2 + [VM],
        scratch_shapes=[
            pltpu.VMEM(((2 * INNER + 1) * SEG, 2 * PAIR), BF16),
            pltpu.VMEM((2 * INNER + 1, PAIR, SEG), BF16),
            pltpu.VMEM((TREE * SEG, PAIR), BF16),
            pltpu.VMEM((TREE * SEG, PAIR), BF16),
            pltpu.VMEM((TREE * SEG, PAIR), BF16),
            pltpu.VMEM(((2 * INNER + 1) * SEG, 2 * PAIR), F32),
            pltpu.VMEM((2 * INNER * SEG, 2 * PAIR), BF16),
            pltpu.VMEM((2, SEG, 2 * SEG), F32),
            pltpu.SemaphoreType.DMA((3 * MEMBERS + 2,)),
        ],
        compiler_params=params(),
        cost_estimate=lasting("back_far"),
        name="back_far",
    )(table, meta, slopes, *queries, below, above, *outs, *grads, lse, *deps)


def back_near_kernel(
    table, meta, slopes, q0, q1, q2, q3, kv0, kv1, kv2, kv3, o0, o1, o2, o3, g0, g1, g2, g3,
    lse, kept, dq0, dq1, dq2, dq3, own,
    pool, turned, queries, outs, grads, result, total, bias, sem,
):
    rows = SEG_DEV * SEG
    copies = loads((kv0, kv1, kv2, kv3), pool, sem, 0)
    copies += loads((q0, q1, q2, q3), queries, sem, MEMBERS)
    copies += loads((o0, o1, o2, o3), outs, sem, 2 * MEMBERS)
    copies += loads((g0, g1, g2, g3), grads, sem, 3 * MEMBERS)
    start_all(copies)
    slope = slope_row(slopes, meta)
    fill_bias(bias, slope)
    pool[TREE * SEG :, :] = jnp.zeros((SEG, 2 * PAIR), BF16)
    clear_all(total, TREE + 1)
    wait_all(copies)
    turn_all(pool, turned, TREE, 0)

    def body(group, span):
        for s in group:
            part = spread(
                0, span, table, s, slope, bias, pool, turned, total, queries, outs, grads, lse
            )
            segment(result, s)[...] = (kept[s] + part).T.astype(BF16)

    by_groups(table, 0, body)
    copies = [
        pltpu.make_async_copy(result.at[pl.ds(j * rows, rows)], target, sem.at[j])
        for j, target in enumerate((dq0, dq1, dq2, dq3))
    ]
    copies.append(
        pltpu.make_async_copy(total.at[pl.ds(0, TREE * SEG)], own, sem.at[MEMBERS])
    )
    start_all(copies)
    wait_all(copies)


def back_near(table, meta, slopes, queries, pairs, outs, grads, lse, kept, deps=()):
    rows = queries[0].shape[0]
    specs = [SM] * 3 + [ANY] * (4 * MEMBERS) + [VM] * 2
    used = len(specs)
    result = pl.pallas_call(
        skipping(back_near_kernel, used, len(deps)),
        out_shape=[shaped((rows, PAIR), BF16)] * MEMBERS + [shaped((TREE * SEG, 2 * PAIR), F32)],
        in_specs=specs + [ANY] * len(deps),
        out_specs=[ANY] * (MEMBERS + 1),
        scratch_shapes=[
            pltpu.VMEM(((TREE + 1) * SEG, 2 * PAIR), BF16),
            pltpu.VMEM((TREE + 1, PAIR, SEG), BF16),
            pltpu.VMEM((TREE * SEG, PAIR), BF16),
            pltpu.VMEM((TREE * SEG, PAIR), BF16),
            pltpu.VMEM((TREE * SEG, PAIR), BF16),
            pltpu.VMEM((TREE * SEG, PAIR), BF16),
            pltpu.VMEM(((TREE + 1) * SEG, 2 * PAIR), F32),
            pltpu.VMEM((2, SEG, 2 * SEG), F32),
            pltpu.SemaphoreType.DMA((4 * MEMBERS,)),
        ],
        compiler_params=params(),
        cost_estimate=lasting("back_near"),
        name="back_near",
    )(table, meta, slopes, *queries, *pairs, *outs, *grads, lse, kept, *deps)
    return result[:MEMBERS], result[MEMBERS]


def gather_back_kernel(table, own, from_above, from_below, k0, k1, k2, k3, total, sem):
    rows = SEG_DEV * SEG
    copy = pltpu.make_async_copy(own, total, sem)
    copy.start()
    copy.wait()
    for at, source in ((UP_AT, from_above), (DOWN_AT, from_below)):

        def add(i, _):
            spot = table[at + i]

            @pl.when(spot >= 0)
            def _add():
                segment(total, spot)[...] += segment(source, i)[...].astype(F32)

            return _

        lax.fori_loop(0, INNER, add, 0)
    for j, target in enumerate((k0, k1, k2, k3)):

        def short(i, _):
            segment(target, i)[...] = segment(total, j * SEG_DEV + i)[...].astype(BF16)
            return _

        lax.fori_loop(0, SEG_DEV, short, 0)


def gather_back(table, own, from_above, from_below, deps=()):
    rows = SEG_DEV * SEG
    specs = [SM, ANY, VM, VM]
    used = len(specs)
    return pl.pallas_call(
        skipping(gather_back_kernel, used, len(deps)),
        out_shape=[shaped((rows, 2 * PAIR), BF16)] * MEMBERS,
        in_specs=specs + [ANY] * len(deps),
        out_specs=[VM] * MEMBERS,
        scratch_shapes=[
            pltpu.VMEM((TREE * SEG, 2 * PAIR), F32),
            pltpu.SemaphoreType.DMA(()),
        ],
        compiler_params=params(),
        cost_estimate=lasting("gather_back"),
        name="gather_back",
    )(table, own, from_above, from_below, *deps)


TILE = 256
def feed_kernel(
    meta, x, vectors, a0, a1, a2, a3, b0, b1, b2, b3,
    w_own, w_other, w_up, hidden_grad,
    mixed_out, middle_out, normed_out, act_out, pre_out, part, sums,
    mixed_own, middle, normed, act, pre_grad, mixed, weight, up, hidden, sem, out_sem,
):
    member, rank = meta[0], meta[3]
    rows, width = x.shape
    half = width // 2
    inner = w_up.shape[1]
    copies = []
    for k, source in enumerate((w_own, w_other)):
        at = pl.multiple_of((rank ^ k) * half, half)
        copies.append(pltpu.make_async_copy(source, weight.at[pl.ds(at, half)], sem.at[k]))
    late = [
        pltpu.make_async_copy(w_up, up, sem.at[2]),
        pltpu.make_async_copy(hidden_grad, hidden, sem.at[3]),
    ]
    start_all(copies + late)
    for k, parts in enumerate(((a0, a1, a2, a3), (b0, b1, b2, b3))):
        for d in range(MEMBERS):
            inside = (member ^ d) * PAIR
            at = pl.multiple_of((rank ^ k) * half + inside, PAIR)
            mixed[:, pl.ds(at, PAIR)] = parts[d][...]
            if k == 0:
                mixed_own[:, pl.ds(pl.multiple_of(inside, PAIR), PAIR)] = parts[d][...]
    stores = [pltpu.make_async_copy(mixed_own, mixed_out, out_sem.at[0])]
    stores[0].start()
    wait_all(copies)

    def column(t, _):
        at = pl.ds(pl.multiple_of(t * TILE, TILE), TILE)
        middle[:, at] = (
            x[:, at].astype(F32) + (dot(mixed[...], weight[:, at]) + vectors[OUT_BIAS : OUT_BIAS + 1, at])
        )
        return _

    lax.fori_loop(0, width // TILE, column, 0)
    stores.append(pltpu.make_async_copy(middle, middle_out, out_sem.at[1]))
    stores[1].start()

    def norm_step(at):
        hat, _scale = normal(middle[at, :])
        normed[at, :] = (hat * vectors[GAIN_F : GAIN_F + 1] + vectors[SHIFT_F : SHIFT_F + 1]).astype(BF16)

    norm_loop(rows, norm_step)
    stores.append(pltpu.make_async_copy(normed, normed_out, out_sem.at[2]))
    stores[2].start()
    wait_all(late)

    def hidden_step(t, _):
        at = pl.ds(pl.multiple_of(t * TILE, TILE), TILE)
        per = width // TILE
        bias = vectors[pl.ds(UP_BIAS + t // per, 1), pl.ds(pl.multiple_of(lax.rem(t, per) * TILE, TILE), TILE)]
        pre = dot(normed[...], up[:, at]) + bias
        square = pre * pre
        c = 0.7978845608028654
        t_ = jnp.tanh(pre * (c + (c * 0.044715) * square))
        low = 0.5 * (1.0 + t_)
        act[:, at] = (pre * low).astype(BF16)
        slope = low + (0.5 * pre) * (1.0 - t_ * t_) * (c + (3.0 * c * 0.044715) * square)
        grad = (hidden[:, at] * slope).astype(BF16)
        pre_grad[:, at] = grad
        sums[0:1, at] = jnp.sum(grad.astype(F32), axis=0, keepdims=True)
        return _

    lax.fori_loop(0, inner // TILE, hidden_step, 0)
    stores.append(pltpu.make_async_copy(act, act_out, out_sem.at[3]))
    stores.append(pltpu.make_async_copy(pre_grad, pre_out, out_sem.at[4]))
    start_all(stores[3:])

    def back(t, _):
        at = pl.ds(pl.multiple_of(t * TILE, TILE), TILE)
        part[:, at] = dot(pre_grad[...], up[at, :], ((1,), (1,))).astype(BF16)
        return _

    lax.fori_loop(0, width // TILE, back, 0)
    wait_all(stores)


def feed(meta, x, vectors, parts_own, parts_other, w_own, w_other, w_up, hidden_grad):
    rows, width = x.shape
    inner = w_up.shape[1]
    half = width // 2
    return pl.pallas_call(
        feed_kernel,
        out_shape=[
            shaped((rows, half), BF16),
            shaped((rows, width), F32),
            shaped((rows, width), BF16),
            shaped((rows, inner), BF16),
            shaped((rows, inner), BF16),
            shaped((rows, width), BF16),
            shaped((8, inner), F32),
        ],
        in_specs=[SM] + [VM] * (2 + 2 * MEMBERS) + [ANY] * 4,
        out_specs=[ANY] * 5 + [VM] * 2,
        scratch_shapes=[
            pltpu.VMEM((rows, half), BF16),
            pltpu.VMEM((rows, width), F32),
            pltpu.VMEM((rows, width), BF16),
            pltpu.VMEM((rows, inner), BF16),
            pltpu.VMEM((rows, inner), BF16),
            pltpu.VMEM((rows, width), BF16),
            pltpu.VMEM((width, width), BF16),
            pltpu.VMEM((width, inner), BF16),
            pltpu.VMEM((rows, inner), F32),
            pltpu.SemaphoreType.DMA((4,)),
            pltpu.SemaphoreType.DMA((5,)),
        ],
        compiler_params=params(),
        cost_estimate=lasting("feed"),
        name="feed",
    )(meta, x, vectors, *parts_own, *parts_other, w_own, w_other, w_up, hidden_grad)


def product_kernel(dims, left, right, out):
    out[...] = dot(left[...], right[...], dims).astype(out.dtype)


def product(name, left, right, turned, kind, deps=()):
    rows, depth = left.shape
    across = right.shape[0] if turned else right.shape[1]
    block = (TILE, depth) if turned else (depth, TILE)
    return pl.pallas_call(
        skipping(partial(product_kernel, ((1,), (1,) if turned else (0,))), 2, len(deps)),
        grid=(across // TILE,),
        out_shape=shaped((rows, across), kind),
        in_specs=[
            pl.BlockSpec((rows, depth), lambda t: (0, 0)),
            pl.BlockSpec(block, (lambda t: (t, 0)) if turned else (lambda t: (0, t))),
        ]
        + [ANY] * len(deps),
        out_specs=pl.BlockSpec((rows, TILE), lambda t: (0, t)),
        compiler_params=params(),
        cost_estimate=lasting(name),
        name=name,
    )(left, right, *deps)


def turn_rows(source, target):
    def step(i, _):
        at = pl.ds(pl.multiple_of(i * SEG, SEG), SEG)
        target[at, :] = source[:, at].astype(F32).T.astype(BF16)
        return _

    lax.fori_loop(0, source.shape[1] // SEG, step, 0)


X_FIRST = (0, 1, 2, 3)
Z_FIRST = (0, 2, 3, 1)
MIXED = (0, 2, 1, 3)
Z_BLOCKS = (8, 4, 12)
DEVICES = 16


def block_place(relative, order):
    place = 0
    for bit in order:
        place = place * 2 + (lax.shift_right_logical(relative, bit) & 1)
    return place


def turn_ordered(tile, target, i, device, order, share):
    for k in range(SEG // share):
        block = i * (SEG // share) + k
        at = block_place(block ^ device, order) * share
        target[pl.ds(pl.multiple_of(at, share), share), :] = tile[k * share : (k + 1) * share]


def turn_source(source, target, device, order, share):
    def step(i, _):
        at = pl.ds(pl.multiple_of(i * SEG, SEG), SEG)
        tile = source[:, at].astype(F32).T.astype(BF16)
        turn_ordered(tile, target, i, device, order, share)
        return _

    lax.fori_loop(0, source.shape[1] // SEG, step, 0)


def feed_grads_kernel(
    meta, grad, act, normed, pre_grad, weight,
    keep_c, send_c0, send_c1, keep_e, send_e0, send_e1, part, turned,
):
    t = pl.program_id(0)
    tiles = pl.num_programs(0) // 2
    width = grad.shape[1]
    half = width // 2
    tile = pre_grad.shape[1]

    @pl.when(t == 0)
    def _first():
        turn_source(grad, turned, meta[4], MIXED, width // DEVICES)

    @pl.when(t == tiles)
    def _second():
        turn_source(normed, turned, meta[4], X_FIRST, width // DEVICES)

    @pl.when(t < tiles)
    def _contract():
        right = act[:, pl.ds(pl.multiple_of(t * tile, tile), tile)]
        keep_c[...] = dot(turned[:half], right).astype(BF16)
        leave = dot(turned[half:], right).astype(BF16)

        @pl.when(t < tiles // 2)
        def _low():
            send_c0[...] = leave

        @pl.when(t >= tiles // 2)
        def _high():
            send_c1[...] = leave

    @pl.when(t >= tiles)
    def _expand():
        keep_e[...] = dot(turned[:half], pre_grad[...]).astype(BF16)
        leave = dot(turned[half:], pre_grad[...]).astype(BF16)

        @pl.when(t < tiles + tiles // 2)
        def _low():
            send_e0[...] = leave

        @pl.when(t >= tiles + tiles // 2)
        def _high():
            send_e1[...] = leave

    part[...] = dot(act[...], weight[...]).astype(BF16)


def feed_grads(meta, grad, act, normed, pre_grad, weight):
    rows, width = grad.shape
    inner = act.shape[1]
    tile = 2 * TILE
    tiles = inner // tile
    piece = width // (2 * tiles)

    def steps(start, number):
        return pl.BlockSpec((width // 2, tile), lambda t: (0, jnp.clip(t - start, 0, number - 1)))

    both = [steps(0, tiles), steps(0, tiles // 2), steps(tiles // 2, tiles // 2)]
    both += [steps(tiles, tiles), steps(tiles, tiles // 2), steps(tiles + tiles // 2, tiles // 2)]
    kept, sent = shaped((width // 2, inner), BF16), shaped((width // 2, inner // 2), BF16)
    whole = pl.BlockSpec((rows, width), lambda t: (0, 0))
    return pl.pallas_call(
        feed_grads_kernel,
        grid=(2 * tiles,),
        out_shape=[kept, sent, sent, kept, sent, sent, shaped((rows, width), BF16)],
        in_specs=[
            SM,
            whole,
            pl.BlockSpec((rows, inner), lambda t: (0, 0)),
            whole,
            pl.BlockSpec((rows, tile), lambda t: (0, jnp.maximum(t - tiles, 0))),
            pl.BlockSpec((inner, piece), lambda t: (0, t)),
        ],
        out_specs=both + [pl.BlockSpec((rows, piece), lambda t: (0, t))],
        scratch_shapes=[pltpu.VMEM((width, rows), BF16)],
        compiler_params=params(),
        cost_estimate=lasting("feed_grads"),
        name="feed_grads",
    )(meta, grad, act, normed, pre_grad, weight)


def in_two(rows8):
    high = rows8.astype(BF16).astype(F32)
    low = rows8 - high
    return jnp.concatenate([high, low, jnp.zeros((SEG - 16, rows8.shape[1]), F32)], axis=0)


def add_half(keep, got, stay, leave):
    half = stay.shape[0]
    stay[...] = keep[:half].astype(F32) + got[:half].astype(F32)
    leave[...] = (keep[half:].astype(F32) + got[half:].astype(F32)).astype(BF16)


TAKE_STEPS = 4


def take_specs(shape):
    rows, across = shape
    if across % (TAKE_STEPS * PAIR) == 0:
        tile, at = across // TAKE_STEPS, lambda t: (0, t)
    else:
        tile, at = across, lambda t: (0, 0)
    return pl.BlockSpec((rows, tile), at), pl.BlockSpec((rows // 2, tile), at)


def add_halves(flags, ins, outs):
    for k, split in enumerate(flags):
        step = partial(add_half, ins[2 * k], ins[2 * k + 1], outs[2 * k], outs[2 * k + 1])
        if split:
            step()
        else:
            pl.when(pl.program_id(0) == 0)(step)


def halves_of(pairs):
    specs, outs, shapes, flags, args = [], [], [], [], []
    for keep, got in pairs:
        whole, part = take_specs(keep.shape)
        half = (keep.shape[0] // 2, keep.shape[1])
        specs += [whole, whole]
        outs += [part, part]
        shapes += [shaped(half, F32), shaped(half, BF16)]
        flags.append(whole.block_shape[1] != keep.shape[1])
        args += [keep, got]
    return specs, outs, shapes, flags, args


def takes_kernel(flags, count, *refs):
    ins, outs = refs[: 2 * len(flags)], refs[2 * len(flags) + count :]
    add_halves(flags, ins, outs)


def takes(name, pairs, deps=()):
    specs, outs, shapes, flags, args = halves_of(pairs)
    got = pl.pallas_call(
        partial(takes_kernel, flags, len(deps)),
        grid=(TAKE_STEPS,),
        out_shape=shapes,
        in_specs=specs + [ANY] * len(deps),
        out_specs=outs,
        compiler_params=params(),
        cost_estimate=lasting(name),
        name=name,
    )(*args, *deps)
    return [tuple(got[2 * k : 2 * k + 2]) for k in range(len(pairs))]


def output_grads_kernel(count, meta, branch, mixed, vectors, extra, *refs):
    ins = refs[: 3 * count]
    keep, send = refs[3 * count : 3 * count + 2]
    outs = refs[3 * count + 2 : -2]
    turned, small = refs[-2:]
    t = pl.program_id(0)
    width, across = branch.shape[1], mixed.shape[1]
    share = width // DEVICES
    half = width // 2

    @pl.when(t == 0)
    def _first():
        turn_source(branch, turned, meta[4], X_FIRST, share)
        for i in range(width // SEG):
            at = slice(i * SEG, (i + 1) * SEG)
            rows8 = jnp.concatenate(
                [vectors[0:4, at], extra[0:2, at], jnp.zeros((2, SEG), F32)], axis=0
            )
            turn_ordered(in_two(rows8).T, small, i, meta[4], X_FIRST, share)
        keep[:, across:] = small[:half].astype(BF16)
        send[:, across:] = small[half:].astype(BF16)

    tile = across // TAKE_STEPS
    at = pl.ds(pl.multiple_of(t * tile, tile), tile)
    keep[:, at] = dot(turned[:half], mixed[:, at]).astype(BF16)
    send[:, at] = dot(turned[half:], mixed[:, at]).astype(BF16)
    for k in range(count):
        kept, low, high = ins[3 * k : 3 * k + 3]

        @pl.when(t < TAKE_STEPS // 2)
        def _low():
            add_half(kept, low, outs[2 * k], outs[2 * k + 1])

        @pl.when(t >= TAKE_STEPS // 2)
        def _high():
            add_half(kept, high, outs[2 * k], outs[2 * k + 1])


def output_grads(meta, branch, mixed, vectors, extra, pairs):
    rows, width = branch.shape
    across = mixed.shape[1]
    half_steps = TAKE_STEPS // 2
    specs, outs, shapes, args = [], [], [], []
    for kept, low, high in pairs:
        high_rows, cols = kept.shape
        tile = cols // TAKE_STEPS
        specs += [
            pl.BlockSpec((high_rows, tile), lambda t: (0, t)),
            pl.BlockSpec((high_rows, tile), lambda t: (0, jnp.minimum(t, half_steps - 1))),
            pl.BlockSpec((high_rows, tile), lambda t: (0, jnp.maximum(t - half_steps, 0))),
        ]
        outs += [pl.BlockSpec((high_rows // 2, tile), lambda t: (0, t))] * 2
        shapes += [shaped((high_rows // 2, cols), F32), shaped((high_rows // 2, cols), BF16)]
        args += [kept, low, high]

    def whole(shape):
        return pl.BlockSpec(shape, lambda t: (0, 0))

    own = whole((width // 2, across + SEG))
    got = pl.pallas_call(
        partial(output_grads_kernel, len(pairs)),
        grid=(TAKE_STEPS,),
        out_shape=[shaped((width // 2, across + SEG), BF16)] * 2 + shapes,
        in_specs=[SM, whole(branch.shape), whole(mixed.shape), whole(vectors.shape), whole(extra.shape)]
        + specs,
        out_specs=[own, own] + outs,
        scratch_shapes=[pltpu.VMEM((width, rows), BF16), pltpu.VMEM((width, SEG), F32)],
        compiler_params=params(),
        cost_estimate=lasting("output_grads"),
        name="output_grads",
    )(meta, branch, mixed, vectors, extra, *args)
    return (got[0], got[1]), [tuple(got[2 + 2 * k : 4 + 2 * k]) for k in range(len(pairs))]


def first_sums_kernel(
    a, got_a, b, got_b, last_b, stay_a, leave_a, stay_b, b1, b2, b3
):
    add_half(a, got_a, stay_a, leave_a)
    rows = stay_b.shape[0]
    cut = got_b.shape[1]
    for cols, got in ((slice(0, cut), got_b), (slice(cut, b.shape[1]), last_b)):
        stay_b[:, cols] = b[:rows, cols].astype(F32) + got[:rows].astype(F32)
        for k, target in enumerate((b1, b2, b3)):
            at = slice((k + 1) * rows, (k + 2) * rows)
            target[:, cols] = (b[at, cols].astype(F32) + got[at].astype(F32)).astype(BF16)


def first_sums(a, b):
    half, across_a = a[0].shape
    across_b = b[0].shape[1]
    part_a, part_b = (half // 2, across_a), (half // 4, across_b)
    return pl.pallas_call(
        first_sums_kernel,
        out_shape=[shaped(part_a, F32), shaped(part_a, BF16), shaped(part_b, F32)]
        + [shaped(part_b, BF16)] * 3,
        in_specs=[VM] * 5,
        out_specs=[VM] * 6,
        compiler_params=params(),
        cost_estimate=lasting("first_sums"),
        name="first_sums",
    )(*a, *b)


def second_sums_kernel(a, got_a, b, g1, g2, g3, stay_a, a1, a2, a3, stay_b, leave_b):
    rows = stay_a.shape[0]
    stay_a[...] = a[:rows] + got_a[:rows].astype(F32)
    for k, target in enumerate((a1, a2, a3)):
        at = slice((k + 1) * rows, (k + 2) * rows)
        target[...] = (a[at] + got_a[at].astype(F32)).astype(BF16)
    total = b[...] + g1[...].astype(F32) + g2[...].astype(F32) + g3[...].astype(F32)
    half = stay_b.shape[0]
    stay_b[...] = total[:half]
    leave_b[...] = total[half:].astype(BF16)


def second_sums(a, b, got_b, deps=()):
    rows, across_a = a[0].shape
    half, across_b = b.shape
    part_a, part_b = (rows // 4, across_a), (half // 2, across_b)
    return pl.pallas_call(
        skipping(second_sums_kernel, 6, len(deps)),
        out_shape=[shaped(part_a, F32)]
        + [shaped(part_a, BF16)] * 3
        + [shaped(part_b, F32), shaped(part_b, BF16)],
        in_specs=[VM] * 6 + [ANY] * len(deps),
        out_specs=[VM] * 6,
        compiler_params=params(),
        cost_estimate=lasting("second_sums"),
        name="second_sums",
    )(*a, b, *got_b, *deps)


def finish_kernel(o, a, g1, g2, g3, b, got_b, output, weight, v0, v1, v2, v3, bias, w0, w1, w2):
    across = output.shape[1]
    output[...] = o[:, :across]
    small = o[:, across:].T
    whole = small[0:8] + small[8:16]
    for k, target in enumerate((v0, v1, v2, v3)):
        target[...] = whole[k : k + 1]
    bias[...] = jnp.concatenate([whole[4:5], whole[5:6]], axis=1)
    total = b[...] + got_b[...].astype(F32)
    cut = a.shape[1]
    rest = b.shape[1] - SEG
    weight[:, :cut] = a[...] + g1[...].astype(F32) + g2[...].astype(F32) + g3[...].astype(F32)
    weight[:, cut:] = total[:, :rest]
    small = total[:, rest:].T
    whole = small[0:8] + small[8:16]
    for k, target in enumerate((w0, w1, w2)):
        target[...] = whole[k : k + 1]


def finish(o, a, got_a, b, got_b):
    rows = o.shape[0]
    vector = shaped((1, rows), F32)
    return pl.pallas_call(
        finish_kernel,
        out_shape=[
            shaped((rows, o.shape[1] - SEG), F32),
            shaped((rows, a.shape[1] + b.shape[1] - SEG), F32),
        ]
        + [vector] * 4
        + [shaped((1, 2 * rows), F32)]
        + [vector] * 3,
        in_specs=[VM] * 7,
        out_specs=[VM] * 10,
        compiler_params=params(),
        cost_estimate=lasting("finish"),
        name="finish",
    )(o, a, *got_a, b, got_b)


def norm_back(hat, scale, up):
    mean_up = jnp.mean(up, axis=-1, keepdims=True)
    mean_both = jnp.mean(up * hat, axis=-1, keepdims=True)
    return scale * (up - mean_up - hat * mean_both)


def middle_back_kernel(
    meta, middle, part, other, grad, gains, weight,
    branch, vectors, g0, g1, g2, g3,
):
    member = meta[0]
    rows, width = middle.shape
    vectors[...] = jnp.zeros_like(vectors)

    def norm_step(at):
        hat, scale = normal(middle[at, :])
        second = part[at, :].astype(F32) + other[at, :].astype(F32)
        given = grad[at, :].astype(F32)
        back = given + norm_back(hat, scale, second * gains[GAIN_F : GAIN_F + 1])
        branch[at, :] = back.astype(BF16)
        vectors[0:1, :] += jnp.sum(second * hat, axis=0, keepdims=True)
        vectors[1:2, :] += jnp.sum(second, axis=0, keepdims=True)
        vectors[2:3, :] += jnp.sum(back, axis=0, keepdims=True)
        vectors[3:4, :] += jnp.sum(given, axis=0, keepdims=True)

    norm_loop(rows, norm_step)
    for d, target in enumerate((g0, g1, g2, g3)):
        at = pl.multiple_of((member ^ d) * PAIR, PAIR)
        target[...] = dot(branch[...], weight[pl.ds(at, PAIR), :], ((1,), (1,))).astype(BF16)


def middle_back(meta, middle, part, other, grad, gains, weight, deps=()):
    rows, width = middle.shape
    specs = [SM] + [VM] * 6
    used = len(specs)
    outs = pl.pallas_call(
        skipping(middle_back_kernel, used, len(deps)),
        out_shape=[shaped((rows, width), BF16), shaped((8, width), F32)]
        + [shaped((rows, PAIR), BF16)] * MEMBERS,
        in_specs=specs + [ANY] * len(deps),
        out_specs=[VM] * (2 + MEMBERS),
        compiler_params=params(),
        cost_estimate=lasting("middle_back"),
        name="middle_back",
    )(meta, middle, part, other, grad, gains, weight, *deps)
    return outs[0], outs[1], outs[2:]


def join_kernel(riders, meta, weight, q0, q1, q2, q3, k0, k1, k2, k3, *refs):
    joined, part, sums = refs[2 * riders : 2 * riders + 3]
    at = 0
    for k in range(riders):
        keep, got, stay = refs[2 * k], refs[2 * k + 1], refs[2 * riders + 3 + k]
        leave = refs[-1].at[:, at : at + keep.shape[1]]
        add_half(keep, got, stay, leave)
        at += keep.shape[1]
    member = meta[0]
    low = lanes((1, PAIR)) < HD
    for d, (query, both) in enumerate(((q0, k0), (q1, k1), (q2, k2), (q3, k3))):
        wide_q = query[...].astype(F32) * (HD ** (-0.5))
        wide_k = pltpu.roll(both[:, :PAIR].astype(F32), HD, 1)
        wide_v = both[:, PAIR:].astype(F32)
        at = (member ^ d) * 3 * PAIR
        for k, tile in enumerate(
            (
                jnp.where(low, wide_q, wide_k),
                jnp.where(low, wide_v, wide_q),
                jnp.where(low, wide_k, wide_v),
            )
        ):
            joined[:, pl.ds(pl.multiple_of(at + k * PAIR, PAIR), PAIR)] = tile.astype(BF16)
        sum_q = jnp.sum(wide_q, axis=0, keepdims=True)
        sum_v = jnp.sum(wide_v, axis=0, keepdims=True)
        spot = pl.multiple_of((member ^ d) * 2 * PAIR, PAIR)
        sums[0:1, pl.ds(spot, PAIR)] = jnp.where(low, sum_q, pltpu.roll(sum_v, HD, 1))
        sums[0:1, pl.ds(pl.multiple_of(spot + PAIR, PAIR), PAIR)] = jnp.where(
            low, pltpu.roll(sum_q, HD, 1), sum_v
        )
    width = weight.shape[0]

    def column(t, _):
        at = pl.ds(pl.multiple_of(t * TILE, TILE), TILE)
        part[:, at] = dot(joined[...], weight[at, :], ((1,), (1,))).astype(BF16)
        return _

    lax.fori_loop(0, width // TILE, column, 0)


def join_stage(meta, weight, query_grads, pair_grads, riders=()):
    rows = query_grads[0].shape[0]
    width, across = weight.shape
    outs = [
        shaped((rows, across), BF16),
        shaped((rows, width), BF16),
        shaped((8, 2 * MEMBERS * PAIR), F32),
    ]
    if riders:
        half = riders[0][0].shape[0] // 2
        outs += [shaped((half, keep.shape[1]), F32) for keep, _got in riders]
        outs.append(shaped((half, sum(keep.shape[1] for keep, _got in riders)), BF16))
    return pl.pallas_call(
        partial(join_kernel, len(riders)),
        out_shape=outs,
        in_specs=[SM] + [VM] * (1 + 2 * MEMBERS + 2 * len(riders)),
        out_specs=[VM] * len(outs),
        compiler_params=params(),
        cost_estimate=lasting("join_stage"),
        name="join_stage",
    )(meta, weight, *query_grads, *pair_grads, *[part for pair in riders for part in pair])


FIRST_PART = 1024


def joined_first_kernel(meta, x, part, normed, joined, keep, send, vectors, turned):
    rows, width = x.shape
    device = meta[4]
    turn_source(normed, turned, device, X_FIRST, width // DEVICES)
    half = width // 2
    tile = TILE

    def column(t, _):
        at = pl.ds(pl.multiple_of(t * tile, tile), tile)
        keep[:, at] = dot(turned[:half], joined[:, at]).astype(BF16)
        send[:, at] = dot(turned[half:], joined[:, at]).astype(BF16)
        return _

    lax.fori_loop(0, keep.shape[1] // tile, column, 0)
    vectors[...] = jnp.zeros_like(vectors)

    def norm_step(at):
        hat, _scale = normal(x[at, :].astype(F32))
        first = part[at, :].astype(F32)
        vectors[0:1, :] += jnp.sum(first * hat, axis=0, keepdims=True)
        vectors[1:2, :] += jnp.sum(first, axis=0, keepdims=True)

    norm_loop(rows, norm_step)


def joined_first(meta, x, part, normed, joined, deps=()):
    rows, width = x.shape
    half = width // 2
    return pl.pallas_call(
        skipping(joined_first_kernel, 5, len(deps)),
        out_shape=[
            shaped((half, FIRST_PART), BF16),
            shaped((half, FIRST_PART), BF16),
            shaped((8, width), F32),
        ],
        in_specs=[SM] + [VM] * 4 + [ANY] * len(deps),
        out_specs=[VM] * 3,
        scratch_shapes=[pltpu.VMEM((width, rows), BF16)],
        compiler_params=params(),
        cost_estimate=lasting("joined_first"),
        name="joined_first",
    )(meta, x, part, normed, joined, *deps)


def joined_second_kernel(
    meta, normed, joined, vectors, other, sums, c, got_c, e, o, got_eo,
    keep, send, last, contract, expand, output, turned, small,
):
    contract[...] = c[...] + got_c[...].astype(F32)
    inner = e.shape[1]
    expand[...] = e[...] + got_eo[:, :inner].astype(F32)
    output[...] = o[...] + got_eo[:, inner:].astype(F32)
    width = normed.shape[1]
    device = meta[4]
    share = width // DEVICES
    turn_source(normed, turned, device, Z_FIRST, share)
    half = width // 2
    across = joined.shape[1] - FIRST_PART
    tile = TILE

    def column(t, _):
        at = pl.ds(pl.multiple_of(t * tile, tile), tile)
        source = pl.ds(pl.multiple_of(FIRST_PART + t * tile, tile), tile)
        keep[:, at] = dot(turned[:half], joined[:, source]).astype(BF16)
        leave = dot(turned[half:], joined[:, source]).astype(BF16)

        @pl.when(t == 0)
        def _first():
            send[...] = leave

        @pl.when(t == 1)
        def _last():
            last[:, :tile] = leave
        return _

    lax.fori_loop(0, across // tile, column, 0)
    for i in range(width // SEG):
        at = slice(i * SEG, (i + 1) * SEG)
        rows8 = jnp.concatenate(
            [vectors[0:2, at] + other[0:2, at], sums[0:1, at], jnp.zeros((5, SEG), F32)], axis=0
        )
        turn_ordered(in_two(rows8).T, small, i, device, Z_FIRST, share)
    keep[:, across:] = small[:half].astype(BF16)
    last[:, tile:] = small[half:].astype(BF16)


def joined_second(meta, normed, joined, vectors, other, sums, c, got_c, e, o, got_eo):
    rows, width = normed.shape
    half = width // 2
    across = joined.shape[1] - FIRST_PART + SEG
    return pl.pallas_call(
        joined_second_kernel,
        out_shape=[
            shaped((half, across), BF16),
            shaped((half, TILE), BF16),
            shaped((half, across - TILE), BF16),
            shaped(c.shape, F32),
            shaped(e.shape, F32),
            shaped(o.shape, F32),
        ],
        in_specs=[SM] + [VM] * 10,
        out_specs=[VM] * 6,
        scratch_shapes=[pltpu.VMEM((width, rows), BF16), pltpu.VMEM((width, SEG), F32)],
        compiler_params=params(),
        cost_estimate=lasting("joined_second"),
        name="joined_second",
    )(meta, normed, joined, vectors, other, sums, c, got_c, e, o, got_eo)


def input_back_kernel(x, part, other, gains, middle_grad, out):
    def norm_step(at):
        hat, scale = normal(x[at, :].astype(F32))
        first = part[at, :].astype(F32) + other[at, :].astype(F32)
        back = norm_back(hat, scale, first * gains[GAIN_A : GAIN_A + 1])
        out[at, :] = (back + middle_grad[at, :].astype(F32)).astype(BF16)

    norm_loop(x.shape[0], norm_step)


def input_back(x, part, other, gains, middle_grad):
    return pl.pallas_call(
        input_back_kernel,
        out_shape=shaped(x.shape, BF16),
        in_specs=[VM] * 5,
        out_specs=VM,
        compiler_params=params(),
        cost_estimate=lasting("input_back"),
        name="input_back",
    )(x, part, other, gains, middle_grad)


def stack_kernel(*refs):
    out, at = refs[-1], 0
    for ref in refs[:-1]:
        rows = ref.shape[0] // out.shape[1]
        out[at : at + rows, :] = ref[...].astype(F32).reshape(rows, out.shape[1])
        at += rows


def stack_vectors(*vectors):
    width = vectors[0].shape[0]
    rows = sum(vector.shape[0] for vector in vectors) // width
    return pl.pallas_call(
        stack_kernel,
        out_shape=shaped((rows, width), F32),
        in_specs=[VM] * len(vectors),
        out_specs=VM,
        name="stack_vectors",
    )(*vectors)


def swap(value):
    return lax.ppermute(value, "tensor", [(0, 1), (1, 0)])


def to_member(value, d):
    count = lax.axis_size("dp")
    return lax.ppermute(value, "dp", [(i, i ^ d) for i in range(count)])


def to_member_across(value, d):
    count = lax.axis_size("dp")
    pairs = [(i * 2 + t, (i ^ d) * 2 + (1 - t)) for i in range(count) for t in range(2)]
    return lax.ppermute(value, ("dp", "tensor"), pairs)


def to_group(value, by):
    count = lax.axis_size("dp")
    step = by * MEMBERS
    return lax.ppermute(value, "dp", [(i, (i + step) % count) for i in range(count)])


def within(parts):
    return [parts[0]] + [to_member(parts[d], d) for d in range(1, MEMBERS)]


def same_kernel(*refs):
    pass


def after_all(value, *others):
    return pl.pallas_call(
        same_kernel,
        out_shape=shaped(value.shape, value.dtype),
        in_specs=[ANY] * (1 + len(others)),
        out_specs=ANY,
        input_output_aliases={0: 0},
        cost_estimate=lasting("after_all"),
        name="after_all",
    )(value, *others)


def reduce_rows(value):
    return lax.psum_scatter(value, "dp", scatter_dimension=0, tiled=True)


def plain_sum(left, right):
    grad = jnp.einsum("td,tf->df", left, right, preferred_element_type=F32)
    return reduce_rows(grad.astype(BF16)).astype(F32)


def plain_sums(x, part, first_low, joined_grad, sums, cotangent, hidden_low, second_low, pre_grad, branch_low, mixed, feed_vectors, extra):
    hat, _scale = normal(x.astype(F32))
    wide = part.astype(F32)
    vectors = jnp.stack([jnp.sum(wide * hat, axis=0), jnp.sum(wide, axis=0)], axis=0)
    vectors = vectors + swap(vectors)
    small = reduce_rows(jnp.concatenate([feed_vectors[:4], extra, vectors, sums[:1]], axis=0).T)
    return (
        plain_sum(cotangent, hidden_low), plain_sum(second_low, pre_grad),
        plain_sum(branch_low, mixed), plain_sum(first_low, joined_grad),
        small[:, 0], small[:, 1], small[:, 2], small[:, 3], small[:, 4:6].T,
        small[:, 6], small[:, 7], small[:, 8],
    )


def shards(
    activations,
    cotangent,
    parent_slot,
    attention_gain,
    attention_shift,
    joined_weight,
    joined_bias,
    output_weight,
    output_bias,
    feed_gain,
    feed_shift,
    expand_weight,
    expand_bias,
    contract_weight,
    contract_bias,
):
    device = lax.axis_index("dp")
    count = lax.axis_size("dp")
    rank = lax.axis_index("tensor")
    member = lax.rem(device, MEMBERS)
    heads_here = joined_weight.shape[1] // (3 * HD)
    width = activations.shape[1]
    inner = expand_weight.shape[1]
    half = output_weight.shape[0]
    meta = jnp.stack(
        [member, device // MEMBERS, rank * heads_here + 2 * member, rank, device]
    ).astype(jnp.int32)
    slopes = jnp.exp2(-8.0 * jnp.arange(1, H + 1, dtype=F32) / H)

    vectors = stack_vectors(
        attention_gain, attention_shift, feed_gain, feed_shift, output_bias, contract_bias,
        joined_bias, expand_bias,
    )
    first_low, queries, pairs = project(meta, activations, vectors, joined_weight)
    table = make_tables(meta, parent_slot)
    pairs = within(pairs)
    queries = within(queries)
    up, down = pack(table, pairs)
    below = to_group(up, 1)
    above = to_group(down, -1)
    hidden_grad = product("hidden_grad", cotangent, contract_weight, True, F32, deps=(up,))
    other_output_weight = swap(output_weight)
    kept, stats = attend_near(table, meta, slopes, queries, pairs)
    outs, lse = attend_far(
        table, meta, slopes, queries, below, above, kept, stats,
        deps=(hidden_grad, other_output_weight),
    )
    parts_other = [to_member_across(outs[d], d) for d in range(MEMBERS)]
    parts_own = within(outs)
    mixed, middle, second_low, hidden_low, pre_grad, second_part, bias_sums = feed(
        meta, activations, vectors,
        parts_own, parts_other, output_weight, other_output_weight, expand_weight, hidden_grad,
    )
    second_other = swap(second_part)
    extra = bias_sums[0].reshape(count, 2, width // count).transpose(1, 0, 2).reshape(2, width)
    by_halves = count == DEVICES
    if by_halves:
        keep_c, c0, c1, keep_e, e0, e1, feed_part = feed_grads(
            meta, cotangent, hidden_low, second_low, pre_grad, contract_weight
        )
        c0, c1, e0, e1 = (to_member(part, 1) for part in (c0, c1, e0, e1))
    else:
        feed_part = product("feed_part", hidden_low, contract_weight, False, BF16)
    branch_low, feed_vectors, grad_parts = middle_back(
        meta, middle, second_part, second_other, cotangent, vectors, output_weight,
        deps=(feed_part,),
    )
    grad_parts = within(grad_parts)
    feed_other = swap(after_all(feed_part, branch_low))
    fill = ()
    if by_halves:
        (keep_o, send_o), ((keep_c, send_c), (keep_e, send_e)) = output_grads(
            meta, branch_low, mixed, feed_vectors, extra, [(keep_c, c0, c1), (keep_e, e0, e1)]
        )
        got_o, got_c, got_e = to_member(send_o, 1), to_member(send_c, 4), to_member(send_e, 2)
        fill = (keep_o,)
    to_below, to_above, kept_grad = back_far(
        table, meta, slopes, queries, below, above, outs, grad_parts, lse, deps=fill
    )
    from_above = to_group(to_below, -1)
    from_below = to_group(to_above, 1)
    query_grads, own = back_near(
        table, meta, slopes, queries, pairs, outs, grad_parts, lse, kept_grad, deps=(feed_other,)
    )
    query_grads = within(query_grads)
    layer_output = (
        middle + (feed_part.astype(F32) + feed_other.astype(F32)) + vectors[CONTRACT_BIAS]
    ).astype(BF16)
    fill = ()
    if by_halves:
        (keep_c, send_c), (keep_e, send_e), (keep_o, send_o) = takes(
            "second_step", [(keep_c, got_c), (keep_e, got_e), (keep_o, got_o)], deps=(own,)
        )
        got_c, got_o = to_member(send_c, 2), to_member(send_o, 2)
        fill = (keep_o,)
    own_pairs = gather_back(
        table, own, from_above, from_below, deps=tuple(query_grads) + (layer_output,) + fill
    )
    pair_grads = within(own_pairs)
    riders = ()
    if by_halves:
        got_e = to_member(after_all(send_e, own_pairs[0]), 4)
        (keep_c, send_c), (keep_o, send_o) = takes(
            "third_step", [(keep_c, got_c), (keep_o, got_o)], deps=(own_pairs[0],)
        )
        got_c, got_o = to_member(send_c, 8), to_member(send_o, 4)
        riders = ((keep_e, got_e), (keep_o, got_o))
    joined_grad, first_part, joined_bias_sums, *ridden = join_stage(
        meta, joined_weight, query_grads, pair_grads, riders
    )
    if by_halves:
        keep_e, keep_o, send_eo = ridden
        got_eo = to_member(send_eo, 8)
        keep_a, send_a, norm_vectors = joined_first(
            meta, activations, first_part, first_low, joined_grad
        )
        got_a = to_member(send_a, 1)
        norm_other = swap(norm_vectors)
        first_other = swap(after_all(first_part, norm_other))
        keep_b, send_b, last_b, contract_done, expand_done, output_sum = joined_second(
            meta, first_low, joined_grad, norm_vectors, norm_other, joined_bias_sums,
            keep_c, got_c, keep_e, keep_o, got_eo,
        )
        got_b, last_b = to_member(send_b, 1), to_member(last_b, 1)
        keep_a, send_a, keep_b, b1, b2, b3 = first_sums((keep_a, got_a), (keep_b, got_b, last_b))
        got_a = to_member(send_a, 2)
        got_b = [to_member(part, d) for part, d in zip((b1, b2, b3), Z_BLOCKS)]
        keep_a, a1, a2, a3, keep_b, send_b = second_sums((keep_a, got_a), keep_b, got_b)
        got_a = [to_member(part, d) for part, d in zip((a1, a2, a3), Z_BLOCKS)]
        got_b = to_member(send_b, 2)
        done = (contract_done, expand_done) + tuple(
            finish(output_sum, keep_a, got_a, keep_b, got_b)
        )
    else:
        first_other = swap(first_part)
        done = plain_sums(
            activations, first_part, first_low, joined_grad, joined_bias_sums, cotangent,
            hidden_low, second_low, pre_grad, branch_low, mixed, feed_vectors, extra,
        )
    input_gradient = input_back(activations, first_part, first_other, vectors, branch_low)
    (
        contract_done, expand_done, output_done, joined_done,
        feed_gain_grad, feed_shift_grad, output_bias_grad, contract_bias_grad, expand_bias_grad,
        gain_grad, shift_grad, joined_bias_grad,
    ) = done

    return (
        layer_output,
        input_gradient,
        gain_grad.reshape(-1),
        shift_grad.reshape(-1),
        joined_done,
        joined_bias_grad.reshape(-1, 1),
        output_done,
        output_bias_grad.reshape(-1),
        feed_gain_grad.reshape(-1),
        feed_shift_grad.reshape(-1),
        expand_done,
        expand_bias_grad.reshape(-1, 1),
        contract_done,
        contract_bias_grad.reshape(-1),
    )


def solution(mesh):
    in_specs = (
        P("dp", None),
        P("dp", None),
        P(),
        P(),
        P(),
        P(None, "tensor"),
        P("tensor"),
        P("tensor", None),
        P(),
        P(),
        P(),
        P(None, "tensor"),
        P("tensor"),
        P("tensor", None),
        P(),
    )
    out_specs = (
        P("dp", None),
        P("dp", None),
        P("dp"),
        P("dp"),
        P("dp", "tensor"),
        P("dp", "tensor"),
        P("dp", "tensor"),
        P("dp"),
        P("dp"),
        P("dp"),
        P("dp", "tensor"),
        P("dp", "tensor"),
        P("dp", "tensor"),
        P("dp"),
    )
    return jax.shard_map(shards, mesh=mesh, in_specs=in_specs, out_specs=out_specs, check_vma=False)
```

```python
from functools import partial

import jax
import jax.numpy as jnp
from jax import lax
from jax.experimental import pallas as pl
from jax.experimental.pallas import tpu as pltpu
from jax.sharding import PartitionSpec as P

H = 16
HD = 64
SEG = 128
SEG_DEV = 5
ANC = 10
TREE = 20
INNER = 12
MEMBERS = 4
PAIR = 2 * HD
POOL = TREE + 2 * INNER
EMPTY = POOL

EPSILON = 1e-05
NEGATIVE = -1e30

F32 = jnp.float32
BF16 = jnp.bfloat16

LISTS = TREE * ANC
SLOT_AT = (0, 2 * LISTS)
LEVEL_AT = (LISTS, 3 * LISTS)
COUNT_AT = (4 * LISTS, 4 * LISTS + TREE)
UP_AT, DOWN_AT, OFFSET_AT, LISTED = 0, INNER, 2 * INNER, 32
ORDER_AT = (4 * LISTS + 2 * TREE, 4 * LISTS + 3 * TREE)
TABLE = 1024
GROUP = 4

GAIN_A, SHIFT_A, GAIN_F, SHIFT_F, OUT_BIAS, CONTRACT_BIAS, JOINED_BIAS, UP_BIAS = range(8)

VM = pl.BlockSpec(memory_space=pltpu.VMEM)
SM = pl.BlockSpec(memory_space=pltpu.SMEM)
ANY = pl.BlockSpec(memory_space=pl.ANY)


def shaped(shape, kind):
    return jax.ShapeDtypeStruct(shape, kind)


def params(mib=60):
    return pltpu.CompilerParams(vmem_limit_bytes=mib * 2**20)


LASTS = {
    "project": 9, "lists": 2, "tables": 2, "pack": 1, "attend_near": 14, "hidden_grad": 5, "attend_far": 15,
    "feed": 18, "feed_grads": 20, "middle_back": 8, "output_grads": 9, "back_far": 14,
    "back_near": 15, "second_step": 5, "gather_back": 5, "third_step": 3, "join_stage": 7,
    "joined_first": 9, "joined_second": 60, "first_sums": 1, "second_sums": 1,
    "input_back": 6, "finish": 2, "feed_part": 4, "after_all": 0,
}
FLOPS_PER_US = 500_000_000


def lasting(name):
    return pl.CostEstimate(flops=LASTS[name] * FLOPS_PER_US, bytes_accessed=0, transcendentals=0)


def skipping(kernel, used, skipped):
    def run(*refs):
        kernel(*refs[:used], *refs[used + skipped :])

    return run


def dot(a, b, dims=((1,), (0,))):
    return lax.dot_general(a, b, (dims, ((), ())), preferred_element_type=F32)


def lanes(shape):
    return lax.broadcasted_iota(jnp.int32, shape, len(shape) - 1)


def rows_of(shape):
    return lax.broadcasted_iota(jnp.int32, shape, len(shape) - 2)


def lists_kernel(count, meta, parent, out, inner):
    member, group = meta[0], meta[1]

    def clear(i, _):
        inner[i] = 0
        return _

    lax.fori_loop(0, count, clear, 0, unroll=8)

    def mark(i, _):
        up = parent[i]

        @pl.when(up >= 0)
        def _mark():
            inner[up] = 1

        return _

    lax.fori_loop(0, count, mark, 0, unroll=4)

    def cover(i, mask):
        up = parent[i]
        ahead = up - i
        ahead = jnp.where(ahead < 0, ahead + count, ahead)
        forward = ahead < TREE
        low = jnp.where(forward, i, up)
        length = jnp.where(forward, ahead, count - ahead)
        length = jnp.where(up >= 0, length, 0)
        start = lax.rem(low + 1 + TREE, TREE)
        bits = lax.shift_left(1, length) - 1
        room = TREE - start
        first = lax.shift_left(bits & (lax.shift_left(1, room) - 1), start)
        second = lax.shift_right_logical(bits, room)
        return mask | first | second

    mask = lax.fori_loop(0, 2 * TREE - 1, cover, 0, unroll=3)
    offset = 0
    for c in range(TREE):
        free = (lax.shift_right_logical(mask, c) & 1) == 0
        offset = jnp.where(free, c, offset)
    out[OFFSET_AT] = offset
    for i in range(2 * INNER):
        out[UP_AT + i] = -1

    def own(p, ranks):
        up_rank, down_rank = ranks
        spot = ((p // SEG_DEV) ^ member) * SEG_DEV + lax.rem(p, SEG_DEV)
        has = inner[group * TREE + p] == 1
        goes_up = has & (p >= offset) & (offset > 0) & (up_rank < INNER)
        goes_down = has & (p < offset) & (down_rank < INNER)

        @pl.when(goes_up)
        def _up():
            out[UP_AT + up_rank] = spot

        @pl.when(goes_down)
        def _down():
            out[DOWN_AT + down_rank] = spot

        return up_rank + goes_up.astype(jnp.int32), down_rank + goes_down.astype(jnp.int32)

    lax.fori_loop(0, TREE, own, (0, 0))


def make_lists(meta, parent):
    count = parent.shape[0]
    return pl.pallas_call(
        partial(lists_kernel, count),
        out_shape=[shaped((LISTED,), jnp.int32), shaped((count,), jnp.int32)],
        in_specs=[SM, SM],
        out_specs=[SM, SM],
        compiler_params=params(8),
        cost_estimate=lasting("lists"),
        name="lists",
    )(meta, parent)


def table_kernel(count, meta, parent, lists, inner, out, place, starts):
    member, group = meta[0], meta[1]
    groups = count // TREE
    below = lax.rem(group + groups - 1, groups)
    above = lax.rem(group + 1, groups)
    offset = lists[OFFSET_AT]

    def known(p, ranks):
        low_rank, high_rank = ranks
        spot = ((p // SEG_DEV) ^ member) * SEG_DEV + lax.rem(p, SEG_DEV)
        place[group * TREE + p] = spot
        low_slot = below * TREE + p
        high_slot = above * TREE + p
        low = (inner[low_slot] == 1) & (p >= offset) & (offset > 0) & (low_rank < INNER)
        high = (inner[high_slot] == 1) & (p < offset) & (high_rank < INNER)
        place[low_slot] = jnp.where(low, TREE + low_rank, EMPTY)
        place[high_slot] = jnp.where(high, TREE + INNER + high_rank, EMPTY)
        return low_rank + low.astype(jnp.int32), high_rank + high.astype(jnp.int32)

    lax.fori_loop(0, TREE, known, (0, 0))

    def chain(q, _):
        slot = group * TREE + ((q // SEG_DEV) ^ member) * SEG_DEV + lax.rem(q, SEG_DEV)
        for i in range(ANC):
            out[SLOT_AT[0] + q * ANC + i] = TREE
            out[SLOT_AT[1] + q * ANC + i] = 2 * INNER
            out[LEVEL_AT[0] + q * ANC + i] = 0
            out[LEVEL_AT[1] + q * ANC + i] = 0

        def step(a, state):
            at, near, far = state
            good = at >= 0
            safe = jnp.maximum(at, 0)
            spot = place[safe]
            is_near = good & (spot < TREE)
            is_far = good & (spot >= TREE)

            @pl.when(is_near)
            def _near():
                out[SLOT_AT[0] + q * ANC + near] = spot
                out[LEVEL_AT[0] + q * ANC + near] = a

            @pl.when(is_far)
            def _far():
                out[SLOT_AT[1] + q * ANC + far] = spot - TREE
                out[LEVEL_AT[1] + q * ANC + far] = a

            return (
                jnp.where(good, parent[safe], -1),
                near + is_near.astype(jnp.int32),
                far + is_far.astype(jnp.int32),
            )

        _end, near, far = lax.fori_loop(0, ANC, step, (slot, 0, 0))
        out[COUNT_AT[0] + q] = near
        out[COUNT_AT[1] + q] = far
        return _

    lax.fori_loop(0, TREE, chain, 0)

    for side in range(2):
        for i in range(ANC + 1):
            starts[i] = 0

        def tally(q, _):
            starts[out[COUNT_AT[side] + q]] += 1
            return _

        lax.fori_loop(0, TREE, tally, 0)
        total = 0
        for i in range(ANC, -1, -1):
            number = starts[i]
            starts[i] = total
            total = total + number

        def put(q, _):
            number = out[COUNT_AT[side] + q]
            at = starts[number]
            out[ORDER_AT[side] + at] = q
            starts[number] = at + 1
            return _

        lax.fori_loop(0, TREE, put, 0)


def make_tables(meta, parent, lists, inner, deps=()):
    count = parent.shape[0]
    return pl.pallas_call(
        skipping(partial(table_kernel, count), 4, len(deps)),
        out_shape=shaped((TABLE,), jnp.int32),
        in_specs=[SM] * 4 + [ANY] * len(deps),
        out_specs=SM,
        scratch_shapes=[pltpu.SMEM((size,), jnp.int32) for size in (count, 16)],
        compiler_params=params(8),
        cost_estimate=lasting("tables"),
        name="tables",
    )(meta, parent, lists, inner, *deps)


def normal(block):
    centered = block - jnp.mean(block, axis=-1, keepdims=True)
    variance = jnp.mean(centered * centered, axis=-1, keepdims=True)
    scale = lax.rsqrt(variance + EPSILON)
    return centered * scale, scale


NORM_ROWS = 128


def norm_loop(rows, body):
    def step(i, _):
        body(pl.ds(pl.multiple_of(i * NORM_ROWS, NORM_ROWS), NORM_ROWS))
        return _

    lax.fori_loop(0, rows // NORM_ROWS, step, 0)


def project_kernel(meta, x, vectors, weight, normed, *outs):
    member = meta[0]
    rows = x.shape[0]

    def norm_step(at):
        hat, _scale = normal(x[at, :].astype(F32))
        normed[at, :] = (
            hat * vectors[GAIN_A : GAIN_A + 1] + vectors[SHIFT_A : SHIFT_A + 1]
        ).astype(BF16)

    norm_loop(rows, norm_step)
    low = lanes((1, PAIR)) < HD

    def one(d, _):
        pair = member ^ d
        block = weight[:, pl.ds(pl.multiple_of(pair * 3 * PAIR, PAIR), 3 * PAIR)]
        both = vectors[JOINED_BIAS : JOINED_BIAS + 1, pl.ds(pl.multiple_of(pair * 2 * PAIR, PAIR), 2 * PAIR)]
        first, second = both[:, :PAIR], both[:, PAIR:]
        query_bias = jnp.where(low, first, pltpu.roll(second, HD, 1))
        value_bias = jnp.where(low, pltpu.roll(first, HD, 1), second)
        joined = dot(normed[...], block)
        t0, t1, t2 = joined[:, :PAIR], joined[:, PAIR : 2 * PAIR], joined[:, 2 * PAIR :]
        queries = (jnp.where(low, t0, t1) + query_bias) * (HD ** (-0.5))
        keys = pltpu.roll(jnp.where(low, t2, t0), HD, 1)
        values = jnp.where(low, t1, t2) + value_bias
        for j in range(MEMBERS):

            @pl.when(d == j)
            def _store():
                outs[j][...] = queries.astype(BF16)
                outs[MEMBERS + j][...] = keys.astype(BF16)
                outs[2 * MEMBERS + j][...] = values.astype(BF16)

        return _

    lax.fori_loop(0, MEMBERS, one, 0)


def project(meta, x, vectors, weight):
    rows, width = x.shape
    outs = pl.pallas_call(
        project_kernel,
        out_shape=[shaped((rows, width), BF16)]
        + [shaped((rows, PAIR), BF16)] * (3 * MEMBERS),
        in_specs=[SM] + [VM] * 3,
        out_specs=[VM] * (1 + 3 * MEMBERS),
        compiler_params=params(),
        cost_estimate=lasting("project"),
        name="project",
    )(meta, x, vectors, weight)
    return outs[0], outs[1 : 1 + MEMBERS], outs[1 + MEMBERS : 1 + 2 * MEMBERS], outs[1 + 2 * MEMBERS :]


def pack_kernel(table, kv0, kv1, kv2, kv3, up, down, sem):
    sources = (kv0, kv1, kv2, kv3)
    for side, at, target in ((0, UP_AT, up), (1, DOWN_AT, down)):
        for i in range(INNER):
            spot = jnp.maximum(table[at + i], 0)
            d, s = spot // SEG_DEV, lax.rem(spot, SEG_DEV)
            for j in range(MEMBERS):

                @pl.when(d == j)
                def _start():
                    pltpu.make_async_copy(
                        sources[j].at[pl.ds(pl.multiple_of(s * SEG, SEG), SEG)],
                        target.at[pl.ds(i * SEG, SEG)],
                        sem.at[side * INNER + i],
                    ).start()

    for side, target in ((0, up), (1, down)):
        for i in range(INNER):
            piece = target.at[pl.ds(i * SEG, SEG)]
            pltpu.make_async_copy(piece, piece, sem.at[side * INNER + i]).wait()


def pack(table, pairs, deps=()):
    out = shaped((INNER * SEG, PAIR), BF16)
    specs = [SM] + [ANY] * MEMBERS
    used = len(specs)
    return pl.pallas_call(
        skipping(pack_kernel, used, len(deps)),
        out_shape=[out, out],
        in_specs=specs + [ANY] * len(deps),
        out_specs=[ANY] * 2,
        scratch_shapes=[pltpu.SemaphoreType.DMA((2 * INNER,))],
        compiler_params=params(8),
        cost_estimate=lasting("pack"),
        name="pack",
    )(table, *pairs, *deps)


LEVELS = (1, 2, 3, 4, 5, 6, 8, 10)


def split_heads(tile):
    low = lanes((SEG, PAIR)) < HD
    wide = tile.astype(F32)
    zero = jnp.zeros_like(wide)
    return jnp.concatenate(
        [jnp.where(low, wide, zero), jnp.where(low, zero, wide)], axis=0
    ).astype(BF16)


def join_heads(turned):
    top = rows_of((PAIR, SEG)) < HD
    return jnp.where(top, turned[:, :SEG], turned[:, SEG:]).T


def slope_row(slopes, meta):
    first = meta[2]
    return jnp.where(lanes((1, 2 * SEG)) < SEG, slopes[first], slopes[first + 1])


def fill_bias(bias, slope):
    shape = (SEG, 2 * SEG)
    offset = lax.rem(lanes(shape), SEG)
    key = rows_of(shape)
    gap = slope * (key - offset).astype(F32)
    bias[0] = jnp.where(key <= offset, gap, NEGATIVE)
    bias[1] = gap


def split_turned(tile):
    top = rows_of((PAIR, SEG)) < HD
    wide = tile.astype(F32).T
    zero = jnp.zeros_like(wide)
    return jnp.concatenate(
        [jnp.where(top, wide, zero), jnp.where(top, zero, wide)], axis=1
    ).astype(BF16)


def start_all(copies):
    for copy in copies:
        copy.start()


def wait_all(copies):
    for copy in copies:
        copy.wait()


def loads(sources, target, sem, first, column=0):
    copies, at = [], 0
    for k, source in enumerate(sources):
        rows, across = source.shape
        into = target.at[pl.ds(at, rows), pl.ds(column, across)]
        copies.append(pltpu.make_async_copy(source, into, sem.at[first + k]))
        at += rows
    return copies


def segment(ref, at):
    return ref.at[pl.ds(pl.multiple_of(at * SEG, SEG), SEG)]


def turn_all(pool, turned, count, first):
    def turn(i, _):
        turned[i] = segment(pool, i)[:, first : first + PAIR].astype(F32).T.astype(BF16)
        return _

    lax.fori_loop(0, count, turn, 0, unroll=4)
    turned[count] = jnp.zeros((PAIR, SEG), BF16)


def entries(table, side, s, span):
    at = s * ANC
    spots = [table[SLOT_AT[side] + at + i] for i in range(span)]
    levels = [table[LEVEL_AT[side] + at + i] for i in range(span)]
    return spots, levels


def level_row(slope, levels, i, count):
    row = slope * (levels[i] * (-SEG)).astype(F32)
    return row + jnp.where(count <= i, NEGATIVE, 0.0)


def by_groups(table, side, body, empty=None):
    def step(g, _):
        group = [table[ORDER_AT[side] + g * GROUP + k] for k in range(GROUP)]
        most = table[COUNT_AT[side] + group[0]]
        if empty is not None:

            @pl.when(most == 0)
            def _none():
                empty(group)

        for below, span in zip((0,) + LEVELS[:-1], LEVELS):

            @pl.when((most > below) & (most <= span))
            def _run():
                body(group, span)

        return _

    lax.fori_loop(0, TREE // GROUP, step, 0)


def chosen_heads(wide):
    top = rows_of((PAIR, SEG)) < HD
    return jnp.where(top, wide[:, :SEG], wide[:, SEG:])


def weigh(side, span, table, s, slope, bias, pool, turned, stacked):
    count = table[COUNT_AT[side] + s]
    spots, levels = entries(table, side, s, span)
    keys = jnp.concatenate([segment(pool, spot)[:, :PAIR] for spot in spots], axis=0)
    whole = dot(keys, stacked)
    scores = []
    for i in range(span):
        raw = whole[i * SEG : (i + 1) * SEG]
        own = side == 0 and i == 0
        scores.append(raw + bias[0 if own else 1] + level_row(slope, levels, i, count))
    top = scores[0]
    for part in scores[1:]:
        top = jnp.maximum(top, part)
    top = jnp.max(top, axis=0, keepdims=True)
    sums, short = None, []
    for i in range(span):
        weights = jnp.exp(scores[i] - top)
        short.append(weights.astype(BF16))
        sums = weights if sums is None else sums + weights
    values = jnp.concatenate([turned[spot] for spot in spots], axis=1)
    out = dot(values, jnp.concatenate(short, axis=0))
    return top, jnp.sum(sums, axis=0, keepdims=True), chosen_heads(out)


def attend_near_kernel(
    table, meta, slopes, q0, q1, q2, q3, k0, k1, k2, k3, v0, v1, v2, v3,
    kept, stats, pool, turned, queries, bias, sem,
):
    copies = loads((k0, k1, k2, k3), pool, sem, 0)
    copies += loads((v0, v1, v2, v3), pool, sem, MEMBERS, PAIR)
    copies += loads((q0, q1, q2, q3), queries, sem, 2 * MEMBERS)
    start_all(copies)
    slope = slope_row(slopes, meta)
    fill_bias(bias, slope)
    pool[TREE * SEG :, :] = jnp.zeros((SEG, 2 * PAIR), BF16)
    wait_all(copies)
    turn_all(pool, turned, TREE, PAIR)

    def body(group, span):
        for s in group:
            stacked = split_turned(segment(queries, s)[...])
            top, total, out = weigh(0, span, table, s, slope, bias, pool, turned, stacked)
            stats[s, 0:1, :] = top
            stats[s, 1:2, :] = total
            kept[s] = out

    by_groups(table, 0, body)


def attend_near(table, meta, slopes, queries, keys, values, deps=()):
    specs = [SM] * 3 + [ANY] * (3 * MEMBERS)
    used = len(specs)
    return pl.pallas_call(
        skipping(attend_near_kernel, used, len(deps)),
        out_shape=[shaped((TREE, PAIR, SEG), F32), shaped((TREE, 8, 2 * SEG), F32)],
        in_specs=specs + [ANY] * len(deps),
        out_specs=[VM, VM],
        scratch_shapes=[
            pltpu.VMEM(((TREE + 1) * SEG, 2 * PAIR), BF16),
            pltpu.VMEM((TREE + 1, PAIR, SEG), BF16),
            pltpu.VMEM((TREE * SEG, PAIR), BF16),
            pltpu.VMEM((2, SEG, 2 * SEG), F32),
            pltpu.SemaphoreType.DMA((3 * MEMBERS,)),
        ],
        compiler_params=params(),
        cost_estimate=lasting("attend_near"),
        name="attend_near",
    )(table, meta, slopes, *queries, *keys, *values, *deps)


def attend_far_kernel(
    table, meta, slopes, q0, q1, q2, q3, k_below, k_above, v_below, v_above, kept, stats,
    o0, o1, o2, o3, lse, pool, turned, queries, result, bias, sem,
):
    rows = SEG_DEV * SEG
    copies = loads((k_below, k_above), pool, sem, 0)
    copies += loads((v_below, v_above), pool, sem, 2, PAIR)
    copies += loads((q0, q1, q2, q3), queries, sem, 4)
    start_all(copies)
    slope = slope_row(slopes, meta)
    fill_bias(bias, slope)
    pool[2 * INNER * SEG :, :] = jnp.zeros((SEG, 2 * PAIR), BF16)
    wait_all(copies)
    turn_all(pool, turned, 2 * INNER, PAIR)

    def finish(s, top, total, out):
        wide = 1.0 / total
        segment(result, s)[...] = (out * chosen_heads(jnp.broadcast_to(wide, (PAIR, 2 * SEG)))).T.astype(BF16)
        lse[s] = top + jnp.log(total)

    def alone(group):
        for s in group:
            finish(s, stats[s, 0:1, :], stats[s, 1:2, :], kept[s])

    def body(group, span):
        shape = (PAIR, 2 * SEG)
        for s in group:
            stacked = split_turned(segment(queries, s)[...])
            top, total, out = weigh(1, span, table, s, slope, bias, pool, turned, stacked)
            near = stats[s, 0:1, :]
            both = jnp.maximum(near, top)
            near_scale = jnp.exp(near - both)
            far_scale = jnp.exp(top - both)
            total = stats[s, 1:2, :] * near_scale + total * far_scale
            out = kept[s] * chosen_heads(jnp.broadcast_to(near_scale, shape)) + out * (
                chosen_heads(jnp.broadcast_to(far_scale, shape))
            )
            finish(s, both, total, out)

    by_groups(table, 1, body, alone)
    copies = [
        pltpu.make_async_copy(result.at[pl.ds(j * rows, rows)], target, sem.at[j])
        for j, target in enumerate((o0, o1, o2, o3))
    ]
    start_all(copies)
    wait_all(copies)


def attend_far(table, meta, slopes, queries, away, kept, stats, deps=()):
    rows = queries[0].shape[0]
    specs = [SM] * 3 + [ANY] * (MEMBERS + 4) + [VM] * 2
    used = len(specs)
    outs = pl.pallas_call(
        skipping(attend_far_kernel, used, len(deps)),
        out_shape=[shaped((rows, PAIR), BF16)] * MEMBERS + [shaped((TREE, 1, 2 * SEG), F32)],
        in_specs=specs + [ANY] * len(deps),
        out_specs=[ANY] * MEMBERS + [VM],
        scratch_shapes=[
            pltpu.VMEM(((2 * INNER + 1) * SEG, 2 * PAIR), BF16),
            pltpu.VMEM((2 * INNER + 1, PAIR, SEG), BF16),
            pltpu.VMEM((TREE * SEG, PAIR), BF16),
            pltpu.VMEM((TREE * SEG, PAIR), BF16),
            pltpu.VMEM((2, SEG, 2 * SEG), F32),
            pltpu.SemaphoreType.DMA((MEMBERS + 4,)),
        ],
        compiler_params=params(),
        cost_estimate=lasting("attend_far"),
        name="attend_far",
    )(table, meta, slopes, *queries, *away, kept, stats, *deps)
    return outs[:MEMBERS], outs[MEMBERS]


def spread(side, span, table, s, slope, bias, pool, turned, total, queries, outs, grads, lse):
    count = table[COUNT_AT[side] + s]
    query = segment(queries, s)[...]
    stacked = split_heads(query)
    grad = segment(grads, s)[...]
    stacked_grad = split_heads(grad)
    product = (grad.astype(F32) * segment(outs, s)[...].astype(F32)).T
    delta = jnp.concatenate(
        [
            jnp.sum(product[:HD], axis=0, keepdims=True),
            jnp.sum(product[HD:], axis=0, keepdims=True),
        ],
        axis=1,
    )
    log_total = lse[s]
    spots, levels = entries(table, side, s, span)
    keys = jnp.concatenate([segment(pool, spot)[:, :PAIR] for spot in spots], axis=0)
    values = jnp.concatenate([segment(pool, spot)[:, PAIR:] for spot in spots], axis=0)
    raw = dot(keys, split_turned(query))
    prob_grad = dot(values, split_turned(grad))
    probs, score_grads = [], []
    for i in range(span):
        at = slice(i * SEG, (i + 1) * SEG)
        row = level_row(slope, levels, i, count) - log_total
        own = side == 0 and i == 0
        prob = jnp.exp(raw[at] + bias[0 if own else 1] + row)
        score_grads.append((prob * (prob_grad[at] - delta)).astype(BF16))
        probs.append(prob.astype(BF16))
    score_grad = jnp.concatenate(score_grads, axis=0)
    key_grad = dot(score_grad, stacked)
    value_grad = dot(jnp.concatenate(probs, axis=0), stacked_grad)
    for i in range(span):
        at = slice(i * SEG, (i + 1) * SEG)
        into = segment(total, spots[i])
        into[:, :PAIR] += key_grad[at]
        into[:, PAIR:] += value_grad[at]
    across = jnp.concatenate([turned[spot] for spot in spots], axis=1)
    return chosen_heads(dot(across, score_grad))


def clear_all(total, count):
    def clear(i, _):
        segment(total, i)[...] = jnp.zeros((SEG, 2 * PAIR), F32)
        return _

    lax.fori_loop(0, count, clear, 0, unroll=True)


def back_far_kernel(
    table, meta, slopes, q0, q1, q2, q3, k_below, k_above, v_below, v_above, o0, o1, o2, o3, g0, g1, g2, g3, lse,
    to_below, to_above, kept,
    pool, turned, queries, outs, grads, total, small, bias, sem,
):
    copies = loads((k_below, k_above), pool, sem, 0)
    copies += loads((v_below, v_above), pool, sem, 2, PAIR)
    copies += loads((q0, q1, q2, q3), queries, sem, 4)
    copies += loads((o0, o1, o2, o3), outs, sem, 4 + MEMBERS)
    copies += loads((g0, g1, g2, g3), grads, sem, 4 + 2 * MEMBERS)
    start_all(copies)
    slope = slope_row(slopes, meta)
    fill_bias(bias, slope)
    pool[2 * INNER * SEG :, :] = jnp.zeros((SEG, 2 * PAIR), BF16)
    clear_all(total, 2 * INNER + 1)
    wait_all(copies)
    turn_all(pool, turned, 2 * INNER, 0)

    def alone(group):
        for s in group:
            kept[s] = jnp.zeros((PAIR, SEG), F32)

    def body(group, span):
        for s in group:
            kept[s] = spread(
                1, span, table, s, slope, bias, pool, turned, total, queries, outs, grads, lse
            )

    by_groups(table, 1, body, alone)

    def shorten(i, _):
        segment(small, i)[...] = segment(total, i)[...].astype(BF16)
        return _

    lax.fori_loop(0, 2 * INNER, shorten, 0)
    copies = [
        pltpu.make_async_copy(
            small.at[pl.ds(k * INNER * SEG, INNER * SEG)], target, sem.at[k]
        )
        for k, target in enumerate((to_below, to_above))
    ]
    start_all(copies)
    wait_all(copies)


def back_far(table, meta, slopes, queries, away, outs, grads, lse, deps=()):
    side = shaped((INNER * SEG, 2 * PAIR), BF16)
    specs = [SM] * 3 + [ANY] * (3 * MEMBERS + 4) + [VM]
    used = len(specs)
    return pl.pallas_call(
        skipping(back_far_kernel, used, len(deps)),
        out_shape=[side, side, shaped((TREE, PAIR, SEG), F32)],
        in_specs=specs + [ANY] * len(deps),
        out_specs=[ANY] * 2 + [VM],
        scratch_shapes=[
            pltpu.VMEM(((2 * INNER + 1) * SEG, 2 * PAIR), BF16),
            pltpu.VMEM((2 * INNER + 1, PAIR, SEG), BF16),
            pltpu.VMEM((TREE * SEG, PAIR), BF16),
            pltpu.VMEM((TREE * SEG, PAIR), BF16),
            pltpu.VMEM((TREE * SEG, PAIR), BF16),
            pltpu.VMEM(((2 * INNER + 1) * SEG, 2 * PAIR), F32),
            pltpu.VMEM((2 * INNER * SEG, 2 * PAIR), BF16),
            pltpu.VMEM((2, SEG, 2 * SEG), F32),
            pltpu.SemaphoreType.DMA((3 * MEMBERS + 4,)),
        ],
        compiler_params=params(),
        cost_estimate=lasting("back_far"),
        name="back_far",
    )(table, meta, slopes, *queries, *away, *outs, *grads, lse, *deps)


def back_near_kernel(
    table, meta, slopes, q0, q1, q2, q3, k0, k1, k2, k3, v0, v1, v2, v3, o0, o1, o2, o3, g0, g1, g2, g3,
    lse, kept, dq0, dq1, dq2, dq3, own,
    pool, turned, queries, outs, grads, result, total, bias, sem,
):
    rows = SEG_DEV * SEG
    copies = loads((k0, k1, k2, k3), pool, sem, 0)
    copies += loads((v0, v1, v2, v3), pool, sem, MEMBERS, PAIR)
    copies += loads((q0, q1, q2, q3), queries, sem, 2 * MEMBERS)
    copies += loads((o0, o1, o2, o3), outs, sem, 3 * MEMBERS)
    copies += loads((g0, g1, g2, g3), grads, sem, 4 * MEMBERS)
    start_all(copies)
    slope = slope_row(slopes, meta)
    fill_bias(bias, slope)
    pool[TREE * SEG :, :] = jnp.zeros((SEG, 2 * PAIR), BF16)
    clear_all(total, TREE + 1)
    wait_all(copies)
    turn_all(pool, turned, TREE, 0)

    def body(group, span):
        for s in group:
            part = spread(
                0, span, table, s, slope, bias, pool, turned, total, queries, outs, grads, lse
            )
            segment(result, s)[...] = (kept[s] + part).T.astype(BF16)

    by_groups(table, 0, body)
    copies = [
        pltpu.make_async_copy(result.at[pl.ds(j * rows, rows)], target, sem.at[j])
        for j, target in enumerate((dq0, dq1, dq2, dq3))
    ]
    copies.append(
        pltpu.make_async_copy(total.at[pl.ds(0, TREE * SEG)], own, sem.at[MEMBERS])
    )
    start_all(copies)
    wait_all(copies)


def back_near(table, meta, slopes, queries, keys, values, outs, grads, lse, kept, deps=()):
    rows = queries[0].shape[0]
    specs = [SM] * 3 + [ANY] * (5 * MEMBERS) + [VM] * 2
    used = len(specs)
    result = pl.pallas_call(
        skipping(back_near_kernel, used, len(deps)),
        out_shape=[shaped((rows, PAIR), BF16)] * MEMBERS + [shaped((TREE * SEG, 2 * PAIR), F32)],
        in_specs=specs + [ANY] * len(deps),
        out_specs=[ANY] * (MEMBERS + 1),
        scratch_shapes=[
            pltpu.VMEM(((TREE + 1) * SEG, 2 * PAIR), BF16),
            pltpu.VMEM((TREE + 1, PAIR, SEG), BF16),
            pltpu.VMEM((TREE * SEG, PAIR), BF16),
            pltpu.VMEM((TREE * SEG, PAIR), BF16),
            pltpu.VMEM((TREE * SEG, PAIR), BF16),
            pltpu.VMEM((TREE * SEG, PAIR), BF16),
            pltpu.VMEM(((TREE + 1) * SEG, 2 * PAIR), F32),
            pltpu.VMEM((2, SEG, 2 * SEG), F32),
            pltpu.SemaphoreType.DMA((5 * MEMBERS,)),
        ],
        compiler_params=params(),
        cost_estimate=lasting("back_near"),
        name="back_near",
    )(table, meta, slopes, *queries, *keys, *values, *outs, *grads, lse, kept, *deps)
    return result[:MEMBERS], result[MEMBERS]


def gather_back_kernel(table, own, from_above, from_below, k0, k1, k2, k3, total, sem):
    rows = SEG_DEV * SEG
    copy = pltpu.make_async_copy(own, total, sem)
    copy.start()
    copy.wait()
    for at, source in ((UP_AT, from_above), (DOWN_AT, from_below)):

        def add(i, _):
            spot = table[at + i]

            @pl.when(spot >= 0)
            def _add():
                segment(total, spot)[...] += segment(source, i)[...].astype(F32)

            return _

        lax.fori_loop(0, INNER, add, 0)
    for j, target in enumerate((k0, k1, k2, k3)):

        def short(i, _):
            segment(target, i)[...] = segment(total, j * SEG_DEV + i)[...].astype(BF16)
            return _

        lax.fori_loop(0, SEG_DEV, short, 0)


def gather_back(table, own, from_above, from_below, deps=()):
    rows = SEG_DEV * SEG
    specs = [SM, ANY, VM, VM]
    used = len(specs)
    return pl.pallas_call(
        skipping(gather_back_kernel, used, len(deps)),
        out_shape=[shaped((rows, 2 * PAIR), BF16)] * MEMBERS,
        in_specs=specs + [ANY] * len(deps),
        out_specs=[VM] * MEMBERS,
        scratch_shapes=[
            pltpu.VMEM((TREE * SEG, 2 * PAIR), F32),
            pltpu.SemaphoreType.DMA(()),
        ],
        compiler_params=params(),
        cost_estimate=lasting("gather_back"),
        name="gather_back",
    )(table, own, from_above, from_below, *deps)


TILE = 256
def feed_kernel(
    meta, x, vectors, a0, a1, a2, a3, b0, b1, b2, b3,
    w_own, w_other, w_up, hidden_grad,
    mixed_out, middle_out, normed_out, act_out, pre_out, part, sums,
    mixed_own, middle, normed, act, pre_grad, mixed, weight, up, hidden, sem, out_sem,
):
    member, rank = meta[0], meta[3]
    rows, width = x.shape
    half = width // 2
    inner = w_up.shape[1]
    copies = []
    for k, source in enumerate((w_own, w_other)):
        at = pl.multiple_of((rank ^ k) * half, half)
        copies.append(pltpu.make_async_copy(source, weight.at[pl.ds(at, half)], sem.at[k]))
    late = [
        pltpu.make_async_copy(w_up, up, sem.at[2]),
        pltpu.make_async_copy(hidden_grad, hidden, sem.at[3]),
    ]
    start_all(copies + late)
    for k, parts in enumerate(((a0, a1, a2, a3), (b0, b1, b2, b3))):
        for d in range(MEMBERS):
            inside = (member ^ d) * PAIR
            at = pl.multiple_of((rank ^ k) * half + inside, PAIR)
            mixed[:, pl.ds(at, PAIR)] = parts[d][...]
            if k == 0:
                mixed_own[:, pl.ds(pl.multiple_of(inside, PAIR), PAIR)] = parts[d][...]
    stores = [pltpu.make_async_copy(mixed_own, mixed_out, out_sem.at[0])]
    stores[0].start()
    wait_all(copies)

    def column(t, _):
        at = pl.ds(pl.multiple_of(t * TILE, TILE), TILE)
        middle[:, at] = (
            x[:, at].astype(F32) + (dot(mixed[...], weight[:, at]) + vectors[OUT_BIAS : OUT_BIAS + 1, at])
        )
        return _

    lax.fori_loop(0, width // TILE, column, 0)
    stores.append(pltpu.make_async_copy(middle, middle_out, out_sem.at[1]))
    stores[1].start()

    def norm_step(at):
        hat, _scale = normal(middle[at, :])
        normed[at, :] = (hat * vectors[GAIN_F : GAIN_F + 1] + vectors[SHIFT_F : SHIFT_F + 1]).astype(BF16)

    norm_loop(rows, norm_step)
    stores.append(pltpu.make_async_copy(normed, normed_out, out_sem.at[2]))
    stores[2].start()
    wait_all(late)

    def hidden_step(t, _):
        at = pl.ds(pl.multiple_of(t * TILE, TILE), TILE)
        per = width // TILE
        bias = vectors[pl.ds(UP_BIAS + t // per, 1), pl.ds(pl.multiple_of(lax.rem(t, per) * TILE, TILE), TILE)]
        pre = dot(normed[...], up[:, at]) + bias
        square = pre * pre
        c = 0.7978845608028654
        t_ = jnp.tanh(pre * (c + (c * 0.044715) * square))
        low = 0.5 * (1.0 + t_)
        act[:, at] = (pre * low).astype(BF16)
        slope = low + (0.5 * pre) * (1.0 - t_ * t_) * (c + (3.0 * c * 0.044715) * square)
        grad = (hidden[:, at] * slope).astype(BF16)
        pre_grad[:, at] = grad
        sums[0:1, at] = jnp.sum(grad.astype(F32), axis=0, keepdims=True)
        return _

    lax.fori_loop(0, inner // TILE, hidden_step, 0)
    stores.append(pltpu.make_async_copy(act, act_out, out_sem.at[3]))
    stores.append(pltpu.make_async_copy(pre_grad, pre_out, out_sem.at[4]))
    start_all(stores[3:])

    def back(t, _):
        at = pl.ds(pl.multiple_of(t * TILE, TILE), TILE)
        part[:, at] = dot(pre_grad[...], up[at, :], ((1,), (1,))).astype(BF16)
        return _

    lax.fori_loop(0, width // TILE, back, 0)
    wait_all(stores)


def feed(meta, x, vectors, parts_own, parts_other, w_own, w_other, w_up, hidden_grad):
    rows, width = x.shape
    inner = w_up.shape[1]
    half = width // 2
    return pl.pallas_call(
        feed_kernel,
        out_shape=[
            shaped((rows, half), BF16),
            shaped((rows, width), F32),
            shaped((rows, width), BF16),
            shaped((rows, inner), BF16),
            shaped((rows, inner), BF16),
            shaped((rows, width), BF16),
            shaped((8, inner), F32),
        ],
        in_specs=[SM] + [VM] * (2 + 2 * MEMBERS) + [ANY] * 4,
        out_specs=[ANY] * 5 + [VM] * 2,
        scratch_shapes=[
            pltpu.VMEM((rows, half), BF16),
            pltpu.VMEM((rows, width), F32),
            pltpu.VMEM((rows, width), BF16),
            pltpu.VMEM((rows, inner), BF16),
            pltpu.VMEM((rows, inner), BF16),
            pltpu.VMEM((rows, width), BF16),
            pltpu.VMEM((width, width), BF16),
            pltpu.VMEM((width, inner), BF16),
            pltpu.VMEM((rows, inner), F32),
            pltpu.SemaphoreType.DMA((4,)),
            pltpu.SemaphoreType.DMA((5,)),
        ],
        compiler_params=params(),
        cost_estimate=lasting("feed"),
        name="feed",
    )(meta, x, vectors, *parts_own, *parts_other, w_own, w_other, w_up, hidden_grad)


def product_kernel(dims, left, right, out):
    out[...] = dot(left[...], right[...], dims).astype(out.dtype)


def product(name, left, right, turned, kind, deps=()):
    rows, depth = left.shape
    across = right.shape[0] if turned else right.shape[1]
    block = (TILE, depth) if turned else (depth, TILE)
    return pl.pallas_call(
        skipping(partial(product_kernel, ((1,), (1,) if turned else (0,))), 2, len(deps)),
        grid=(across // TILE,),
        out_shape=shaped((rows, across), kind),
        in_specs=[
            pl.BlockSpec((rows, depth), lambda t: (0, 0)),
            pl.BlockSpec(block, (lambda t: (t, 0)) if turned else (lambda t: (0, t))),
        ]
        + [ANY] * len(deps),
        out_specs=pl.BlockSpec((rows, TILE), lambda t: (0, t)),
        compiler_params=params(),
        cost_estimate=lasting(name),
        name=name,
    )(left, right, *deps)


def turn_rows(source, target):
    def step(i, _):
        at = pl.ds(pl.multiple_of(i * SEG, SEG), SEG)
        target[at, :] = source[:, at].astype(F32).T.astype(BF16)
        return _

    lax.fori_loop(0, source.shape[1] // SEG, step, 0)


X_FIRST = (0, 1, 2, 3)
Z_FIRST = (0, 2, 3, 1)
MIXED = (0, 2, 1, 3)
Z_BLOCKS = (8, 4, 12)
DEVICES = 16


def block_place(relative, order):
    place = 0
    for bit in order:
        place = place * 2 + (lax.shift_right_logical(relative, bit) & 1)
    return place


def turn_ordered(tile, target, i, device, order, share):
    for k in range(SEG // share):
        block = i * (SEG // share) + k
        at = block_place(block ^ device, order) * share
        target[pl.ds(pl.multiple_of(at, share), share), :] = tile[k * share : (k + 1) * share]


def turn_source(source, target, device, order, share):
    def step(i, _):
        at = pl.ds(pl.multiple_of(i * SEG, SEG), SEG)
        tile = source[:, at].astype(F32).T.astype(BF16)
        turn_ordered(tile, target, i, device, order, share)
        return _

    lax.fori_loop(0, source.shape[1] // SEG, step, 0)


def feed_grads_kernel(
    meta, grad, act, normed, pre_grad, weight,
    keep_c, send_c0, send_c1, keep_e, send_e0, send_e1, part, turned,
):
    t = pl.program_id(0)
    tiles = pl.num_programs(0) // 2
    width = grad.shape[1]
    half = width // 2
    tile = pre_grad.shape[1]

    @pl.when(t == 0)
    def _first():
        turn_source(grad, turned, meta[4], MIXED, width // DEVICES)

    @pl.when(t == tiles)
    def _second():
        turn_source(normed, turned, meta[4], X_FIRST, width // DEVICES)

    @pl.when(t < tiles)
    def _contract():
        right = act[:, pl.ds(pl.multiple_of(t * tile, tile), tile)]
        keep_c[...] = dot(turned[:half], right).astype(BF16)
        leave = dot(turned[half:], right).astype(BF16)

        @pl.when(t < tiles // 2)
        def _low():
            send_c0[...] = leave

        @pl.when(t >= tiles // 2)
        def _high():
            send_c1[...] = leave

    @pl.when(t >= tiles)
    def _expand():
        keep_e[...] = dot(turned[:half], pre_grad[...]).astype(BF16)
        leave = dot(turned[half:], pre_grad[...]).astype(BF16)

        @pl.when(t < tiles + tiles // 2)
        def _low():
            send_e0[...] = leave

        @pl.when(t >= tiles + tiles // 2)
        def _high():
            send_e1[...] = leave

    part[...] = dot(act[...], weight[...]).astype(BF16)


def feed_grads(meta, grad, act, normed, pre_grad, weight):
    rows, width = grad.shape
    inner = act.shape[1]
    tile = 2 * TILE
    tiles = inner // tile
    piece = width // (2 * tiles)

    def steps(start, number):
        return pl.BlockSpec((width // 2, tile), lambda t: (0, jnp.clip(t - start, 0, number - 1)))

    both = [steps(0, tiles), steps(0, tiles // 2), steps(tiles // 2, tiles // 2)]
    both += [steps(tiles, tiles), steps(tiles, tiles // 2), steps(tiles + tiles // 2, tiles // 2)]
    kept, sent = shaped((width // 2, inner), BF16), shaped((width // 2, inner // 2), BF16)
    whole = pl.BlockSpec((rows, width), lambda t: (0, 0))
    return pl.pallas_call(
        feed_grads_kernel,
        grid=(2 * tiles,),
        out_shape=[kept, sent, sent, kept, sent, sent, shaped((rows, width), BF16)],
        in_specs=[
            SM,
            whole,
            pl.BlockSpec((rows, inner), lambda t: (0, 0)),
            whole,
            pl.BlockSpec((rows, tile), lambda t: (0, jnp.maximum(t - tiles, 0))),
            pl.BlockSpec((inner, piece), lambda t: (0, t)),
        ],
        out_specs=both + [pl.BlockSpec((rows, piece), lambda t: (0, t))],
        scratch_shapes=[pltpu.VMEM((width, rows), BF16)],
        compiler_params=params(),
        cost_estimate=lasting("feed_grads"),
        name="feed_grads",
    )(meta, grad, act, normed, pre_grad, weight)


def in_two(rows8):
    high = rows8.astype(BF16).astype(F32)
    low = rows8 - high
    return jnp.concatenate([high, low, jnp.zeros((SEG - 16, rows8.shape[1]), F32)], axis=0)


def add_half(keep, got, stay, leave):
    half = stay.shape[0]
    stay[...] = keep[:half].astype(F32) + got[:half].astype(F32)
    leave[...] = (keep[half:].astype(F32) + got[half:].astype(F32)).astype(BF16)


TAKE_STEPS = 4


def take_specs(shape):
    rows, across = shape
    if across % (TAKE_STEPS * PAIR) == 0:
        tile, at = across // TAKE_STEPS, lambda t: (0, t)
    else:
        tile, at = across, lambda t: (0, 0)
    return pl.BlockSpec((rows, tile), at), pl.BlockSpec((rows // 2, tile), at)


def add_halves(flags, ins, outs):
    for k, split in enumerate(flags):
        step = partial(add_half, ins[2 * k], ins[2 * k + 1], outs[2 * k], outs[2 * k + 1])
        if split:
            step()
        else:
            pl.when(pl.program_id(0) == 0)(step)


def halves_of(pairs):
    specs, outs, shapes, flags, args = [], [], [], [], []
    for keep, got in pairs:
        whole, part = take_specs(keep.shape)
        half = (keep.shape[0] // 2, keep.shape[1])
        specs += [whole, whole]
        outs += [part, part]
        shapes += [shaped(half, F32), shaped(half, BF16)]
        flags.append(whole.block_shape[1] != keep.shape[1])
        args += [keep, got]
    return specs, outs, shapes, flags, args


def takes_kernel(flags, count, *refs):
    ins, outs = refs[: 2 * len(flags)], refs[2 * len(flags) + count :]
    add_halves(flags, ins, outs)


def takes(name, pairs, deps=()):
    specs, outs, shapes, flags, args = halves_of(pairs)
    got = pl.pallas_call(
        partial(takes_kernel, flags, len(deps)),
        grid=(TAKE_STEPS,),
        out_shape=shapes,
        in_specs=specs + [ANY] * len(deps),
        out_specs=outs,
        compiler_params=params(),
        cost_estimate=lasting(name),
        name=name,
    )(*args, *deps)
    return [tuple(got[2 * k : 2 * k + 2]) for k in range(len(pairs))]


def output_grads_kernel(count, meta, branch, mixed, vectors, extra, *refs):
    ins = refs[: 3 * count]
    keep, send = refs[3 * count : 3 * count + 2]
    outs = refs[3 * count + 2 : -2]
    turned, small = refs[-2:]
    t = pl.program_id(0)
    width, across = branch.shape[1], mixed.shape[1]
    share = width // DEVICES
    half = width // 2

    @pl.when(t == 0)
    def _first():
        turn_source(branch, turned, meta[4], X_FIRST, share)
        for i in range(width // SEG):
            at = slice(i * SEG, (i + 1) * SEG)
            rows8 = jnp.concatenate(
                [vectors[0:4, at], extra[0:2, at], jnp.zeros((2, SEG), F32)], axis=0
            )
            turn_ordered(in_two(rows8).T, small, i, meta[4], X_FIRST, share)
        keep[:, across:] = small[:half].astype(BF16)
        send[:, across:] = small[half:].astype(BF16)

    tile = across // TAKE_STEPS
    at = pl.ds(pl.multiple_of(t * tile, tile), tile)
    keep[:, at] = dot(turned[:half], mixed[:, at]).astype(BF16)
    send[:, at] = dot(turned[half:], mixed[:, at]).astype(BF16)
    for k in range(count):
        kept, low, high = ins[3 * k : 3 * k + 3]

        @pl.when(t < TAKE_STEPS // 2)
        def _low():
            add_half(kept, low, outs[2 * k], outs[2 * k + 1])

        @pl.when(t >= TAKE_STEPS // 2)
        def _high():
            add_half(kept, high, outs[2 * k], outs[2 * k + 1])


def output_grads(meta, branch, mixed, vectors, extra, pairs):
    rows, width = branch.shape
    across = mixed.shape[1]
    half_steps = TAKE_STEPS // 2
    specs, outs, shapes, args = [], [], [], []
    for kept, low, high in pairs:
        high_rows, cols = kept.shape
        tile = cols // TAKE_STEPS
        specs += [
            pl.BlockSpec((high_rows, tile), lambda t: (0, t)),
            pl.BlockSpec((high_rows, tile), lambda t: (0, jnp.minimum(t, half_steps - 1))),
            pl.BlockSpec((high_rows, tile), lambda t: (0, jnp.maximum(t - half_steps, 0))),
        ]
        outs += [pl.BlockSpec((high_rows // 2, tile), lambda t: (0, t))] * 2
        shapes += [shaped((high_rows // 2, cols), F32), shaped((high_rows // 2, cols), BF16)]
        args += [kept, low, high]

    def whole(shape):
        return pl.BlockSpec(shape, lambda t: (0, 0))

    own = whole((width // 2, across + SEG))
    got = pl.pallas_call(
        partial(output_grads_kernel, len(pairs)),
        grid=(TAKE_STEPS,),
        out_shape=[shaped((width // 2, across + SEG), BF16)] * 2 + shapes,
        in_specs=[SM, whole(branch.shape), whole(mixed.shape), whole(vectors.shape), whole(extra.shape)]
        + specs,
        out_specs=[own, own] + outs,
        scratch_shapes=[pltpu.VMEM((width, rows), BF16), pltpu.VMEM((width, SEG), F32)],
        compiler_params=params(),
        cost_estimate=lasting("output_grads"),
        name="output_grads",
    )(meta, branch, mixed, vectors, extra, *args)
    return (got[0], got[1]), [tuple(got[2 + 2 * k : 4 + 2 * k]) for k in range(len(pairs))]


def first_sums_kernel(
    a, got_a, b, got_b, last_b, stay_a, leave_a, stay_b, b1, b2, b3
):
    add_half(a, got_a, stay_a, leave_a)
    rows = stay_b.shape[0]
    cut = got_b.shape[1]
    for cols, got in ((slice(0, cut), got_b), (slice(cut, b.shape[1]), last_b)):
        stay_b[:, cols] = b[:rows, cols].astype(F32) + got[:rows].astype(F32)
        for k, target in enumerate((b1, b2, b3)):
            at = slice((k + 1) * rows, (k + 2) * rows)
            target[:, cols] = (b[at, cols].astype(F32) + got[at].astype(F32)).astype(BF16)


def first_sums(a, b):
    half, across_a = a[0].shape
    across_b = b[0].shape[1]
    part_a, part_b = (half // 2, across_a), (half // 4, across_b)
    return pl.pallas_call(
        first_sums_kernel,
        out_shape=[shaped(part_a, F32), shaped(part_a, BF16), shaped(part_b, F32)]
        + [shaped(part_b, BF16)] * 3,
        in_specs=[VM] * 5,
        out_specs=[VM] * 6,
        compiler_params=params(),
        cost_estimate=lasting("first_sums"),
        name="first_sums",
    )(*a, *b)


def second_sums_kernel(a, got_a, b, g1, g2, g3, stay_a, a1, a2, a3, stay_b, leave_b):
    rows = stay_a.shape[0]
    stay_a[...] = a[:rows] + got_a[:rows].astype(F32)
    for k, target in enumerate((a1, a2, a3)):
        at = slice((k + 1) * rows, (k + 2) * rows)
        target[...] = (a[at] + got_a[at].astype(F32)).astype(BF16)
    total = b[...] + g1[...].astype(F32) + g2[...].astype(F32) + g3[...].astype(F32)
    half = stay_b.shape[0]
    stay_b[...] = total[:half]
    leave_b[...] = total[half:].astype(BF16)


def second_sums(a, b, got_b, deps=()):
    rows, across_a = a[0].shape
    half, across_b = b.shape
    part_a, part_b = (rows // 4, across_a), (half // 2, across_b)
    return pl.pallas_call(
        skipping(second_sums_kernel, 6, len(deps)),
        out_shape=[shaped(part_a, F32)]
        + [shaped(part_a, BF16)] * 3
        + [shaped(part_b, F32), shaped(part_b, BF16)],
        in_specs=[VM] * 6 + [ANY] * len(deps),
        out_specs=[VM] * 6,
        compiler_params=params(),
        cost_estimate=lasting("second_sums"),
        name="second_sums",
    )(*a, b, *got_b, *deps)


def finish_kernel(o, a, g1, g2, g3, b, got_b, output, weight, v0, v1, v2, v3, bias, w0, w1, w2):
    across = output.shape[1]
    output[...] = o[:, :across]
    small = o[:, across:].T
    whole = small[0:8] + small[8:16]
    for k, target in enumerate((v0, v1, v2, v3)):
        target[...] = whole[k : k + 1]
    bias[...] = jnp.concatenate([whole[4:5], whole[5:6]], axis=1)
    total = b[...] + got_b[...].astype(F32)
    cut = a.shape[1]
    rest = b.shape[1] - SEG
    weight[:, :cut] = a[...] + g1[...].astype(F32) + g2[...].astype(F32) + g3[...].astype(F32)
    weight[:, cut:] = total[:, :rest]
    small = total[:, rest:].T
    whole = small[0:8] + small[8:16]
    for k, target in enumerate((w0, w1, w2)):
        target[...] = whole[k : k + 1]


def finish(o, a, got_a, b, got_b):
    rows = o.shape[0]
    vector = shaped((1, rows), F32)
    return pl.pallas_call(
        finish_kernel,
        out_shape=[
            shaped((rows, o.shape[1] - SEG), F32),
            shaped((rows, a.shape[1] + b.shape[1] - SEG), F32),
        ]
        + [vector] * 4
        + [shaped((1, 2 * rows), F32)]
        + [vector] * 3,
        in_specs=[VM] * 7,
        out_specs=[VM] * 10,
        compiler_params=params(),
        cost_estimate=lasting("finish"),
        name="finish",
    )(o, a, *got_a, b, got_b)


def norm_back(hat, scale, up):
    mean_up = jnp.mean(up, axis=-1, keepdims=True)
    mean_both = jnp.mean(up * hat, axis=-1, keepdims=True)
    return scale * (up - mean_up - hat * mean_both)


def middle_back_kernel(
    meta, middle, part, other, grad, gains, weight,
    branch, vectors, g0, g1, g2, g3,
):
    member = meta[0]
    rows, width = middle.shape
    vectors[...] = jnp.zeros_like(vectors)

    def norm_step(at):
        hat, scale = normal(middle[at, :])
        second = part[at, :].astype(F32) + other[at, :].astype(F32)
        given = grad[at, :].astype(F32)
        back = given + norm_back(hat, scale, second * gains[GAIN_F : GAIN_F + 1])
        branch[at, :] = back.astype(BF16)
        vectors[0:1, :] += jnp.sum(second * hat, axis=0, keepdims=True)
        vectors[1:2, :] += jnp.sum(second, axis=0, keepdims=True)
        vectors[2:3, :] += jnp.sum(back, axis=0, keepdims=True)
        vectors[3:4, :] += jnp.sum(given, axis=0, keepdims=True)

    norm_loop(rows, norm_step)
    for d, target in enumerate((g0, g1, g2, g3)):
        at = pl.multiple_of((member ^ d) * PAIR, PAIR)
        target[...] = dot(branch[...], weight[pl.ds(at, PAIR), :], ((1,), (1,))).astype(BF16)


def middle_back(meta, middle, part, other, grad, gains, weight, deps=()):
    rows, width = middle.shape
    specs = [SM] + [VM] * 6
    used = len(specs)
    outs = pl.pallas_call(
        skipping(middle_back_kernel, used, len(deps)),
        out_shape=[shaped((rows, width), BF16), shaped((8, width), F32)]
        + [shaped((rows, PAIR), BF16)] * MEMBERS,
        in_specs=specs + [ANY] * len(deps),
        out_specs=[VM] * (2 + MEMBERS),
        compiler_params=params(),
        cost_estimate=lasting("middle_back"),
        name="middle_back",
    )(meta, middle, part, other, grad, gains, weight, *deps)
    return outs[0], outs[1], outs[2:]


def join_kernel(riders, meta, weight, q0, q1, q2, q3, k0, k1, k2, k3, *refs):
    joined, part, sums = refs[2 * riders : 2 * riders + 3]
    at = 0
    for k in range(riders):
        keep, got, stay = refs[2 * k], refs[2 * k + 1], refs[2 * riders + 3 + k]
        leave = refs[-1].at[:, at : at + keep.shape[1]]
        add_half(keep, got, stay, leave)
        at += keep.shape[1]
    member = meta[0]
    low = lanes((1, PAIR)) < HD
    for d, (query, both) in enumerate(((q0, k0), (q1, k1), (q2, k2), (q3, k3))):
        wide_q = query[...].astype(F32) * (HD ** (-0.5))
        wide_k = pltpu.roll(both[:, :PAIR].astype(F32), HD, 1)
        wide_v = both[:, PAIR:].astype(F32)
        at = (member ^ d) * 3 * PAIR
        for k, tile in enumerate(
            (
                jnp.where(low, wide_q, wide_k),
                jnp.where(low, wide_v, wide_q),
                jnp.where(low, wide_k, wide_v),
            )
        ):
            joined[:, pl.ds(pl.multiple_of(at + k * PAIR, PAIR), PAIR)] = tile.astype(BF16)
        sum_q = jnp.sum(wide_q, axis=0, keepdims=True)
        sum_v = jnp.sum(wide_v, axis=0, keepdims=True)
        spot = pl.multiple_of((member ^ d) * 2 * PAIR, PAIR)
        sums[0:1, pl.ds(spot, PAIR)] = jnp.where(low, sum_q, pltpu.roll(sum_v, HD, 1))
        sums[0:1, pl.ds(pl.multiple_of(spot + PAIR, PAIR), PAIR)] = jnp.where(
            low, pltpu.roll(sum_q, HD, 1), sum_v
        )
    width = weight.shape[0]

    def column(t, _):
        at = pl.ds(pl.multiple_of(t * TILE, TILE), TILE)
        part[:, at] = dot(joined[...], weight[at, :], ((1,), (1,))).astype(BF16)
        return _

    lax.fori_loop(0, width // TILE, column, 0)


def join_stage(meta, weight, query_grads, pair_grads, riders=()):
    rows = query_grads[0].shape[0]
    width, across = weight.shape
    outs = [
        shaped((rows, across), BF16),
        shaped((rows, width), BF16),
        shaped((8, 2 * MEMBERS * PAIR), F32),
    ]
    if riders:
        half = riders[0][0].shape[0] // 2
        outs += [shaped((half, keep.shape[1]), F32) for keep, _got in riders]
        outs.append(shaped((half, sum(keep.shape[1] for keep, _got in riders)), BF16))
    return pl.pallas_call(
        partial(join_kernel, len(riders)),
        out_shape=outs,
        in_specs=[SM] + [VM] * (1 + 2 * MEMBERS + 2 * len(riders)),
        out_specs=[VM] * len(outs),
        compiler_params=params(),
        cost_estimate=lasting("join_stage"),
        name="join_stage",
    )(meta, weight, *query_grads, *pair_grads, *[part for pair in riders for part in pair])


FIRST_PART = 1024


def joined_first_kernel(meta, x, part, normed, joined, keep, send, vectors, turned):
    rows, width = x.shape
    device = meta[4]
    turn_source(normed, turned, device, X_FIRST, width // DEVICES)
    half = width // 2
    tile = TILE

    def column(t, _):
        at = pl.ds(pl.multiple_of(t * tile, tile), tile)
        keep[:, at] = dot(turned[:half], joined[:, at]).astype(BF16)
        send[:, at] = dot(turned[half:], joined[:, at]).astype(BF16)
        return _

    lax.fori_loop(0, keep.shape[1] // tile, column, 0)
    vectors[...] = jnp.zeros_like(vectors)

    def norm_step(at):
        hat, _scale = normal(x[at, :].astype(F32))
        first = part[at, :].astype(F32)
        vectors[0:1, :] += jnp.sum(first * hat, axis=0, keepdims=True)
        vectors[1:2, :] += jnp.sum(first, axis=0, keepdims=True)

    norm_loop(rows, norm_step)


def joined_first(meta, x, part, normed, joined, deps=()):
    rows, width = x.shape
    half = width // 2
    return pl.pallas_call(
        skipping(joined_first_kernel, 5, len(deps)),
        out_shape=[
            shaped((half, FIRST_PART), BF16),
            shaped((half, FIRST_PART), BF16),
            shaped((8, width), F32),
        ],
        in_specs=[SM] + [VM] * 4 + [ANY] * len(deps),
        out_specs=[VM] * 3,
        scratch_shapes=[pltpu.VMEM((width, rows), BF16)],
        compiler_params=params(),
        cost_estimate=lasting("joined_first"),
        name="joined_first",
    )(meta, x, part, normed, joined, *deps)


def joined_second_kernel(
    meta, normed, joined, vectors, other, sums, c, got_c, e, o, got_eo,
    keep, send, last, contract, expand, output, turned, small,
):
    contract[...] = c[...] + got_c[...].astype(F32)
    inner = e.shape[1]
    expand[...] = e[...] + got_eo[:, :inner].astype(F32)
    output[...] = o[...] + got_eo[:, inner:].astype(F32)
    width = normed.shape[1]
    device = meta[4]
    share = width // DEVICES
    turn_source(normed, turned, device, Z_FIRST, share)
    half = width // 2
    across = joined.shape[1] - FIRST_PART
    tile = TILE

    def column(t, _):
        at = pl.ds(pl.multiple_of(t * tile, tile), tile)
        source = pl.ds(pl.multiple_of(FIRST_PART + t * tile, tile), tile)
        keep[:, at] = dot(turned[:half], joined[:, source]).astype(BF16)
        leave = dot(turned[half:], joined[:, source]).astype(BF16)

        @pl.when(t == 0)
        def _first():
            send[...] = leave

        @pl.when(t == 1)
        def _last():
            last[:, :tile] = leave
        return _

    lax.fori_loop(0, across // tile, column, 0)
    for i in range(width // SEG):
        at = slice(i * SEG, (i + 1) * SEG)
        rows8 = jnp.concatenate(
            [vectors[0:2, at] + other[0:2, at], sums[0:1, at], jnp.zeros((5, SEG), F32)], axis=0
        )
        turn_ordered(in_two(rows8).T, small, i, device, Z_FIRST, share)
    keep[:, across:] = small[:half].astype(BF16)
    last[:, tile:] = small[half:].astype(BF16)


def joined_second(meta, normed, joined, vectors, other, sums, c, got_c, e, o, got_eo):
    rows, width = normed.shape
    half = width // 2
    across = joined.shape[1] - FIRST_PART + SEG
    return pl.pallas_call(
        joined_second_kernel,
        out_shape=[
            shaped((half, across), BF16),
            shaped((half, TILE), BF16),
            shaped((half, across - TILE), BF16),
            shaped(c.shape, F32),
            shaped(e.shape, F32),
            shaped(o.shape, F32),
        ],
        in_specs=[SM] + [VM] * 10,
        out_specs=[VM] * 6,
        scratch_shapes=[pltpu.VMEM((width, rows), BF16), pltpu.VMEM((width, SEG), F32)],
        compiler_params=params(),
        cost_estimate=lasting("joined_second"),
        name="joined_second",
    )(meta, normed, joined, vectors, other, sums, c, got_c, e, o, got_eo)


def input_back_kernel(x, part, other, gains, middle_grad, out):
    def norm_step(at):
        hat, scale = normal(x[at, :].astype(F32))
        first = part[at, :].astype(F32) + other[at, :].astype(F32)
        back = norm_back(hat, scale, first * gains[GAIN_A : GAIN_A + 1])
        out[at, :] = (back + middle_grad[at, :].astype(F32)).astype(BF16)

    norm_loop(x.shape[0], norm_step)


def input_back(x, part, other, gains, middle_grad):
    return pl.pallas_call(
        input_back_kernel,
        out_shape=shaped(x.shape, BF16),
        in_specs=[VM] * 5,
        out_specs=VM,
        compiler_params=params(),
        cost_estimate=lasting("input_back"),
        name="input_back",
    )(x, part, other, gains, middle_grad)


def stack_kernel(*refs):
    out, at = refs[-1], 0
    for ref in refs[:-1]:
        rows = ref.shape[0] // out.shape[1]
        out[at : at + rows, :] = ref[...].astype(F32).reshape(rows, out.shape[1])
        at += rows


def stack_vectors(*vectors):
    width = vectors[0].shape[0]
    rows = sum(vector.shape[0] for vector in vectors) // width
    return pl.pallas_call(
        stack_kernel,
        out_shape=shaped((rows, width), F32),
        in_specs=[VM] * len(vectors),
        out_specs=VM,
        name="stack_vectors",
    )(*vectors)


def swap(value):
    return lax.ppermute(value, "tensor", [(0, 1), (1, 0)])


def to_member(value, d):
    count = lax.axis_size("dp")
    return lax.ppermute(value, "dp", [(i, i ^ d) for i in range(count)])


def to_member_across(value, d):
    count = lax.axis_size("dp")
    pairs = [(i * 2 + t, (i ^ d) * 2 + (1 - t)) for i in range(count) for t in range(2)]
    return lax.ppermute(value, ("dp", "tensor"), pairs)


def to_group(value, by):
    count = lax.axis_size("dp")
    step = by * MEMBERS
    return lax.ppermute(value, "dp", [(i, (i + step) % count) for i in range(count)])


def within(parts):
    return [parts[0]] + [to_member(parts[d], d) for d in range(1, MEMBERS)]


def same_kernel(*refs):
    pass


def after_all(value, *others):
    return pl.pallas_call(
        same_kernel,
        out_shape=shaped(value.shape, value.dtype),
        in_specs=[ANY] * (1 + len(others)),
        out_specs=ANY,
        input_output_aliases={0: 0},
        cost_estimate=lasting("after_all"),
        name="after_all",
    )(value, *others)


def reduce_rows(value):
    return lax.psum_scatter(value, "dp", scatter_dimension=0, tiled=True)


def plain_sum(left, right):
    grad = jnp.einsum("td,tf->df", left, right, preferred_element_type=F32)
    return reduce_rows(grad.astype(BF16)).astype(F32)


def plain_sums(x, part, first_low, joined_grad, sums, cotangent, hidden_low, second_low, pre_grad, branch_low, mixed, feed_vectors, extra):
    hat, _scale = normal(x.astype(F32))
    wide = part.astype(F32)
    vectors = jnp.stack([jnp.sum(wide * hat, axis=0), jnp.sum(wide, axis=0)], axis=0)
    vectors = vectors + swap(vectors)
    small = reduce_rows(jnp.concatenate([feed_vectors[:4], extra, vectors, sums[:1]], axis=0).T)
    return (
        plain_sum(cotangent, hidden_low), plain_sum(second_low, pre_grad),
        plain_sum(branch_low, mixed), plain_sum(first_low, joined_grad),
        small[:, 0], small[:, 1], small[:, 2], small[:, 3], small[:, 4:6].T,
        small[:, 6], small[:, 7], small[:, 8],
    )


def shards(
    activations,
    cotangent,
    parent_slot,
    attention_gain,
    attention_shift,
    joined_weight,
    joined_bias,
    output_weight,
    output_bias,
    feed_gain,
    feed_shift,
    expand_weight,
    expand_bias,
    contract_weight,
    contract_bias,
):
    device = lax.axis_index("dp")
    count = lax.axis_size("dp")
    rank = lax.axis_index("tensor")
    member = lax.rem(device, MEMBERS)
    heads_here = joined_weight.shape[1] // (3 * HD)
    width = activations.shape[1]
    inner = expand_weight.shape[1]
    half = output_weight.shape[0]
    meta = jnp.stack(
        [member, device // MEMBERS, rank * heads_here + 2 * member, rank, device]
    ).astype(jnp.int32)
    slopes = jnp.exp2(-8.0 * jnp.arange(1, H + 1, dtype=F32) / H)

    vectors = stack_vectors(
        attention_gain, attention_shift, feed_gain, feed_shift, output_bias, contract_bias,
        joined_bias, expand_bias,
    )
    first_low, queries, keys, values = project(meta, activations, vectors, joined_weight)
    lists, inner_marks = make_lists(meta, parent_slot)
    keys = within(keys)
    k_up, k_down = pack(lists, keys)
    k_below, k_above = to_group(k_up, 1), to_group(k_down, -1)
    values = within(values)
    v_up, v_down = pack(lists, values, deps=(k_up,))
    v_below, v_above = to_group(v_up, 1), to_group(v_down, -1)
    queries = within(queries)
    table = make_tables(meta, parent_slot, lists, inner_marks, deps=(k_up,))
    other_output_weight = swap(output_weight)
    kept, stats = attend_near(
        table, meta, slopes, queries, keys, values, deps=(k_below, k_above)
    )
    away = (k_below, k_above, v_below, v_above)
    outs, lse = attend_far(
        table, meta, slopes, queries, away, kept, stats, deps=(other_output_weight,)
    )
    hidden_grad = product("hidden_grad", cotangent, contract_weight, True, F32, deps=(outs[0],))
    parts_other = [to_member_across(outs[d], d) for d in range(MEMBERS)]
    parts_own = within(outs)
    mixed, middle, second_low, hidden_low, pre_grad, second_part, bias_sums = feed(
        meta, activations, vectors,
        parts_own, parts_other, output_weight, other_output_weight, expand_weight, hidden_grad,
    )
    second_other = swap(second_part)
    extra = bias_sums[0].reshape(count, 2, width // count).transpose(1, 0, 2).reshape(2, width)
    by_halves = count == DEVICES
    if by_halves:
        keep_c, c0, c1, keep_e, e0, e1, feed_part = feed_grads(
            meta, cotangent, hidden_low, second_low, pre_grad, contract_weight
        )
        c0, c1, e0, e1 = (to_member(part, 1) for part in (c0, c1, e0, e1))
    else:
        feed_part = product("feed_part", hidden_low, contract_weight, False, BF16)
    branch_low, feed_vectors, grad_parts = middle_back(
        meta, middle, second_part, second_other, cotangent, vectors, output_weight,
        deps=(feed_part,),
    )
    grad_parts = within(grad_parts)
    feed_other = swap(after_all(feed_part, branch_low))
    fill = ()
    if by_halves:
        (keep_o, send_o), ((keep_c, send_c), (keep_e, send_e)) = output_grads(
            meta, branch_low, mixed, feed_vectors, extra, [(keep_c, c0, c1), (keep_e, e0, e1)]
        )
        got_o, got_c, got_e = to_member(send_o, 1), to_member(send_c, 4), to_member(send_e, 2)
        fill = (keep_o,)
    to_below, to_above, kept_grad = back_far(
        table, meta, slopes, queries, away, outs, grad_parts, lse, deps=fill
    )
    from_above = to_group(to_below, -1)
    from_below = to_group(to_above, 1)
    query_grads, own = back_near(
        table, meta, slopes, queries, keys, values, outs, grad_parts, lse, kept_grad, deps=(feed_other,)
    )
    query_grads = within(query_grads)
    layer_output = (
        middle + (feed_part.astype(F32) + feed_other.astype(F32)) + vectors[CONTRACT_BIAS]
    ).astype(BF16)
    fill = ()
    if by_halves:
        (keep_c, send_c), (keep_e, send_e), (keep_o, send_o) = takes(
            "second_step", [(keep_c, got_c), (keep_e, got_e), (keep_o, got_o)], deps=(own,)
        )
        got_c, got_o = to_member(send_c, 2), to_member(send_o, 2)
        fill = (keep_o,)
    own_pairs = gather_back(
        lists, own, from_above, from_below, deps=tuple(query_grads) + (layer_output,) + fill
    )
    pair_grads = within(own_pairs)
    riders = ()
    if by_halves:
        got_e = to_member(after_all(send_e, own_pairs[0]), 4)
        (keep_c, send_c), (keep_o, send_o) = takes(
            "third_step", [(keep_c, got_c), (keep_o, got_o)], deps=(own_pairs[0],)
        )
        got_c, got_o = to_member(send_c, 8), to_member(send_o, 4)
        riders = ((keep_e, got_e), (keep_o, got_o))
    joined_grad, first_part, joined_bias_sums, *ridden = join_stage(
        meta, joined_weight, query_grads, pair_grads, riders
    )
    if by_halves:
        keep_e, keep_o, send_eo = ridden
        got_eo = to_member(send_eo, 8)
        keep_a, send_a, norm_vectors = joined_first(
            meta, activations, first_part, first_low, joined_grad
        )
        got_a = to_member(send_a, 1)
        norm_other = swap(norm_vectors)
        first_other = swap(after_all(first_part, norm_other))
        keep_b, send_b, last_b, contract_done, expand_done, output_sum = joined_second(
            meta, first_low, joined_grad, norm_vectors, norm_other, joined_bias_sums,
            keep_c, got_c, keep_e, keep_o, got_eo,
        )
        got_b, last_b = to_member(send_b, 1), to_member(last_b, 1)
        keep_a, send_a, keep_b, b1, b2, b3 = first_sums((keep_a, got_a), (keep_b, got_b, last_b))
        got_a = to_member(send_a, 2)
        got_b = [to_member(part, d) for part, d in zip((b1, b2, b3), Z_BLOCKS)]
        keep_a, a1, a2, a3, keep_b, send_b = second_sums((keep_a, got_a), keep_b, got_b)
        got_a = [to_member(part, d) for part, d in zip((a1, a2, a3), Z_BLOCKS)]
        got_b = to_member(send_b, 2)
        done = (contract_done, expand_done) + tuple(
            finish(output_sum, keep_a, got_a, keep_b, got_b)
        )
    else:
        first_other = swap(first_part)
        done = plain_sums(
            activations, first_part, first_low, joined_grad, joined_bias_sums, cotangent,
            hidden_low, second_low, pre_grad, branch_low, mixed, feed_vectors, extra,
        )
    input_gradient = input_back(activations, first_part, first_other, vectors, branch_low)
    (
        contract_done, expand_done, output_done, joined_done,
        feed_gain_grad, feed_shift_grad, output_bias_grad, contract_bias_grad, expand_bias_grad,
        gain_grad, shift_grad, joined_bias_grad,
    ) = done

    return (
        layer_output,
        input_gradient,
        gain_grad.reshape(-1),
        shift_grad.reshape(-1),
        joined_done,
        joined_bias_grad.reshape(-1, 1),
        output_done,
        output_bias_grad.reshape(-1),
        feed_gain_grad.reshape(-1),
        feed_shift_grad.reshape(-1),
        expand_done,
        expand_bias_grad.reshape(-1, 1),
        contract_done,
        contract_bias_grad.reshape(-1),
    )


def solution(mesh):
    in_specs = (
        P("dp", None),
        P("dp", None),
        P(),
        P(),
        P(),
        P(None, "tensor"),
        P("tensor"),
        P("tensor", None),
        P(),
        P(),
        P(),
        P(None, "tensor"),
        P("tensor"),
        P("tensor", None),
        P(),
    )
    out_specs = (
        P("dp", None),
        P("dp", None),
        P("dp"),
        P("dp"),
        P("dp", "tensor"),
        P("dp", "tensor"),
        P("dp", "tensor"),
        P("dp"),
        P("dp"),
        P("dp"),
        P("dp", "tensor"),
        P("dp", "tensor"),
        P("dp", "tensor"),
        P("dp"),
    )
    return jax.shard_map(shards, mesh=mesh, in_specs=in_specs, out_specs=out_specs, check_vma=False)
```

```python
from functools import partial

import jax
import jax.numpy as jnp
from jax import lax
from jax.experimental import pallas as pl
from jax.experimental.pallas import tpu as pltpu
from jax.sharding import PartitionSpec as P

H = 16
HD = 64
SEG = 128
SEG_DEV = 5
ANC = 10
TREE = 20
INNER = 12
MEMBERS = 4
PAIR = 2 * HD
POOL = TREE + 2 * INNER
EMPTY = POOL

EPSILON = 1e-05
NEGATIVE = -1e30

F32 = jnp.float32
BF16 = jnp.bfloat16

LISTS = TREE * ANC
SLOT_AT = (0, 2 * LISTS)
LEVEL_AT = (LISTS, 3 * LISTS)
COUNT_AT = (4 * LISTS, 4 * LISTS + TREE)
UP_AT, DOWN_AT, OFFSET_AT, LISTED = 0, INNER, 2 * INNER, 32
ORDER_AT = (4 * LISTS + 2 * TREE, 4 * LISTS + 3 * TREE)
TABLE = 1024
GROUP = 4

GAIN_A, SHIFT_A, GAIN_F, SHIFT_F, OUT_BIAS, CONTRACT_BIAS, JOINED_BIAS, UP_BIAS = range(8)

VM = pl.BlockSpec(memory_space=pltpu.VMEM)
SM = pl.BlockSpec(memory_space=pltpu.SMEM)
ANY = pl.BlockSpec(memory_space=pl.ANY)


def shaped(shape, kind):
    return jax.ShapeDtypeStruct(shape, kind)


def params(mib=60):
    return pltpu.CompilerParams(vmem_limit_bytes=mib * 2**20)


LASTS = {
    "project": 9, "lists": 2, "tables": 2, "pack": 1, "attend_near": 14, "hidden_grad": 5, "attend_far": 15,
    "feed": 18, "feed_grads": 20, "middle_back": 8, "output_grads": 9, "back_far": 14,
    "back_near": 15, "second_step": 5, "gather_back": 5, "third_step": 3, "join_stage": 7,
    "joined_first": 9, "joined_second": 60, "first_sums": 1, "second_sums": 1,
    "input_back": 6, "finish": 2, "feed_part": 4, "after_all": 0,
}
FLOPS_PER_US = 500_000_000


def lasting(name):
    return pl.CostEstimate(flops=LASTS[name] * FLOPS_PER_US, bytes_accessed=0, transcendentals=0)


def skipping(kernel, used, skipped):
    def run(*refs):
        kernel(*refs[:used], *refs[used + skipped :])

    return run


def dot(a, b, dims=((1,), (0,))):
    return lax.dot_general(a, b, (dims, ((), ())), preferred_element_type=F32)


def lanes(shape):
    return lax.broadcasted_iota(jnp.int32, shape, len(shape) - 1)


def rows_of(shape):
    return lax.broadcasted_iota(jnp.int32, shape, len(shape) - 2)


def lists_kernel(count, meta, parent, out, inner):
    member, group = meta[0], meta[1]

    def clear(i, _):
        inner[i] = 0
        return _

    lax.fori_loop(0, count, clear, 0, unroll=8)

    def mark(i, _):
        up = parent[i]

        @pl.when(up >= 0)
        def _mark():
            inner[up] = 1

        return _

    lax.fori_loop(0, count, mark, 0, unroll=4)

    def cover(i, mask):
        up = parent[i]
        ahead = up - i
        ahead = jnp.where(ahead < 0, ahead + count, ahead)
        forward = ahead < TREE
        low = jnp.where(forward, i, up)
        length = jnp.where(forward, ahead, count - ahead)
        length = jnp.where(up >= 0, length, 0)
        start = lax.rem(low + 1 + TREE, TREE)
        bits = lax.shift_left(1, length) - 1
        room = TREE - start
        first = lax.shift_left(bits & (lax.shift_left(1, room) - 1), start)
        second = lax.shift_right_logical(bits, room)
        return mask | first | second

    mask = lax.fori_loop(0, 2 * TREE - 1, cover, 0, unroll=3)
    offset = 0
    for c in range(TREE):
        free = (lax.shift_right_logical(mask, c) & 1) == 0
        offset = jnp.where(free, c, offset)
    out[OFFSET_AT] = offset
    for i in range(2 * INNER):
        out[UP_AT + i] = -1

    def own(p, ranks):
        up_rank, down_rank = ranks
        spot = ((p // SEG_DEV) ^ member) * SEG_DEV + lax.rem(p, SEG_DEV)
        has = inner[group * TREE + p] == 1
        goes_up = has & (p >= offset) & (offset > 0) & (up_rank < INNER)
        goes_down = has & (p < offset) & (down_rank < INNER)

        @pl.when(goes_up)
        def _up():
            out[UP_AT + up_rank] = spot

        @pl.when(goes_down)
        def _down():
            out[DOWN_AT + down_rank] = spot

        return up_rank + goes_up.astype(jnp.int32), down_rank + goes_down.astype(jnp.int32)

    lax.fori_loop(0, TREE, own, (0, 0))


def make_lists(meta, parent):
    count = parent.shape[0]
    return pl.pallas_call(
        partial(lists_kernel, count),
        out_shape=[shaped((LISTED,), jnp.int32), shaped((count,), jnp.int32)],
        in_specs=[SM, SM],
        out_specs=[SM, SM],
        compiler_params=params(8),
        cost_estimate=lasting("lists"),
        name="lists",
    )(meta, parent)


def table_kernel(count, meta, parent, lists, inner, out, place, starts):
    member, group = meta[0], meta[1]
    groups = count // TREE
    below = lax.rem(group + groups - 1, groups)
    above = lax.rem(group + 1, groups)
    offset = lists[OFFSET_AT]

    def known(p, ranks):
        low_rank, high_rank = ranks
        spot = ((p // SEG_DEV) ^ member) * SEG_DEV + lax.rem(p, SEG_DEV)
        place[group * TREE + p] = spot
        low_slot = below * TREE + p
        high_slot = above * TREE + p
        low = (inner[low_slot] == 1) & (p >= offset) & (offset > 0) & (low_rank < INNER)
        high = (inner[high_slot] == 1) & (p < offset) & (high_rank < INNER)
        place[low_slot] = jnp.where(low, TREE + low_rank, EMPTY)
        place[high_slot] = jnp.where(high, TREE + INNER + high_rank, EMPTY)
        return low_rank + low.astype(jnp.int32), high_rank + high.astype(jnp.int32)

    lax.fori_loop(0, TREE, known, (0, 0))

    def chain(q, _):
        slot = group * TREE + ((q // SEG_DEV) ^ member) * SEG_DEV + lax.rem(q, SEG_DEV)
        for i in range(ANC):
            out[SLOT_AT[0] + q * ANC + i] = TREE
            out[SLOT_AT[1] + q * ANC + i] = 2 * INNER
            out[LEVEL_AT[0] + q * ANC + i] = 0
            out[LEVEL_AT[1] + q * ANC + i] = 0

        def step(a, state):
            at, near, far = state
            good = at >= 0
            safe = jnp.maximum(at, 0)
            spot = place[safe]
            is_near = good & (spot < TREE)
            is_far = good & (spot >= TREE)

            @pl.when(is_near)
            def _near():
                out[SLOT_AT[0] + q * ANC + near] = spot
                out[LEVEL_AT[0] + q * ANC + near] = a

            @pl.when(is_far)
            def _far():
                out[SLOT_AT[1] + q * ANC + far] = spot - TREE
                out[LEVEL_AT[1] + q * ANC + far] = a

            return (
                jnp.where(good, parent[safe], -1),
                near + is_near.astype(jnp.int32),
                far + is_far.astype(jnp.int32),
            )

        _end, near, far = lax.fori_loop(0, ANC, step, (slot, 0, 0))
        out[COUNT_AT[0] + q] = near
        out[COUNT_AT[1] + q] = far
        return _

    lax.fori_loop(0, TREE, chain, 0)

    for side in range(2):
        for i in range(ANC + 1):
            starts[i] = 0

        def tally(q, _):
            starts[out[COUNT_AT[side] + q]] += 1
            return _

        lax.fori_loop(0, TREE, tally, 0)
        total = 0
        for i in range(ANC, -1, -1):
            number = starts[i]
            starts[i] = total
            total = total + number

        def put(q, _):
            number = out[COUNT_AT[side] + q]
            at = starts[number]
            out[ORDER_AT[side] + at] = q
            starts[number] = at + 1
            return _

        lax.fori_loop(0, TREE, put, 0)


def make_tables(meta, parent, lists, inner, deps=()):
    count = parent.shape[0]
    return pl.pallas_call(
        skipping(partial(table_kernel, count), 4, len(deps)),
        out_shape=shaped((TABLE,), jnp.int32),
        in_specs=[SM] * 4 + [ANY] * len(deps),
        out_specs=SM,
        scratch_shapes=[pltpu.SMEM((size,), jnp.int32) for size in (count, 16)],
        compiler_params=params(8),
        cost_estimate=lasting("tables"),
        name="tables",
    )(meta, parent, lists, inner, *deps)


def normal(block):
    centered = block - jnp.mean(block, axis=-1, keepdims=True)
    variance = jnp.mean(centered * centered, axis=-1, keepdims=True)
    scale = lax.rsqrt(variance + EPSILON)
    return centered * scale, scale


NORM_ROWS = 128


def norm_loop(rows, body):
    def step(i, _):
        body(pl.ds(pl.multiple_of(i * NORM_ROWS, NORM_ROWS), NORM_ROWS))
        return _

    lax.fori_loop(0, rows // NORM_ROWS, step, 0, unroll=True)


def project_kernel(meta, x, vectors, weight, normed, *outs):
    member = meta[0]
    rows = x.shape[0]

    def norm_step(at):
        hat, _scale = normal(x[at, :].astype(F32))
        normed[at, :] = (
            hat * vectors[GAIN_A : GAIN_A + 1] + vectors[SHIFT_A : SHIFT_A + 1]
        ).astype(BF16)

    norm_loop(rows, norm_step)
    low = lanes((1, PAIR)) < HD

    def one(d, _):
        pair = member ^ d
        block = weight[:, pl.ds(pl.multiple_of(pair * 3 * PAIR, PAIR), 3 * PAIR)]
        both = vectors[JOINED_BIAS : JOINED_BIAS + 1, pl.ds(pl.multiple_of(pair * 2 * PAIR, PAIR), 2 * PAIR)]
        first, second = both[:, :PAIR], both[:, PAIR:]
        query_bias = jnp.where(low, first, pltpu.roll(second, HD, 1))
        value_bias = jnp.where(low, pltpu.roll(first, HD, 1), second)
        joined = dot(normed[...], block)
        t0, t1, t2 = joined[:, :PAIR], joined[:, PAIR : 2 * PAIR], joined[:, 2 * PAIR :]
        queries = (jnp.where(low, t0, t1) + query_bias) * (HD ** (-0.5))
        keys = pltpu.roll(jnp.where(low, t2, t0), HD, 1)
        values = jnp.where(low, t1, t2) + value_bias
        for j in range(MEMBERS):

            @pl.when(d == j)
            def _store():
                outs[j][...] = queries.astype(BF16)
                outs[MEMBERS + j][...] = keys.astype(BF16)
                outs[2 * MEMBERS + j][...] = values.astype(BF16)

        return _

    lax.fori_loop(0, MEMBERS, one, 0, unroll=True)


def project(meta, x, vectors, weight):
    rows, width = x.shape
    outs = pl.pallas_call(
        project_kernel,
        out_shape=[shaped((rows, width), BF16)]
        + [shaped((rows, PAIR), BF16)] * (3 * MEMBERS),
        in_specs=[SM] + [VM] * 3,
        out_specs=[VM] * (1 + 3 * MEMBERS),
        compiler_params=params(),
        cost_estimate=lasting("project"),
        name="project",
    )(meta, x, vectors, weight)
    return outs[0], outs[1 : 1 + MEMBERS], outs[1 + MEMBERS : 1 + 2 * MEMBERS], outs[1 + 2 * MEMBERS :]


def pack_kernel(table, kv0, kv1, kv2, kv3, up, down, sem):
    sources = (kv0, kv1, kv2, kv3)
    for side, at, target in ((0, UP_AT, up), (1, DOWN_AT, down)):
        for i in range(INNER):
            spot = jnp.maximum(table[at + i], 0)
            d, s = spot // SEG_DEV, lax.rem(spot, SEG_DEV)
            for j in range(MEMBERS):

                @pl.when(d == j)
                def _start():
                    pltpu.make_async_copy(
                        sources[j].at[pl.ds(pl.multiple_of(s * SEG, SEG), SEG)],
                        target.at[pl.ds(i * SEG, SEG)],
                        sem.at[side * INNER + i],
                    ).start()

    for side, target in ((0, up), (1, down)):
        for i in range(INNER):
            piece = target.at[pl.ds(i * SEG, SEG)]
            pltpu.make_async_copy(piece, piece, sem.at[side * INNER + i]).wait()


def pack(table, pairs, deps=()):
    out = shaped((INNER * SEG, PAIR), BF16)
    specs = [SM] + [ANY] * MEMBERS
    used = len(specs)
    return pl.pallas_call(
        skipping(pack_kernel, used, len(deps)),
        out_shape=[out, out],
        in_specs=specs + [ANY] * len(deps),
        out_specs=[ANY] * 2,
        scratch_shapes=[pltpu.SemaphoreType.DMA((2 * INNER,))],
        compiler_params=params(8),
        cost_estimate=lasting("pack"),
        name="pack",
    )(table, *pairs, *deps)


LEVELS = (1, 2, 3, 4, 5, 6, 8, 10)


def split_heads(tile):
    low = lanes((SEG, PAIR)) < HD
    wide = tile.astype(F32)
    zero = jnp.zeros_like(wide)
    return jnp.concatenate(
        [jnp.where(low, wide, zero), jnp.where(low, zero, wide)], axis=0
    ).astype(BF16)


def join_heads(turned):
    top = rows_of((PAIR, SEG)) < HD
    return jnp.where(top, turned[:, :SEG], turned[:, SEG:]).T


def slope_row(slopes, meta):
    first = meta[2]
    return jnp.where(lanes((1, 2 * SEG)) < SEG, slopes[first], slopes[first + 1])


def fill_bias(bias, slope):
    shape = (SEG, 2 * SEG)
    offset = lax.rem(lanes(shape), SEG)
    key = rows_of(shape)
    gap = slope * (key - offset).astype(F32)
    bias[0] = jnp.where(key <= offset, gap, NEGATIVE)
    bias[1] = gap


def split_turned(tile):
    top = rows_of((PAIR, SEG)) < HD
    wide = tile.astype(F32).T
    zero = jnp.zeros_like(wide)
    return jnp.concatenate(
        [jnp.where(top, wide, zero), jnp.where(top, zero, wide)], axis=1
    ).astype(BF16)


def start_all(copies):
    for copy in copies:
        copy.start()


def wait_all(copies):
    for copy in copies:
        copy.wait()


def loads(sources, target, sem, first, column=0):
    copies, at = [], 0
    for k, source in enumerate(sources):
        rows, across = source.shape
        into = target.at[pl.ds(at, rows), pl.ds(column, across)]
        copies.append(pltpu.make_async_copy(source, into, sem.at[first + k]))
        at += rows
    return copies


def segment(ref, at):
    return ref.at[pl.ds(pl.multiple_of(at * SEG, SEG), SEG)]


def turn_all(pool, turned, count, first):
    def turn(i, _):
        turned[i] = segment(pool, i)[:, first : first + PAIR].astype(F32).T.astype(BF16)
        return _

    lax.fori_loop(0, count, turn, 0, unroll=4)
    turned[count] = jnp.zeros((PAIR, SEG), BF16)


def entries(table, side, s, span):
    at = s * ANC
    spots = [table[SLOT_AT[side] + at + i] for i in range(span)]
    levels = [table[LEVEL_AT[side] + at + i] for i in range(span)]
    return spots, levels


def level_row(slope, levels, i, count):
    row = slope * (levels[i] * (-SEG)).astype(F32)
    return row + jnp.where(count <= i, NEGATIVE, 0.0)


def by_groups(table, side, body, empty=None):
    def step(g, _):
        group = [table[ORDER_AT[side] + g * GROUP + k] for k in range(GROUP)]
        most = table[COUNT_AT[side] + group[0]]
        if empty is not None:

            @pl.when(most == 0)
            def _none():
                empty(group)

        for below, span in zip((0,) + LEVELS[:-1], LEVELS):

            @pl.when((most > below) & (most <= span))
            def _run():
                body(group, span)

        return _

    lax.fori_loop(0, TREE // GROUP, step, 0)


def chosen_heads(wide):
    top = rows_of((PAIR, SEG)) < HD
    return jnp.where(top, wide[:, :SEG], wide[:, SEG:])


def weigh(side, span, table, s, slope, bias, pool, turned, stacked):
    count = table[COUNT_AT[side] + s]
    spots, levels = entries(table, side, s, span)
    keys = jnp.concatenate([segment(pool, spot)[:, :PAIR] for spot in spots], axis=0)
    whole = dot(keys, stacked)
    scores = []
    for i in range(span):
        raw = whole[i * SEG : (i + 1) * SEG]
        own = side == 0 and i == 0
        scores.append(raw + bias[0 if own else 1] + level_row(slope, levels, i, count))
    top = scores[0]
    for part in scores[1:]:
        top = jnp.maximum(top, part)
    top = jnp.max(top, axis=0, keepdims=True)
    sums, short = None, []
    for i in range(span):
        weights = jnp.exp(scores[i] - top)
        short.append(weights.astype(BF16))
        sums = weights if sums is None else sums + weights
    values = jnp.concatenate([turned[spot] for spot in spots], axis=1)
    out = dot(values, jnp.concatenate(short, axis=0))
    return top, jnp.sum(sums, axis=0, keepdims=True), chosen_heads(out)


def attend_near_kernel(
    table, meta, slopes, q0, q1, q2, q3, k0, k1, k2, k3, v0, v1, v2, v3,
    kept, stats, pool, turned, queries, bias, sem,
):
    copies = loads((k0, k1, k2, k3), pool, sem, 0)
    copies += loads((v0, v1, v2, v3), pool, sem, MEMBERS, PAIR)
    copies += loads((q0, q1, q2, q3), queries, sem, 2 * MEMBERS)
    start_all(copies)
    slope = slope_row(slopes, meta)
    fill_bias(bias, slope)
    pool[TREE * SEG :, :] = jnp.zeros((SEG, 2 * PAIR), BF16)
    wait_all(copies)
    turn_all(pool, turned, TREE, PAIR)

    def body(group, span):
        for s in group:
            stacked = split_turned(segment(queries, s)[...])
            top, total, out = weigh(0, span, table, s, slope, bias, pool, turned, stacked)
            stats[s, 0:1, :] = top
            stats[s, 1:2, :] = total
            kept[s] = out

    by_groups(table, 0, body)


def attend_near(table, meta, slopes, queries, keys, values, deps=()):
    specs = [SM] * 3 + [ANY] * (3 * MEMBERS)
    used = len(specs)
    return pl.pallas_call(
        skipping(attend_near_kernel, used, len(deps)),
        out_shape=[shaped((TREE, PAIR, SEG), F32), shaped((TREE, 8, 2 * SEG), F32)],
        in_specs=specs + [ANY] * len(deps),
        out_specs=[VM, VM],
        scratch_shapes=[
            pltpu.VMEM(((TREE + 1) * SEG, 2 * PAIR), BF16),
            pltpu.VMEM((TREE + 1, PAIR, SEG), BF16),
            pltpu.VMEM((TREE * SEG, PAIR), BF16),
            pltpu.VMEM((2, SEG, 2 * SEG), F32),
            pltpu.SemaphoreType.DMA((3 * MEMBERS,)),
        ],
        compiler_params=params(),
        cost_estimate=lasting("attend_near"),
        name="attend_near",
    )(table, meta, slopes, *queries, *keys, *values, *deps)


def attend_far_kernel(
    table, meta, slopes, q0, q1, q2, q3, k_below, k_above, v_below, v_above, kept, stats,
    o0, o1, o2, o3, lse, pool, turned, queries, result, bias, sem,
):
    rows = SEG_DEV * SEG
    copies = loads((k_below, k_above), pool, sem, 0)
    copies += loads((v_below, v_above), pool, sem, 2, PAIR)
    copies += loads((q0, q1, q2, q3), queries, sem, 4)
    start_all(copies)
    slope = slope_row(slopes, meta)
    fill_bias(bias, slope)
    pool[2 * INNER * SEG :, :] = jnp.zeros((SEG, 2 * PAIR), BF16)
    wait_all(copies)
    turn_all(pool, turned, 2 * INNER, PAIR)

    def finish(s, top, total, out):
        wide = 1.0 / total
        segment(result, s)[...] = (out * chosen_heads(jnp.broadcast_to(wide, (PAIR, 2 * SEG)))).T.astype(BF16)
        lse[s] = top + jnp.log(total)

    def alone(group):
        for s in group:
            finish(s, stats[s, 0:1, :], stats[s, 1:2, :], kept[s])

    def body(group, span):
        shape = (PAIR, 2 * SEG)
        for s in group:
            stacked = split_turned(segment(queries, s)[...])
            top, total, out = weigh(1, span, table, s, slope, bias, pool, turned, stacked)
            near = stats[s, 0:1, :]
            both = jnp.maximum(near, top)
            near_scale = jnp.exp(near - both)
            far_scale = jnp.exp(top - both)
            total = stats[s, 1:2, :] * near_scale + total * far_scale
            out = kept[s] * chosen_heads(jnp.broadcast_to(near_scale, shape)) + out * (
                chosen_heads(jnp.broadcast_to(far_scale, shape))
            )
            finish(s, both, total, out)

    by_groups(table, 1, body, alone)
    copies = [
        pltpu.make_async_copy(result.at[pl.ds(j * rows, rows)], target, sem.at[j])
        for j, target in enumerate((o0, o1, o2, o3))
    ]
    start_all(copies)
    wait_all(copies)


def attend_far(table, meta, slopes, queries, away, kept, stats, deps=()):
    rows = queries[0].shape[0]
    specs = [SM] * 3 + [ANY] * (MEMBERS + 4) + [VM] * 2
    used = len(specs)
    outs = pl.pallas_call(
        skipping(attend_far_kernel, used, len(deps)),
        out_shape=[shaped((rows, PAIR), BF16)] * MEMBERS + [shaped((TREE, 1, 2 * SEG), F32)],
        in_specs=specs + [ANY] * len(deps),
        out_specs=[ANY] * MEMBERS + [VM],
        scratch_shapes=[
            pltpu.VMEM(((2 * INNER + 1) * SEG, 2 * PAIR), BF16),
            pltpu.VMEM((2 * INNER + 1, PAIR, SEG), BF16),
            pltpu.VMEM((TREE * SEG, PAIR), BF16),
            pltpu.VMEM((TREE * SEG, PAIR), BF16),
            pltpu.VMEM((2, SEG, 2 * SEG), F32),
            pltpu.SemaphoreType.DMA((MEMBERS + 4,)),
        ],
        compiler_params=params(),
        cost_estimate=lasting("attend_far"),
        name="attend_far",
    )(table, meta, slopes, *queries, *away, kept, stats, *deps)
    return outs[:MEMBERS], outs[MEMBERS]


def spread(side, span, table, s, slope, bias, pool, turned, total, queries, outs, grads, lse):
    count = table[COUNT_AT[side] + s]
    query = segment(queries, s)[...]
    stacked = split_heads(query)
    grad = segment(grads, s)[...]
    stacked_grad = split_heads(grad)
    product = (grad.astype(F32) * segment(outs, s)[...].astype(F32)).T
    delta = jnp.concatenate(
        [
            jnp.sum(product[:HD], axis=0, keepdims=True),
            jnp.sum(product[HD:], axis=0, keepdims=True),
        ],
        axis=1,
    )
    log_total = lse[s]
    spots, levels = entries(table, side, s, span)
    keys = jnp.concatenate([segment(pool, spot)[:, :PAIR] for spot in spots], axis=0)
    values = jnp.concatenate([segment(pool, spot)[:, PAIR:] for spot in spots], axis=0)
    raw = dot(keys, split_turned(query))
    prob_grad = dot(values, split_turned(grad))
    probs, score_grads = [], []
    for i in range(span):
        at = slice(i * SEG, (i + 1) * SEG)
        row = level_row(slope, levels, i, count) - log_total
        own = side == 0 and i == 0
        prob = jnp.exp(raw[at] + bias[0 if own else 1] + row)
        score_grads.append((prob * (prob_grad[at] - delta)).astype(BF16))
        probs.append(prob.astype(BF16))
    score_grad = jnp.concatenate(score_grads, axis=0)
    key_grad = dot(score_grad, stacked)
    value_grad = dot(jnp.concatenate(probs, axis=0), stacked_grad)
    for i in range(span):
        at = slice(i * SEG, (i + 1) * SEG)
        into = segment(total, spots[i])
        into[:, :PAIR] += key_grad[at]
        into[:, PAIR:] += value_grad[at]
    across = jnp.concatenate([turned[spot] for spot in spots], axis=1)
    return chosen_heads(dot(across, score_grad))


def clear_all(total, count):
    def clear(i, _):
        segment(total, i)[...] = jnp.zeros((SEG, 2 * PAIR), F32)
        return _

    lax.fori_loop(0, count, clear, 0, unroll=True)


def back_far_kernel(
    table, meta, slopes, q0, q1, q2, q3, k_below, k_above, v_below, v_above, o0, o1, o2, o3, g0, g1, g2, g3, lse,
    to_below, to_above, kept,
    pool, turned, queries, outs, grads, total, small, bias, sem,
):
    copies = loads((k_below, k_above), pool, sem, 0)
    copies += loads((v_below, v_above), pool, sem, 2, PAIR)
    copies += loads((q0, q1, q2, q3), queries, sem, 4)
    copies += loads((o0, o1, o2, o3), outs, sem, 4 + MEMBERS)
    copies += loads((g0, g1, g2, g3), grads, sem, 4 + 2 * MEMBERS)
    start_all(copies)
    slope = slope_row(slopes, meta)
    fill_bias(bias, slope)
    pool[2 * INNER * SEG :, :] = jnp.zeros((SEG, 2 * PAIR), BF16)
    clear_all(total, 2 * INNER + 1)
    wait_all(copies)
    turn_all(pool, turned, 2 * INNER, 0)

    def alone(group):
        for s in group:
            kept[s] = jnp.zeros((PAIR, SEG), F32)

    def body(group, span):
        for s in group:
            kept[s] = spread(
                1, span, table, s, slope, bias, pool, turned, total, queries, outs, grads, lse
            )

    by_groups(table, 1, body, alone)

    def shorten(i, _):
        segment(small, i)[...] = segment(total, i)[...].astype(BF16)
        return _

    lax.fori_loop(0, 2 * INNER, shorten, 0)
    copies = [
        pltpu.make_async_copy(
            small.at[pl.ds(k * INNER * SEG, INNER * SEG)], target, sem.at[k]
        )
        for k, target in enumerate((to_below, to_above))
    ]
    start_all(copies)
    wait_all(copies)


def back_far(table, meta, slopes, queries, away, outs, grads, lse, deps=()):
    side = shaped((INNER * SEG, 2 * PAIR), BF16)
    specs = [SM] * 3 + [ANY] * (3 * MEMBERS + 4) + [VM]
    used = len(specs)
    return pl.pallas_call(
        skipping(back_far_kernel, used, len(deps)),
        out_shape=[side, side, shaped((TREE, PAIR, SEG), F32)],
        in_specs=specs + [ANY] * len(deps),
        out_specs=[ANY] * 2 + [VM],
        scratch_shapes=[
            pltpu.VMEM(((2 * INNER + 1) * SEG, 2 * PAIR), BF16),
            pltpu.VMEM((2 * INNER + 1, PAIR, SEG), BF16),
            pltpu.VMEM((TREE * SEG, PAIR), BF16),
            pltpu.VMEM((TREE * SEG, PAIR), BF16),
            pltpu.VMEM((TREE * SEG, PAIR), BF16),
            pltpu.VMEM(((2 * INNER + 1) * SEG, 2 * PAIR), F32),
            pltpu.VMEM((2 * INNER * SEG, 2 * PAIR), BF16),
            pltpu.VMEM((2, SEG, 2 * SEG), F32),
            pltpu.SemaphoreType.DMA((3 * MEMBERS + 4,)),
        ],
        compiler_params=params(),
        cost_estimate=lasting("back_far"),
        name="back_far",
    )(table, meta, slopes, *queries, *away, *outs, *grads, lse, *deps)


def back_near_kernel(
    table, meta, slopes, q0, q1, q2, q3, k0, k1, k2, k3, v0, v1, v2, v3, o0, o1, o2, o3, g0, g1, g2, g3,
    lse, kept, dq0, dq1, dq2, dq3, own,
    pool, turned, queries, outs, grads, result, total, bias, sem,
):
    rows = SEG_DEV * SEG
    copies = loads((k0, k1, k2, k3), pool, sem, 0)
    copies += loads((v0, v1, v2, v3), pool, sem, MEMBERS, PAIR)
    copies += loads((q0, q1, q2, q3), queries, sem, 2 * MEMBERS)
    copies += loads((o0, o1, o2, o3), outs, sem, 3 * MEMBERS)
    copies += loads((g0, g1, g2, g3), grads, sem, 4 * MEMBERS)
    start_all(copies)
    slope = slope_row(slopes, meta)
    fill_bias(bias, slope)
    pool[TREE * SEG :, :] = jnp.zeros((SEG, 2 * PAIR), BF16)
    clear_all(total, TREE + 1)
    wait_all(copies)
    turn_all(pool, turned, TREE, 0)

    def body(group, span):
        for s in group:
            part = spread(
                0, span, table, s, slope, bias, pool, turned, total, queries, outs, grads, lse
            )
            segment(result, s)[...] = (kept[s] + part).T.astype(BF16)

    by_groups(table, 0, body)
    copies = [
        pltpu.make_async_copy(result.at[pl.ds(j * rows, rows)], target, sem.at[j])
        for j, target in enumerate((dq0, dq1, dq2, dq3))
    ]
    copies.append(
        pltpu.make_async_copy(total.at[pl.ds(0, TREE * SEG)], own, sem.at[MEMBERS])
    )
    start_all(copies)
    wait_all(copies)


def back_near(table, meta, slopes, queries, keys, values, outs, grads, lse, kept, deps=()):
    rows = queries[0].shape[0]
    specs = [SM] * 3 + [ANY] * (5 * MEMBERS) + [VM] * 2
    used = len(specs)
    result = pl.pallas_call(
        skipping(back_near_kernel, used, len(deps)),
        out_shape=[shaped((rows, PAIR), BF16)] * MEMBERS + [shaped((TREE * SEG, 2 * PAIR), F32)],
        in_specs=specs + [ANY] * len(deps),
        out_specs=[ANY] * (MEMBERS + 1),
        scratch_shapes=[
            pltpu.VMEM(((TREE + 1) * SEG, 2 * PAIR), BF16),
            pltpu.VMEM((TREE + 1, PAIR, SEG), BF16),
            pltpu.VMEM((TREE * SEG, PAIR), BF16),
            pltpu.VMEM((TREE * SEG, PAIR), BF16),
            pltpu.VMEM((TREE * SEG, PAIR), BF16),
            pltpu.VMEM((TREE * SEG, PAIR), BF16),
            pltpu.VMEM(((TREE + 1) * SEG, 2 * PAIR), F32),
            pltpu.VMEM((2, SEG, 2 * SEG), F32),
            pltpu.SemaphoreType.DMA((5 * MEMBERS,)),
        ],
        compiler_params=params(),
        cost_estimate=lasting("back_near"),
        name="back_near",
    )(table, meta, slopes, *queries, *keys, *values, *outs, *grads, lse, kept, *deps)
    return result[:MEMBERS], result[MEMBERS]


def gather_back_kernel(table, own, from_above, from_below, k0, k1, k2, k3, total, sem):
    rows = SEG_DEV * SEG
    copy = pltpu.make_async_copy(own, total, sem)
    copy.start()
    copy.wait()
    for at, source in ((UP_AT, from_above), (DOWN_AT, from_below)):

        def add(i, _):
            spot = table[at + i]

            @pl.when(spot >= 0)
            def _add():
                segment(total, spot)[...] += segment(source, i)[...].astype(F32)

            return _

        lax.fori_loop(0, INNER, add, 0)
    for j, target in enumerate((k0, k1, k2, k3)):

        def short(i, _):
            segment(target, i)[...] = segment(total, j * SEG_DEV + i)[...].astype(BF16)
            return _

        lax.fori_loop(0, SEG_DEV, short, 0)


def gather_back(table, own, from_above, from_below, deps=()):
    rows = SEG_DEV * SEG
    specs = [SM, ANY, VM, VM]
    used = len(specs)
    return pl.pallas_call(
        skipping(gather_back_kernel, used, len(deps)),
        out_shape=[shaped((rows, 2 * PAIR), BF16)] * MEMBERS,
        in_specs=specs + [ANY] * len(deps),
        out_specs=[VM] * MEMBERS,
        scratch_shapes=[
            pltpu.VMEM((TREE * SEG, 2 * PAIR), F32),
            pltpu.SemaphoreType.DMA(()),
        ],
        compiler_params=params(),
        cost_estimate=lasting("gather_back"),
        name="gather_back",
    )(table, own, from_above, from_below, *deps)


TILE = 256
def feed_kernel(
    meta, x, vectors, a0, a1, a2, a3, b0, b1, b2, b3,
    w_own, w_other, w_up, hidden_grad,
    mixed_out, middle_out, normed_out, act_out, pre_out, part, sums,
    mixed_own, middle, normed, act, pre_grad, mixed, weight, up, hidden, sem, out_sem,
):
    member, rank = meta[0], meta[3]
    rows, width = x.shape
    half = width // 2
    inner = w_up.shape[1]
    copies = []
    for k, source in enumerate((w_own, w_other)):
        at = pl.multiple_of((rank ^ k) * half, half)
        copies.append(pltpu.make_async_copy(source, weight.at[pl.ds(at, half)], sem.at[k]))
    late = [
        pltpu.make_async_copy(w_up, up, sem.at[2]),
        pltpu.make_async_copy(hidden_grad, hidden, sem.at[3]),
    ]
    start_all(copies + late)
    for k, parts in enumerate(((a0, a1, a2, a3), (b0, b1, b2, b3))):
        for d in range(MEMBERS):
            inside = (member ^ d) * PAIR
            at = pl.multiple_of((rank ^ k) * half + inside, PAIR)
            mixed[:, pl.ds(at, PAIR)] = parts[d][...]
            if k == 0:
                mixed_own[:, pl.ds(pl.multiple_of(inside, PAIR), PAIR)] = parts[d][...]
    stores = [pltpu.make_async_copy(mixed_own, mixed_out, out_sem.at[0])]
    stores[0].start()
    wait_all(copies)

    def column(t, _):
        at = pl.ds(pl.multiple_of(t * TILE, TILE), TILE)
        middle[:, at] = (
            x[:, at].astype(F32) + (dot(mixed[...], weight[:, at]) + vectors[OUT_BIAS : OUT_BIAS + 1, at])
        )
        return _

    lax.fori_loop(0, width // TILE, column, 0, unroll=2)
    stores.append(pltpu.make_async_copy(middle, middle_out, out_sem.at[1]))
    stores[1].start()

    def norm_step(at):
        hat, _scale = normal(middle[at, :])
        normed[at, :] = (hat * vectors[GAIN_F : GAIN_F + 1] + vectors[SHIFT_F : SHIFT_F + 1]).astype(BF16)

    norm_loop(rows, norm_step)
    stores.append(pltpu.make_async_copy(normed, normed_out, out_sem.at[2]))
    stores[2].start()
    wait_all(late)

    def hidden_step(t, _):
        at = pl.ds(pl.multiple_of(t * TILE, TILE), TILE)
        per = width // TILE
        bias = vectors[pl.ds(UP_BIAS + t // per, 1), pl.ds(pl.multiple_of(lax.rem(t, per) * TILE, TILE), TILE)]
        pre = dot(normed[...], up[:, at]) + bias
        square = pre * pre
        c = 0.7978845608028654
        t_ = jnp.tanh(pre * (c + (c * 0.044715) * square))
        low = 0.5 * (1.0 + t_)
        act[:, at] = (pre * low).astype(BF16)
        slope = low + (0.5 * pre) * (1.0 - t_ * t_) * (c + (3.0 * c * 0.044715) * square)
        grad = (hidden[:, at] * slope).astype(BF16)
        pre_grad[:, at] = grad
        sums[0:1, at] = jnp.sum(grad.astype(F32), axis=0, keepdims=True)
        return _

    lax.fori_loop(0, inner // TILE, hidden_step, 0, unroll=2)
    stores.append(pltpu.make_async_copy(act, act_out, out_sem.at[3]))
    stores.append(pltpu.make_async_copy(pre_grad, pre_out, out_sem.at[4]))
    start_all(stores[3:])

    def back(t, _):
        at = pl.ds(pl.multiple_of(t * TILE, TILE), TILE)
        part[:, at] = dot(pre_grad[...], up[at, :], ((1,), (1,))).astype(BF16)
        return _

    lax.fori_loop(0, width // TILE, back, 0, unroll=2)
    wait_all(stores)


def feed(meta, x, vectors, parts_own, parts_other, w_own, w_other, w_up, hidden_grad):
    rows, width = x.shape
    inner = w_up.shape[1]
    half = width // 2
    return pl.pallas_call(
        feed_kernel,
        out_shape=[
            shaped((rows, half), BF16),
            shaped((rows, width), F32),
            shaped((rows, width), BF16),
            shaped((rows, inner), BF16),
            shaped((rows, inner), BF16),
            shaped((rows, width), BF16),
            shaped((8, inner), F32),
        ],
        in_specs=[SM] + [VM] * (2 + 2 * MEMBERS) + [ANY] * 4,
        out_specs=[ANY] * 5 + [VM] * 2,
        scratch_shapes=[
            pltpu.VMEM((rows, half), BF16),
            pltpu.VMEM((rows, width), F32),
            pltpu.VMEM((rows, width), BF16),
            pltpu.VMEM((rows, inner), BF16),
            pltpu.VMEM((rows, inner), BF16),
            pltpu.VMEM((rows, width), BF16),
            pltpu.VMEM((width, width), BF16),
            pltpu.VMEM((width, inner), BF16),
            pltpu.VMEM((rows, inner), F32),
            pltpu.SemaphoreType.DMA((4,)),
            pltpu.SemaphoreType.DMA((5,)),
        ],
        compiler_params=params(),
        cost_estimate=lasting("feed"),
        name="feed",
    )(meta, x, vectors, *parts_own, *parts_other, w_own, w_other, w_up, hidden_grad)


def product_kernel(dims, left, right, out):
    out[...] = dot(left[...], right[...], dims).astype(out.dtype)


def product(name, left, right, turned, kind, deps=()):
    rows, depth = left.shape
    across = right.shape[0] if turned else right.shape[1]
    block = (TILE, depth) if turned else (depth, TILE)
    return pl.pallas_call(
        skipping(partial(product_kernel, ((1,), (1,) if turned else (0,))), 2, len(deps)),
        grid=(across // TILE,),
        out_shape=shaped((rows, across), kind),
        in_specs=[
            pl.BlockSpec((rows, depth), lambda t: (0, 0)),
            pl.BlockSpec(block, (lambda t: (t, 0)) if turned else (lambda t: (0, t))),
        ]
        + [ANY] * len(deps),
        out_specs=pl.BlockSpec((rows, TILE), lambda t: (0, t)),
        compiler_params=params(),
        cost_estimate=lasting(name),
        name=name,
    )(left, right, *deps)


def turn_rows(source, target):
    def step(i, _):
        at = pl.ds(pl.multiple_of(i * SEG, SEG), SEG)
        target[at, :] = source[:, at].astype(F32).T.astype(BF16)
        return _

    lax.fori_loop(0, source.shape[1] // SEG, step, 0)


X_FIRST = (0, 1, 2, 3)
Z_FIRST = (0, 2, 3, 1)
MIXED = (0, 2, 1, 3)
Z_BLOCKS = (8, 4, 12)
DEVICES = 16


def block_place(relative, order):
    place = 0
    for bit in order:
        place = place * 2 + (lax.shift_right_logical(relative, bit) & 1)
    return place


def turn_ordered(tile, target, i, device, order, share):
    for k in range(SEG // share):
        block = i * (SEG // share) + k
        at = block_place(block ^ device, order) * share
        target[pl.ds(pl.multiple_of(at, share), share), :] = tile[k * share : (k + 1) * share]


def turn_source(source, target, device, order, share):
    def step(i, _):
        at = pl.ds(pl.multiple_of(i * SEG, SEG), SEG)
        tile = source[:, at].astype(F32).T.astype(BF16)
        turn_ordered(tile, target, i, device, order, share)
        return _

    lax.fori_loop(0, source.shape[1] // SEG, step, 0)


def feed_grads_kernel(
    meta, grad, act, normed, pre_grad, weight,
    keep_c, send_c0, send_c1, keep_e, send_e0, send_e1, part, turned,
):
    t = pl.program_id(0)
    tiles = pl.num_programs(0) // 2
    width = grad.shape[1]
    half = width // 2
    tile = pre_grad.shape[1]

    @pl.when(t == 0)
    def _first():
        turn_source(grad, turned, meta[4], MIXED, width // DEVICES)

    @pl.when(t == tiles)
    def _second():
        turn_source(normed, turned, meta[4], X_FIRST, width // DEVICES)

    @pl.when(t < tiles)
    def _contract():
        right = act[:, pl.ds(pl.multiple_of(t * tile, tile), tile)]
        keep_c[...] = dot(turned[:half], right).astype(BF16)
        leave = dot(turned[half:], right).astype(BF16)

        @pl.when(t < tiles // 2)
        def _low():
            send_c0[...] = leave

        @pl.when(t >= tiles // 2)
        def _high():
            send_c1[...] = leave

    @pl.when(t >= tiles)
    def _expand():
        keep_e[...] = dot(turned[:half], pre_grad[...]).astype(BF16)
        leave = dot(turned[half:], pre_grad[...]).astype(BF16)

        @pl.when(t < tiles + tiles // 2)
        def _low():
            send_e0[...] = leave

        @pl.when(t >= tiles + tiles // 2)
        def _high():
            send_e1[...] = leave

    part[...] = dot(act[...], weight[...]).astype(BF16)


def feed_grads(meta, grad, act, normed, pre_grad, weight):
    rows, width = grad.shape
    inner = act.shape[1]
    tile = 2 * TILE
    tiles = inner // tile
    piece = width // (2 * tiles)

    def steps(start, number):
        return pl.BlockSpec((width // 2, tile), lambda t: (0, jnp.clip(t - start, 0, number - 1)))

    both = [steps(0, tiles), steps(0, tiles // 2), steps(tiles // 2, tiles // 2)]
    both += [steps(tiles, tiles), steps(tiles, tiles // 2), steps(tiles + tiles // 2, tiles // 2)]
    kept, sent = shaped((width // 2, inner), BF16), shaped((width // 2, inner // 2), BF16)
    whole = pl.BlockSpec((rows, width), lambda t: (0, 0))
    return pl.pallas_call(
        feed_grads_kernel,
        grid=(2 * tiles,),
        out_shape=[kept, sent, sent, kept, sent, sent, shaped((rows, width), BF16)],
        in_specs=[
            SM,
            whole,
            pl.BlockSpec((rows, inner), lambda t: (0, 0)),
            whole,
            pl.BlockSpec((rows, tile), lambda t: (0, jnp.maximum(t - tiles, 0))),
            pl.BlockSpec((inner, piece), lambda t: (0, t)),
        ],
        out_specs=both + [pl.BlockSpec((rows, piece), lambda t: (0, t))],
        scratch_shapes=[pltpu.VMEM((width, rows), BF16)],
        compiler_params=params(),
        cost_estimate=lasting("feed_grads"),
        name="feed_grads",
    )(meta, grad, act, normed, pre_grad, weight)


def in_two(rows8):
    high = rows8.astype(BF16).astype(F32)
    low = rows8 - high
    return jnp.concatenate([high, low, jnp.zeros((SEG - 16, rows8.shape[1]), F32)], axis=0)


def add_half(keep, got, stay, leave):
    half = stay.shape[0]
    stay[...] = keep[:half].astype(F32) + got[:half].astype(F32)
    leave[...] = (keep[half:].astype(F32) + got[half:].astype(F32)).astype(BF16)


TAKE_STEPS = 4


def take_specs(shape):
    rows, across = shape
    if across % (TAKE_STEPS * PAIR) == 0:
        tile, at = across // TAKE_STEPS, lambda t: (0, t)
    else:
        tile, at = across, lambda t: (0, 0)
    return pl.BlockSpec((rows, tile), at), pl.BlockSpec((rows // 2, tile), at)


def add_halves(flags, ins, outs):
    for k, split in enumerate(flags):
        step = partial(add_half, ins[2 * k], ins[2 * k + 1], outs[2 * k], outs[2 * k + 1])
        if split:
            step()
        else:
            pl.when(pl.program_id(0) == 0)(step)


def halves_of(pairs):
    specs, outs, shapes, flags, args = [], [], [], [], []
    for keep, got in pairs:
        whole, part = take_specs(keep.shape)
        half = (keep.shape[0] // 2, keep.shape[1])
        specs += [whole, whole]
        outs += [part, part]
        shapes += [shaped(half, F32), shaped(half, BF16)]
        flags.append(whole.block_shape[1] != keep.shape[1])
        args += [keep, got]
    return specs, outs, shapes, flags, args


def takes_kernel(flags, count, *refs):
    ins, outs = refs[: 2 * len(flags)], refs[2 * len(flags) + count :]
    add_halves(flags, ins, outs)


def takes(name, pairs, deps=()):
    specs, outs, shapes, flags, args = halves_of(pairs)
    got = pl.pallas_call(
        partial(takes_kernel, flags, len(deps)),
        grid=(TAKE_STEPS,),
        out_shape=shapes,
        in_specs=specs + [ANY] * len(deps),
        out_specs=outs,
        compiler_params=params(),
        cost_estimate=lasting(name),
        name=name,
    )(*args, *deps)
    return [tuple(got[2 * k : 2 * k + 2]) for k in range(len(pairs))]


def output_grads_kernel(count, meta, branch, mixed, vectors, sums, *refs):
    ins = refs[: 3 * count]
    keep, send = refs[3 * count : 3 * count + 2]
    outs = refs[3 * count + 2 : -2]
    turned, small = refs[-2:]
    t = pl.program_id(0)
    width, across = branch.shape[1], mixed.shape[1]
    share = width // DEVICES
    half = width // 2

    @pl.when(t == 0)
    def _first():
        turn_source(branch, turned, meta[4], X_FIRST, share)
        for i in range(width // SEG):
            at = slice(i * SEG, (i + 1) * SEG)
            low = lanes((1, SEG)) < share
            one = sums[0:1, 2 * i * SEG : (2 * i + 1) * SEG]
            two = sums[0:1, (2 * i + 1) * SEG : (2 * i + 2) * SEG]
            rows8 = jnp.concatenate(
                [
                    vectors[0:4, at],
                    jnp.where(low, one, pltpu.roll(two, share, 1)),
                    jnp.where(low, pltpu.roll(one, share, 1), two),
                    jnp.zeros((2, SEG), F32),
                ],
                axis=0,
            )
            turn_ordered(in_two(rows8).T, small, i, meta[4], X_FIRST, share)
        keep[:, across:] = small[:half].astype(BF16)
        send[:, across:] = small[half:].astype(BF16)

    tile = across // TAKE_STEPS
    at = pl.ds(pl.multiple_of(t * tile, tile), tile)
    keep[:, at] = dot(turned[:half], mixed[:, at]).astype(BF16)
    send[:, at] = dot(turned[half:], mixed[:, at]).astype(BF16)
    for k in range(count):
        kept, low, high = ins[3 * k : 3 * k + 3]

        @pl.when(t < TAKE_STEPS // 2)
        def _low():
            add_half(kept, low, outs[2 * k], outs[2 * k + 1])

        @pl.when(t >= TAKE_STEPS // 2)
        def _high():
            add_half(kept, high, outs[2 * k], outs[2 * k + 1])


def output_grads(meta, branch, mixed, vectors, sums, pairs):
    rows, width = branch.shape
    across = mixed.shape[1]
    half_steps = TAKE_STEPS // 2
    specs, outs, shapes, args = [], [], [], []
    for kept, low, high in pairs:
        high_rows, cols = kept.shape
        tile = cols // TAKE_STEPS
        specs += [
            pl.BlockSpec((high_rows, tile), lambda t: (0, t)),
            pl.BlockSpec((high_rows, tile), lambda t: (0, jnp.minimum(t, half_steps - 1))),
            pl.BlockSpec((high_rows, tile), lambda t: (0, jnp.maximum(t - half_steps, 0))),
        ]
        outs += [pl.BlockSpec((high_rows // 2, tile), lambda t: (0, t))] * 2
        shapes += [shaped((high_rows // 2, cols), F32), shaped((high_rows // 2, cols), BF16)]
        args += [kept, low, high]

    def whole(shape):
        return pl.BlockSpec(shape, lambda t: (0, 0))

    own = whole((width // 2, across + SEG))
    got = pl.pallas_call(
        partial(output_grads_kernel, len(pairs)),
        grid=(TAKE_STEPS,),
        out_shape=[shaped((width // 2, across + SEG), BF16)] * 2 + shapes,
        in_specs=[SM, whole(branch.shape), whole(mixed.shape), whole(vectors.shape), whole(sums.shape)]
        + specs,
        out_specs=[own, own] + outs,
        scratch_shapes=[pltpu.VMEM((width, rows), BF16), pltpu.VMEM((width, SEG), F32)],
        compiler_params=params(),
        cost_estimate=lasting("output_grads"),
        name="output_grads",
    )(meta, branch, mixed, vectors, sums, *args)
    return (got[0], got[1]), [tuple(got[2 + 2 * k : 4 + 2 * k]) for k in range(len(pairs))]


def first_sums_kernel(
    a, got_a, b, got_b, last_b, stay_a, leave_a, stay_b, b1, b2, b3
):
    add_half(a, got_a, stay_a, leave_a)
    rows = stay_b.shape[0]
    cut = got_b.shape[1]
    for cols, got in ((slice(0, cut), got_b), (slice(cut, b.shape[1]), last_b)):
        stay_b[:, cols] = b[:rows, cols].astype(F32) + got[:rows].astype(F32)
        for k, target in enumerate((b1, b2, b3)):
            at = slice((k + 1) * rows, (k + 2) * rows)
            target[:, cols] = (b[at, cols].astype(F32) + got[at].astype(F32)).astype(BF16)


def first_sums(a, b):
    half, across_a = a[0].shape
    across_b = b[0].shape[1]
    part_a, part_b = (half // 2, across_a), (half // 4, across_b)
    return pl.pallas_call(
        first_sums_kernel,
        out_shape=[shaped(part_a, F32), shaped(part_a, BF16), shaped(part_b, F32)]
        + [shaped(part_b, BF16)] * 3,
        in_specs=[VM] * 5,
        out_specs=[VM] * 6,
        compiler_params=params(),
        cost_estimate=lasting("first_sums"),
        name="first_sums",
    )(*a, *b)


def second_sums_kernel(a, got_a, b, g1, g2, g3, stay_a, a1, a2, a3, stay_b, leave_b):
    rows = stay_a.shape[0]
    stay_a[...] = a[:rows] + got_a[:rows].astype(F32)
    for k, target in enumerate((a1, a2, a3)):
        at = slice((k + 1) * rows, (k + 2) * rows)
        target[...] = (a[at] + got_a[at].astype(F32)).astype(BF16)
    total = b[...] + g1[...].astype(F32) + g2[...].astype(F32) + g3[...].astype(F32)
    half = stay_b.shape[0]
    stay_b[...] = total[:half]
    leave_b[...] = total[half:].astype(BF16)


def second_sums(a, b, got_b, deps=()):
    rows, across_a = a[0].shape
    half, across_b = b.shape
    part_a, part_b = (rows // 4, across_a), (half // 2, across_b)
    return pl.pallas_call(
        skipping(second_sums_kernel, 6, len(deps)),
        out_shape=[shaped(part_a, F32)]
        + [shaped(part_a, BF16)] * 3
        + [shaped(part_b, F32), shaped(part_b, BF16)],
        in_specs=[VM] * 6 + [ANY] * len(deps),
        out_specs=[VM] * 6,
        compiler_params=params(),
        cost_estimate=lasting("second_sums"),
        name="second_sums",
    )(*a, b, *got_b, *deps)


def finish_kernel(o, a, g1, g2, g3, b, got_b, output, weight, v0, v1, v2, v3, bias, w0, w1, w2):
    across = output.shape[1]
    output[...] = o[:, :across]
    small = o[:, across:].T
    whole = small[0:8] + small[8:16]
    for k, target in enumerate((v0, v1, v2, v3)):
        target[...] = whole[k : k + 1]
    bias[...] = jnp.concatenate([whole[4:5], whole[5:6]], axis=1)
    total = b[...] + got_b[...].astype(F32)
    cut = a.shape[1]
    rest = b.shape[1] - SEG
    weight[:, :cut] = a[...] + g1[...].astype(F32) + g2[...].astype(F32) + g3[...].astype(F32)
    weight[:, cut:] = total[:, :rest]
    small = total[:, rest:].T
    whole = small[0:8] + small[8:16]
    for k, target in enumerate((w0, w1, w2)):
        target[...] = whole[k : k + 1]


def finish(o, a, got_a, b, got_b):
    rows = o.shape[0]
    vector = shaped((1, rows), F32)
    return pl.pallas_call(
        finish_kernel,
        out_shape=[
            shaped((rows, o.shape[1] - SEG), F32),
            shaped((rows, a.shape[1] + b.shape[1] - SEG), F32),
        ]
        + [vector] * 4
        + [shaped((1, 2 * rows), F32)]
        + [vector] * 3,
        in_specs=[VM] * 7,
        out_specs=[VM] * 10,
        compiler_params=params(),
        cost_estimate=lasting("finish"),
        name="finish",
    )(o, a, *got_a, b, got_b)


def norm_back(hat, scale, up):
    mean_up = jnp.mean(up, axis=-1, keepdims=True)
    mean_both = jnp.mean(up * hat, axis=-1, keepdims=True)
    return scale * (up - mean_up - hat * mean_both)


def middle_back_kernel(
    meta, middle, part, other, grad, gains, weight,
    branch, vectors, g0, g1, g2, g3,
):
    member = meta[0]
    rows, width = middle.shape
    vectors[...] = jnp.zeros_like(vectors)

    def norm_step(at):
        hat, scale = normal(middle[at, :])
        second = part[at, :].astype(F32) + other[at, :].astype(F32)
        given = grad[at, :].astype(F32)
        back = given + norm_back(hat, scale, second * gains[GAIN_F : GAIN_F + 1])
        branch[at, :] = back.astype(BF16)
        vectors[0:1, :] += jnp.sum(second * hat, axis=0, keepdims=True)
        vectors[1:2, :] += jnp.sum(second, axis=0, keepdims=True)
        vectors[2:3, :] += jnp.sum(back, axis=0, keepdims=True)
        vectors[3:4, :] += jnp.sum(given, axis=0, keepdims=True)

    norm_loop(rows, norm_step)
    for d, target in enumerate((g0, g1, g2, g3)):
        at = pl.multiple_of((member ^ d) * PAIR, PAIR)
        target[...] = dot(branch[...], weight[pl.ds(at, PAIR), :], ((1,), (1,))).astype(BF16)


def middle_back(meta, middle, part, other, grad, gains, weight, deps=()):
    rows, width = middle.shape
    specs = [SM] + [VM] * 6
    used = len(specs)
    outs = pl.pallas_call(
        skipping(middle_back_kernel, used, len(deps)),
        out_shape=[shaped((rows, width), BF16), shaped((8, width), F32)]
        + [shaped((rows, PAIR), BF16)] * MEMBERS,
        in_specs=specs + [ANY] * len(deps),
        out_specs=[VM] * (2 + MEMBERS),
        compiler_params=params(),
        cost_estimate=lasting("middle_back"),
        name="middle_back",
    )(meta, middle, part, other, grad, gains, weight, *deps)
    return outs[0], outs[1], outs[2:]


def join_kernel(riders, meta, weight, q0, q1, q2, q3, k0, k1, k2, k3, *refs):
    joined, part, sums = refs[2 * riders : 2 * riders + 3]
    at = 0
    for k in range(riders):
        keep, got, stay = refs[2 * k], refs[2 * k + 1], refs[2 * riders + 3 + k]
        leave = refs[-1].at[:, at : at + keep.shape[1]]
        add_half(keep, got, stay, leave)
        at += keep.shape[1]
    member = meta[0]
    low = lanes((1, PAIR)) < HD
    for d, (query, both) in enumerate(((q0, k0), (q1, k1), (q2, k2), (q3, k3))):
        wide_q = query[...].astype(F32) * (HD ** (-0.5))
        wide_k = pltpu.roll(both[:, :PAIR].astype(F32), HD, 1)
        wide_v = both[:, PAIR:].astype(F32)
        at = (member ^ d) * 3 * PAIR
        for k, tile in enumerate(
            (
                jnp.where(low, wide_q, wide_k),
                jnp.where(low, wide_v, wide_q),
                jnp.where(low, wide_k, wide_v),
            )
        ):
            joined[:, pl.ds(pl.multiple_of(at + k * PAIR, PAIR), PAIR)] = tile.astype(BF16)
        sum_q = jnp.sum(wide_q, axis=0, keepdims=True)
        sum_v = jnp.sum(wide_v, axis=0, keepdims=True)
        spot = pl.multiple_of((member ^ d) * 2 * PAIR, PAIR)
        sums[0:1, pl.ds(spot, PAIR)] = jnp.where(low, sum_q, pltpu.roll(sum_v, HD, 1))
        sums[0:1, pl.ds(pl.multiple_of(spot + PAIR, PAIR), PAIR)] = jnp.where(
            low, pltpu.roll(sum_q, HD, 1), sum_v
        )
    width = weight.shape[0]

    def column(t, _):
        at = pl.ds(pl.multiple_of(t * TILE, TILE), TILE)
        part[:, at] = dot(joined[...], weight[at, :], ((1,), (1,))).astype(BF16)
        return _

    lax.fori_loop(0, width // TILE, column, 0)


def join_stage(meta, weight, query_grads, pair_grads, riders=()):
    rows = query_grads[0].shape[0]
    width, across = weight.shape
    outs = [
        shaped((rows, across), BF16),
        shaped((rows, width), BF16),
        shaped((8, 2 * MEMBERS * PAIR), F32),
    ]
    if riders:
        half = riders[0][0].shape[0] // 2
        outs += [shaped((half, keep.shape[1]), F32) for keep, _got in riders]
        outs.append(shaped((half, sum(keep.shape[1] for keep, _got in riders)), BF16))
    return pl.pallas_call(
        partial(join_kernel, len(riders)),
        out_shape=outs,
        in_specs=[SM] + [VM] * (1 + 2 * MEMBERS + 2 * len(riders)),
        out_specs=[VM] * len(outs),
        compiler_params=params(),
        cost_estimate=lasting("join_stage"),
        name="join_stage",
    )(meta, weight, *query_grads, *pair_grads, *[part for pair in riders for part in pair])


FIRST_PART = 1024


def joined_first_kernel(meta, x, part, normed, joined, keep, send, vectors, turned):
    rows, width = x.shape
    device = meta[4]
    turn_source(normed, turned, device, X_FIRST, width // DEVICES)
    half = width // 2
    tile = TILE

    def column(t, _):
        at = pl.ds(pl.multiple_of(t * tile, tile), tile)
        keep[:, at] = dot(turned[:half], joined[:, at]).astype(BF16)
        send[:, at] = dot(turned[half:], joined[:, at]).astype(BF16)
        return _

    lax.fori_loop(0, keep.shape[1] // tile, column, 0)
    vectors[...] = jnp.zeros_like(vectors)

    def norm_step(at):
        hat, _scale = normal(x[at, :].astype(F32))
        first = part[at, :].astype(F32)
        vectors[0:1, :] += jnp.sum(first * hat, axis=0, keepdims=True)
        vectors[1:2, :] += jnp.sum(first, axis=0, keepdims=True)

    norm_loop(rows, norm_step)


def joined_first(meta, x, part, normed, joined, deps=()):
    rows, width = x.shape
    half = width // 2
    return pl.pallas_call(
        skipping(joined_first_kernel, 5, len(deps)),
        out_shape=[
            shaped((half, FIRST_PART), BF16),
            shaped((half, FIRST_PART), BF16),
            shaped((8, width), F32),
        ],
        in_specs=[SM] + [VM] * 4 + [ANY] * len(deps),
        out_specs=[VM] * 3,
        scratch_shapes=[pltpu.VMEM((width, rows), BF16)],
        compiler_params=params(),
        cost_estimate=lasting("joined_first"),
        name="joined_first",
    )(meta, x, part, normed, joined, *deps)


def joined_second_kernel(
    meta, normed, joined, vectors, other, sums, c, got_c, e, o, got_eo,
    keep, send, last, contract, expand, output, turned, small,
):
    contract[...] = c[...] + got_c[...].astype(F32)
    inner = e.shape[1]
    expand[...] = e[...] + got_eo[:, :inner].astype(F32)
    output[...] = o[...] + got_eo[:, inner:].astype(F32)
    width = normed.shape[1]
    device = meta[4]
    share = width // DEVICES
    turn_source(normed, turned, device, Z_FIRST, share)
    half = width // 2
    across = joined.shape[1] - FIRST_PART
    tile = TILE

    def column(t, _):
        at = pl.ds(pl.multiple_of(t * tile, tile), tile)
        source = pl.ds(pl.multiple_of(FIRST_PART + t * tile, tile), tile)
        keep[:, at] = dot(turned[:half], joined[:, source]).astype(BF16)
        leave = dot(turned[half:], joined[:, source]).astype(BF16)

        @pl.when(t == 0)
        def _first():
            send[...] = leave

        @pl.when(t == 1)
        def _last():
            last[:, :tile] = leave
        return _

    lax.fori_loop(0, across // tile, column, 0)
    for i in range(width // SEG):
        at = slice(i * SEG, (i + 1) * SEG)
        rows8 = jnp.concatenate(
            [vectors[0:2, at] + other[0:2, at], sums[0:1, at], jnp.zeros((5, SEG), F32)], axis=0
        )
        turn_ordered(in_two(rows8).T, small, i, device, Z_FIRST, share)
    keep[:, across:] = small[:half].astype(BF16)
    last[:, tile:] = small[half:].astype(BF16)


def joined_second(meta, normed, joined, vectors, other, sums, c, got_c, e, o, got_eo):
    rows, width = normed.shape
    half = width // 2
    across = joined.shape[1] - FIRST_PART + SEG
    return pl.pallas_call(
        joined_second_kernel,
        out_shape=[
            shaped((half, across), BF16),
            shaped((half, TILE), BF16),
            shaped((half, across - TILE), BF16),
            shaped(c.shape, F32),
            shaped(e.shape, F32),
            shaped(o.shape, F32),
        ],
        in_specs=[SM] + [VM] * 10,
        out_specs=[VM] * 6,
        scratch_shapes=[pltpu.VMEM((width, rows), BF16), pltpu.VMEM((width, SEG), F32)],
        compiler_params=params(),
        cost_estimate=lasting("joined_second"),
        name="joined_second",
    )(meta, normed, joined, vectors, other, sums, c, got_c, e, o, got_eo)


def input_back_kernel(x, part, other, gains, middle_grad, out):
    def norm_step(at):
        hat, scale = normal(x[at, :].astype(F32))
        first = part[at, :].astype(F32) + other[at, :].astype(F32)
        back = norm_back(hat, scale, first * gains[GAIN_A : GAIN_A + 1])
        out[at, :] = (back + middle_grad[at, :].astype(F32)).astype(BF16)

    norm_loop(x.shape[0], norm_step)


def input_back(x, part, other, gains, middle_grad):
    return pl.pallas_call(
        input_back_kernel,
        out_shape=shaped(x.shape, BF16),
        in_specs=[VM] * 5,
        out_specs=VM,
        compiler_params=params(),
        cost_estimate=lasting("input_back"),
        name="input_back",
    )(x, part, other, gains, middle_grad)


def stack_kernel(*refs):
    out, at = refs[-1], 0
    for ref in refs[:-1]:
        rows = ref.shape[0] // out.shape[1]
        out[at : at + rows, :] = ref[...].astype(F32).reshape(rows, out.shape[1])
        at += rows


def stack_vectors(*vectors):
    width = vectors[0].shape[0]
    rows = sum(vector.shape[0] for vector in vectors) // width
    return pl.pallas_call(
        stack_kernel,
        out_shape=shaped((rows, width), F32),
        in_specs=[VM] * len(vectors),
        out_specs=VM,
        name="stack_vectors",
    )(*vectors)


def swap(value):
    return lax.ppermute(value, "tensor", [(0, 1), (1, 0)])


def to_member(value, d):
    count = lax.axis_size("dp")
    return lax.ppermute(value, "dp", [(i, i ^ d) for i in range(count)])


def to_member_across(value, d):
    count = lax.axis_size("dp")
    pairs = [(i * 2 + t, (i ^ d) * 2 + (1 - t)) for i in range(count) for t in range(2)]
    return lax.ppermute(value, ("dp", "tensor"), pairs)


def to_group(value, by):
    count = lax.axis_size("dp")
    step = by * MEMBERS
    return lax.ppermute(value, "dp", [(i, (i + step) % count) for i in range(count)])


def within(parts):
    return [parts[0]] + [to_member(parts[d], d) for d in range(1, MEMBERS)]


def same_kernel(*refs):
    pass


def after_all(value, *others):
    return pl.pallas_call(
        same_kernel,
        out_shape=shaped(value.shape, value.dtype),
        in_specs=[ANY] * (1 + len(others)),
        out_specs=ANY,
        input_output_aliases={0: 0},
        cost_estimate=lasting("after_all"),
        name="after_all",
    )(value, *others)


def reduce_rows(value):
    return lax.psum_scatter(value, "dp", scatter_dimension=0, tiled=True)


def plain_sum(left, right):
    grad = jnp.einsum("td,tf->df", left, right, preferred_element_type=F32)
    return reduce_rows(grad.astype(BF16)).astype(F32)


def plain_sums(x, part, first_low, joined_grad, sums, cotangent, hidden_low, second_low, pre_grad, branch_low, mixed, feed_vectors, extra):
    hat, _scale = normal(x.astype(F32))
    wide = part.astype(F32)
    vectors = jnp.stack([jnp.sum(wide * hat, axis=0), jnp.sum(wide, axis=0)], axis=0)
    vectors = vectors + swap(vectors)
    small = reduce_rows(jnp.concatenate([feed_vectors[:4], extra, vectors, sums[:1]], axis=0).T)
    return (
        plain_sum(cotangent, hidden_low), plain_sum(second_low, pre_grad),
        plain_sum(branch_low, mixed), plain_sum(first_low, joined_grad),
        small[:, 0], small[:, 1], small[:, 2], small[:, 3], small[:, 4:6].T,
        small[:, 6], small[:, 7], small[:, 8],
    )


def shards(
    activations,
    cotangent,
    parent_slot,
    attention_gain,
    attention_shift,
    joined_weight,
    joined_bias,
    output_weight,
    output_bias,
    feed_gain,
    feed_shift,
    expand_weight,
    expand_bias,
    contract_weight,
    contract_bias,
):
    device = lax.axis_index("dp")
    count = lax.axis_size("dp")
    rank = lax.axis_index("tensor")
    member = lax.rem(device, MEMBERS)
    heads_here = joined_weight.shape[1] // (3 * HD)
    width = activations.shape[1]
    inner = expand_weight.shape[1]
    half = output_weight.shape[0]
    meta = jnp.stack(
        [member, device // MEMBERS, rank * heads_here + 2 * member, rank, device]
    ).astype(jnp.int32)
    slopes = jnp.exp2(-8.0 * jnp.arange(1, H + 1, dtype=F32) / H)

    vectors = stack_vectors(
        attention_gain, attention_shift, feed_gain, feed_shift, output_bias, contract_bias,
        joined_bias, expand_bias,
    )
    first_low, queries, keys, values = project(meta, activations, vectors, joined_weight)
    lists, inner_marks = make_lists(meta, parent_slot)
    keys = within(keys)
    k_up, k_down = pack(lists, keys)
    k_below, k_above = to_group(k_up, 1), to_group(k_down, -1)
    values = within(values)
    v_up, v_down = pack(lists, values, deps=(k_up,))
    v_below, v_above = to_group(v_up, 1), to_group(v_down, -1)
    queries = within(queries)
    table = make_tables(meta, parent_slot, lists, inner_marks, deps=(k_up,))
    other_output_weight = swap(output_weight)
    kept, stats = attend_near(
        table, meta, slopes, queries, keys, values, deps=(k_below, k_above)
    )
    away = (k_below, k_above, v_below, v_above)
    outs, lse = attend_far(
        table, meta, slopes, queries, away, kept, stats, deps=(other_output_weight,)
    )
    hidden_grad = product("hidden_grad", cotangent, contract_weight, True, F32, deps=(outs[0],))
    parts_other = [to_member_across(outs[d], d) for d in range(MEMBERS)]
    parts_own = within(outs)
    mixed, middle, second_low, hidden_low, pre_grad, second_part, bias_sums = feed(
        meta, activations, vectors,
        parts_own, parts_other, output_weight, other_output_weight, expand_weight, hidden_grad,
    )
    second_other = swap(second_part)
    by_halves = count == DEVICES
    if by_halves:
        keep_c, c0, c1, keep_e, e0, e1, feed_part = feed_grads(
            meta, cotangent, hidden_low, second_low, pre_grad, contract_weight
        )
        c0, c1, e0, e1 = (to_member(part, 1) for part in (c0, c1, e0, e1))
    else:
        feed_part = product("feed_part", hidden_low, contract_weight, False, BF16)
    branch_low, feed_vectors, grad_parts = middle_back(
        meta, middle, second_part, second_other, cotangent, vectors, output_weight,
        deps=(feed_part,),
    )
    grad_parts = within(grad_parts)
    feed_other = swap(after_all(feed_part, branch_low))
    fill = ()
    if by_halves:
        (keep_o, send_o), ((keep_c, send_c), (keep_e, send_e)) = output_grads(
            meta, branch_low, mixed, feed_vectors, bias_sums, [(keep_c, c0, c1), (keep_e, e0, e1)]
        )
        got_o, got_c, got_e = to_member(send_o, 1), to_member(send_c, 4), to_member(send_e, 2)
        fill = (keep_o,)
    to_below, to_above, kept_grad = back_far(
        table, meta, slopes, queries, away, outs, grad_parts, lse, deps=fill
    )
    from_above = to_group(to_below, -1)
    from_below = to_group(to_above, 1)
    query_grads, own = back_near(
        table, meta, slopes, queries, keys, values, outs, grad_parts, lse, kept_grad, deps=(feed_other,)
    )
    query_grads = within(query_grads)
    layer_output = (
        middle + (feed_part.astype(F32) + feed_other.astype(F32)) + vectors[CONTRACT_BIAS]
    ).astype(BF16)
    fill = ()
    if by_halves:
        (keep_c, send_c), (keep_e, send_e), (keep_o, send_o) = takes(
            "second_step", [(keep_c, got_c), (keep_e, got_e), (keep_o, got_o)], deps=(own,)
        )
        got_c, got_o = to_member(send_c, 2), to_member(send_o, 2)
        fill = (keep_o,)
    own_pairs = gather_back(
        lists, own, from_above, from_below, deps=tuple(query_grads) + (layer_output,) + fill
    )
    pair_grads = within(own_pairs)
    riders = ()
    if by_halves:
        got_e = to_member(after_all(send_e, own_pairs[0]), 4)
        (keep_c, send_c), (keep_o, send_o) = takes(
            "third_step", [(keep_c, got_c), (keep_o, got_o)], deps=(own_pairs[0],)
        )
        got_c, got_o = to_member(send_c, 8), to_member(send_o, 4)
        riders = ((keep_e, got_e), (keep_o, got_o))
    joined_grad, first_part, joined_bias_sums, *ridden = join_stage(
        meta, joined_weight, query_grads, pair_grads, riders
    )
    if by_halves:
        keep_e, keep_o, send_eo = ridden
        got_eo = to_member(send_eo, 8)
        keep_a, send_a, norm_vectors = joined_first(
            meta, activations, first_part, first_low, joined_grad
        )
        got_a = to_member(send_a, 1)
        norm_other = swap(norm_vectors)
        first_other = swap(after_all(first_part, norm_other))
        keep_b, send_b, last_b, contract_done, expand_done, output_sum = joined_second(
            meta, first_low, joined_grad, norm_vectors, norm_other, joined_bias_sums,
            keep_c, got_c, keep_e, keep_o, got_eo,
        )
        got_b, last_b = to_member(send_b, 1), to_member(last_b, 1)
        keep_a, send_a, keep_b, b1, b2, b3 = first_sums((keep_a, got_a), (keep_b, got_b, last_b))
        got_a = to_member(send_a, 2)
        got_b = [to_member(part, d) for part, d in zip((b1, b2, b3), Z_BLOCKS)]
        keep_a, a1, a2, a3, keep_b, send_b = second_sums((keep_a, got_a), keep_b, got_b)
        got_a = [to_member(part, d) for part, d in zip((a1, a2, a3), Z_BLOCKS)]
        got_b = to_member(send_b, 2)
        done = (contract_done, expand_done) + tuple(
            finish(output_sum, keep_a, got_a, keep_b, got_b)
        )
    else:
        first_other = swap(first_part)
        extra = bias_sums[0].reshape(count, 2, width // count).transpose(1, 0, 2).reshape(2, width)
        done = plain_sums(
            activations, first_part, first_low, joined_grad, joined_bias_sums, cotangent,
            hidden_low, second_low, pre_grad, branch_low, mixed, feed_vectors, extra,
        )
    input_gradient = input_back(activations, first_part, first_other, vectors, branch_low)
    (
        contract_done, expand_done, output_done, joined_done,
        feed_gain_grad, feed_shift_grad, output_bias_grad, contract_bias_grad, expand_bias_grad,
        gain_grad, shift_grad, joined_bias_grad,
    ) = done

    return (
        layer_output,
        input_gradient,
        gain_grad.reshape(-1),
        shift_grad.reshape(-1),
        joined_done,
        joined_bias_grad.reshape(-1, 1),
        output_done,
        output_bias_grad.reshape(-1),
        feed_gain_grad.reshape(-1),
        feed_shift_grad.reshape(-1),
        expand_done,
        expand_bias_grad.reshape(-1, 1),
        contract_done,
        contract_bias_grad.reshape(-1),
    )


def solution(mesh):
    in_specs = (
        P("dp", None),
        P("dp", None),
        P(),
        P(),
        P(),
        P(None, "tensor"),
        P("tensor"),
        P("tensor", None),
        P(),
        P(),
        P(),
        P(None, "tensor"),
        P("tensor"),
        P("tensor", None),
        P(),
    )
    out_specs = (
        P("dp", None),
        P("dp", None),
        P("dp"),
        P("dp"),
        P("dp", "tensor"),
        P("dp", "tensor"),
        P("dp", "tensor"),
        P("dp"),
        P("dp"),
        P("dp"),
        P("dp", "tensor"),
        P("dp", "tensor"),
        P("dp", "tensor"),
        P("dp"),
    )
    return jax.shard_map(shards, mesh=mesh, in_specs=in_specs, out_specs=out_specs, check_vma=False)
```

```python
from functools import partial

import jax
import jax.numpy as jnp
from jax import lax
from jax.experimental import pallas as pl
from jax.experimental.pallas import tpu as pltpu
from jax.sharding import PartitionSpec as P

H = 16
HD = 64
SEG = 128
SEG_DEV = 5
ANC = 10
TREE = 20
INNER = 12
MEMBERS = 4
PAIR = 2 * HD
POOL = TREE + 2 * INNER
EMPTY = POOL

EPSILON = 1e-05
NEGATIVE = -1e30

F32 = jnp.float32
BF16 = jnp.bfloat16

LISTS = TREE * ANC
SLOT_AT = (0, 2 * LISTS)
LEVEL_AT = (LISTS, 3 * LISTS)
COUNT_AT = (4 * LISTS, 4 * LISTS + TREE)
UP_AT, DOWN_AT, OFFSET_AT, LISTED = 0, INNER, 2 * INNER, 32
ORDER_AT = (4 * LISTS + 2 * TREE, 4 * LISTS + 3 * TREE)
TABLE = 1024
GROUP = 4

GAIN_A, SHIFT_A, GAIN_F, SHIFT_F, OUT_BIAS, CONTRACT_BIAS, JOINED_BIAS, UP_BIAS = range(8)

VM = pl.BlockSpec(memory_space=pltpu.VMEM)
SM = pl.BlockSpec(memory_space=pltpu.SMEM)
ANY = pl.BlockSpec(memory_space=pl.ANY)


def shaped(shape, kind):
    return jax.ShapeDtypeStruct(shape, kind)


def params(mib=30):
    return pltpu.CompilerParams(vmem_limit_bytes=mib * 2**20)


LASTS = {
    "project": 9, "lists": 2, "tables": 2, "pack": 1, "attend_near": 14, "hidden_grad": 5, "attend_far": 15,
    "feed": 18, "feed_grads": 20, "middle_back": 8, "output_grads": 9, "back_far": 14,
    "back_near": 15, "second_step": 5, "gather_back": 5, "third_step": 3, "join_stage": 7,
    "joined_first": 9, "joined_second": 60, "first_sums": 1, "second_sums": 1,
    "input_back": 6, "finish": 2, "feed_part": 4, "after_all": 0,
}
FLOPS_PER_US = 500_000_000


def lasting(name):
    return pl.CostEstimate(flops=LASTS[name] * FLOPS_PER_US, bytes_accessed=0, transcendentals=0)


def skipping(kernel, used, skipped):
    def run(*refs):
        kernel(*refs[:used], *refs[used + skipped :])

    return run


def dot(a, b, dims=((1,), (0,))):
    return lax.dot_general(a, b, (dims, ((), ())), preferred_element_type=F32)


def lanes(shape):
    return lax.broadcasted_iota(jnp.int32, shape, len(shape) - 1)


def rows_of(shape):
    return lax.broadcasted_iota(jnp.int32, shape, len(shape) - 2)


def lists_kernel(count, meta, parent, out, inner):
    member, group = meta[0], meta[1]

    def clear(i, _):
        inner[i] = 0
        return _

    lax.fori_loop(0, count, clear, 0, unroll=8)

    def mark(i, _):
        up = parent[i]

        @pl.when(up >= 0)
        def _mark():
            inner[up] = 1

        return _

    lax.fori_loop(0, count, mark, 0, unroll=4)

    def cover(i, mask):
        up = parent[i]
        ahead = up - i
        ahead = jnp.where(ahead < 0, ahead + count, ahead)
        forward = ahead < TREE
        low = jnp.where(forward, i, up)
        length = jnp.where(forward, ahead, count - ahead)
        length = jnp.where(up >= 0, length, 0)
        start = lax.rem(low + 1 + TREE, TREE)
        bits = lax.shift_left(1, length) - 1
        room = TREE - start
        first = lax.shift_left(bits & (lax.shift_left(1, room) - 1), start)
        second = lax.shift_right_logical(bits, room)
        return mask | first | second

    mask = lax.fori_loop(0, 2 * TREE - 1, cover, 0, unroll=3)
    offset = 0
    for c in range(TREE):
        free = (lax.shift_right_logical(mask, c) & 1) == 0
        offset = jnp.where(free, c, offset)
    out[OFFSET_AT] = offset
    for i in range(2 * INNER):
        out[UP_AT + i] = -1

    def own(p, ranks):
        up_rank, down_rank = ranks
        spot = ((p // SEG_DEV) ^ member) * SEG_DEV + lax.rem(p, SEG_DEV)
        has = inner[group * TREE + p] == 1
        goes_up = has & (p >= offset) & (offset > 0) & (up_rank < INNER)
        goes_down = has & (p < offset) & (down_rank < INNER)

        @pl.when(goes_up)
        def _up():
            out[UP_AT + up_rank] = spot

        @pl.when(goes_down)
        def _down():
            out[DOWN_AT + down_rank] = spot

        return up_rank + goes_up.astype(jnp.int32), down_rank + goes_down.astype(jnp.int32)

    lax.fori_loop(0, TREE, own, (0, 0))


def make_lists(meta, parent):
    count = parent.shape[0]
    return pl.pallas_call(
        partial(lists_kernel, count),
        out_shape=[shaped((LISTED,), jnp.int32), shaped((count,), jnp.int32)],
        in_specs=[SM, SM],
        out_specs=[SM, SM],
        compiler_params=params(8),
        cost_estimate=lasting("lists"),
        name="lists",
    )(meta, parent)


def table_kernel(count, meta, parent, lists, inner, out, place, starts):
    member, group = meta[0], meta[1]
    groups = count // TREE
    below = lax.rem(group + groups - 1, groups)
    above = lax.rem(group + 1, groups)
    offset = lists[OFFSET_AT]

    def known(p, ranks):
        low_rank, high_rank = ranks
        spot = ((p // SEG_DEV) ^ member) * SEG_DEV + lax.rem(p, SEG_DEV)
        place[group * TREE + p] = spot
        low_slot = below * TREE + p
        high_slot = above * TREE + p
        low = (inner[low_slot] == 1) & (p >= offset) & (offset > 0) & (low_rank < INNER)
        high = (inner[high_slot] == 1) & (p < offset) & (high_rank < INNER)
        place[low_slot] = jnp.where(low, TREE + low_rank, EMPTY)
        place[high_slot] = jnp.where(high, TREE + INNER + high_rank, EMPTY)
        return low_rank + low.astype(jnp.int32), high_rank + high.astype(jnp.int32)

    lax.fori_loop(0, TREE, known, (0, 0))

    def chain(q, _):
        slot = group * TREE + ((q // SEG_DEV) ^ member) * SEG_DEV + lax.rem(q, SEG_DEV)
        for i in range(ANC):
            out[SLOT_AT[0] + q * ANC + i] = TREE
            out[SLOT_AT[1] + q * ANC + i] = 2 * INNER
            out[LEVEL_AT[0] + q * ANC + i] = 0
            out[LEVEL_AT[1] + q * ANC + i] = 0

        def step(a, state):
            at, near, far = state
            good = at >= 0
            safe = jnp.maximum(at, 0)
            spot = place[safe]
            is_near = good & (spot < TREE)
            is_far = good & (spot >= TREE)

            @pl.when(is_near)
            def _near():
                out[SLOT_AT[0] + q * ANC + near] = spot
                out[LEVEL_AT[0] + q * ANC + near] = a

            @pl.when(is_far)
            def _far():
                out[SLOT_AT[1] + q * ANC + far] = spot - TREE
                out[LEVEL_AT[1] + q * ANC + far] = a

            return (
                jnp.where(good, parent[safe], -1),
                near + is_near.astype(jnp.int32),
                far + is_far.astype(jnp.int32),
            )

        _end, near, far = lax.fori_loop(0, ANC, step, (slot, 0, 0))
        out[COUNT_AT[0] + q] = near
        out[COUNT_AT[1] + q] = far
        return _

    lax.fori_loop(0, TREE, chain, 0)

    for side in range(2):
        for i in range(ANC + 1):
            starts[i] = 0

        def tally(q, _):
            starts[out[COUNT_AT[side] + q]] += 1
            return _

        lax.fori_loop(0, TREE, tally, 0)
        total = 0
        for i in range(ANC, -1, -1):
            number = starts[i]
            starts[i] = total
            total = total + number

        def put(q, _):
            number = out[COUNT_AT[side] + q]
            at = starts[number]
            out[ORDER_AT[side] + at] = q
            starts[number] = at + 1
            return _

        lax.fori_loop(0, TREE, put, 0)


def make_tables(meta, parent, lists, inner, deps=()):
    count = parent.shape[0]
    return pl.pallas_call(
        skipping(partial(table_kernel, count), 4, len(deps)),
        out_shape=shaped((TABLE,), jnp.int32),
        in_specs=[SM] * 4 + [ANY] * len(deps),
        out_specs=SM,
        scratch_shapes=[pltpu.SMEM((size,), jnp.int32) for size in (count, 16)],
        compiler_params=params(8),
        cost_estimate=lasting("tables"),
        name="tables",
    )(meta, parent, lists, inner, *deps)


def normal(block):
    centered = block - jnp.mean(block, axis=-1, keepdims=True)
    variance = jnp.mean(centered * centered, axis=-1, keepdims=True)
    scale = lax.rsqrt(variance + EPSILON)
    return centered * scale, scale


NORM_ROWS = 128


def norm_loop(rows, body):
    def step(i, _):
        body(pl.ds(pl.multiple_of(i * NORM_ROWS, NORM_ROWS), NORM_ROWS))
        return _

    lax.fori_loop(0, rows // NORM_ROWS, step, 0, unroll=True)


def project_kernel(meta, x, vectors, weight, normed, *outs):
    member = meta[0]
    rows = x.shape[0]

    def norm_step(at):
        hat, _scale = normal(x[at, :].astype(F32))
        normed[at, :] = (
            hat * vectors[GAIN_A : GAIN_A + 1] + vectors[SHIFT_A : SHIFT_A + 1]
        ).astype(BF16)

    norm_loop(rows, norm_step)
    low = lanes((1, PAIR)) < HD

    def one(d, _):
        pair = member ^ d
        block = weight[:, pl.ds(pl.multiple_of(pair * 3 * PAIR, PAIR), 3 * PAIR)]
        both = vectors[JOINED_BIAS : JOINED_BIAS + 1, pl.ds(pl.multiple_of(pair * 2 * PAIR, PAIR), 2 * PAIR)]
        first, second = both[:, :PAIR], both[:, PAIR:]
        query_bias = jnp.where(low, first, pltpu.roll(second, HD, 1))
        value_bias = jnp.where(low, pltpu.roll(first, HD, 1), second)
        joined = dot(normed[...], block)
        t0, t1, t2 = joined[:, :PAIR], joined[:, PAIR : 2 * PAIR], joined[:, 2 * PAIR :]
        queries = (jnp.where(low, t0, t1) + query_bias) * (HD ** (-0.5))
        keys = pltpu.roll(jnp.where(low, t2, t0), HD, 1)
        values = jnp.where(low, t1, t2) + value_bias
        for j in range(MEMBERS):

            @pl.when(d == j)
            def _store():
                outs[j][...] = queries.astype(BF16)
                outs[MEMBERS + j][...] = keys.astype(BF16)
                outs[2 * MEMBERS + j][...] = values.astype(BF16)

        return _

    lax.fori_loop(0, MEMBERS, one, 0, unroll=True)


def project(meta, x, vectors, weight):
    rows, width = x.shape
    outs = pl.pallas_call(
        project_kernel,
        out_shape=[shaped((rows, width), BF16)]
        + [shaped((rows, PAIR), BF16)] * (3 * MEMBERS),
        in_specs=[SM] + [VM] * 3,
        out_specs=[VM] * (1 + 3 * MEMBERS),
        compiler_params=params(),
        cost_estimate=lasting("project"),
        name="project",
    )(meta, x, vectors, weight)
    return outs[0], outs[1 : 1 + MEMBERS], outs[1 + MEMBERS : 1 + 2 * MEMBERS], outs[1 + 2 * MEMBERS :]


def pack_kernel(table, kv0, kv1, kv2, kv3, up, down, sem):
    sources = (kv0, kv1, kv2, kv3)
    for side, at, target in ((0, UP_AT, up), (1, DOWN_AT, down)):
        for i in range(INNER):
            spot = jnp.maximum(table[at + i], 0)
            d, s = spot // SEG_DEV, lax.rem(spot, SEG_DEV)
            for j in range(MEMBERS):

                @pl.when(d == j)
                def _start():
                    pltpu.make_async_copy(
                        sources[j].at[pl.ds(pl.multiple_of(s * SEG, SEG), SEG)],
                        target.at[pl.ds(i * SEG, SEG)],
                        sem.at[side * INNER + i],
                    ).start()

    for side, target in ((0, up), (1, down)):
        for i in range(INNER):
            piece = target.at[pl.ds(i * SEG, SEG)]
            pltpu.make_async_copy(piece, piece, sem.at[side * INNER + i]).wait()


def pack(table, pairs, deps=()):
    out = shaped((INNER * SEG, PAIR), BF16)
    specs = [SM] + [ANY] * MEMBERS
    used = len(specs)
    return pl.pallas_call(
        skipping(pack_kernel, used, len(deps)),
        out_shape=[out, out],
        in_specs=specs + [ANY] * len(deps),
        out_specs=[ANY] * 2,
        scratch_shapes=[pltpu.SemaphoreType.DMA((2 * INNER,))],
        compiler_params=params(8),
        cost_estimate=lasting("pack"),
        name="pack",
    )(table, *pairs, *deps)


LEVELS = (1, 2, 3, 4, 5, 6, 8, 10)


def split_heads(tile):
    low = lanes((SEG, PAIR)) < HD
    wide = tile.astype(F32)
    zero = jnp.zeros_like(wide)
    return jnp.concatenate(
        [jnp.where(low, wide, zero), jnp.where(low, zero, wide)], axis=0
    ).astype(BF16)


def join_heads(turned):
    top = rows_of((PAIR, SEG)) < HD
    return jnp.where(top, turned[:, :SEG], turned[:, SEG:]).T


def slope_row(slopes, meta):
    first = meta[2]
    return jnp.where(lanes((1, 2 * SEG)) < SEG, slopes[first], slopes[first + 1])


def fill_bias(bias, slope):
    shape = (SEG, 2 * SEG)
    offset = lax.rem(lanes(shape), SEG)
    key = rows_of(shape)
    gap = slope * (key - offset).astype(F32)
    bias[0] = jnp.where(key <= offset, gap, NEGATIVE)
    bias[1] = gap


def split_turned(tile):
    top = rows_of((PAIR, SEG)) < HD
    wide = tile.astype(F32).T
    zero = jnp.zeros_like(wide)
    return jnp.concatenate(
        [jnp.where(top, wide, zero), jnp.where(top, zero, wide)], axis=1
    ).astype(BF16)


def start_all(copies):
    for copy in copies:
        copy.start()


def wait_all(copies):
    for copy in copies:
        copy.wait()


def loads(sources, target, sem, first, column=0):
    copies, at = [], 0
    for k, source in enumerate(sources):
        rows, across = source.shape
        into = target.at[pl.ds(at, rows), pl.ds(column, across)]
        copies.append(pltpu.make_async_copy(source, into, sem.at[first + k]))
        at += rows
    return copies


def segment(ref, at):
    return ref.at[pl.ds(pl.multiple_of(at * SEG, SEG), SEG)]


def turn_all(pool, turned, count, first):
    def turn(i, _):
        turned[i] = segment(pool, i)[:, first : first + PAIR].astype(F32).T.astype(BF16)
        return _

    lax.fori_loop(0, count, turn, 0, unroll=4)
    turned[count] = jnp.zeros((PAIR, SEG), BF16)


def entries(table, side, s, span):
    at = s * ANC
    spots = [table[SLOT_AT[side] + at + i] for i in range(span)]
    levels = [table[LEVEL_AT[side] + at + i] for i in range(span)]
    return spots, levels


def level_row(slope, levels, i, count):
    row = slope * (levels[i] * (-SEG)).astype(F32)
    return row + jnp.where(count <= i, NEGATIVE, 0.0)


def by_groups(table, side, body, empty=None):
    def step(g, _):
        group = [table[ORDER_AT[side] + g * GROUP + k] for k in range(GROUP)]
        most = table[COUNT_AT[side] + group[0]]
        if empty is not None:

            @pl.when(most == 0)
            def _none():
                empty(group)

        for below, span in zip((0,) + LEVELS[:-1], LEVELS):

            @pl.when((most > below) & (most <= span))
            def _run():
                body(group, span)

        return _

    lax.fori_loop(0, TREE // GROUP, step, 0)


def chosen_heads(wide):
    top = rows_of((PAIR, SEG)) < HD
    return jnp.where(top, wide[:, :SEG], wide[:, SEG:])


def weigh(side, span, table, s, slope, bias, pool, turned, stacked):
    count = table[COUNT_AT[side] + s]
    spots, levels = entries(table, side, s, span)
    keys = jnp.concatenate([segment(pool, spot)[:, :PAIR] for spot in spots], axis=0)
    whole = dot(keys, stacked)
    scores = []
    for i in range(span):
        raw = whole[i * SEG : (i + 1) * SEG]
        own = side == 0 and i == 0
        scores.append(raw + bias[0 if own else 1] + level_row(slope, levels, i, count))
    top = scores[0]
    for part in scores[1:]:
        top = jnp.maximum(top, part)
    top = jnp.max(top, axis=0, keepdims=True)
    sums, short = None, []
    for i in range(span):
        weights = jnp.exp(scores[i] - top)
        short.append(weights.astype(BF16))
        sums = weights if sums is None else sums + weights
    values = jnp.concatenate([turned[spot] for spot in spots], axis=1)
    out = dot(values, jnp.concatenate(short, axis=0))
    return top, jnp.sum(sums, axis=0, keepdims=True), chosen_heads(out)


def attend_near_kernel(
    table, meta, slopes, q0, q1, q2, q3, k0, k1, k2, k3, v0, v1, v2, v3,
    kept, stats, pool, turned, queries, bias, sem,
):
    copies = loads((k0, k1, k2, k3), pool, sem, 0)
    copies += loads((v0, v1, v2, v3), pool, sem, MEMBERS, PAIR)
    copies += loads((q0, q1, q2, q3), queries, sem, 2 * MEMBERS)
    start_all(copies)
    slope = slope_row(slopes, meta)
    fill_bias(bias, slope)
    pool[TREE * SEG :, :] = jnp.zeros((SEG, 2 * PAIR), BF16)
    wait_all(copies)
    turn_all(pool, turned, TREE, PAIR)

    def body(group, span):
        for s in group:
            stacked = split_turned(segment(queries, s)[...])
            top, total, out = weigh(0, span, table, s, slope, bias, pool, turned, stacked)
            stats[s, 0:1, :] = top
            stats[s, 1:2, :] = total
            kept[s] = out

    by_groups(table, 0, body)


def attend_near(table, meta, slopes, queries, keys, values, deps=()):
    specs = [SM] * 3 + [ANY] * (3 * MEMBERS)
    used = len(specs)
    return pl.pallas_call(
        skipping(attend_near_kernel, used, len(deps)),
        out_shape=[shaped((TREE, PAIR, SEG), F32), shaped((TREE, 8, 2 * SEG), F32)],
        in_specs=specs + [ANY] * len(deps),
        out_specs=[VM, VM],
        scratch_shapes=[
            pltpu.VMEM(((TREE + 1) * SEG, 2 * PAIR), BF16),
            pltpu.VMEM((TREE + 1, PAIR, SEG), BF16),
            pltpu.VMEM((TREE * SEG, PAIR), BF16),
            pltpu.VMEM((2, SEG, 2 * SEG), F32),
            pltpu.SemaphoreType.DMA((3 * MEMBERS,)),
        ],
        compiler_params=params(),
        cost_estimate=lasting("attend_near"),
        name="attend_near",
    )(table, meta, slopes, *queries, *keys, *values, *deps)


def attend_far_kernel(
    table, meta, slopes, q0, q1, q2, q3, k_below, k_above, v_below, v_above, kept, stats,
    o0, o1, o2, o3, lse, pool, turned, queries, result, bias, sem,
):
    rows = SEG_DEV * SEG
    copies = loads((k_below, k_above), pool, sem, 0)
    copies += loads((v_below, v_above), pool, sem, 2, PAIR)
    copies += loads((q0, q1, q2, q3), queries, sem, 4)
    start_all(copies)
    slope = slope_row(slopes, meta)
    fill_bias(bias, slope)
    pool[2 * INNER * SEG :, :] = jnp.zeros((SEG, 2 * PAIR), BF16)
    wait_all(copies)
    turn_all(pool, turned, 2 * INNER, PAIR)

    def finish(s, top, total, out):
        wide = 1.0 / total
        segment(result, s)[...] = (out * chosen_heads(jnp.broadcast_to(wide, (PAIR, 2 * SEG)))).T.astype(BF16)
        lse[s] = top + jnp.log(total)

    def alone(group):
        for s in group:
            finish(s, stats[s, 0:1, :], stats[s, 1:2, :], kept[s])

    def body(group, span):
        shape = (PAIR, 2 * SEG)
        for s in group:
            stacked = split_turned(segment(queries, s)[...])
            top, total, out = weigh(1, span, table, s, slope, bias, pool, turned, stacked)
            near = stats[s, 0:1, :]
            both = jnp.maximum(near, top)
            near_scale = jnp.exp(near - both)
            far_scale = jnp.exp(top - both)
            total = stats[s, 1:2, :] * near_scale + total * far_scale
            out = kept[s] * chosen_heads(jnp.broadcast_to(near_scale, shape)) + out * (
                chosen_heads(jnp.broadcast_to(far_scale, shape))
            )
            finish(s, both, total, out)

    by_groups(table, 1, body, alone)
    copies = [
        pltpu.make_async_copy(result.at[pl.ds(j * rows, rows)], target, sem.at[j])
        for j, target in enumerate((o0, o1, o2, o3))
    ]
    start_all(copies)
    wait_all(copies)


def attend_far(table, meta, slopes, queries, away, kept, stats, deps=()):
    rows = queries[0].shape[0]
    specs = [SM] * 3 + [ANY] * (MEMBERS + 4) + [VM] * 2
    used = len(specs)
    outs = pl.pallas_call(
        skipping(attend_far_kernel, used, len(deps)),
        out_shape=[shaped((rows, PAIR), BF16)] * MEMBERS + [shaped((TREE, 1, 2 * SEG), F32)],
        in_specs=specs + [ANY] * len(deps),
        out_specs=[ANY] * MEMBERS + [VM],
        scratch_shapes=[
            pltpu.VMEM(((2 * INNER + 1) * SEG, 2 * PAIR), BF16),
            pltpu.VMEM((2 * INNER + 1, PAIR, SEG), BF16),
            pltpu.VMEM((TREE * SEG, PAIR), BF16),
            pltpu.VMEM((TREE * SEG, PAIR), BF16),
            pltpu.VMEM((2, SEG, 2 * SEG), F32),
            pltpu.SemaphoreType.DMA((MEMBERS + 4,)),
        ],
        compiler_params=params(),
        cost_estimate=lasting("attend_far"),
        name="attend_far",
    )(table, meta, slopes, *queries, *away, kept, stats, *deps)
    return outs[:MEMBERS], outs[MEMBERS]


def spread(side, span, table, s, slope, bias, pool, turned, total, queries, outs, grads, lse):
    count = table[COUNT_AT[side] + s]
    query = segment(queries, s)[...]
    stacked = split_heads(query)
    grad = segment(grads, s)[...]
    stacked_grad = split_heads(grad)
    product = (grad.astype(F32) * segment(outs, s)[...].astype(F32)).T
    delta = jnp.concatenate(
        [
            jnp.sum(product[:HD], axis=0, keepdims=True),
            jnp.sum(product[HD:], axis=0, keepdims=True),
        ],
        axis=1,
    )
    log_total = lse[s]
    spots, levels = entries(table, side, s, span)
    keys = jnp.concatenate([segment(pool, spot)[:, :PAIR] for spot in spots], axis=0)
    values = jnp.concatenate([segment(pool, spot)[:, PAIR:] for spot in spots], axis=0)
    raw = dot(keys, split_turned(query))
    prob_grad = dot(values, split_turned(grad))
    probs, score_grads = [], []
    for i in range(span):
        at = slice(i * SEG, (i + 1) * SEG)
        row = level_row(slope, levels, i, count) - log_total
        own = side == 0 and i == 0
        prob = jnp.exp(raw[at] + bias[0 if own else 1] + row)
        score_grads.append((prob * (prob_grad[at] - delta)).astype(BF16))
        probs.append(prob.astype(BF16))
    score_grad = jnp.concatenate(score_grads, axis=0)
    key_grad = dot(score_grad, stacked)
    value_grad = dot(jnp.concatenate(probs, axis=0), stacked_grad)
    for i in range(span):
        at = slice(i * SEG, (i + 1) * SEG)
        into = segment(total, spots[i])
        into[:, :PAIR] += key_grad[at]
        into[:, PAIR:] += value_grad[at]
    across = jnp.concatenate([turned[spot] for spot in spots], axis=1)
    return chosen_heads(dot(across, score_grad))


def clear_all(total, count):
    def clear(i, _):
        segment(total, i)[...] = jnp.zeros((SEG, 2 * PAIR), F32)
        return _

    lax.fori_loop(0, count, clear, 0, unroll=True)


def back_far_kernel(
    table, meta, slopes, q0, q1, q2, q3, k_below, k_above, v_below, v_above, o0, o1, o2, o3, g0, g1, g2, g3, lse,
    to_below, to_above, kept,
    pool, turned, queries, outs, grads, total, small, bias, sem,
):
    copies = loads((k_below, k_above), pool, sem, 0)
    copies += loads((v_below, v_above), pool, sem, 2, PAIR)
    copies += loads((q0, q1, q2, q3), queries, sem, 4)
    copies += loads((o0, o1, o2, o3), outs, sem, 4 + MEMBERS)
    copies += loads((g0, g1, g2, g3), grads, sem, 4 + 2 * MEMBERS)
    start_all(copies)
    slope = slope_row(slopes, meta)
    fill_bias(bias, slope)
    pool[2 * INNER * SEG :, :] = jnp.zeros((SEG, 2 * PAIR), BF16)
    clear_all(total, 2 * INNER + 1)
    wait_all(copies)
    turn_all(pool, turned, 2 * INNER, 0)

    def alone(group):
        for s in group:
            kept[s] = jnp.zeros((PAIR, SEG), F32)

    def body(group, span):
        for s in group:
            kept[s] = spread(
                1, span, table, s, slope, bias, pool, turned, total, queries, outs, grads, lse
            )

    by_groups(table, 1, body, alone)

    def shorten(i, _):
        segment(small, i)[...] = segment(total, i)[...].astype(BF16)
        return _

    lax.fori_loop(0, 2 * INNER, shorten, 0)
    copies = [
        pltpu.make_async_copy(
            small.at[pl.ds(k * INNER * SEG, INNER * SEG)], target, sem.at[k]
        )
        for k, target in enumerate((to_below, to_above))
    ]
    start_all(copies)
    wait_all(copies)


def back_far(table, meta, slopes, queries, away, outs, grads, lse, deps=()):
    side = shaped((INNER * SEG, 2 * PAIR), BF16)
    specs = [SM] * 3 + [ANY] * (3 * MEMBERS + 4) + [VM]
    used = len(specs)
    return pl.pallas_call(
        skipping(back_far_kernel, used, len(deps)),
        out_shape=[side, side, shaped((TREE, PAIR, SEG), F32)],
        in_specs=specs + [ANY] * len(deps),
        out_specs=[ANY] * 2 + [VM],
        scratch_shapes=[
            pltpu.VMEM(((2 * INNER + 1) * SEG, 2 * PAIR), BF16),
            pltpu.VMEM((2 * INNER + 1, PAIR, SEG), BF16),
            pltpu.VMEM((TREE * SEG, PAIR), BF16),
            pltpu.VMEM((TREE * SEG, PAIR), BF16),
            pltpu.VMEM((TREE * SEG, PAIR), BF16),
            pltpu.VMEM(((2 * INNER + 1) * SEG, 2 * PAIR), F32),
            pltpu.VMEM((2 * INNER * SEG, 2 * PAIR), BF16),
            pltpu.VMEM((2, SEG, 2 * SEG), F32),
            pltpu.SemaphoreType.DMA((3 * MEMBERS + 4,)),
        ],
        compiler_params=params(),
        cost_estimate=lasting("back_far"),
        name="back_far",
    )(table, meta, slopes, *queries, *away, *outs, *grads, lse, *deps)


def back_near_kernel(
    table, meta, slopes, q0, q1, q2, q3, k0, k1, k2, k3, v0, v1, v2, v3, o0, o1, o2, o3, g0, g1, g2, g3,
    lse, kept, dq0, dq1, dq2, dq3, own,
    pool, turned, queries, outs, grads, result, total, bias, sem,
):
    rows = SEG_DEV * SEG
    copies = loads((k0, k1, k2, k3), pool, sem, 0)
    copies += loads((v0, v1, v2, v3), pool, sem, MEMBERS, PAIR)
    copies += loads((q0, q1, q2, q3), queries, sem, 2 * MEMBERS)
    copies += loads((o0, o1, o2, o3), outs, sem, 3 * MEMBERS)
    copies += loads((g0, g1, g2, g3), grads, sem, 4 * MEMBERS)
    start_all(copies)
    slope = slope_row(slopes, meta)
    fill_bias(bias, slope)
    pool[TREE * SEG :, :] = jnp.zeros((SEG, 2 * PAIR), BF16)
    clear_all(total, TREE + 1)
    wait_all(copies)
    turn_all(pool, turned, TREE, 0)

    def body(group, span):
        for s in group:
            part = spread(
                0, span, table, s, slope, bias, pool, turned, total, queries, outs, grads, lse
            )
            segment(result, s)[...] = (kept[s] + part).T.astype(BF16)

    by_groups(table, 0, body)
    copies = [
        pltpu.make_async_copy(result.at[pl.ds(j * rows, rows)], target, sem.at[j])
        for j, target in enumerate((dq0, dq1, dq2, dq3))
    ]
    copies.append(
        pltpu.make_async_copy(total.at[pl.ds(0, TREE * SEG)], own, sem.at[MEMBERS])
    )
    start_all(copies)
    wait_all(copies)


def back_near(table, meta, slopes, queries, keys, values, outs, grads, lse, kept, deps=()):
    rows = queries[0].shape[0]
    specs = [SM] * 3 + [ANY] * (5 * MEMBERS) + [VM] * 2
    used = len(specs)
    result = pl.pallas_call(
        skipping(back_near_kernel, used, len(deps)),
        out_shape=[shaped((rows, PAIR), BF16)] * MEMBERS + [shaped((TREE * SEG, 2 * PAIR), F32)],
        in_specs=specs + [ANY] * len(deps),
        out_specs=[ANY] * (MEMBERS + 1),
        scratch_shapes=[
            pltpu.VMEM(((TREE + 1) * SEG, 2 * PAIR), BF16),
            pltpu.VMEM((TREE + 1, PAIR, SEG), BF16),
            pltpu.VMEM((TREE * SEG, PAIR), BF16),
            pltpu.VMEM((TREE * SEG, PAIR), BF16),
            pltpu.VMEM((TREE * SEG, PAIR), BF16),
            pltpu.VMEM((TREE * SEG, PAIR), BF16),
            pltpu.VMEM(((TREE + 1) * SEG, 2 * PAIR), F32),
            pltpu.VMEM((2, SEG, 2 * SEG), F32),
            pltpu.SemaphoreType.DMA((5 * MEMBERS,)),
        ],
        compiler_params=params(),
        cost_estimate=lasting("back_near"),
        name="back_near",
    )(table, meta, slopes, *queries, *keys, *values, *outs, *grads, lse, kept, *deps)
    return result[:MEMBERS], result[MEMBERS]


def gather_back_kernel(table, own, from_above, from_below, k0, k1, k2, k3, total, sem):
    rows = SEG_DEV * SEG
    copy = pltpu.make_async_copy(own, total, sem)
    copy.start()
    copy.wait()
    for at, source in ((UP_AT, from_above), (DOWN_AT, from_below)):

        def add(i, _):
            spot = table[at + i]

            @pl.when(spot >= 0)
            def _add():
                segment(total, spot)[...] += segment(source, i)[...].astype(F32)

            return _

        lax.fori_loop(0, INNER, add, 0)
    for j, target in enumerate((k0, k1, k2, k3)):

        def short(i, _):
            segment(target, i)[...] = segment(total, j * SEG_DEV + i)[...].astype(BF16)
            return _

        lax.fori_loop(0, SEG_DEV, short, 0)


def gather_back(table, own, from_above, from_below, deps=()):
    rows = SEG_DEV * SEG
    specs = [SM, ANY, VM, VM]
    used = len(specs)
    return pl.pallas_call(
        skipping(gather_back_kernel, used, len(deps)),
        out_shape=[shaped((rows, 2 * PAIR), BF16)] * MEMBERS,
        in_specs=specs + [ANY] * len(deps),
        out_specs=[VM] * MEMBERS,
        scratch_shapes=[
            pltpu.VMEM((TREE * SEG, 2 * PAIR), F32),
            pltpu.SemaphoreType.DMA(()),
        ],
        compiler_params=params(),
        cost_estimate=lasting("gather_back"),
        name="gather_back",
    )(table, own, from_above, from_below, *deps)


TILE = 256
def feed_kernel(
    meta, x, vectors, a0, a1, a2, a3, b0, b1, b2, b3,
    w_own, w_other, w_up, hidden_grad,
    mixed_out, middle_out, normed_out, act_out, pre_out, part, sums,
    mixed_own, middle, normed, act, pre_grad, mixed, weight, up, hidden, sem, out_sem,
):
    member, rank = meta[0], meta[3]
    rows, width = x.shape
    half = width // 2
    inner = w_up.shape[1]
    copies = []
    for k, source in enumerate((w_own, w_other)):
        at = pl.multiple_of((rank ^ k) * half, half)
        copies.append(pltpu.make_async_copy(source, weight.at[pl.ds(at, half)], sem.at[k]))
    late = [
        pltpu.make_async_copy(w_up, up, sem.at[2]),
        pltpu.make_async_copy(hidden_grad, hidden, sem.at[3]),
    ]
    start_all(copies + late)
    for k, parts in enumerate(((a0, a1, a2, a3), (b0, b1, b2, b3))):
        for d in range(MEMBERS):
            inside = (member ^ d) * PAIR
            at = pl.multiple_of((rank ^ k) * half + inside, PAIR)
            mixed[:, pl.ds(at, PAIR)] = parts[d][...]
            if k == 0:
                mixed_own[:, pl.ds(pl.multiple_of(inside, PAIR), PAIR)] = parts[d][...]
    stores = [pltpu.make_async_copy(mixed_own, mixed_out, out_sem.at[0])]
    stores[0].start()
    wait_all(copies)

    def column(t, _):
        at = pl.ds(pl.multiple_of(t * TILE, TILE), TILE)
        middle[:, at] = (
            x[:, at].astype(F32) + (dot(mixed[...], weight[:, at]) + vectors[OUT_BIAS : OUT_BIAS + 1, at])
        )
        return _

    lax.fori_loop(0, width // TILE, column, 0, unroll=2)
    stores.append(pltpu.make_async_copy(middle, middle_out, out_sem.at[1]))
    stores[1].start()

    def norm_step(at):
        hat, _scale = normal(middle[at, :])
        normed[at, :] = (hat * vectors[GAIN_F : GAIN_F + 1] + vectors[SHIFT_F : SHIFT_F + 1]).astype(BF16)

    norm_loop(rows, norm_step)
    stores.append(pltpu.make_async_copy(normed, normed_out, out_sem.at[2]))
    stores[2].start()
    wait_all(late)

    def hidden_step(t, _):
        at = pl.ds(pl.multiple_of(t * TILE, TILE), TILE)
        per = width // TILE
        bias = vectors[pl.ds(UP_BIAS + t // per, 1), pl.ds(pl.multiple_of(lax.rem(t, per) * TILE, TILE), TILE)]
        pre = dot(normed[...], up[:, at]) + bias
        square = pre * pre
        c = 0.7978845608028654
        t_ = jnp.tanh(pre * (c + (c * 0.044715) * square))
        low = 0.5 * (1.0 + t_)
        act[:, at] = (pre * low).astype(BF16)
        slope = low + (0.5 * pre) * (1.0 - t_ * t_) * (c + (3.0 * c * 0.044715) * square)
        grad = (hidden[:, at] * slope).astype(BF16)
        pre_grad[:, at] = grad
        sums[0:1, at] = jnp.sum(grad.astype(F32), axis=0, keepdims=True)
        return _

    lax.fori_loop(0, inner // TILE, hidden_step, 0, unroll=2)
    stores.append(pltpu.make_async_copy(act, act_out, out_sem.at[3]))
    stores.append(pltpu.make_async_copy(pre_grad, pre_out, out_sem.at[4]))
    start_all(stores[3:])

    def back(t, _):
        at = pl.ds(pl.multiple_of(t * TILE, TILE), TILE)
        part[:, at] = dot(pre_grad[...], up[at, :], ((1,), (1,))).astype(BF16)
        return _

    lax.fori_loop(0, width // TILE, back, 0, unroll=2)
    wait_all(stores)


def feed(meta, x, vectors, parts_own, parts_other, w_own, w_other, w_up, hidden_grad):
    rows, width = x.shape
    inner = w_up.shape[1]
    half = width // 2
    return pl.pallas_call(
        feed_kernel,
        out_shape=[
            shaped((rows, half), BF16),
            shaped((rows, width), F32),
            shaped((rows, width), BF16),
            shaped((rows, inner), BF16),
            shaped((rows, inner), BF16),
            shaped((rows, width), BF16),
            shaped((8, inner), F32),
        ],
        in_specs=[SM] + [VM] * (2 + 2 * MEMBERS) + [ANY] * 4,
        out_specs=[ANY] * 5 + [VM] * 2,
        scratch_shapes=[
            pltpu.VMEM((rows, half), BF16),
            pltpu.VMEM((rows, width), F32),
            pltpu.VMEM((rows, width), BF16),
            pltpu.VMEM((rows, inner), BF16),
            pltpu.VMEM((rows, inner), BF16),
            pltpu.VMEM((rows, width), BF16),
            pltpu.VMEM((width, width), BF16),
            pltpu.VMEM((width, inner), BF16),
            pltpu.VMEM((rows, inner), F32),
            pltpu.SemaphoreType.DMA((4,)),
            pltpu.SemaphoreType.DMA((5,)),
        ],
        compiler_params=params(),
        cost_estimate=lasting("feed"),
        name="feed",
    )(meta, x, vectors, *parts_own, *parts_other, w_own, w_other, w_up, hidden_grad)


def product_kernel(dims, left, right, out):
    out[...] = dot(left[...], right[...], dims).astype(out.dtype)


def product(name, left, right, turned, kind, deps=()):
    rows, depth = left.shape
    across = right.shape[0] if turned else right.shape[1]
    block = (TILE, depth) if turned else (depth, TILE)
    return pl.pallas_call(
        skipping(partial(product_kernel, ((1,), (1,) if turned else (0,))), 2, len(deps)),
        grid=(across // TILE,),
        out_shape=shaped((rows, across), kind),
        in_specs=[
            pl.BlockSpec((rows, depth), lambda t: (0, 0)),
            pl.BlockSpec(block, (lambda t: (t, 0)) if turned else (lambda t: (0, t))),
        ]
        + [ANY] * len(deps),
        out_specs=pl.BlockSpec((rows, TILE), lambda t: (0, t)),
        compiler_params=params(),
        cost_estimate=lasting(name),
        name=name,
    )(left, right, *deps)


def turn_rows(source, target):
    def step(i, _):
        at = pl.ds(pl.multiple_of(i * SEG, SEG), SEG)
        target[at, :] = source[:, at].astype(F32).T.astype(BF16)
        return _

    lax.fori_loop(0, source.shape[1] // SEG, step, 0)


X_FIRST = (0, 1, 2, 3)
Z_FIRST = (0, 2, 3, 1)
MIXED = (0, 2, 1, 3)
Z_BLOCKS = (8, 4, 12)
DEVICES = 16


def block_place(relative, order):
    place = 0
    for bit in order:
        place = place * 2 + (lax.shift_right_logical(relative, bit) & 1)
    return place


def turn_ordered(tile, target, i, device, order, share):
    for k in range(SEG // share):
        block = i * (SEG // share) + k
        at = block_place(block ^ device, order) * share
        target[pl.ds(pl.multiple_of(at, share), share), :] = tile[k * share : (k + 1) * share]


def turn_source(source, target, device, order, share):
    def step(i, _):
        at = pl.ds(pl.multiple_of(i * SEG, SEG), SEG)
        tile = source[:, at].astype(F32).T.astype(BF16)
        turn_ordered(tile, target, i, device, order, share)
        return _

    lax.fori_loop(0, source.shape[1] // SEG, step, 0)


def feed_grads_kernel(
    meta, grad, act, normed, pre_grad, weight,
    keep_c, send_c0, send_c1, keep_e, send_e0, send_e1, part, turned,
):
    t = pl.program_id(0)
    tiles = pl.num_programs(0) // 2
    width = grad.shape[1]
    half = width // 2
    tile = pre_grad.shape[1]

    @pl.when(t == 0)
    def _first():
        turn_source(grad, turned, meta[4], MIXED, width // DEVICES)

    @pl.when(t == tiles)
    def _second():
        turn_source(normed, turned, meta[4], X_FIRST, width // DEVICES)

    @pl.when(t < tiles)
    def _contract():
        right = act[:, pl.ds(pl.multiple_of(t * tile, tile), tile)]
        keep_c[...] = dot(turned[:half], right).astype(BF16)
        leave = dot(turned[half:], right).astype(BF16)

        @pl.when(t < tiles // 2)
        def _low():
            send_c0[...] = leave

        @pl.when(t >= tiles // 2)
        def _high():
            send_c1[...] = leave

    @pl.when(t >= tiles)
    def _expand():
        keep_e[...] = dot(turned[:half], pre_grad[...]).astype(BF16)
        leave = dot(turned[half:], pre_grad[...]).astype(BF16)

        @pl.when(t < tiles + tiles // 2)
        def _low():
            send_e0[...] = leave

        @pl.when(t >= tiles + tiles // 2)
        def _high():
            send_e1[...] = leave

    part[...] = dot(act[...], weight[...]).astype(BF16)


def feed_grads(meta, grad, act, normed, pre_grad, weight):
    rows, width = grad.shape
    inner = act.shape[1]
    tile = 2 * TILE
    tiles = inner // tile
    piece = width // (2 * tiles)

    def steps(start, number):
        return pl.BlockSpec((width // 2, tile), lambda t: (0, jnp.clip(t - start, 0, number - 1)))

    both = [steps(0, tiles), steps(0, tiles // 2), steps(tiles // 2, tiles // 2)]
    both += [steps(tiles, tiles), steps(tiles, tiles // 2), steps(tiles + tiles // 2, tiles // 2)]
    kept, sent = shaped((width // 2, inner), BF16), shaped((width // 2, inner // 2), BF16)
    whole = pl.BlockSpec((rows, width), lambda t: (0, 0))
    return pl.pallas_call(
        feed_grads_kernel,
        grid=(2 * tiles,),
        out_shape=[kept, sent, sent, kept, sent, sent, shaped((rows, width), BF16)],
        in_specs=[
            SM,
            whole,
            pl.BlockSpec((rows, inner), lambda t: (0, 0)),
            whole,
            pl.BlockSpec((rows, tile), lambda t: (0, jnp.maximum(t - tiles, 0))),
            pl.BlockSpec((inner, piece), lambda t: (0, t)),
        ],
        out_specs=both + [pl.BlockSpec((rows, piece), lambda t: (0, t))],
        scratch_shapes=[pltpu.VMEM((width, rows), BF16)],
        compiler_params=params(),
        cost_estimate=lasting("feed_grads"),
        name="feed_grads",
    )(meta, grad, act, normed, pre_grad, weight)


def in_two(rows8):
    high = rows8.astype(BF16).astype(F32)
    low = rows8 - high
    return jnp.concatenate([high, low, jnp.zeros((SEG - 16, rows8.shape[1]), F32)], axis=0)


def add_half(keep, got, stay, leave):
    half = stay.shape[0]
    stay[...] = keep[:half].astype(F32) + got[:half].astype(F32)
    leave[...] = (keep[half:].astype(F32) + got[half:].astype(F32)).astype(BF16)


TAKE_STEPS = 4


def take_specs(shape):
    rows, across = shape
    if across % (TAKE_STEPS * PAIR) == 0:
        tile, at = across // TAKE_STEPS, lambda t: (0, t)
    else:
        tile, at = across, lambda t: (0, 0)
    return pl.BlockSpec((rows, tile), at), pl.BlockSpec((rows // 2, tile), at)


def add_halves(flags, ins, outs):
    for k, split in enumerate(flags):
        step = partial(add_half, ins[2 * k], ins[2 * k + 1], outs[2 * k], outs[2 * k + 1])
        if split:
            step()
        else:
            pl.when(pl.program_id(0) == 0)(step)


def halves_of(pairs):
    specs, outs, shapes, flags, args = [], [], [], [], []
    for keep, got in pairs:
        whole, part = take_specs(keep.shape)
        half = (keep.shape[0] // 2, keep.shape[1])
        specs += [whole, whole]
        outs += [part, part]
        shapes += [shaped(half, F32), shaped(half, BF16)]
        flags.append(whole.block_shape[1] != keep.shape[1])
        args += [keep, got]
    return specs, outs, shapes, flags, args


def takes_kernel(flags, count, *refs):
    ins, outs = refs[: 2 * len(flags)], refs[2 * len(flags) + count :]
    add_halves(flags, ins, outs)


def takes(name, pairs, deps=()):
    specs, outs, shapes, flags, args = halves_of(pairs)
    got = pl.pallas_call(
        partial(takes_kernel, flags, len(deps)),
        grid=(TAKE_STEPS,),
        out_shape=shapes,
        in_specs=specs + [ANY] * len(deps),
        out_specs=outs,
        compiler_params=params(),
        cost_estimate=lasting(name),
        name=name,
    )(*args, *deps)
    return [tuple(got[2 * k : 2 * k + 2]) for k in range(len(pairs))]


def output_grads_kernel(count, meta, branch, mixed, vectors, sums, *refs):
    ins = refs[: 3 * count]
    keep, send = refs[3 * count : 3 * count + 2]
    outs = refs[3 * count + 2 : -2]
    turned, small = refs[-2:]
    t = pl.program_id(0)
    width, across = branch.shape[1], mixed.shape[1]
    share = width // DEVICES
    half = width // 2

    @pl.when(t == 0)
    def _first():
        turn_source(branch, turned, meta[4], X_FIRST, share)
        for i in range(width // SEG):
            at = slice(i * SEG, (i + 1) * SEG)
            low = lanes((1, SEG)) < share
            one = sums[0:1, 2 * i * SEG : (2 * i + 1) * SEG]
            two = sums[0:1, (2 * i + 1) * SEG : (2 * i + 2) * SEG]
            rows8 = jnp.concatenate(
                [
                    vectors[0:4, at],
                    jnp.where(low, one, pltpu.roll(two, share, 1)),
                    jnp.where(low, pltpu.roll(one, share, 1), two),
                    jnp.zeros((2, SEG), F32),
                ],
                axis=0,
            )
            turn_ordered(in_two(rows8).T, small, i, meta[4], X_FIRST, share)
        keep[:, across:] = small[:half].astype(BF16)
        send[:, across:] = small[half:].astype(BF16)

    tile = across // TAKE_STEPS
    at = pl.ds(pl.multiple_of(t * tile, tile), tile)
    keep[:, at] = dot(turned[:half], mixed[:, at]).astype(BF16)
    send[:, at] = dot(turned[half:], mixed[:, at]).astype(BF16)
    for k in range(count):
        kept, low, high = ins[3 * k : 3 * k + 3]

        @pl.when(t < TAKE_STEPS // 2)
        def _low():
            add_half(kept, low, outs[2 * k], outs[2 * k + 1])

        @pl.when(t >= TAKE_STEPS // 2)
        def _high():
            add_half(kept, high, outs[2 * k], outs[2 * k + 1])


def output_grads(meta, branch, mixed, vectors, sums, pairs):
    rows, width = branch.shape
    across = mixed.shape[1]
    half_steps = TAKE_STEPS // 2
    specs, outs, shapes, args = [], [], [], []
    for kept, low, high in pairs:
        high_rows, cols = kept.shape
        tile = cols // TAKE_STEPS
        specs += [
            pl.BlockSpec((high_rows, tile), lambda t: (0, t)),
            pl.BlockSpec((high_rows, tile), lambda t: (0, jnp.minimum(t, half_steps - 1))),
            pl.BlockSpec((high_rows, tile), lambda t: (0, jnp.maximum(t - half_steps, 0))),
        ]
        outs += [pl.BlockSpec((high_rows // 2, tile), lambda t: (0, t))] * 2
        shapes += [shaped((high_rows // 2, cols), F32), shaped((high_rows // 2, cols), BF16)]
        args += [kept, low, high]

    def whole(shape):
        return pl.BlockSpec(shape, lambda t: (0, 0))

    own = whole((width // 2, across + SEG))
    got = pl.pallas_call(
        partial(output_grads_kernel, len(pairs)),
        grid=(TAKE_STEPS,),
        out_shape=[shaped((width // 2, across + SEG), BF16)] * 2 + shapes,
        in_specs=[SM, whole(branch.shape), whole(mixed.shape), whole(vectors.shape), whole(sums.shape)]
        + specs,
        out_specs=[own, own] + outs,
        scratch_shapes=[pltpu.VMEM((width, rows), BF16), pltpu.VMEM((width, SEG), F32)],
        compiler_params=params(),
        cost_estimate=lasting("output_grads"),
        name="output_grads",
    )(meta, branch, mixed, vectors, sums, *args)
    return (got[0], got[1]), [tuple(got[2 + 2 * k : 4 + 2 * k]) for k in range(len(pairs))]


def first_sums_kernel(
    a, got_a, b, got_b, last_b, stay_a, leave_a, stay_b, b1, b2, b3
):
    add_half(a, got_a, stay_a, leave_a)
    rows = stay_b.shape[0]
    cut = got_b.shape[1]
    for cols, got in ((slice(0, cut), got_b), (slice(cut, b.shape[1]), last_b)):
        stay_b[:, cols] = b[:rows, cols].astype(F32) + got[:rows].astype(F32)
        for k, target in enumerate((b1, b2, b3)):
            at = slice((k + 1) * rows, (k + 2) * rows)
            target[:, cols] = (b[at, cols].astype(F32) + got[at].astype(F32)).astype(BF16)


def first_sums(a, b):
    half, across_a = a[0].shape
    across_b = b[0].shape[1]
    part_a, part_b = (half // 2, across_a), (half // 4, across_b)
    return pl.pallas_call(
        first_sums_kernel,
        out_shape=[shaped(part_a, F32), shaped(part_a, BF16), shaped(part_b, F32)]
        + [shaped(part_b, BF16)] * 3,
        in_specs=[VM] * 5,
        out_specs=[VM] * 6,
        compiler_params=params(),
        cost_estimate=lasting("first_sums"),
        name="first_sums",
    )(*a, *b)


def second_sums_kernel(a, got_a, b, g1, g2, g3, stay_a, a1, a2, a3, stay_b, leave_b):
    rows = stay_a.shape[0]
    stay_a[...] = a[:rows] + got_a[:rows].astype(F32)
    for k, target in enumerate((a1, a2, a3)):
        at = slice((k + 1) * rows, (k + 2) * rows)
        target[...] = (a[at] + got_a[at].astype(F32)).astype(BF16)
    total = b[...] + g1[...].astype(F32) + g2[...].astype(F32) + g3[...].astype(F32)
    half = stay_b.shape[0]
    stay_b[...] = total[:half]
    leave_b[...] = total[half:].astype(BF16)


def second_sums(a, b, got_b, deps=()):
    rows, across_a = a[0].shape
    half, across_b = b.shape
    part_a, part_b = (rows // 4, across_a), (half // 2, across_b)
    return pl.pallas_call(
        skipping(second_sums_kernel, 6, len(deps)),
        out_shape=[shaped(part_a, F32)]
        + [shaped(part_a, BF16)] * 3
        + [shaped(part_b, F32), shaped(part_b, BF16)],
        in_specs=[VM] * 6 + [ANY] * len(deps),
        out_specs=[VM] * 6,
        compiler_params=params(),
        cost_estimate=lasting("second_sums"),
        name="second_sums",
    )(*a, b, *got_b, *deps)


def finish_kernel(o, a, g1, g2, g3, b, got_b, output, weight, v0, v1, v2, v3, bias, w0, w1, w2):
    across = output.shape[1]
    output[...] = o[:, :across]
    small = o[:, across:].T
    whole = small[0:8] + small[8:16]
    for k, target in enumerate((v0, v1, v2, v3)):
        target[...] = whole[k : k + 1]
    bias[...] = jnp.concatenate([whole[4:5], whole[5:6]], axis=1)
    total = b[...] + got_b[...].astype(F32)
    cut = a.shape[1]
    rest = b.shape[1] - SEG
    weight[:, :cut] = a[...] + g1[...].astype(F32) + g2[...].astype(F32) + g3[...].astype(F32)
    weight[:, cut:] = total[:, :rest]
    small = total[:, rest:].T
    whole = small[0:8] + small[8:16]
    for k, target in enumerate((w0, w1, w2)):
        target[...] = whole[k : k + 1]


def finish(o, a, got_a, b, got_b):
    rows = o.shape[0]
    vector = shaped((1, rows), F32)
    return pl.pallas_call(
        finish_kernel,
        out_shape=[
            shaped((rows, o.shape[1] - SEG), F32),
            shaped((rows, a.shape[1] + b.shape[1] - SEG), F32),
        ]
        + [vector] * 4
        + [shaped((1, 2 * rows), F32)]
        + [vector] * 3,
        in_specs=[VM] * 7,
        out_specs=[VM] * 10,
        compiler_params=params(),
        cost_estimate=lasting("finish"),
        name="finish",
    )(o, a, *got_a, b, got_b)


def norm_back(hat, scale, up):
    mean_up = jnp.mean(up, axis=-1, keepdims=True)
    mean_both = jnp.mean(up * hat, axis=-1, keepdims=True)
    return scale * (up - mean_up - hat * mean_both)


def middle_back_kernel(
    meta, middle, part, other, grad, gains, weight,
    branch, vectors, g0, g1, g2, g3,
):
    member = meta[0]
    rows, width = middle.shape
    vectors[...] = jnp.zeros_like(vectors)

    def norm_step(at):
        hat, scale = normal(middle[at, :])
        second = part[at, :].astype(F32) + other[at, :].astype(F32)
        given = grad[at, :].astype(F32)
        back = given + norm_back(hat, scale, second * gains[GAIN_F : GAIN_F + 1])
        branch[at, :] = back.astype(BF16)
        vectors[0:1, :] += jnp.sum(second * hat, axis=0, keepdims=True)
        vectors[1:2, :] += jnp.sum(second, axis=0, keepdims=True)
        vectors[2:3, :] += jnp.sum(back, axis=0, keepdims=True)
        vectors[3:4, :] += jnp.sum(given, axis=0, keepdims=True)

    norm_loop(rows, norm_step)
    for d, target in enumerate((g0, g1, g2, g3)):
        at = pl.multiple_of((member ^ d) * PAIR, PAIR)
        target[...] = dot(branch[...], weight[pl.ds(at, PAIR), :], ((1,), (1,))).astype(BF16)


def middle_back(meta, middle, part, other, grad, gains, weight, deps=()):
    rows, width = middle.shape
    specs = [SM] + [VM] * 6
    used = len(specs)
    outs = pl.pallas_call(
        skipping(middle_back_kernel, used, len(deps)),
        out_shape=[shaped((rows, width), BF16), shaped((8, width), F32)]
        + [shaped((rows, PAIR), BF16)] * MEMBERS,
        in_specs=specs + [ANY] * len(deps),
        out_specs=[VM] * (2 + MEMBERS),
        compiler_params=params(),
        cost_estimate=lasting("middle_back"),
        name="middle_back",
    )(meta, middle, part, other, grad, gains, weight, *deps)
    return outs[0], outs[1], outs[2:]


def join_kernel(riders, meta, weight, q0, q1, q2, q3, k0, k1, k2, k3, *refs):
    joined, part, sums = refs[2 * riders : 2 * riders + 3]
    at = 0
    for k in range(riders):
        keep, got, stay = refs[2 * k], refs[2 * k + 1], refs[2 * riders + 3 + k]
        leave = refs[-1].at[:, at : at + keep.shape[1]]
        add_half(keep, got, stay, leave)
        at += keep.shape[1]
    member = meta[0]
    low = lanes((1, PAIR)) < HD
    for d, (query, both) in enumerate(((q0, k0), (q1, k1), (q2, k2), (q3, k3))):
        wide_q = query[...].astype(F32) * (HD ** (-0.5))
        wide_k = pltpu.roll(both[:, :PAIR].astype(F32), HD, 1)
        wide_v = both[:, PAIR:].astype(F32)
        at = (member ^ d) * 3 * PAIR
        for k, tile in enumerate(
            (
                jnp.where(low, wide_q, wide_k),
                jnp.where(low, wide_v, wide_q),
                jnp.where(low, wide_k, wide_v),
            )
        ):
            joined[:, pl.ds(pl.multiple_of(at + k * PAIR, PAIR), PAIR)] = tile.astype(BF16)
        sum_q = jnp.sum(wide_q, axis=0, keepdims=True)
        sum_v = jnp.sum(wide_v, axis=0, keepdims=True)
        spot = pl.multiple_of((member ^ d) * 2 * PAIR, PAIR)
        sums[0:1, pl.ds(spot, PAIR)] = jnp.where(low, sum_q, pltpu.roll(sum_v, HD, 1))
        sums[0:1, pl.ds(pl.multiple_of(spot + PAIR, PAIR), PAIR)] = jnp.where(
            low, pltpu.roll(sum_q, HD, 1), sum_v
        )
    width = weight.shape[0]

    def column(t, _):
        at = pl.ds(pl.multiple_of(t * TILE, TILE), TILE)
        part[:, at] = dot(joined[...], weight[at, :], ((1,), (1,))).astype(BF16)
        return _

    lax.fori_loop(0, width // TILE, column, 0)


def join_stage(meta, weight, query_grads, pair_grads, riders=()):
    rows = query_grads[0].shape[0]
    width, across = weight.shape
    outs = [
        shaped((rows, across), BF16),
        shaped((rows, width), BF16),
        shaped((8, 2 * MEMBERS * PAIR), F32),
    ]
    if riders:
        half = riders[0][0].shape[0] // 2
        outs += [shaped((half, keep.shape[1]), F32) for keep, _got in riders]
        outs.append(shaped((half, sum(keep.shape[1] for keep, _got in riders)), BF16))
    return pl.pallas_call(
        partial(join_kernel, len(riders)),
        out_shape=outs,
        in_specs=[SM] + [VM] * (1 + 2 * MEMBERS + 2 * len(riders)),
        out_specs=[VM] * len(outs),
        compiler_params=params(),
        cost_estimate=lasting("join_stage"),
        name="join_stage",
    )(meta, weight, *query_grads, *pair_grads, *[part for pair in riders for part in pair])


FIRST_PART = 1024


def joined_first_kernel(meta, x, part, normed, joined, keep, send, vectors, turned):
    rows, width = x.shape
    device = meta[4]
    turn_source(normed, turned, device, X_FIRST, width // DEVICES)
    half = width // 2
    tile = TILE

    def column(t, _):
        at = pl.ds(pl.multiple_of(t * tile, tile), tile)
        keep[:, at] = dot(turned[:half], joined[:, at]).astype(BF16)
        send[:, at] = dot(turned[half:], joined[:, at]).astype(BF16)
        return _

    lax.fori_loop(0, keep.shape[1] // tile, column, 0)
    vectors[...] = jnp.zeros_like(vectors)

    def norm_step(at):
        hat, _scale = normal(x[at, :].astype(F32))
        first = part[at, :].astype(F32)
        vectors[0:1, :] += jnp.sum(first * hat, axis=0, keepdims=True)
        vectors[1:2, :] += jnp.sum(first, axis=0, keepdims=True)

    norm_loop(rows, norm_step)


def joined_first(meta, x, part, normed, joined, deps=()):
    rows, width = x.shape
    half = width // 2
    return pl.pallas_call(
        skipping(joined_first_kernel, 5, len(deps)),
        out_shape=[
            shaped((half, FIRST_PART), BF16),
            shaped((half, FIRST_PART), BF16),
            shaped((8, width), F32),
        ],
        in_specs=[SM] + [VM] * 4 + [ANY] * len(deps),
        out_specs=[VM] * 3,
        scratch_shapes=[pltpu.VMEM((width, rows), BF16)],
        compiler_params=params(),
        cost_estimate=lasting("joined_first"),
        name="joined_first",
    )(meta, x, part, normed, joined, *deps)


def joined_second_kernel(
    meta, normed, joined, vectors, other, sums, c, got_c, e, o, got_eo,
    keep, send, last, contract, expand, output, turned, small,
):
    contract[...] = c[...] + got_c[...].astype(F32)
    inner = e.shape[1]
    expand[...] = e[...] + got_eo[:, :inner].astype(F32)
    output[...] = o[...] + got_eo[:, inner:].astype(F32)
    width = normed.shape[1]
    device = meta[4]
    share = width // DEVICES
    turn_source(normed, turned, device, Z_FIRST, share)
    half = width // 2
    across = joined.shape[1] - FIRST_PART
    tile = TILE

    def column(t, _):
        at = pl.ds(pl.multiple_of(t * tile, tile), tile)
        source = pl.ds(pl.multiple_of(FIRST_PART + t * tile, tile), tile)
        keep[:, at] = dot(turned[:half], joined[:, source]).astype(BF16)
        leave = dot(turned[half:], joined[:, source]).astype(BF16)

        @pl.when(t == 0)
        def _first():
            send[...] = leave

        @pl.when(t == 1)
        def _last():
            last[:, :tile] = leave
        return _

    lax.fori_loop(0, across // tile, column, 0)
    for i in range(width // SEG):
        at = slice(i * SEG, (i + 1) * SEG)
        rows8 = jnp.concatenate(
            [vectors[0:2, at] + other[0:2, at], sums[0:1, at], jnp.zeros((5, SEG), F32)], axis=0
        )
        turn_ordered(in_two(rows8).T, small, i, device, Z_FIRST, share)
    keep[:, across:] = small[:half].astype(BF16)
    last[:, tile:] = small[half:].astype(BF16)


def joined_second(meta, normed, joined, vectors, other, sums, c, got_c, e, o, got_eo):
    rows, width = normed.shape
    half = width // 2
    across = joined.shape[1] - FIRST_PART + SEG
    return pl.pallas_call(
        joined_second_kernel,
        out_shape=[
            shaped((half, across), BF16),
            shaped((half, TILE), BF16),
            shaped((half, across - TILE), BF16),
            shaped(c.shape, F32),
            shaped(e.shape, F32),
            shaped(o.shape, F32),
        ],
        in_specs=[SM] + [VM] * 10,
        out_specs=[VM] * 6,
        scratch_shapes=[pltpu.VMEM((width, rows), BF16), pltpu.VMEM((width, SEG), F32)],
        compiler_params=params(),
        cost_estimate=lasting("joined_second"),
        name="joined_second",
    )(meta, normed, joined, vectors, other, sums, c, got_c, e, o, got_eo)


def input_back_kernel(x, part, other, gains, middle_grad, out):
    def norm_step(at):
        hat, scale = normal(x[at, :].astype(F32))
        first = part[at, :].astype(F32) + other[at, :].astype(F32)
        back = norm_back(hat, scale, first * gains[GAIN_A : GAIN_A + 1])
        out[at, :] = (back + middle_grad[at, :].astype(F32)).astype(BF16)

    norm_loop(x.shape[0], norm_step)


def input_back(x, part, other, gains, middle_grad):
    return pl.pallas_call(
        input_back_kernel,
        out_shape=shaped(x.shape, BF16),
        in_specs=[VM] * 5,
        out_specs=VM,
        compiler_params=params(),
        cost_estimate=lasting("input_back"),
        name="input_back",
    )(x, part, other, gains, middle_grad)


def stack_kernel(*refs):
    out, at = refs[-1], 0
    for ref in refs[:-1]:
        rows = ref.shape[0] // out.shape[1]
        out[at : at + rows, :] = ref[...].astype(F32).reshape(rows, out.shape[1])
        at += rows


def stack_vectors(*vectors):
    width = vectors[0].shape[0]
    rows = sum(vector.shape[0] for vector in vectors) // width
    return pl.pallas_call(
        stack_kernel,
        out_shape=shaped((rows, width), F32),
        in_specs=[VM] * len(vectors),
        out_specs=VM,
        name="stack_vectors",
    )(*vectors)


def swap(value):
    return lax.ppermute(value, "tensor", [(0, 1), (1, 0)])


def to_member(value, d):
    count = lax.axis_size("dp")
    return lax.ppermute(value, "dp", [(i, i ^ d) for i in range(count)])


def to_member_across(value, d):
    count = lax.axis_size("dp")
    pairs = [(i * 2 + t, (i ^ d) * 2 + (1 - t)) for i in range(count) for t in range(2)]
    return lax.ppermute(value, ("dp", "tensor"), pairs)


def to_group(value, by):
    count = lax.axis_size("dp")
    step = by * MEMBERS
    return lax.ppermute(value, "dp", [(i, (i + step) % count) for i in range(count)])


def within(parts):
    return [parts[0]] + [to_member(parts[d], d) for d in range(1, MEMBERS)]


def same_kernel(*refs):
    pass


def after_all(value, *others):
    return pl.pallas_call(
        same_kernel,
        out_shape=shaped(value.shape, value.dtype),
        in_specs=[ANY] * (1 + len(others)),
        out_specs=ANY,
        input_output_aliases={0: 0},
        cost_estimate=lasting("after_all"),
        name="after_all",
    )(value, *others)


def reduce_rows(value):
    return lax.psum_scatter(value, "dp", scatter_dimension=0, tiled=True)


def plain_sum(left, right):
    grad = jnp.einsum("td,tf->df", left, right, preferred_element_type=F32)
    return reduce_rows(grad.astype(BF16)).astype(F32)


def plain_sums(x, part, first_low, joined_grad, sums, cotangent, hidden_low, second_low, pre_grad, branch_low, mixed, feed_vectors, extra):
    hat, _scale = normal(x.astype(F32))
    wide = part.astype(F32)
    vectors = jnp.stack([jnp.sum(wide * hat, axis=0), jnp.sum(wide, axis=0)], axis=0)
    vectors = vectors + swap(vectors)
    small = reduce_rows(jnp.concatenate([feed_vectors[:4], extra, vectors, sums[:1]], axis=0).T)
    return (
        plain_sum(cotangent, hidden_low), plain_sum(second_low, pre_grad),
        plain_sum(branch_low, mixed), plain_sum(first_low, joined_grad),
        small[:, 0], small[:, 1], small[:, 2], small[:, 3], small[:, 4:6].T,
        small[:, 6], small[:, 7], small[:, 8],
    )


def shards(
    activations,
    cotangent,
    parent_slot,
    attention_gain,
    attention_shift,
    joined_weight,
    joined_bias,
    output_weight,
    output_bias,
    feed_gain,
    feed_shift,
    expand_weight,
    expand_bias,
    contract_weight,
    contract_bias,
):
    device = lax.axis_index("dp")
    count = lax.axis_size("dp")
    rank = lax.axis_index("tensor")
    member = lax.rem(device, MEMBERS)
    heads_here = joined_weight.shape[1] // (3 * HD)
    width = activations.shape[1]
    inner = expand_weight.shape[1]
    half = output_weight.shape[0]
    meta = jnp.stack(
        [member, device // MEMBERS, rank * heads_here + 2 * member, rank, device]
    ).astype(jnp.int32)
    slopes = jnp.exp2(-8.0 * jnp.arange(1, H + 1, dtype=F32) / H)

    vectors = stack_vectors(
        attention_gain, attention_shift, feed_gain, feed_shift, output_bias, contract_bias,
        joined_bias, expand_bias,
    )
    first_low, queries, keys, values = project(meta, activations, vectors, joined_weight)
    lists, inner_marks = make_lists(meta, parent_slot)
    keys = within(keys)
    k_up, k_down = pack(lists, keys)
    k_below, k_above = to_group(k_up, 1), to_group(k_down, -1)
    values = within(values)
    v_up, v_down = pack(lists, values, deps=(k_up,))
    v_below, v_above = to_group(v_up, 1), to_group(v_down, -1)
    queries = within(queries)
    table = make_tables(meta, parent_slot, lists, inner_marks, deps=(k_up,))
    other_output_weight = swap(output_weight)
    kept, stats = attend_near(
        table, meta, slopes, queries, keys, values, deps=(k_below, k_above)
    )
    away = (k_below, k_above, v_below, v_above)
    outs, lse = attend_far(
        table, meta, slopes, queries, away, kept, stats, deps=(other_output_weight,)
    )
    hidden_grad = product("hidden_grad", cotangent, contract_weight, True, F32, deps=(outs[0],))
    parts_other = [to_member_across(outs[d], d) for d in range(MEMBERS)]
    parts_own = within(outs)
    mixed, middle, second_low, hidden_low, pre_grad, second_part, bias_sums = feed(
        meta, activations, vectors,
        parts_own, parts_other, output_weight, other_output_weight, expand_weight, hidden_grad,
    )
    second_other = swap(second_part)
    by_halves = count == DEVICES
    if by_halves:
        keep_c, c0, c1, keep_e, e0, e1, feed_part = feed_grads(
            meta, cotangent, hidden_low, second_low, pre_grad, contract_weight
        )
        c0, c1, e0, e1 = (to_member(part, 1) for part in (c0, c1, e0, e1))
    else:
        feed_part = product("feed_part", hidden_low, contract_weight, False, BF16)
    branch_low, feed_vectors, grad_parts = middle_back(
        meta, middle, second_part, second_other, cotangent, vectors, output_weight,
        deps=(feed_part,),
    )
    grad_parts = within(grad_parts)
    feed_other = swap(after_all(feed_part, branch_low))
    fill = ()
    if by_halves:
        (keep_o, send_o), ((keep_c, send_c), (keep_e, send_e)) = output_grads(
            meta, branch_low, mixed, feed_vectors, bias_sums, [(keep_c, c0, c1), (keep_e, e0, e1)]
        )
        got_o, got_c, got_e = to_member(send_o, 1), to_member(send_c, 4), to_member(send_e, 2)
        fill = (keep_o,)
    to_below, to_above, kept_grad = back_far(
        table, meta, slopes, queries, away, outs, grad_parts, lse, deps=fill
    )
    from_above = to_group(to_below, -1)
    from_below = to_group(to_above, 1)
    query_grads, own = back_near(
        table, meta, slopes, queries, keys, values, outs, grad_parts, lse, kept_grad, deps=(feed_other,)
    )
    query_grads = within(query_grads)
    layer_output = (
        middle + (feed_part.astype(F32) + feed_other.astype(F32)) + vectors[CONTRACT_BIAS]
    ).astype(BF16)
    fill = ()
    if by_halves:
        (keep_c, send_c), (keep_e, send_e), (keep_o, send_o) = takes(
            "second_step", [(keep_c, got_c), (keep_e, got_e), (keep_o, got_o)], deps=(own,)
        )
        got_c, got_o = to_member(send_c, 2), to_member(send_o, 2)
        fill = (keep_o,)
    own_pairs = gather_back(
        lists, own, from_above, from_below, deps=tuple(query_grads) + (layer_output,) + fill
    )
    pair_grads = within(own_pairs)
    riders = ()
    if by_halves:
        got_e = to_member(after_all(send_e, own_pairs[0]), 4)
        (keep_c, send_c), (keep_o, send_o) = takes(
            "third_step", [(keep_c, got_c), (keep_o, got_o)], deps=(own_pairs[0],)
        )
        got_c, got_o = to_member(send_c, 8), to_member(send_o, 4)
        riders = ((keep_e, got_e), (keep_o, got_o))
    joined_grad, first_part, joined_bias_sums, *ridden = join_stage(
        meta, joined_weight, query_grads, pair_grads, riders
    )
    if by_halves:
        keep_e, keep_o, send_eo = ridden
        got_eo = to_member(send_eo, 8)
        keep_a, send_a, norm_vectors = joined_first(
            meta, activations, first_part, first_low, joined_grad
        )
        got_a = to_member(send_a, 1)
        norm_other = swap(norm_vectors)
        first_other = swap(after_all(first_part, norm_other))
        keep_b, send_b, last_b, contract_done, expand_done, output_sum = joined_second(
            meta, first_low, joined_grad, norm_vectors, norm_other, joined_bias_sums,
            keep_c, got_c, keep_e, keep_o, got_eo,
        )
        got_b, last_b = to_member(send_b, 1), to_member(last_b, 1)
        keep_a, send_a, keep_b, b1, b2, b3 = first_sums((keep_a, got_a), (keep_b, got_b, last_b))
        got_a = to_member(send_a, 2)
        got_b = [to_member(part, d) for part, d in zip((b1, b2, b3), Z_BLOCKS)]
        keep_a, a1, a2, a3, keep_b, send_b = second_sums((keep_a, got_a), keep_b, got_b)
        got_a = [to_member(part, d) for part, d in zip((a1, a2, a3), Z_BLOCKS)]
        got_b = to_member(send_b, 2)
        done = (contract_done, expand_done) + tuple(
            finish(output_sum, keep_a, got_a, keep_b, got_b)
        )
    else:
        first_other = swap(first_part)
        extra = bias_sums[0].reshape(count, 2, width // count).transpose(1, 0, 2).reshape(2, width)
        done = plain_sums(
            activations, first_part, first_low, joined_grad, joined_bias_sums, cotangent,
            hidden_low, second_low, pre_grad, branch_low, mixed, feed_vectors, extra,
        )
    input_gradient = input_back(activations, first_part, first_other, vectors, branch_low)
    (
        contract_done, expand_done, output_done, joined_done,
        feed_gain_grad, feed_shift_grad, output_bias_grad, contract_bias_grad, expand_bias_grad,
        gain_grad, shift_grad, joined_bias_grad,
    ) = done

    return (
        layer_output,
        input_gradient,
        gain_grad.reshape(-1),
        shift_grad.reshape(-1),
        joined_done,
        joined_bias_grad.reshape(-1, 1),
        output_done,
        output_bias_grad.reshape(-1),
        feed_gain_grad.reshape(-1),
        feed_shift_grad.reshape(-1),
        expand_done,
        expand_bias_grad.reshape(-1, 1),
        contract_done,
        contract_bias_grad.reshape(-1),
    )


def solution(mesh):
    in_specs = (
        P("dp", None),
        P("dp", None),
        P(),
        P(),
        P(),
        P(None, "tensor"),
        P("tensor"),
        P("tensor", None),
        P(),
        P(),
        P(),
        P(None, "tensor"),
        P("tensor"),
        P("tensor", None),
        P(),
    )
    out_specs = (
        P("dp", None),
        P("dp", None),
        P("dp"),
        P("dp"),
        P("dp", "tensor"),
        P("dp", "tensor"),
        P("dp", "tensor"),
        P("dp"),
        P("dp"),
        P("dp"),
        P("dp", "tensor"),
        P("dp", "tensor"),
        P("dp", "tensor"),
        P("dp"),
    )
    return jax.shard_map(shards, mesh=mesh, in_specs=in_specs, out_specs=out_specs, check_vma=False)
```
